32 devices in a mesh: groups: 2 (over x), att: 8 (over z, y), exp: 2 (over core).
Axes of the slice: x: 2, y: 2, z: 4, core: 2. Of those that a mesh axis runs over, the one named last changes fastest.
Arguments:
- query: bfloat16 [2048, 2048], P(('groups', 'att'), 'exp'), parts along dimension 0, may hold values from -9 to 9
- new_key: bfloat16 [2048, 256], P(('groups', 'att'), 'exp'), parts along dimension 0, may hold values from -6 to 6
- new_value: bfloat16 [2048, 256], P(('groups', 'att'), 'exp'), parts along dimension 0, may hold values from -6 to 6
- cache_keys: bfloat16 [2048, 64, 256], P(('groups', 'att'), None, 'exp'), parts along dimension 0, may hold values from -9 to 9
- cache_values: bfloat16 [2048, 64, 256], P(('groups', 'att'), None, 'exp'), parts along dimension 0, may hold values from -6 to 6
- lengths: int32 [2048], P(('groups', 'att')), parts along dimension 0, may hold values from 2 to 64, as said below
- out_proj: bfloat16 [2048, 2880], P('exp'), may hold values from -0.125 to 0.125
- residual: bfloat16 [2048, 2880], P(('groups', 'att', 'exp')), parts along dimension 0, may hold values from -6 to 6
- norm_gain: float32 [2880], replicated, may hold values from 0.25 to 1.75
- router: float32 [2880, 8], replicated, may hold values from -0.21875 to 0.21875
- routes: int32 [2048, 4], P(('groups', 'att', 'exp')), parts along dimension 0, may hold values from 0 to 7, all different within a row; in each aligned block of 64 rows (0 to 63, 64 to 127, ...) at most 64 rows name the same one
- w_gate: bfloat16 [8, 2880, 1440], P('att', None, 'exp'), may hold values from -0.109375 to 0.109375
- w_up: bfloat16 [8, 2880, 1440], P('att', None, 'exp'), may hold values from -0.109375 to 0.109375
- w_down: bfloat16 [8, 1440, 2880], P('att', 'exp'), may hold values from -0.15625 to 0.15625
Outputs:
- mixed: bfloat16 [2048, 2880], P(('groups', 'att', 'exp')), parts along dimension 0
The draws below stay inside these ranges and needn't reach their ends.
There are 2 independent parts, one for each index of `groups`. The reference program is written for one: setup_inputs(seed, part) draws one part's arguments, and reference() takes and returns one part's arrays. A program takes and returns all parts, laid end to end along the dimension named above; an argument that names none is the same for every part. Nothing has to cross between parts.
Inputs may be any that keep to these rules, and one draw needn't show every extreme that they name: `routes`: each row names 4 different experts. Among the 64 rows of one device (aligned blocks in order) no expert is named more than 64 times, and that count is reached in every draw. `lengths`: every eighth request, starting with the first, uses all 64 cached positions.
All inputs are finite; a program needn't handle non-finite values.
Results may differ from the reference program's by a relative error of at most 0.0065.
Values may be sent and summed in bfloat16 or wider, within the bound.
No kernel may reach another device: no remote copies, remote signals or barrier semaphores. Data moves between devices by JAX's collectives and lax.ppermute only.
A program may use at most 128 MiB of HBM per device.

```python
import math
import jax
import jax.numpy as jnp
import numpy as np
from jax import lax

D = 2880
QH = 32
KVH = 4
HEAD = 64
HID = 1440
TOP = 4
CACHE = 64
EXPERTS = 8
ROWS = 1024
ROW_DEV = 64
CAP = 64
N_EXP = 2


def draw_query(key, part):
    shaped = (ROWS, QH * HEAD)
    values = jnp.clip(jax.random.normal(jax.random.fold_in(key, 1), shaped, jnp.float32), -4.0, 4.0)
    return values.astype(jnp.bfloat16)


def draw_cache_keys(key, part):
    shaped = (ROWS, CACHE, KVH * HEAD)
    values = jnp.clip(jax.random.normal(jax.random.fold_in(key, 2), shaped, jnp.float32), -4.0, 4.0)
    return values.astype(jnp.bfloat16)


def draw_lengths(key, part):
    filled = jax.random.randint(jax.random.fold_in(key, 3), (ROWS,), 2, CACHE + 1)
    row_index = jnp.arange(ROWS)
    return jnp.where(row_index % 8 == 0, CACHE, filled).astype(jnp.int32)


def levels(stream_key, extent, split, least, high):
    level = 1.0
    for axis_at, shards_of in split:
        draws = jax.random.uniform(jax.random.fold_in(jax.random.fold_in(stream_key, 6), axis_at), (shards_of,), jnp.float32, least / len(split), high / len(split))
        level = level * jnp.repeat(jnp.exp(draws), extent[axis_at] // shards_of).reshape((-1,) + (1,) * (len(extent) - 1 - axis_at))
    return level


def routed_block(own_key, own, number, rows, count, top, reach, slope):
    sequence = jax.random.permutation(own_key, count)
    packed, common = shares(count, rows * top, reach, slope, True), shares(count, rows * top, reach, slope, False)
    places = jnp.arange(count)

    def named(tallies, rotation):
        used = int((tallies > 0).sum())
        fixed = max(1, used // 4)
        shifted = fixed + (places - fixed + rotation * (used - fixed)) % max(1, count - fixed)
        return jnp.zeros((count,), jnp.int32).at[sequence[jnp.where(places < fixed, places, shifted)]].set(jnp.asarray(tallies, jnp.int32))

    tallies = jnp.where(number % 4 == 0, named(packed, number // 4), named(common, number - number // 4 - 1))
    mixed = jax.random.permutation(jax.random.fold_in(own, 3), count)
    donor, sink = mixed[0:count // 2 * 2:2], mixed[1:count // 2 * 2:2]
    room = jnp.minimum(tallies[donor] - 1, reach - tallies[sink]) // 2
    room = jnp.where((donor == sequence[0]) | (sink == sequence[0]) | (tallies[sink] == 0), 0, jnp.maximum(room, 0))
    shifted = jax.random.randint(jax.random.fold_in(own, 4), (count // 2,), 0, 1 << 20) % (room + 1)
    tallies = tallies.at[donor].add(-shifted).at[sink].add(shifted)
    items = jnp.searchsorted(jnp.cumsum(tallies), jnp.arange(rows * top), side="right").astype(jnp.int32)
    grid = items.reshape(top, rows).T
    grid = grid[jax.random.permutation(jax.random.fold_in(own, 1), rows)]
    rotation = jax.random.randint(jax.random.fold_in(own, 2), (rows, 1), 0, top)
    return jnp.take_along_axis(grid, (jnp.arange(top)[None, :] + rotation) % top, axis=1)


def shares(count, total, reach, lean, full):
    portions = [(1 << 20) // math.isqrt(standing ** lean) + 1 for standing in range(1, count + 1)]
    largest = reach if full else min(reach, max(-(-total // count), total * portions[0] // sum(portions)))
    least = 1 if total - largest >= count - 1 else 0
    counts, rest = [largest] + [least] * (count - 1), total - largest - least * (count - 1)
    while rest > 0:
        movable = [i for i in range(1, count) if counts[i] < largest] or [i for i in range(1, count) if counts[i] < reach]
        whole, left = sum([portions[i] for i in movable]), rest
        for i in movable:
            extra = min(reach - counts[i], max(1, left * portions[i] // whole), rest)
            counts[i] = counts[i] + extra
            rest = rest - extra
    return np.array(counts)


def noise(stream_key, dims, scale, most, pieces=(), dtype=jnp.bfloat16):
    gain = levels(stream_key, dims, pieces, -0.22, 0.18) if pieces else 1.0
    drawn = jax.random.normal(stream_key, dims, jnp.float32) * scale * gain
    return jnp.minimum(jnp.maximum(drawn, -most), most).astype(dtype)


def setup_inputs(seed: int = 0, part: int = 0) -> dict:
    keys = jax.random.split(jax.random.key(seed), 15)
    part_keys = jax.random.split(jax.random.fold_in(keys[14], part), 15)
    query = draw_query(jax.random.fold_in(jax.random.fold_in(keys[14], part), 71), part)
    new_key = noise(part_keys[1], (ROWS, KVH * HEAD), 1.0, 6.0, ((0, 8), (1, 2)))
    new_value = noise(part_keys[2], (ROWS, KVH * HEAD), 1.0, 6.0, ((0, 8), (1, 2)))
    cache_keys = draw_cache_keys(jax.random.fold_in(jax.random.fold_in(keys[14], part), 71), part)
    cache_values = noise(part_keys[4], (ROWS, CACHE, KVH * HEAD), 1.0, 6.0, ((0, 8), (2, 2)))
    lengths = draw_lengths(jax.random.fold_in(jax.random.fold_in(keys[14], part), 71), part)
    out_proj = noise(keys[6], (QH * HEAD, D), (QH * HEAD) ** -0.5, 0.125, ((0, 2),))
    residual = noise(part_keys[7], (ROWS, D), 1.0, 6.0, ((0, 16),))
    norm_gain = jnp.clip(1.0 + 0.15 * jax.random.normal(keys[8], (D,), jnp.float32), 0.25, 1.75)
    router = noise(keys[9], (D, EXPERTS), (D // 4) ** -0.5, 0.21875, (), jnp.float32)
    routes_keys = jax.random.split(jax.random.fold_in(part_keys[10], 1), ROWS // ROW_DEV)
    routes_turns = jax.random.permutation(jax.random.fold_in(part_keys[10], 3), ROWS // ROW_DEV)
    routes = jax.vmap(lambda own, number: routed_block(jax.random.fold_in(part_keys[10], 2), own, number, ROW_DEV, EXPERTS, TOP, CAP, 2))(routes_keys, routes_turns).reshape((ROWS, TOP))
    w_gate = noise(keys[11], (EXPERTS, D, HID), D ** -0.5, 0.109375, ((0, 8), (2, 2)))
    w_up = noise(keys[12], (EXPERTS, D, HID), D ** -0.5, 0.109375, ((0, 8), (2, 2)))
    w_down = noise(keys[13], (EXPERTS, HID, D), HID ** -0.5, 0.15625, ((0, 8), (1, 2)))
    return {"query": query, "new_key": new_key, "new_value": new_value, "cache_keys": cache_keys, "cache_values": cache_values, "lengths": lengths, "out_proj": out_proj, "residual": residual, "norm_gain": norm_gain, "router": router, "routes": routes, "w_gate": w_gate, "w_up": w_up, "w_down": w_down}


def attend(query, new_key, new_value, cache_keys, cache_values, lengths):
    requests = query.shape[0]
    group_size = QH // KVH
    inverse_root = 1.0 / math.sqrt(HEAD)
    queries = query.astype(jnp.float32).reshape(requests, KVH, group_size, HEAD)
    cached_k = cache_keys.astype(jnp.float32).reshape(requests, CACHE, KVH, HEAD)
    cached_v = cache_values.astype(jnp.float32).reshape(requests, CACHE, KVH, HEAD)
    fresh_k = new_key.astype(jnp.float32).reshape(requests, KVH, HEAD)
    fresh_v = new_value.astype(jnp.float32).reshape(requests, KVH, HEAD)
    cached_scores = jnp.einsum('rjgd,rljd->rjgl', queries, cached_k) * inverse_root
    fresh_scores = jnp.einsum('rjgd,rjd->rjg', queries, fresh_k) * inverse_root
    live_mask = jnp.arange(CACHE)[None, :] < lengths[:, None]
    cached_scores = jnp.where(live_mask[:, None, None, :], cached_scores, -1e+30)
    highest = jnp.maximum(lax.optimization_barrier(jnp.max(cached_scores, axis=-1)), fresh_scores)
    cached_exp = jnp.exp(cached_scores - highest[..., None])
    fresh_exp = jnp.exp(fresh_scores - highest)
    totals = lax.optimization_barrier(jnp.sum(cached_exp, axis=-1)) + fresh_exp
    cached_probs = (cached_exp / totals[..., None]).astype(jnp.bfloat16)
    fresh_probs = (fresh_exp / totals).astype(jnp.bfloat16)
    output = jnp.einsum('rjgl,rljd->rjgd', cached_probs.astype(jnp.float32), cached_v)
    output = output + fresh_probs.astype(jnp.float32)[..., None] * fresh_v[:, :, None, :]
    return output.astype(jnp.bfloat16).reshape(requests, QH * HEAD)

def reference(query, new_key, new_value, cache_keys, cache_values, lengths, out_proj, residual, norm_gain, router, routes, w_gate, w_up, w_down):
    attended = attend(query, new_key, new_value, cache_keys, cache_values, lengths)
    hidden_state = residual.astype(jnp.float32) + jnp.dot(attended, out_proj, preferred_element_type=jnp.float32)
    mean_square = lax.optimization_barrier(jnp.mean(hidden_state * hidden_state, axis=-1, keepdims=True))
    normed = (hidden_state * lax.rsqrt(mean_square + 1e-05) * norm_gain).astype(jnp.bfloat16)
    logits = jnp.dot(normed.astype(jnp.float32), router, precision=lax.Precision.HIGHEST)
    chosen_logits = jnp.take_along_axis(logits, routes, axis=1)
    squashed = jax.nn.sigmoid(chosen_logits)
    gate_weights = squashed / lax.optimization_barrier(jnp.sum(squashed, axis=1, keepdims=True))
    flat_routes = routes.reshape(-1)
    most_rows = ROWS // ROW_DEV * CAP
    span = HID // N_EXP

    def one_expert(expert, table):
        picks = jnp.nonzero(flat_routes == expert, size=most_rows, fill_value=ROWS * TOP)[0].astype(jnp.int32)
        source_rows = jnp.minimum(picks // TOP, ROWS - 1).astype(jnp.int32)
        inputs = normed[source_rows]
        gate_part = jnp.dot(inputs, w_gate[expert], preferred_element_type=jnp.float32)
        up_part = jnp.dot(inputs, w_up[expert], preferred_element_type=jnp.float32)
        activated = (jax.nn.silu(gate_part) * up_part).astype(jnp.bfloat16)
        down_matrix = w_down[expert]
        total = jnp.zeros((most_rows, D), jnp.float32)
        for half in range(N_EXP):
            piece = jnp.dot(activated[:, half * span:(half + 1) * span], down_matrix[half * span:(half + 1) * span], preferred_element_type=jnp.float32)
            piece = lax.optimization_barrier(piece.astype(jnp.bfloat16))
            total = total + piece.astype(jnp.float32)
        result = total.astype(jnp.bfloat16)
        return table.at[picks].set(result, mode='drop')
    table = lax.fori_loop(0, EXPERTS, one_expert, jnp.zeros((ROWS * TOP, D), jnp.bfloat16))
    expert_out = table.reshape(ROWS, TOP, D).astype(jnp.float32)
    combined = lax.optimization_barrier(jnp.sum(gate_weights[:, :, None] * expert_out, axis=1))
    return (hidden_state + combined).astype(jnp.bfloat16)
```

```python
import math

import jax
import jax.numpy as jnp
from jax import lax
from jax.experimental import pallas as pl
from jax.experimental.pallas import tpu as pltpu
from jax.sharding import PartitionSpec as P

HEAD = 64
SUB = 8
STEP = 16


def attend_rows(
    queries, fresh_k, fresh_v, keys, values, live, heads, slots, width, cache_len
):
    group_size = heads // slots
    lane = lax.broadcasted_iota(jnp.int32, (SUB, width), 1)
    slot_of_lane = lane // HEAD
    pieces = []
    for head in range(heads):
        block, slot, home = head // slots, head % slots, head // group_size
        piece = queries[:, block * width : (block + 1) * width]
        if slot != home:
            piece = pltpu.roll(piece, ((home - slot) * HEAD) % width, 1)
        pieces.append(jnp.where(slot_of_lane == home, piece, 0.0))
    placed = jnp.stack(pieces, axis=0)
    fresh_scores = jnp.sum(placed * fresh_k[None], axis=-1, keepdims=True)
    rows = placed.reshape(heads * SUB, width).astype(jnp.bfloat16)
    spread = lax.dot_general(
        rows, keys, (((1,), (1,)), ((), ())), preferred_element_type=jnp.float32
    ).reshape(heads, SUB, SUB * cache_len)
    row = lax.broadcasted_iota(jnp.int32, (SUB, width), 0)
    per = width // cache_len
    scores = spread[:, :, :width]
    for part in range(1, SUB // per):
        scores = jnp.where(
            (row // per == part)[None], spread[:, :, part * width : (part + 1) * width], scores
        )
    valid = (lane // cache_len == row % per) & (lane % cache_len < live)
    scores = jnp.where(valid[None], scores, -1e30)
    highest = jnp.maximum(jnp.max(scores, axis=-1, keepdims=True), fresh_scores)
    cached_exp = jnp.exp(scores - highest)
    fresh_exp = jnp.exp(fresh_scores - highest)
    scale = 1.0 / (jnp.sum(cached_exp, axis=-1, keepdims=True) + fresh_exp)
    probs = cached_exp * scale
    fresh_probs = (fresh_exp * scale).astype(jnp.bfloat16).astype(jnp.float32)
    wide = jnp.concatenate(
        [jnp.where((row // per == part)[None], probs, 0.0) for part in range(SUB // per)], axis=-1
    )
    wide = wide.reshape(heads * SUB, SUB * cache_len).astype(jnp.bfloat16)
    output = jnp.dot(wide, values, preferred_element_type=jnp.float32).reshape(heads, SUB, width)
    output = output + fresh_probs * fresh_v[None]
    blocks = []
    for block in range(heads // slots):
        merged = None
        for slot in range(slots):
            head = block * slots + slot
            home = head // group_size
            piece = output[head]
            if slot != home:
                piece = pltpu.roll(piece, ((slot - home) * HEAD) % width, 1)
            merged = piece if merged is None else jnp.where(slot_of_lane == slot, piece, merged)
        blocks.append(merged)
    return jnp.concatenate(blocks, axis=-1)


def attend_kernel(
    where_ref, lengths_ref, q_ref, nk_ref, nv_ref, k_ref, v_ref, w_hbm, out_ref, att_ref, w_ref, sem
):
    step = pl.program_id(0)
    copy = pltpu.make_async_copy(w_hbm, w_ref, sem)

    @pl.when(step == 0)
    def _():
        copy.start()

    width = nk_ref.shape[1]
    slots = width // HEAD
    heads = q_ref.shape[1] // HEAD
    cache_len = k_ref.shape[1]
    first = (where_ref[0] + step) * STEP
    row = lax.broadcasted_iota(jnp.int32, (SUB, width), 0)
    queries = q_ref[...].astype(jnp.float32) * (1.0 / math.sqrt(HEAD))
    fresh_k = nk_ref[...].astype(jnp.float32)
    fresh_v = nv_ref[...].astype(jnp.float32)
    halves = []
    for sub in range(STEP // SUB):
        live = jnp.zeros((SUB, width), jnp.int32)
        for i in range(SUB):
            live = jnp.where(row == i, lengths_ref[first + sub * SUB + i], live)
        span = slice(sub * SUB, (sub + 1) * SUB)
        halves.append(
            attend_rows(
                queries[span],
                fresh_k[span],
                fresh_v[span],
                k_ref[span].reshape(SUB * cache_len, width),
                v_ref[span].reshape(SUB * cache_len, width),
                live,
                heads,
                slots,
                width,
                cache_len,
            )
        )
    att_ref[pl.ds(pl.multiple_of(step * STEP, STEP), STEP), :] = jnp.concatenate(
        halves, axis=0
    ).astype(jnp.bfloat16)

    @pl.when(step == pl.num_programs(0) - 1)
    def _():
        copy.wait()
        out_ref[...] = jnp.dot(att_ref[...], w_ref[...], preferred_element_type=jnp.float32)


def attend_project(
    start, rows, query, new_key, new_value, cache_keys, cache_values, lengths, out_proj
):
    steps = rows // STEP
    width = new_key.shape[1]
    cache_len = cache_keys.shape[1]
    columns = out_proj.shape[1]
    flat = lambda i, where, lengths: (where[0] + i, 0)
    cube = lambda i, where, lengths: (where[0] + i, 0, 0)
    return pl.pallas_call(
        attend_kernel,
        out_shape=jax.ShapeDtypeStruct((rows, columns), jnp.float32),
        grid_spec=pltpu.PrefetchScalarGridSpec(
            num_scalar_prefetch=2,
            grid=(steps,),
            in_specs=[
                pl.BlockSpec((STEP, query.shape[1]), flat),
                pl.BlockSpec((STEP, width), flat),
                pl.BlockSpec((STEP, width), flat),
                pl.BlockSpec((STEP, cache_len, width), cube),
                pl.BlockSpec((STEP, cache_len, width), cube),
                pl.BlockSpec(memory_space=pl.ANY),
            ],
            out_specs=pl.BlockSpec((rows, columns), lambda i, where, lengths: (0, 0)),
            scratch_shapes=[
                pltpu.VMEM((rows, query.shape[1]), jnp.bfloat16),
                pltpu.VMEM(out_proj.shape, jnp.bfloat16),
                pltpu.SemaphoreType.DMA,
            ],
        ),
        compiler_params=pltpu.CompilerParams(
            dimension_semantics=("arbitrary",), vmem_limit_bytes=40 * 1024 * 1024
        ),
        cost_estimate=pl.CostEstimate(
            flops=2 * rows * query.shape[1] * columns,
            bytes_accessed=2 * out_proj.size + 4 * rows * cache_len * width,
            transcendentals=0,
        ),
    )(
        jnp.full((1,), start * steps, jnp.int32),
        lengths,
        query,
        new_key,
        new_value,
        cache_keys,
        cache_values,
        out_proj,
    )


def per_device(
    query,
    new_key,
    new_value,
    cache_keys,
    cache_values,
    lengths,
    out_proj,
    residual,
    norm_gain,
    router,
    routes,
    w_gate,
    w_up,
    w_down,
):
    core = lax.axis_index("exp")
    own_rows, width = residual.shape
    operands = (query, new_key, new_value, cache_keys, cache_values, lengths, out_proj)
    theirs = attend_project(1 - core, own_rows, *operands)
    swapped = lax.ppermute(theirs, "exp", [(0, 1), (1, 0)])
    mine = attend_project(core, own_rows, *operands)
    hidden_state = residual.astype(jnp.float32) + mine + swapped
    mean_square = jnp.mean(hidden_state * hidden_state, axis=-1, keepdims=True)
    normed = (hidden_state * lax.rsqrt(mean_square + 1e-05) * norm_gain).astype(jnp.bfloat16)
    logits = jnp.dot(normed.astype(jnp.float32), router, precision=lax.Precision.HIGHEST)
    experts = router.shape[1]
    chosen = jnp.any(routes[:, :, None] == jnp.arange(experts)[None, None, :], axis=1)
    squashed = jnp.where(chosen, jax.nn.sigmoid(logits), 0.0)
    gates = squashed / jnp.sum(squashed, axis=1, keepdims=True)
    upper = gates.astype(jnp.bfloat16)
    lower = (gates - upper.astype(jnp.float32)).astype(jnp.bfloat16)
    payload = jnp.concatenate([normed, upper, lower], axis=1)
    everything = lax.all_gather(payload, ("att", "exp"), axis=0, tiled=True)
    rows = everything[:, :width]
    expert = lax.axis_index("att")
    weight = lax.dynamic_slice_in_dim(everything, width + expert, 1, 1).astype(jnp.float32)
    weight = weight + lax.dynamic_slice_in_dim(everything, width + experts + expert, 1, 1).astype(
        jnp.float32
    )
    gate_part = jnp.dot(rows, w_gate[0], preferred_element_type=jnp.float32)
    up_part = jnp.dot(rows, w_up[0], preferred_element_type=jnp.float32)
    activated = (jax.nn.silu(gate_part) * up_part).astype(jnp.bfloat16)
    result = jnp.dot(activated, w_down[0], preferred_element_type=jnp.float32)
    weighted = (result * weight).astype(jnp.bfloat16)
    combined = lax.psum_scatter(weighted, ("att", "exp"), scatter_dimension=0, tiled=True)
    return (hidden_state + combined.astype(jnp.float32)).astype(jnp.bfloat16)


def solution(mesh):
    in_specs = (
        P(("groups", "att"), "exp"),
        P(("groups", "att"), "exp"),
        P(("groups", "att"), "exp"),
        P(("groups", "att"), None, "exp"),
        P(("groups", "att"), None, "exp"),
        P(("groups", "att")),
        P("exp", None),
        P(("groups", "att", "exp"), None),
        P(),
        P(),
        P(("groups", "att", "exp"), None),
        P("att", None, "exp"),
        P("att", None, "exp"),
        P("att", "exp", None),
    )
    out_specs = P(("groups", "att", "exp"), None)
    return jax.shard_map(
        per_device, mesh=mesh, in_specs=in_specs, out_specs=out_specs, check_vma=False
    )
```

```python
import math

import jax
import jax.numpy as jnp
from jax import lax
from jax.experimental import pallas as pl
from jax.experimental.pallas import tpu as pltpu
from jax.sharding import PartitionSpec as P

HEAD = 64
SUB = 8
STEP = 16
VMEM = 56 * 1024 * 1024
EXPERT_VMEM = 40 * 1024 * 1024


def attend_rows(
    queries, fresh_k, fresh_v, keys, values, live, heads, slots, width, cache_len
):
    group_size = heads // slots
    lane = lax.broadcasted_iota(jnp.int32, (SUB, width), 1)
    slot_of_lane = lane // HEAD
    pieces = []
    for head in range(heads):
        block, slot, home = head // slots, head % slots, head // group_size
        piece = queries[:, block * width : (block + 1) * width]
        if slot != home:
            piece = pltpu.roll(piece, ((home - slot) * HEAD) % width, 1)
        pieces.append(jnp.where(slot_of_lane == home, piece, 0.0))
    placed = jnp.stack(pieces, axis=0)
    fresh_scores = jnp.sum(placed * fresh_k[None], axis=-1, keepdims=True)
    rows = placed.reshape(heads * SUB, width).astype(jnp.bfloat16)
    spread = lax.dot_general(
        rows, keys, (((1,), (1,)), ((), ())), preferred_element_type=jnp.float32
    ).reshape(heads, SUB, SUB * cache_len)
    row = lax.broadcasted_iota(jnp.int32, (SUB, width), 0)
    per = width // cache_len
    scores = spread[:, :, :width]
    for part in range(1, SUB // per):
        scores = jnp.where(
            (row // per == part)[None], spread[:, :, part * width : (part + 1) * width], scores
        )
    valid = (lane // cache_len == row % per) & (lane % cache_len < live)
    scores = jnp.where(valid[None], scores, -1e30)
    highest = jnp.maximum(jnp.max(scores, axis=-1, keepdims=True), fresh_scores)
    cached_exp = jnp.exp(scores - highest)
    fresh_exp = jnp.exp(fresh_scores - highest)
    scale = 1.0 / (jnp.sum(cached_exp, axis=-1, keepdims=True) + fresh_exp)
    probs = cached_exp * scale
    fresh_probs = (fresh_exp * scale).astype(jnp.bfloat16).astype(jnp.float32)
    wide = jnp.concatenate(
        [jnp.where((row // per == part)[None], probs, 0.0) for part in range(SUB // per)], axis=-1
    )
    wide = wide.reshape(heads * SUB, SUB * cache_len).astype(jnp.bfloat16)
    output = jnp.dot(wide, values, preferred_element_type=jnp.float32).reshape(heads, SUB, width)
    output = output + fresh_probs * fresh_v[None]
    blocks = []
    for block in range(heads // slots):
        merged = None
        for slot in range(slots):
            head = block * slots + slot
            home = head // group_size
            piece = output[head]
            if slot != home:
                piece = pltpu.roll(piece, ((slot - home) * HEAD) % width, 1)
            merged = piece if merged is None else jnp.where(slot_of_lane == slot, piece, merged)
        blocks.append(merged)
    return jnp.concatenate(blocks, axis=-1)


def attend_kernel(
    where_ref, lengths_ref, q_ref, nk_ref, nv_ref, k_ref, v_ref, w_hbm, out_ref, att_ref, w_ref, sem
):
    step = pl.program_id(0)
    copy = pltpu.make_async_copy(w_hbm, w_ref, sem)

    @pl.when(step == 0)
    def _():
        copy.start()

    width = nk_ref.shape[1]
    slots = width // HEAD
    heads = q_ref.shape[1] // HEAD
    cache_len = k_ref.shape[1]
    first = (where_ref[0] + step) * STEP
    row = lax.broadcasted_iota(jnp.int32, (SUB, width), 0)
    queries = q_ref[...].astype(jnp.float32) * (1.0 / math.sqrt(HEAD))
    fresh_k = nk_ref[...].astype(jnp.float32)
    fresh_v = nv_ref[...].astype(jnp.float32)
    halves = []
    for sub in range(STEP // SUB):
        live = jnp.zeros((SUB, width), jnp.int32)
        for i in range(SUB):
            live = jnp.where(row == i, lengths_ref[first + sub * SUB + i], live)
        span = slice(sub * SUB, (sub + 1) * SUB)
        halves.append(
            attend_rows(
                queries[span],
                fresh_k[span],
                fresh_v[span],
                k_ref[span].reshape(SUB * cache_len, width),
                v_ref[span].reshape(SUB * cache_len, width),
                live,
                heads,
                slots,
                width,
                cache_len,
            )
        )
    att_ref[pl.ds(pl.multiple_of(step * STEP, STEP), STEP), :] = jnp.concatenate(
        halves, axis=0
    ).astype(jnp.bfloat16)

    @pl.when(step == pl.num_programs(0) - 1)
    def _():
        copy.wait()
        out_ref[...] = lax.dot_general(
            att_ref[...], w_ref[...], (((1,), (1,)), ((), ())), preferred_element_type=jnp.float32
        )


def attend_project(
    start, rows, query, new_key, new_value, cache_keys, cache_values, lengths, out_proj
):
    steps = rows // STEP
    width = new_key.shape[1]
    cache_len = cache_keys.shape[1]
    columns = out_proj.shape[0]
    flat = lambda i, where, lengths: (where[0] + i, 0)
    cube = lambda i, where, lengths: (where[0] + i, 0, 0)
    return pl.pallas_call(
        attend_kernel,
        out_shape=jax.ShapeDtypeStruct((rows, columns), jnp.float32),
        grid_spec=pltpu.PrefetchScalarGridSpec(
            num_scalar_prefetch=2,
            grid=(steps,),
            in_specs=[
                pl.BlockSpec((STEP, query.shape[1]), flat),
                pl.BlockSpec((STEP, width), flat),
                pl.BlockSpec((STEP, width), flat),
                pl.BlockSpec((STEP, cache_len, width), cube),
                pl.BlockSpec((STEP, cache_len, width), cube),
                pl.BlockSpec(memory_space=pl.ANY),
            ],
            out_specs=pl.BlockSpec((rows, columns), lambda i, where, lengths: (0, 0)),
            scratch_shapes=[
                pltpu.VMEM((rows, query.shape[1]), jnp.bfloat16),
                pltpu.VMEM(out_proj.shape, jnp.bfloat16),
                pltpu.SemaphoreType.DMA,
            ],
        ),
        compiler_params=pltpu.CompilerParams(
            dimension_semantics=("arbitrary",), vmem_limit_bytes=VMEM
        ),
        cost_estimate=pl.CostEstimate(
            flops=2 * rows * query.shape[1] * columns,
            bytes_accessed=2 * out_proj.size + 4 * rows * cache_len * width,
            transcendentals=0,
        ),
    )(
        jnp.full((1,), start * steps, jnp.int32),
        lengths,
        query,
        new_key,
        new_value,
        cache_keys,
        cache_values,
        out_proj,
    )


def norm_kernel(
    mine_ref, swapped_ref, residual_ref, gain_ref, router_ref, routes_ref, hidden_ref, payload_ref
):
    hidden = residual_ref[...].astype(jnp.float32) + (mine_ref[...] + swapped_ref[...])
    hidden_ref[...] = hidden
    rows, width = hidden.shape
    mean_square = jnp.sum(hidden * hidden, axis=-1, keepdims=True) * (1.0 / width)
    normed = (hidden * lax.rsqrt(mean_square + 1e-05) * gain_ref[...]).astype(jnp.bfloat16)
    payload_ref[:, :width] = normed
    rest = router_ref[...]
    experts = rest.shape[0]
    terms = []
    for _ in range(3):
        term = rest.astype(jnp.bfloat16).astype(jnp.float32)
        terms.append(term)
        rest = rest - term
    parts = lax.dot_general(
        jnp.concatenate(terms, axis=0).astype(jnp.bfloat16),
        normed,
        (((1,), (1,)), ((), ())),
        preferred_element_type=jnp.float32,
    )
    logits = parts[:experts] + parts[experts : 2 * experts] + parts[2 * experts :]
    number = lax.broadcasted_iota(jnp.int32, (experts, rows), 0)
    chosen = number == routes_ref[0:1, :]
    for k in range(1, routes_ref.shape[0]):
        chosen = chosen | (number == routes_ref[k : k + 1, :])
    squashed = jnp.where(chosen, 1.0 / (1.0 + jnp.exp(-logits)), 0.0)
    gates = squashed / jnp.sum(squashed, axis=0, keepdims=True)
    upper = gates.astype(jnp.bfloat16).astype(jnp.float32)
    both = jnp.concatenate([upper, gates - upper], axis=0).astype(jnp.bfloat16)
    tail = payload_ref.shape[1] - width
    place = lax.broadcasted_iota(jnp.int32, (2 * experts, tail), 0)
    lane = lax.broadcasted_iota(jnp.int32, (2 * experts, tail), 1)
    placed = lax.dot_general(
        both,
        (place == lane).astype(jnp.bfloat16),
        (((0,), (0,)), ((), ())),
        preferred_element_type=jnp.float32,
    )
    payload_ref[:, width:] = placed.astype(jnp.bfloat16)


def norm_route(mine, swapped, residual, norm_gain, router, routes):
    rows, width = residual.shape
    experts = router.shape[1]
    wide = -(-(width + 2 * experts) // 128) * 128
    return pl.pallas_call(
        norm_kernel,
        out_shape=(
            jax.ShapeDtypeStruct((rows, width), jnp.float32),
            jax.ShapeDtypeStruct((rows, wide), jnp.bfloat16),
        ),
        compiler_params=pltpu.CompilerParams(vmem_limit_bytes=EXPERT_VMEM),
    )(mine, swapped, residual, norm_gain[None, :], router.T, routes.T)


def expert_kernel(count, experts, which_ref, *refs):
    blocks, refs = refs[:count], refs[count:]
    gate_hbm, up_hbm, down_hbm = refs[:3]
    outs, refs = refs[3 : 3 + count], refs[3 + count :]
    gate_ref, up_ref, down_ref, act_ref, sems = refs
    hidden, width = down_ref.shape
    spans = [(at, min(256, hidden - at)) for at in range(0, hidden, 256)]
    copies = []
    for i, (at, size) in enumerate(spans):
        span = pl.ds(at, size)
        copies.append(pltpu.make_async_copy(gate_hbm.at[0, span], gate_ref.at[span], sems.at[2 * i]))
        copies.append(pltpu.make_async_copy(up_hbm.at[0, span], up_ref.at[span], sems.at[2 * i + 1]))
    last = pltpu.make_async_copy(down_hbm.at[0], down_ref, sems.at[2 * len(spans)])
    for copy in copies + [last]:
        copy.start()
    rows = jnp.concatenate([block[...] for block in blocks], axis=0)
    base = width // 128 * 128
    tail = rows[:, base:].astype(jnp.float32)
    lane = lax.broadcasted_iota(jnp.int32, tail.shape, 1) - (width - base)
    named = (lane == which_ref[0]) | (lane == which_ref[0] + experts)
    weight = jnp.sum(jnp.where(named, tail, 0.0), axis=-1, keepdims=True)
    inputs = rows[:, :width]
    across = (((1,), (1,)), ((), ()))
    for i, (at, size) in enumerate(spans):
        span = pl.ds(at, size)
        copies[2 * i].wait()
        gate = lax.dot_general(
            inputs, gate_ref[span, :], across, preferred_element_type=jnp.float32
        )
        copies[2 * i + 1].wait()
        up = lax.dot_general(inputs, up_ref[span, :], across, preferred_element_type=jnp.float32)
        act_ref[:, span] = (gate / (1.0 + jnp.exp(-gate)) * up).astype(jnp.bfloat16)
    last.wait()
    for at in range(0, width, 768):
        size = min(768, width - at)
        part = jnp.dot(
            act_ref[...], down_ref[:, at : at + size], preferred_element_type=jnp.float32
        )
        part = (part * weight).astype(jnp.bfloat16)
        first = 0
        for out in outs:
            out[:, at : at + size] = part[first : first + out.shape[0]]
            first += out.shape[0]


def run_expert(which, blocks, gate_t, up_t, down, experts):
    _, hidden, width = down.shape
    rows = sum(block.shape[0] for block in blocks)
    count = len(blocks)
    spans = -(-hidden // 256)
    hbm = pl.BlockSpec(memory_space=pl.ANY)
    vmem = pl.BlockSpec(memory_space=pltpu.VMEM)
    return pl.pallas_call(
        lambda *refs: expert_kernel(count, experts, *refs),
        out_shape=[jax.ShapeDtypeStruct((b.shape[0], width), jnp.bfloat16) for b in blocks],
        in_specs=[pl.BlockSpec(memory_space=pltpu.SMEM)] + [vmem] * count + [hbm] * 3,
        out_specs=[vmem] * count,
        scratch_shapes=[
            pltpu.VMEM((hidden, width), jnp.bfloat16),
            pltpu.VMEM((hidden, width), jnp.bfloat16),
            pltpu.VMEM((hidden, width), jnp.bfloat16),
            pltpu.VMEM((rows, hidden), jnp.bfloat16),
            pltpu.SemaphoreType.DMA((2 * spans + 1,)),
        ],
        compiler_params=pltpu.CompilerParams(vmem_limit_bytes=EXPERT_VMEM),
        cost_estimate=pl.CostEstimate(
            flops=6 * rows * hidden * width, bytes_accessed=6 * hidden * width, transcendentals=0
        ),
    )(which, *blocks, gate_t, up_t, down)


def ring_pairs(chips, cores, turn):
    order = list(range(0, chips, 2)) + list(range(1, chips, 2))[::-1]
    return [
        (order[p] * cores + core, order[(p + turn) % chips] * cores + core)
        for p in range(chips)
        for core in range(cores)
    ]


def add_up(*terms):
    total = terms[0].astype(jnp.float32)
    for term in terms[1:]:
        total = total + term.astype(jnp.float32)
    return total


def per_device(
    query,
    new_key,
    new_value,
    cache_keys,
    cache_values,
    lengths,
    out_proj,
    residual,
    norm_gain,
    router,
    routes,
    w_gate,
    w_up,
    w_down,
):
    chips, cores = lax.axis_size("att"), lax.axis_size("exp")
    core = lax.axis_index("exp")
    own_rows = residual.shape[0]
    ring = ("att", "exp")

    def send_right(x):
        return lax.ppermute(x, ring, ring_pairs(chips, cores, 1))

    def send_left(x):
        return lax.ppermute(x, ring, ring_pairs(chips, cores, -1))

    def swap(x):
        return lax.ppermute(x, "exp", [(0, 1), (1, 0)])

    operands = (query, new_key, new_value, cache_keys, cache_values, lengths, out_proj.T)
    theirs = attend_project(1 - core, own_rows, *operands)
    swapped = swap(theirs)
    mine = attend_project(core, own_rows, *operands)
    hidden_state, payload = norm_route(mine, swapped, residual, norm_gain, router, routes)

    gate_t, up_t = w_gate.transpose(0, 2, 1), w_up.transpose(0, 2, 1)
    which = jnp.full((1,), lax.axis_index("att"), jnp.int32)
    experts = router.shape[1]

    def expert(*blocks):
        return run_expert(which, blocks, gate_t, up_t, w_down, experts)

    far = chips // 2
    middle = own_rows // 2
    from_left, from_right = [payload], [payload]
    for k in range(1, far + 1):
        right, left = from_left[-1], from_right[-1]
        if k == far:
            right, left = right[:middle], left[middle:]
        from_left.append(send_right(right))
        from_right.append(send_left(left))
    own, own_other = expert(payload, swap(payload))
    own_sum = add_up(own, swap(own_other))
    sums = [None]
    for k in range(1, far + 1):
        a, b = from_left[k], from_right[k]
        kept_a, other_a, kept_b, other_b = expert(a, swap(a), b, swap(b))
        sums.append(((kept_a, swap(other_a)), (kept_b, swap(other_b))))
    back_a = add_up(*sums[far][0]).astype(jnp.bfloat16)
    back_b = add_up(*sums[far][1]).astype(jnp.bfloat16)
    for k in range(far - 1, -1, -1):
        got_a, got_b = send_left(back_a), send_right(back_b)
        if k == far - 1:
            got_a = jnp.pad(got_a, ((0, own_rows - middle), (0, 0)))
            got_b = jnp.pad(got_b, ((middle, 0), (0, 0)))
        if k > 0:
            back_a = add_up(*sums[k][0], got_a).astype(jnp.bfloat16)
            back_b = add_up(*sums[k][1], got_b).astype(jnp.bfloat16)
    combined = own_sum + add_up(got_a, got_b)
    return (hidden_state + combined).astype(jnp.bfloat16)


def solution(mesh):
    in_specs = (
        P(("groups", "att"), "exp"),
        P(("groups", "att"), "exp"),
        P(("groups", "att"), "exp"),
        P(("groups", "att"), None, "exp"),
        P(("groups", "att"), None, "exp"),
        P(("groups", "att")),
        P("exp", None),
        P(("groups", "att", "exp"), None),
        P(),
        P(),
        P(("groups", "att", "exp"), None),
        P("att", None, "exp"),
        P("att", None, "exp"),
        P("att", "exp", None),
    )
    out_specs = P(("groups", "att", "exp"), None)
    return jax.shard_map(
        per_device, mesh=mesh, in_specs=in_specs, out_specs=out_specs, check_vma=False
    )
```

```python
import math

import jax
import jax.numpy as jnp
from jax import lax
from jax.experimental import pallas as pl
from jax.experimental.pallas import tpu as pltpu
from jax.sharding import PartitionSpec as P

HEAD = 64
SUB = 8
STEP = 16
VMEM = 56 * 1024 * 1024
EXPERT_VMEM = 56 * 1024 * 1024


def attend_rows(
    queries, fresh_k, fresh_v, keys, values, live, heads, slots, width, cache_len
):
    group_size = heads // slots
    lane = lax.broadcasted_iota(jnp.int32, (SUB, width), 1)
    slot_of_lane = lane // HEAD
    pieces = []
    for head in range(heads):
        block, slot, home = head // slots, head % slots, head // group_size
        piece = queries[:, block * width : (block + 1) * width]
        if slot != home:
            piece = pltpu.roll(piece, ((home - slot) * HEAD) % width, 1)
        pieces.append(jnp.where(slot_of_lane == home, piece, 0.0))
    placed = jnp.stack(pieces, axis=0)
    fresh_scores = jnp.sum(placed * fresh_k[None], axis=-1, keepdims=True)
    rows = placed.reshape(heads * SUB, width).astype(jnp.bfloat16)
    spread = lax.dot_general(
        rows, keys, (((1,), (1,)), ((), ())), preferred_element_type=jnp.float32
    ).reshape(heads, SUB, SUB * cache_len)
    row = lax.broadcasted_iota(jnp.int32, (SUB, width), 0)
    per = width // cache_len
    scores = spread[:, :, :width]
    for part in range(1, SUB // per):
        scores = jnp.where(
            (row // per == part)[None], spread[:, :, part * width : (part + 1) * width], scores
        )
    valid = (lane // cache_len == row % per) & (lane % cache_len < live)
    scores = jnp.where(valid[None], scores, -1e30)
    highest = jnp.maximum(jnp.max(scores, axis=-1, keepdims=True), fresh_scores)
    cached_exp = jnp.exp(scores - highest)
    fresh_exp = jnp.exp(fresh_scores - highest)
    scale = 1.0 / (jnp.sum(cached_exp, axis=-1, keepdims=True) + fresh_exp)
    probs = cached_exp * scale
    fresh_probs = (fresh_exp * scale).astype(jnp.bfloat16).astype(jnp.float32)
    wide = jnp.concatenate(
        [jnp.where((row // per == part)[None], probs, 0.0) for part in range(SUB // per)], axis=-1
    )
    wide = wide.reshape(heads * SUB, SUB * cache_len).astype(jnp.bfloat16)
    output = jnp.dot(wide, values, preferred_element_type=jnp.float32).reshape(heads, SUB, width)
    output = output + fresh_probs * fresh_v[None]
    blocks = []
    for block in range(heads // slots):
        merged = None
        for slot in range(slots):
            head = block * slots + slot
            home = head // group_size
            piece = output[head]
            if slot != home:
                piece = pltpu.roll(piece, ((slot - home) * HEAD) % width, 1)
            merged = piece if merged is None else jnp.where(slot_of_lane == slot, piece, merged)
        blocks.append(merged)
    return jnp.concatenate(blocks, axis=-1)


def attend_kernel(
    where_ref, lengths_ref, q_ref, nk_ref, nv_ref, k_ref, v_ref, w_hbm, out_ref, att_ref, w_ref, sem
):
    step = pl.program_id(0)
    copy = pltpu.make_async_copy(w_hbm, w_ref, sem)

    @pl.when(step == 0)
    def _():
        copy.start()

    width = nk_ref.shape[1]
    slots = width // HEAD
    heads = q_ref.shape[1] // HEAD
    cache_len = k_ref.shape[1]
    first = (where_ref[0] + step) * STEP
    row = lax.broadcasted_iota(jnp.int32, (SUB, width), 0)
    queries = q_ref[...].astype(jnp.float32) * (1.0 / math.sqrt(HEAD))
    fresh_k = nk_ref[...].astype(jnp.float32)
    fresh_v = nv_ref[...].astype(jnp.float32)
    halves = []
    for sub in range(STEP // SUB):
        live = jnp.zeros((SUB, width), jnp.int32)
        for i in range(SUB):
            live = jnp.where(row == i, lengths_ref[first + sub * SUB + i], live)
        span = slice(sub * SUB, (sub + 1) * SUB)
        halves.append(
            attend_rows(
                queries[span],
                fresh_k[span],
                fresh_v[span],
                k_ref[span].reshape(SUB * cache_len, width),
                v_ref[span].reshape(SUB * cache_len, width),
                live,
                heads,
                slots,
                width,
                cache_len,
            )
        )
    att_ref[pl.ds(pl.multiple_of(step * STEP, STEP), STEP), :] = jnp.concatenate(
        halves, axis=0
    ).astype(jnp.bfloat16)

    @pl.when(step == pl.num_programs(0) - 1)
    def _():
        copy.wait()
        columns = w_ref.shape[0]
        for at in range(0, columns, 768):
            size = min(768, columns - at)
            turned = lax.dot_general(
                w_ref[at : at + size, :],
                att_ref[...],
                (((1,), (1,)), ((), ())),
                preferred_element_type=jnp.float32,
            )
            out_ref[:, at : at + size] = turned.T


def attend_project(
    start, rows, query, new_key, new_value, cache_keys, cache_values, lengths, out_proj
):
    steps = rows // STEP
    width = new_key.shape[1]
    cache_len = cache_keys.shape[1]
    columns = out_proj.shape[0]
    flat = lambda i, where, lengths: (where[0] + i, 0)
    cube = lambda i, where, lengths: (where[0] + i, 0, 0)
    return pl.pallas_call(
        attend_kernel,
        out_shape=jax.ShapeDtypeStruct((rows, columns), jnp.float32),
        grid_spec=pltpu.PrefetchScalarGridSpec(
            num_scalar_prefetch=2,
            grid=(steps,),
            in_specs=[
                pl.BlockSpec((STEP, query.shape[1]), flat),
                pl.BlockSpec((STEP, width), flat),
                pl.BlockSpec((STEP, width), flat),
                pl.BlockSpec((STEP, cache_len, width), cube),
                pl.BlockSpec((STEP, cache_len, width), cube),
                pl.BlockSpec(memory_space=pl.ANY),
            ],
            out_specs=pl.BlockSpec((rows, columns), lambda i, where, lengths: (0, 0)),
            scratch_shapes=[
                pltpu.VMEM((rows, query.shape[1]), jnp.bfloat16),
                pltpu.VMEM(out_proj.shape, jnp.bfloat16),
                pltpu.SemaphoreType.DMA,
            ],
        ),
        compiler_params=pltpu.CompilerParams(
            dimension_semantics=("arbitrary",), vmem_limit_bytes=VMEM
        ),
        cost_estimate=pl.CostEstimate(
            flops=2 * rows * query.shape[1] * columns,
            bytes_accessed=2 * out_proj.size + 4 * rows * cache_len * width,
            transcendentals=0,
        ),
    )(
        jnp.full((1,), start * steps, jnp.int32),
        lengths,
        query,
        new_key,
        new_value,
        cache_keys,
        cache_values,
        out_proj,
    )


def norm_kernel(
    mine_ref, swapped_ref, residual_ref, gain_ref, router_ref, routes_ref, hidden_ref, payload_ref
):
    hidden = residual_ref[...].astype(jnp.float32) + (mine_ref[...] + swapped_ref[...])
    hidden_ref[...] = hidden
    rows, width = hidden.shape
    mean_square = jnp.sum(hidden * hidden, axis=-1, keepdims=True) * (1.0 / width)
    normed = (hidden * lax.rsqrt(mean_square + 1e-05) * gain_ref[...]).astype(jnp.bfloat16)
    payload_ref[:, :width] = normed
    rest = router_ref[...]
    experts = rest.shape[0]
    terms = []
    for _ in range(3):
        term = rest.astype(jnp.bfloat16).astype(jnp.float32)
        terms.append(term)
        rest = rest - term
    parts = lax.dot_general(
        jnp.concatenate(terms, axis=0).astype(jnp.bfloat16),
        normed,
        (((1,), (1,)), ((), ())),
        preferred_element_type=jnp.float32,
    )
    logits = parts[:experts] + parts[experts : 2 * experts] + parts[2 * experts :]
    number = lax.broadcasted_iota(jnp.int32, (experts, rows), 0)
    chosen = number == routes_ref[0:1, :]
    for k in range(1, routes_ref.shape[0]):
        chosen = chosen | (number == routes_ref[k : k + 1, :])
    squashed = jnp.where(chosen, 1.0 / (1.0 + jnp.exp(-logits)), 0.0)
    gates = squashed / jnp.sum(squashed, axis=0, keepdims=True)
    upper = gates.astype(jnp.bfloat16).astype(jnp.float32)
    both = jnp.concatenate([upper, gates - upper], axis=0).astype(jnp.bfloat16)
    tail = payload_ref.shape[1] - width
    place = lax.broadcasted_iota(jnp.int32, (2 * experts, tail), 0)
    lane = lax.broadcasted_iota(jnp.int32, (2 * experts, tail), 1)
    placed = lax.dot_general(
        both,
        (place == lane).astype(jnp.bfloat16),
        (((0,), (0,)), ((), ())),
        preferred_element_type=jnp.float32,
    )
    payload_ref[:, width:] = placed.astype(jnp.bfloat16)


def norm_route(mine, swapped, residual, norm_gain, router, routes):
    rows, width = residual.shape
    experts = router.shape[1]
    wide = -(-(width + 2 * experts) // 128) * 128
    return pl.pallas_call(
        norm_kernel,
        out_shape=(
            jax.ShapeDtypeStruct((rows, width), jnp.float32),
            jax.ShapeDtypeStruct((rows, wide), jnp.bfloat16),
        ),
        compiler_params=pltpu.CompilerParams(vmem_limit_bytes=EXPERT_VMEM),
    )(mine, swapped, residual, norm_gain[None, :], router.T, routes.T)


def expert_kernel(count, experts, which_ref, *refs):
    blocks, refs = refs[:count], refs[count:]
    gate_hbm, up_hbm, down_hbm = refs[:3]
    outs, refs = refs[3 : 3 + count], refs[3 + count :]
    gate_ref, up_ref, down_ref, act_ref, sems = refs
    hidden, width = down_ref.shape
    spans = [(at, min(256, hidden - at)) for at in range(0, hidden, 256)]
    copies = []
    for i, (at, size) in enumerate(spans):
        span = pl.ds(at, size)
        copies.append(pltpu.make_async_copy(gate_hbm.at[0, span], gate_ref.at[span], sems.at[2 * i]))
        copies.append(pltpu.make_async_copy(up_hbm.at[0, span], up_ref.at[span], sems.at[2 * i + 1]))
    last = pltpu.make_async_copy(down_hbm.at[0], down_ref, sems.at[2 * len(spans)])
    for copy in copies + [last]:
        copy.start()
    rows = jnp.concatenate([block[...] for block in blocks], axis=0)
    base = width // 128 * 128
    tail = rows[:, base:].astype(jnp.float32)
    lane = lax.broadcasted_iota(jnp.int32, tail.shape, 1) - (width - base)
    named = (lane == which_ref[0]) | (lane == which_ref[0] + experts)
    weight = jnp.sum(jnp.where(named, tail, 0.0), axis=-1, keepdims=True)
    turned = rows[:, :width].T
    for i, (at, size) in enumerate(spans):
        span = slice(at, at + size)
        copies[2 * i].wait()
        gate = jnp.dot(gate_ref[span, :], turned, preferred_element_type=jnp.float32)
        copies[2 * i + 1].wait()
        up = jnp.dot(up_ref[span, :], turned, preferred_element_type=jnp.float32)
        act_ref[:, span] = (gate / (1.0 + jnp.exp(-gate)) * up).T.astype(jnp.bfloat16)
    last.wait()
    for at in range(0, width, 768):
        size = min(768, width - at)
        part = jnp.dot(
            act_ref[...], down_ref[:, at : at + size], preferred_element_type=jnp.float32
        )
        part = (part * weight).astype(jnp.bfloat16)
        first = 0
        for out in outs:
            out[:, at : at + size] = part[first : first + out.shape[0]]
            first += out.shape[0]


def run_expert(which, blocks, gate_t, up_t, down, experts):
    _, hidden, width = down.shape
    rows = sum(block.shape[0] for block in blocks)
    count = len(blocks)
    spans = -(-hidden // 256)
    hbm = pl.BlockSpec(memory_space=pl.ANY)
    vmem = pl.BlockSpec(memory_space=pltpu.VMEM)
    return pl.pallas_call(
        lambda *refs: expert_kernel(count, experts, *refs),
        out_shape=[jax.ShapeDtypeStruct((b.shape[0], width), jnp.bfloat16) for b in blocks],
        in_specs=[pl.BlockSpec(memory_space=pltpu.SMEM)] + [vmem] * count + [hbm] * 3,
        out_specs=[vmem] * count,
        scratch_shapes=[
            pltpu.VMEM((hidden, width), jnp.bfloat16),
            pltpu.VMEM((hidden, width), jnp.bfloat16),
            pltpu.VMEM((hidden, width), jnp.bfloat16),
            pltpu.VMEM((rows, hidden), jnp.bfloat16),
            pltpu.SemaphoreType.DMA((2 * spans + 1,)),
        ],
        compiler_params=pltpu.CompilerParams(vmem_limit_bytes=EXPERT_VMEM),
        cost_estimate=pl.CostEstimate(
            flops=6 * rows * hidden * width, bytes_accessed=6 * hidden * width, transcendentals=0
        ),
    )(which, *blocks, gate_t, up_t, down)


def total_of(terms, out_ref):
    whole = [term for term in terms if not isinstance(term, tuple)]
    total = whole[0][...].astype(jnp.float32)
    for term in whole[1:]:
        total = total + term[...].astype(jnp.float32)
    rows = out_ref.shape[0]
    for term in terms:
        if isinstance(term, tuple):
            ref, first = term
            size = ref.shape[0]
            pieces = []
            if first:
                pieces.append(total[:first])
            pieces.append(total[first : first + size] + ref[...].astype(jnp.float32))
            if first + size < rows:
                pieces.append(total[first + size :])
            total = jnp.concatenate(pieces, axis=0)
    out_ref[...] = total.astype(out_ref.dtype)


def add_kernel(firsts, *refs):
    ins, outs = refs[: len(refs) - len(firsts)], refs[len(refs) - len(firsts) :]
    each = len(ins) // len(firsts)
    for i, (first, out) in enumerate(zip(firsts, outs)):
        terms = list(ins[i * each : (i + 1) * each])
        if terms[-1].shape != out.shape:
            terms[-1] = (terms[-1], first)
        total_of(terms, out)


def add_all(*sums, firsts=None, dtype=jnp.bfloat16):
    firsts = firsts or (0,) * len(sums)
    return pl.pallas_call(
        lambda *refs: add_kernel(firsts, *refs),
        out_shape=[jax.ShapeDtypeStruct(terms[0].shape, dtype) for terms in sums],
        compiler_params=pltpu.CompilerParams(vmem_limit_bytes=EXPERT_VMEM),
    )(*[term for terms in sums for term in terms])


def ring_pairs(chips, cores, turn):
    order = list(range(0, chips, 2)) + list(range(1, chips, 2))[::-1]
    return [
        (order[p] * cores + core, order[(p + turn) % chips] * cores + core)
        for p in range(chips)
        for core in range(cores)
    ]


def per_device(
    query,
    new_key,
    new_value,
    cache_keys,
    cache_values,
    lengths,
    out_proj,
    residual,
    norm_gain,
    router,
    routes,
    w_gate,
    w_up,
    w_down,
):
    chips, cores = lax.axis_size("att"), lax.axis_size("exp")
    core = lax.axis_index("exp")
    own_rows = residual.shape[0]
    ring = ("att", "exp")

    def send_right(x):
        return lax.ppermute(x, ring, ring_pairs(chips, cores, 1))

    def send_left(x):
        return lax.ppermute(x, ring, ring_pairs(chips, cores, -1))

    def swap(x):
        return lax.ppermute(x, "exp", [(0, 1), (1, 0)])

    operands = (query, new_key, new_value, cache_keys, cache_values, lengths, out_proj.T)
    theirs = attend_project(1 - core, own_rows, *operands)
    swapped = swap(theirs)
    mine = attend_project(core, own_rows, *operands)
    hidden_state, payload = norm_route(mine, swapped, residual, norm_gain, router, routes)

    gate_t, up_t = w_gate.transpose(0, 2, 1), w_up.transpose(0, 2, 1)
    which = jnp.full((1,), lax.axis_index("att"), jnp.int32)
    experts = router.shape[1]

    def expert(*blocks):
        return run_expert(which, blocks, gate_t, up_t, w_down, experts)

    far = chips // 2
    middle = own_rows // 2
    own, own_other = expert(payload, swap(payload))
    sums = [(own, swap(own_other))]
    done = [own, own_other]
    right = left = payload
    for k in range(1, far + 1):
        if k == far:
            right, left = right[:middle], left[middle:]
        right, left = send_right(right), send_left(left)
        right, left, *done = lax.optimization_barrier((right, left, *done))
        done = expert(right, swap(right), left, swap(left))
        sums.append((done[0], swap(done[1]), done[2], swap(done[3])))
    back_a, back_b = add_all(sums[far][:2], sums[far][2:])
    for k in range(far - 1, -1, -1):
        got_a, got_b = send_left(back_a), send_right(back_b)
        if k > 0:
            back_a, back_b = add_all(
                (*sums[k][:2], got_a), (*sums[k][2:], got_b), firsts=(0, middle)
            )
    if got_a.shape[0] != own_rows:
        got_a, got_b = jnp.concatenate([got_a, got_b], axis=0), jnp.zeros_like(own)
    return add_all((hidden_state, *sums[0], got_a, got_b))[0]


def solution(mesh):
    in_specs = (
        P(("groups", "att"), "exp"),
        P(("groups", "att"), "exp"),
        P(("groups", "att"), "exp"),
        P(("groups", "att"), None, "exp"),
        P(("groups", "att"), None, "exp"),
        P(("groups", "att")),
        P("exp", None),
        P(("groups", "att", "exp"), None),
        P(),
        P(),
        P(("groups", "att", "exp"), None),
        P("att", None, "exp"),
        P("att", None, "exp"),
        P("att", "exp", None),
    )
    out_specs = P(("groups", "att", "exp"), None)
    return jax.shard_map(
        per_device, mesh=mesh, in_specs=in_specs, out_specs=out_specs, check_vma=False
    )
```

```python
import math

import jax
import jax.numpy as jnp
from jax import lax
from jax.experimental import pallas as pl
from jax.experimental.pallas import tpu as pltpu
from jax.sharding import PartitionSpec as P

HEAD = 64
SUB = 8
STEP = 16
GRANT = 16 * 1024 * 1024
ACROSS = (((1,), (1,)), ((), ()))


def attend_rows(queries, fresh_k, fresh_v, keys, values, live, offset, heads, slots, cache_len):
    width = keys.shape[1]
    group_size = heads // slots
    slot_of_lane = lax.broadcasted_iota(jnp.int32, (SUB, width), 1) // HEAD
    pieces = []
    for head in range(heads):
        block, slot, home = head // slots, head % slots, head // group_size
        piece = queries[:, block * width : (block + 1) * width]
        if slot != home:
            piece = pltpu.roll(piece, ((home - slot) * HEAD) % width, 1)
        pieces.append(jnp.where(slot_of_lane == home, piece, 0.0))
    rows = jnp.concatenate(pieces, axis=0).astype(jnp.bfloat16)
    count = heads * SUB
    request = lax.broadcasted_iota(jnp.int32, (cache_len, count), 1) % SUB
    place = lax.broadcasted_iota(jnp.int32, (cache_len, count), 0)
    spread = lax.dot_general(keys, rows, ACROSS, preferred_element_type=jnp.float32)
    scores = spread[:cache_len]
    for r in range(1, SUB):
        scores = jnp.where(request == r, spread[r * cache_len : (r + 1) * cache_len], scores)
    scores = jnp.where(place < live, scores, -1e30)
    fresh = lax.dot_general(fresh_k, rows, ACROSS, preferred_element_type=jnp.float32)
    fresh_place = lax.broadcasted_iota(jnp.int32, fresh.shape, 0)
    fresh_own = fresh_place == offset + lax.broadcasted_iota(jnp.int32, fresh.shape, 1) % SUB
    fresh_scores = jnp.sum(jnp.where(fresh_own, fresh, 0.0), axis=0, keepdims=True)
    highest = jnp.maximum(jnp.max(scores, axis=0, keepdims=True), fresh_scores)
    cached_exp = jnp.exp(scores - highest)
    fresh_exp = jnp.exp(fresh_scores - highest)
    scale = 1.0 / (jnp.sum(cached_exp, axis=0, keepdims=True) + fresh_exp)
    probs = cached_exp * scale
    fresh_probs = jnp.where(fresh_own, fresh_exp * scale, 0.0)
    per = width // cache_len
    turned = jnp.concatenate(
        [jnp.where(request % per == i, probs, 0.0) for i in range(per)] + [fresh_probs], axis=0
    ).T
    group = lax.broadcasted_iota(jnp.int32, (count, width), 0) % SUB // per
    wide = jnp.concatenate(
        [jnp.where(group == part, turned[:, :width], 0.0) for part in range(SUB // per)], axis=1
    ).astype(jnp.bfloat16)
    output = jnp.dot(wide, values, preferred_element_type=jnp.float32)
    output = output + jnp.dot(
        turned[:, width:].astype(jnp.bfloat16), fresh_v, preferred_element_type=jnp.float32
    )
    blocks = []
    for block in range(heads // slots):
        merged = None
        for slot in range(slots):
            head = block * slots + slot
            home = head // group_size
            piece = output[head * SUB : (head + 1) * SUB]
            if slot != home:
                piece = pltpu.roll(piece, ((slot - home) * HEAD) % width, 1)
            merged = piece if merged is None else jnp.where(slot_of_lane == slot, piece, merged)
        blocks.append(merged)
    return jnp.concatenate(blocks, axis=-1)


def attend_step(at, first, lengths_ref, q_ref, nk_ref, nv_ref, k_ref, v_ref, att_ref):
    width = nk_ref.shape[1]
    slots = width // HEAD
    heads = q_ref.shape[1] // HEAD
    cache_len = k_ref.shape[1]
    request = lax.broadcasted_iota(jnp.int32, (1, heads * SUB), 1) % SUB
    span = slice(at, at + STEP)
    queries = q_ref[span].astype(jnp.float32) * (1.0 / math.sqrt(HEAD))
    halves = []
    for sub in range(0, STEP, SUB):
        live = jnp.zeros(request.shape, jnp.int32)
        for i in range(SUB):
            live = jnp.where(request == i, lengths_ref[first + at + sub + i], live)
        part = slice(at + sub, at + sub + SUB)
        halves.append(
            attend_rows(
                queries[sub : sub + SUB],
                nk_ref[span],
                nv_ref[span],
                k_ref[part].reshape(SUB * cache_len, width),
                v_ref[part].reshape(SUB * cache_len, width),
                live,
                sub,
                heads,
                slots,
                cache_len,
            )
        )
    att_ref[span, :] = jnp.concatenate(halves, axis=0).astype(jnp.bfloat16)


def project(att_ref, w_ref, out_ref):
    columns = w_ref.shape[0]
    for at in range(0, columns, 768):
        size = min(768, columns - at)
        turned = lax.dot_general(
            w_ref[at : at + size, :], att_ref[...], ACROSS, preferred_element_type=jnp.float32
        )
        out_ref[:, at : at + size] = turned.T


def first_kernel(
    core_ref, lengths_ref, q_hbm, nk_hbm, nv_hbm, k_hbm, v_hbm, w_hbm,
    out_ref, w_ref, own_k, own_v, q_ref, nk_ref, nv_ref, k_ref, v_ref, att_ref, sems,
):
    rows = out_ref.shape[0]
    theirs = pl.multiple_of((1 - core_ref[0]) * rows, rows)
    mine = pl.multiple_of(core_ref[0] * rows, rows)
    copies = []

    def bring(source, target):
        copy = pltpu.make_async_copy(source, target, sems.at[len(copies)])
        copy.start()
        copies.append(copy)
        return copy

    small = [
        bring(source.at[pl.ds(theirs, rows)], target)
        for source, target in ((q_hbm, q_ref), (nk_hbm, nk_ref), (nv_hbm, nv_ref))
    ]
    cache = []
    for at in range(0, rows, STEP):
        span = pl.ds(theirs + at, STEP)
        cache.append(
            (
                bring(k_hbm.at[span], k_ref.at[pl.ds(at, STEP)]),
                bring(v_hbm.at[span], v_ref.at[pl.ds(at, STEP)]),
            )
        )
    pieces = 4
    columns = w_ref.shape[0]
    size = -(-columns // pieces // 16) * 16
    weights = []
    for at in range(0, columns, size):
        span = pl.ds(at, min(size, columns - at))
        weights.append(bring(w_hbm.at[span], w_ref.at[span]))
    later = [
        bring(k_hbm.at[pl.ds(mine, rows)], own_k),
        bring(v_hbm.at[pl.ds(mine, rows)], own_v),
    ]
    for copy in small:
        copy.wait()
    for at in range(0, rows, STEP):
        for copy in cache[at // STEP]:
            copy.wait()
        attend_step(at, theirs, lengths_ref, q_ref, nk_ref, nv_ref, k_ref, v_ref, att_ref)
    for copy in weights:
        copy.wait()
    project(att_ref, w_ref, out_ref)
    for copy in later:
        copy.wait()


def second_kernel(
    core_ref, lengths_ref, q_ref, nk_ref, nv_ref, k_ref, v_ref, w_ref, out_ref, att_ref
):
    rows = out_ref.shape[0]
    mine = pl.multiple_of(core_ref[0] * rows, rows)
    own = [ref.at[pl.ds(mine, rows)] for ref in (q_ref, nk_ref, nv_ref)]
    for at in range(0, rows, STEP):
        attend_step(at, mine, lengths_ref, *own, k_ref, v_ref, att_ref)
    project(att_ref, w_ref, out_ref)


def attend_theirs(core, rows, lengths, query, new_key, new_value, cache_keys, cache_values, w):
    cache = (rows,) + cache_keys.shape[1:]
    columns = w.shape[0]
    smem = pl.BlockSpec(memory_space=pltpu.SMEM)
    vmem = pl.BlockSpec(memory_space=pltpu.VMEM)
    hbm = pl.BlockSpec(memory_space=pltpu.HBM)
    copies = 3 + 2 * (rows // STEP) + 4 + 2
    return pl.pallas_call(
        first_kernel,
        out_shape=(
            jax.ShapeDtypeStruct((rows, columns), jnp.float32),
            jax.ShapeDtypeStruct(w.shape, jnp.bfloat16),
            jax.ShapeDtypeStruct(cache, jnp.bfloat16),
            jax.ShapeDtypeStruct(cache, jnp.bfloat16),
        ),
        in_specs=[smem, smem] + [hbm] * 6,
        out_specs=[vmem] * 4,
        scratch_shapes=[
            pltpu.VMEM((rows, query.shape[1]), jnp.bfloat16),
            pltpu.VMEM((rows, new_key.shape[1]), jnp.bfloat16),
            pltpu.VMEM((rows, new_key.shape[1]), jnp.bfloat16),
            pltpu.VMEM(cache, jnp.bfloat16),
            pltpu.VMEM(cache, jnp.bfloat16),
            pltpu.VMEM((rows, query.shape[1]), jnp.bfloat16),
            pltpu.SemaphoreType.DMA((copies,)),
        ],
        compiler_params=pltpu.CompilerParams(vmem_limit_bytes=GRANT),
        cost_estimate=pl.CostEstimate(
            flops=2 * rows * w.size, bytes_accessed=2 * w.size, transcendentals=0
        ),
    )(
        core,
        lengths,
        *(
            pltpu.with_memory_space_constraint(x, pltpu.HBM)
            for x in (query, new_key, new_value, cache_keys, cache_values, w)
        ),
    )


def attend_mine(core, rows, lengths, query, new_key, new_value, own_keys, own_values, w):
    smem = pl.BlockSpec(memory_space=pltpu.SMEM)
    vmem = pl.BlockSpec(memory_space=pltpu.VMEM)
    return pl.pallas_call(
        second_kernel,
        out_shape=jax.ShapeDtypeStruct((rows, w.shape[0]), jnp.float32),
        in_specs=[smem, smem] + [vmem] * 6,
        out_specs=vmem,
        scratch_shapes=[pltpu.VMEM((rows, query.shape[1]), jnp.bfloat16)],
        compiler_params=pltpu.CompilerParams(vmem_limit_bytes=GRANT),
        cost_estimate=pl.CostEstimate(
            flops=2 * rows * w.size, bytes_accessed=2 * w.size, transcendentals=0
        ),
    )(core, lengths, query, new_key, new_value, own_keys, own_values, w)


def norm_kernel(
    mine_ref, swapped_ref, residual_ref, gain_ref, router_ref, routes_ref, hidden_ref, payload_ref
):
    hidden = residual_ref[...].astype(jnp.float32) + (mine_ref[...] + swapped_ref[...])
    hidden_ref[...] = hidden
    rows, width = hidden.shape
    mean_square = jnp.sum(hidden * hidden, axis=-1, keepdims=True) * (1.0 / width)
    normed = (hidden * lax.rsqrt(mean_square + 1e-05) * gain_ref[...]).astype(jnp.bfloat16)
    payload_ref[:, :width] = normed
    rest = router_ref[...]
    experts = rest.shape[0]
    terms = []
    for _ in range(3):
        term = rest.astype(jnp.bfloat16).astype(jnp.float32)
        terms.append(term)
        rest = rest - term
    parts = lax.dot_general(
        jnp.concatenate(terms, axis=0).astype(jnp.bfloat16),
        normed,
        (((1,), (1,)), ((), ())),
        preferred_element_type=jnp.float32,
    )
    logits = parts[:experts] + parts[experts : 2 * experts] + parts[2 * experts :]
    number = lax.broadcasted_iota(jnp.int32, (experts, rows), 0)
    chosen = number == routes_ref[0:1, :]
    for k in range(1, routes_ref.shape[0]):
        chosen = chosen | (number == routes_ref[k : k + 1, :])
    squashed = jnp.where(chosen, 1.0 / (1.0 + jnp.exp(-logits)), 0.0)
    gates = squashed / jnp.sum(squashed, axis=0, keepdims=True)
    upper = gates.astype(jnp.bfloat16).astype(jnp.float32)
    both = jnp.concatenate([upper, gates - upper], axis=0).astype(jnp.bfloat16)
    tail = payload_ref.shape[1] - width
    place = lax.broadcasted_iota(jnp.int32, (2 * experts, tail), 0)
    lane = lax.broadcasted_iota(jnp.int32, (2 * experts, tail), 1)
    placed = lax.dot_general(
        both,
        (place == lane).astype(jnp.bfloat16),
        (((0,), (0,)), ((), ())),
        preferred_element_type=jnp.float32,
    )
    payload_ref[:, width:] = placed.astype(jnp.bfloat16)


def norm_route(mine, swapped, residual, norm_gain, router, routes):
    rows, width = residual.shape
    experts = router.shape[1]
    wide = -(-(width + 2 * experts) // 128) * 128
    return pl.pallas_call(
        norm_kernel,
        out_shape=(
            jax.ShapeDtypeStruct((rows, width), jnp.float32),
            jax.ShapeDtypeStruct((rows, wide), jnp.bfloat16),
        ),
        compiler_params=pltpu.CompilerParams(vmem_limit_bytes=GRANT),
    )(mine, swapped, residual, norm_gain[None, :], router.T, routes.T)


def expert_kernel(count, experts, which_ref, *refs):
    blocks, refs = refs[:count], refs[count:]
    gate_ref, up_ref, down_ref = refs[:3]
    outs, refs = refs[3 : 3 + count], refs[3 + count :]
    (act_ref,) = refs
    _, hidden, width = down_ref.shape
    spans = [(at, min(256, hidden - at)) for at in range(0, hidden, 256)]
    rows = jnp.concatenate([block[...] for block in blocks], axis=0)
    base = width // 128 * 128
    tail = rows[:, base:].astype(jnp.float32)
    lane = lax.broadcasted_iota(jnp.int32, tail.shape, 1) - (width - base)
    named = (lane == which_ref[0]) | (lane == which_ref[0] + experts)
    weight = jnp.sum(jnp.where(named, tail, 0.0), axis=-1, keepdims=True)
    turned = rows[:, :width].T
    for at, size in spans:
        span = slice(at, at + size)
        gate = jnp.dot(gate_ref[0, span, :], turned, preferred_element_type=jnp.float32)
        up = jnp.dot(up_ref[0, span, :], turned, preferred_element_type=jnp.float32)
        act_ref[:, span] = (gate / (1.0 + jnp.exp(-gate)) * up).T.astype(jnp.bfloat16)
    for at in range(0, width, 768):
        size = min(768, width - at)
        part = jnp.dot(
            act_ref[...], down_ref[0, :, at : at + size], preferred_element_type=jnp.float32
        )
        part = (part * weight).astype(jnp.bfloat16)
        first = 0
        for out in outs:
            out[:, at : at + size] = part[first : first + out.shape[0]]
            first += out.shape[0]


def run_expert(which, blocks, gate_t, up_t, down, experts):
    _, hidden, width = down.shape
    rows = sum(block.shape[0] for block in blocks)
    count = len(blocks)
    vmem = pl.BlockSpec(memory_space=pltpu.VMEM)
    return pl.pallas_call(
        lambda *refs: expert_kernel(count, experts, *refs),
        out_shape=[jax.ShapeDtypeStruct((b.shape[0], width), jnp.bfloat16) for b in blocks],
        in_specs=[pl.BlockSpec(memory_space=pltpu.SMEM)] + [vmem] * (count + 3),
        out_specs=[vmem] * count,
        scratch_shapes=[pltpu.VMEM((rows, hidden), jnp.bfloat16)],
        compiler_params=pltpu.CompilerParams(vmem_limit_bytes=GRANT),
        cost_estimate=pl.CostEstimate(
            flops=6 * rows * hidden * width, bytes_accessed=6 * hidden * width, transcendentals=0
        ),
    )(which, *blocks, gate_t, up_t, down)


def total_of(terms, out_ref):
    whole = [term for term in terms if not isinstance(term, tuple)]
    total = whole[0][...].astype(jnp.float32)
    for term in whole[1:]:
        total = total + term[...].astype(jnp.float32)
    rows = out_ref.shape[0]
    for term in terms:
        if isinstance(term, tuple):
            ref, first = term
            size = ref.shape[0]
            pieces = []
            if first:
                pieces.append(total[:first])
            pieces.append(total[first : first + size] + ref[...].astype(jnp.float32))
            if first + size < rows:
                pieces.append(total[first + size :])
            total = jnp.concatenate(pieces, axis=0)
    out_ref[...] = total.astype(out_ref.dtype)


def add_kernel(firsts, *refs):
    ins, outs = refs[: len(refs) - len(firsts)], refs[len(refs) - len(firsts) :]
    each = len(ins) // len(firsts)
    for i, (first, out) in enumerate(zip(firsts, outs)):
        terms = list(ins[i * each : (i + 1) * each])
        if terms[-1].shape != out.shape:
            terms[-1] = (terms[-1], first)
        total_of(terms, out)


def add_all(*sums, firsts=None, dtype=jnp.bfloat16):
    firsts = firsts or (0,) * len(sums)
    return pl.pallas_call(
        lambda *refs: add_kernel(firsts, *refs),
        out_shape=[jax.ShapeDtypeStruct(terms[0].shape, dtype) for terms in sums],
        compiler_params=pltpu.CompilerParams(vmem_limit_bytes=GRANT),
    )(*[term for terms in sums for term in terms])


def ring_pairs(chips, cores, turn):
    order = list(range(0, chips, 2)) + list(range(1, chips, 2))[::-1]
    return [
        (order[p] * cores + core, order[(p + turn) % chips] * cores + core)
        for p in range(chips)
        for core in range(cores)
    ]


def per_device(
    query,
    new_key,
    new_value,
    cache_keys,
    cache_values,
    lengths,
    out_proj,
    residual,
    norm_gain,
    router,
    routes,
    w_gate,
    w_up,
    w_down,
):
    chips, cores = lax.axis_size("att"), lax.axis_size("exp")
    core = lax.axis_index("exp")
    own_rows = residual.shape[0]
    ring = ("att", "exp")

    def send_right(x):
        return lax.ppermute(x, ring, ring_pairs(chips, cores, 1))

    def send_left(x):
        return lax.ppermute(x, ring, ring_pairs(chips, cores, -1))

    def swap(x):
        return lax.ppermute(x, "exp", [(0, 1), (1, 0)])

    where = jnp.full((1,), core, jnp.int32)
    small = (where, own_rows, lengths, query, new_key, new_value)
    theirs, w_out, own_keys, own_values = attend_theirs(
        *small, cache_keys, cache_values, out_proj.T
    )
    swapped = swap(theirs)
    mine = attend_mine(*small, own_keys, own_values, w_out)
    hidden_state, payload = norm_route(mine, swapped, residual, norm_gain, router, routes)

    gate_t, up_t = w_gate.transpose(0, 2, 1), w_up.transpose(0, 2, 1)
    which = jnp.full((1,), lax.axis_index("att"), jnp.int32)
    experts = router.shape[1]

    def expert(*blocks):
        return run_expert(which, blocks, gate_t, up_t, w_down, experts)

    far = chips // 2
    middle = own_rows // 2
    own, own_other = expert(payload, swap(payload))
    sums = [(own, swap(own_other))]
    done = [own, own_other]
    right = left = payload
    for k in range(1, far + 1):
        if k == far:
            right, left = right[:middle], left[middle:]
        right, left = send_right(right), send_left(left)
        right, left, *done = lax.optimization_barrier((right, left, *done))
        done = expert(right, swap(right), left, swap(left))
        sums.append((done[0], swap(done[1]), done[2], swap(done[3])))
    back_a, back_b = add_all(sums[far][:2], sums[far][2:])
    for k in range(far - 1, -1, -1):
        got_a, got_b = send_left(back_a), send_right(back_b)
        if k > 0:
            back_a, back_b = add_all(
                (*sums[k][:2], got_a), (*sums[k][2:], got_b), firsts=(0, middle)
            )
    if got_a.shape[0] != own_rows:
        got_a, got_b = jnp.concatenate([got_a, got_b], axis=0), jnp.zeros_like(own)
    return add_all((hidden_state, *sums[0], got_a, got_b))[0]


def solution(mesh):
    in_specs = (
        P(("groups", "att"), "exp"),
        P(("groups", "att"), "exp"),
        P(("groups", "att"), "exp"),
        P(("groups", "att"), None, "exp"),
        P(("groups", "att"), None, "exp"),
        P(("groups", "att")),
        P("exp", None),
        P(("groups", "att", "exp"), None),
        P(),
        P(),
        P(("groups", "att", "exp"), None),
        P("att", None, "exp"),
        P("att", None, "exp"),
        P("att", "exp", None),
    )
    out_specs = P(("groups", "att", "exp"), None)
    return jax.shard_map(
        per_device, mesh=mesh, in_specs=in_specs, out_specs=out_specs, check_vma=False
    )
```

```python
import math

import jax
import jax.numpy as jnp
from jax import lax
from jax.experimental import pallas as pl
from jax.experimental.pallas import tpu as pltpu
from jax.sharding import PartitionSpec as P

HEAD = 64
SUB = 8
STEP = 16
GRANT = 12 * 1024 * 1024
ACROSS = (((1,), (1,)), ((), ()))


def attend_rows(queries, fresh_k, fresh_v, keys, values, live, offset, heads, slots, cache_len):
    width = keys.shape[1]
    group_size = heads // slots
    slot_of_lane = lax.broadcasted_iota(jnp.int32, (SUB, width), 1) // HEAD
    pieces = []
    for head in range(heads):
        block, slot, home = head // slots, head % slots, head // group_size
        piece = queries[:, block * width : (block + 1) * width]
        if slot != home:
            piece = pltpu.roll(piece, ((home - slot) * HEAD) % width, 1)
        pieces.append(jnp.where(slot_of_lane == home, piece, 0.0))
    rows = jnp.concatenate(pieces, axis=0).astype(jnp.bfloat16)
    count = heads * SUB
    request = lax.broadcasted_iota(jnp.int32, (cache_len, count), 1) % SUB
    place = lax.broadcasted_iota(jnp.int32, (cache_len, count), 0)
    spread = lax.dot_general(keys, rows, ACROSS, preferred_element_type=jnp.float32)
    scores = spread[:cache_len]
    for r in range(1, SUB):
        scores = jnp.where(request == r, spread[r * cache_len : (r + 1) * cache_len], scores)
    scores = jnp.where(place < live, scores, -1e30)
    fresh = lax.dot_general(fresh_k, rows, ACROSS, preferred_element_type=jnp.float32)
    fresh_place = lax.broadcasted_iota(jnp.int32, fresh.shape, 0)
    fresh_own = fresh_place == offset + lax.broadcasted_iota(jnp.int32, fresh.shape, 1) % SUB
    fresh_scores = jnp.sum(jnp.where(fresh_own, fresh, 0.0), axis=0, keepdims=True)
    highest = jnp.maximum(jnp.max(scores, axis=0, keepdims=True), fresh_scores)
    cached_exp = jnp.exp(scores - highest)
    fresh_exp = jnp.exp(fresh_scores - highest)
    scale = 1.0 / (jnp.sum(cached_exp, axis=0, keepdims=True) + fresh_exp)
    probs = cached_exp * scale
    fresh_probs = jnp.where(fresh_own, fresh_exp * scale, 0.0)
    per = width // cache_len
    turned = jnp.concatenate(
        [jnp.where(request % per == i, probs, 0.0) for i in range(per)] + [fresh_probs], axis=0
    ).T
    group = lax.broadcasted_iota(jnp.int32, (count, width), 0) % SUB // per
    wide = jnp.concatenate(
        [jnp.where(group == part, turned[:, :width], 0.0) for part in range(SUB // per)], axis=1
    ).astype(jnp.bfloat16)
    output = jnp.dot(wide, values, preferred_element_type=jnp.float32)
    output = output + jnp.dot(
        turned[:, width:].astype(jnp.bfloat16), fresh_v, preferred_element_type=jnp.float32
    )
    blocks = []
    for block in range(heads // slots):
        merged = None
        for slot in range(slots):
            head = block * slots + slot
            home = head // group_size
            piece = output[head * SUB : (head + 1) * SUB]
            if slot != home:
                piece = pltpu.roll(piece, ((slot - home) * HEAD) % width, 1)
            merged = piece if merged is None else jnp.where(slot_of_lane == slot, piece, merged)
        blocks.append(merged)
    return jnp.concatenate(blocks, axis=-1)


def attend_step(at, first, lengths_ref, q_ref, nk_ref, nv_ref, k_ref, v_ref, att_ref):
    width = nk_ref.shape[1]
    slots = width // HEAD
    heads = q_ref.shape[1] // HEAD
    cache_len = k_ref.shape[1]
    request = lax.broadcasted_iota(jnp.int32, (1, heads * SUB), 1) % SUB
    span = slice(at, at + STEP)
    queries = q_ref[span].astype(jnp.float32) * (1.0 / math.sqrt(HEAD))
    halves = []
    for sub in range(0, STEP, SUB):
        live = jnp.zeros(request.shape, jnp.int32)
        for i in range(SUB):
            live = jnp.where(request == i, lengths_ref[first + at + sub + i], live)
        part = slice(at + sub, at + sub + SUB)
        halves.append(
            attend_rows(
                queries[sub : sub + SUB],
                nk_ref[span],
                nv_ref[span],
                k_ref[part].reshape(SUB * cache_len, width),
                v_ref[part].reshape(SUB * cache_len, width),
                live,
                sub,
                heads,
                slots,
                cache_len,
            )
        )
    att_ref[span, :] = jnp.concatenate(halves, axis=0).astype(jnp.bfloat16)


def project(att_ref, w_ref, out_ref):
    columns = w_ref.shape[0]
    for at in range(0, columns, 768):
        size = min(768, columns - at)
        turned = lax.dot_general(
            w_ref[at : at + size, :], att_ref[...], ACROSS, preferred_element_type=jnp.float32
        )
        out_ref[:, at : at + size] = turned.T


def first_kernel(
    core_ref, lengths_ref, q_hbm, nk_hbm, nv_hbm, k_hbm, v_hbm, w_hbm,
    out_ref, w_ref, own_k, own_v, q_ref, nk_ref, nv_ref, k_ref, v_ref, att_ref, sems,
):
    rows = out_ref.shape[0]
    theirs = pl.multiple_of((1 - core_ref[0]) * rows, rows)
    mine = pl.multiple_of(core_ref[0] * rows, rows)
    copies = []

    def bring(source, target):
        copy = pltpu.make_async_copy(source, target, sems.at[len(copies)])
        copy.start()
        copies.append(copy)
        return copy

    small = [
        bring(source.at[pl.ds(theirs, rows)], target)
        for source, target in ((q_hbm, q_ref), (nk_hbm, nk_ref), (nv_hbm, nv_ref))
    ]
    cache = []
    for at in range(0, rows, STEP):
        span = pl.ds(theirs + at, STEP)
        cache.append(
            (
                bring(k_hbm.at[span], k_ref.at[pl.ds(at, STEP)]),
                bring(v_hbm.at[span], v_ref.at[pl.ds(at, STEP)]),
            )
        )
    pieces = 4
    columns = w_ref.shape[0]
    size = -(-columns // pieces // 16) * 16
    weights = []
    for at in range(0, columns, size):
        span = pl.ds(at, min(size, columns - at))
        weights.append(bring(w_hbm.at[span], w_ref.at[span]))
    later = [
        bring(k_hbm.at[pl.ds(mine, rows)], own_k),
        bring(v_hbm.at[pl.ds(mine, rows)], own_v),
    ]
    for copy in small:
        copy.wait()
    for at in range(0, rows, STEP):
        for copy in cache[at // STEP]:
            copy.wait()
        attend_step(at, theirs, lengths_ref, q_ref, nk_ref, nv_ref, k_ref, v_ref, att_ref)
    for copy in weights:
        copy.wait()
    project(att_ref, w_ref, out_ref)
    for copy in later:
        copy.wait()


def second_kernel(
    core_ref, lengths_ref, q_ref, nk_ref, nv_ref, k_ref, v_ref, w_ref, gate_hbm, up_hbm,
    out_ref, gate_ref, up_ref, att_ref, sems,
):
    copies = [
        pltpu.make_async_copy(gate_hbm.at[0], gate_ref, sems.at[0]),
        pltpu.make_async_copy(up_hbm.at[0], up_ref, sems.at[1]),
    ]
    for copy in copies:
        copy.start()
    rows = out_ref.shape[0]
    mine = pl.multiple_of(core_ref[0] * rows, rows)
    own = [ref.at[pl.ds(mine, rows)] for ref in (q_ref, nk_ref, nv_ref)]
    for at in range(0, rows, STEP):
        attend_step(at, mine, lengths_ref, *own, k_ref, v_ref, att_ref)
    project(att_ref, w_ref, out_ref)
    for copy in copies:
        copy.wait()


def attend_theirs(core, rows, lengths, query, new_key, new_value, cache_keys, cache_values, w):
    cache = (rows,) + cache_keys.shape[1:]
    columns = w.shape[0]
    smem = pl.BlockSpec(memory_space=pltpu.SMEM)
    vmem = pl.BlockSpec(memory_space=pltpu.VMEM)
    hbm = pl.BlockSpec(memory_space=pltpu.HBM)
    copies = 3 + 2 * (rows // STEP) + 4 + 2
    return pl.pallas_call(
        first_kernel,
        out_shape=(
            jax.ShapeDtypeStruct((rows, columns), jnp.float32),
            jax.ShapeDtypeStruct(w.shape, jnp.bfloat16),
            jax.ShapeDtypeStruct(cache, jnp.bfloat16),
            jax.ShapeDtypeStruct(cache, jnp.bfloat16),
        ),
        in_specs=[smem, smem] + [hbm] * 6,
        out_specs=[vmem] * 4,
        scratch_shapes=[
            pltpu.VMEM((rows, query.shape[1]), jnp.bfloat16),
            pltpu.VMEM((rows, new_key.shape[1]), jnp.bfloat16),
            pltpu.VMEM((rows, new_key.shape[1]), jnp.bfloat16),
            pltpu.VMEM(cache, jnp.bfloat16),
            pltpu.VMEM(cache, jnp.bfloat16),
            pltpu.VMEM((rows, query.shape[1]), jnp.bfloat16),
            pltpu.SemaphoreType.DMA((copies,)),
        ],
        compiler_params=pltpu.CompilerParams(vmem_limit_bytes=GRANT),
        cost_estimate=pl.CostEstimate(
            flops=2 * rows * w.size, bytes_accessed=2 * w.size, transcendentals=0
        ),
    )(
        core,
        lengths,
        *(
            pltpu.with_memory_space_constraint(x, pltpu.HBM)
            for x in (query, new_key, new_value, cache_keys, cache_values, w)
        ),
    )


def attend_mine(
    core, rows, lengths, query, new_key, new_value, own_keys, own_values, w, gate_t, up_t
):
    smem = pl.BlockSpec(memory_space=pltpu.SMEM)
    vmem = pl.BlockSpec(memory_space=pltpu.VMEM)
    hbm = pl.BlockSpec(memory_space=pltpu.HBM)
    return pl.pallas_call(
        second_kernel,
        out_shape=(
            jax.ShapeDtypeStruct((rows, w.shape[0]), jnp.float32),
            jax.ShapeDtypeStruct(gate_t.shape[1:], jnp.bfloat16),
            jax.ShapeDtypeStruct(up_t.shape[1:], jnp.bfloat16),
        ),
        in_specs=[smem, smem] + [vmem] * 6 + [hbm] * 2,
        out_specs=[vmem] * 3,
        scratch_shapes=[
            pltpu.VMEM((rows, query.shape[1]), jnp.bfloat16),
            pltpu.SemaphoreType.DMA((2,)),
        ],
        compiler_params=pltpu.CompilerParams(vmem_limit_bytes=GRANT),
        cost_estimate=pl.CostEstimate(
            flops=2 * rows * w.size, bytes_accessed=4 * gate_t.size, transcendentals=0
        ),
    )(
        core,
        lengths,
        query,
        new_key,
        new_value,
        own_keys,
        own_values,
        w,
        pltpu.with_memory_space_constraint(gate_t, pltpu.HBM),
        pltpu.with_memory_space_constraint(up_t, pltpu.HBM),
    )


def norm_kernel(
    mine_ref, swapped_ref, residual_ref, gain_ref, router_ref, routes_ref, hidden_ref, payload_ref
):
    hidden = residual_ref[...].astype(jnp.float32) + (mine_ref[...] + swapped_ref[...])
    hidden_ref[...] = hidden
    rows, width = hidden.shape
    mean_square = jnp.sum(hidden * hidden, axis=-1, keepdims=True) * (1.0 / width)
    normed = (hidden * lax.rsqrt(mean_square + 1e-05) * gain_ref[...]).astype(jnp.bfloat16)
    payload_ref[:, :width] = normed
    rest = router_ref[...]
    experts = rest.shape[0]
    terms = []
    for _ in range(3):
        term = rest.astype(jnp.bfloat16).astype(jnp.float32)
        terms.append(term)
        rest = rest - term
    parts = lax.dot_general(
        jnp.concatenate(terms, axis=0).astype(jnp.bfloat16),
        normed,
        (((1,), (1,)), ((), ())),
        preferred_element_type=jnp.float32,
    )
    logits = parts[:experts] + parts[experts : 2 * experts] + parts[2 * experts :]
    number = lax.broadcasted_iota(jnp.int32, (experts, rows), 0)
    chosen = number == routes_ref[0:1, :]
    for k in range(1, routes_ref.shape[0]):
        chosen = chosen | (number == routes_ref[k : k + 1, :])
    squashed = jnp.where(chosen, 1.0 / (1.0 + jnp.exp(-logits)), 0.0)
    gates = squashed / jnp.sum(squashed, axis=0, keepdims=True)
    upper = gates.astype(jnp.bfloat16).astype(jnp.float32)
    both = jnp.concatenate([upper, gates - upper], axis=0).astype(jnp.bfloat16)
    tail = payload_ref.shape[1] - width
    place = lax.broadcasted_iota(jnp.int32, (2 * experts, tail), 0)
    lane = lax.broadcasted_iota(jnp.int32, (2 * experts, tail), 1)
    placed = lax.dot_general(
        both,
        (place == lane).astype(jnp.bfloat16),
        (((0,), (0,)), ((), ())),
        preferred_element_type=jnp.float32,
    )
    payload_ref[:, width:] = placed.astype(jnp.bfloat16)


def norm_route(mine, swapped, residual, norm_gain, router, routes):
    rows, width = residual.shape
    experts = router.shape[1]
    wide = -(-(width + 2 * experts) // 128) * 128
    return pl.pallas_call(
        norm_kernel,
        out_shape=(
            jax.ShapeDtypeStruct((rows, width), jnp.float32),
            jax.ShapeDtypeStruct((rows, wide), jnp.bfloat16),
        ),
        compiler_params=pltpu.CompilerParams(vmem_limit_bytes=GRANT),
    )(mine, swapped, residual, norm_gain[None, :], router.T, routes.T)


def expert_kernel(count, experts, bring, which_ref, *refs):
    blocks, refs = refs[:count], refs[count:]
    gate_ref, up_ref, down_ref = refs[:3]
    outs, refs = refs[3 : 3 + count], refs[3 + count :]
    copy = None
    if bring:
        kept_ref, act_ref, sem = refs
        copy = pltpu.make_async_copy(down_ref.at[0], kept_ref, sem)
        copy.start()
        down_ref = kept_ref
    else:
        (act_ref,) = refs
    hidden, width = gate_ref.shape
    rows = jnp.concatenate([block[...] for block in blocks], axis=0)
    base = width // 128 * 128
    tail = rows[:, base:].astype(jnp.float32)
    lane = lax.broadcasted_iota(jnp.int32, tail.shape, 1) - (width - base)
    named = (lane == which_ref[0]) | (lane == which_ref[0] + experts)
    weight = jnp.sum(jnp.where(named, tail, 0.0), axis=-1, keepdims=True)
    turned = rows[:, :width].T
    for at in range(0, hidden, 256):
        span = slice(at, min(at + 256, hidden))
        gate = jnp.dot(gate_ref[span, :], turned, preferred_element_type=jnp.float32)
        up = jnp.dot(up_ref[span, :], turned, preferred_element_type=jnp.float32)
        act_ref[:, span] = (gate / (1.0 + jnp.exp(-gate)) * up).T.astype(jnp.bfloat16)
    if copy is not None:
        copy.wait()
    for at in range(0, width, 768):
        span = slice(at, min(at + 768, width))
        part = jnp.dot(act_ref[...], down_ref[:, span], preferred_element_type=jnp.float32)
        part = (part * weight).astype(jnp.bfloat16)
        first = 0
        for out in outs:
            out[:, span] = part[first : first + out.shape[0]]
            first += out.shape[0]


def run_expert(which, blocks, gate_t, up_t, down, experts):
    hidden, width = gate_t.shape
    bring = down.ndim == 3
    rows = sum(block.shape[0] for block in blocks)
    count = len(blocks)
    vmem = pl.BlockSpec(memory_space=pltpu.VMEM)
    outs = [jax.ShapeDtypeStruct((b.shape[0], width), jnp.bfloat16) for b in blocks]
    scratch = [pltpu.VMEM((rows, hidden), jnp.bfloat16)]
    source = vmem
    if bring:
        outs.append(jax.ShapeDtypeStruct((hidden, width), jnp.bfloat16))
        scratch.append(pltpu.SemaphoreType.DMA)
        down = pltpu.with_memory_space_constraint(down, pltpu.HBM)
        source = pl.BlockSpec(memory_space=pltpu.HBM)
    return pl.pallas_call(
        lambda *refs: expert_kernel(count, experts, bring, *refs),
        out_shape=outs,
        in_specs=[pl.BlockSpec(memory_space=pltpu.SMEM)] + [vmem] * (count + 2) + [source],
        out_specs=[vmem] * len(outs),
        scratch_shapes=scratch,
        compiler_params=pltpu.CompilerParams(vmem_limit_bytes=GRANT),
        cost_estimate=pl.CostEstimate(
            flops=6 * rows * hidden * width, bytes_accessed=6 * hidden * width, transcendentals=0
        ),
    )(which, *blocks, gate_t, up_t, down)


def add_kernel(plan, *refs):
    count = sum(len(terms) for terms in plan)
    ins, outs = refs[:count], refs[count:]
    at = 0
    for terms, out in zip(plan, outs):
        size = out.shape[0]
        total = None
        for first in terms:
            term = ins[at][first : first + size].astype(jnp.float32)
            total = term if total is None else total + term
            at += 1
        out[...] = total.astype(out.dtype)


def add_parts(rows, *sums):
    plan = [[first for _, first in terms] for terms in sums]
    width = sums[0][0][0].shape[1]
    return pl.pallas_call(
        lambda *refs: add_kernel(plan, *refs),
        out_shape=[jax.ShapeDtypeStruct((rows, width), jnp.bfloat16) for _ in sums],
        compiler_params=pltpu.CompilerParams(vmem_limit_bytes=GRANT),
    )(*[array for terms in sums for array, _ in terms])


def finish_kernel(parts, *refs):
    hidden_ref, own_ref, other_ref = refs[:3]
    out_ref = refs[-1]
    total = hidden_ref[...] + own_ref[...].astype(jnp.float32) + other_ref[...].astype(jnp.float32)
    at = 3
    for first, size, count in parts:
        piece = total[first : first + size]
        for ref in refs[at : at + count]:
            piece = piece + ref[...].astype(jnp.float32)
        at += count
        out_ref[first : first + size, :] = piece.astype(out_ref.dtype)


def finish(hidden_state, own, other, *halves):
    parts, first = [], 0
    for arrays in halves:
        parts.append((first, arrays[0].shape[0], len(arrays)))
        first += arrays[0].shape[0]
    return pl.pallas_call(
        lambda *refs: finish_kernel(parts, *refs),
        out_shape=jax.ShapeDtypeStruct(hidden_state.shape, jnp.bfloat16),
        compiler_params=pltpu.CompilerParams(vmem_limit_bytes=GRANT),
    )(hidden_state, own, other, *[array for arrays in halves for array in arrays])


def ring_pairs(chips, cores, turn):
    order = list(range(0, chips, 2)) + list(range(1, chips, 2))[::-1]
    return [
        (order[p] * cores + core, order[(p + turn) % chips] * cores + core)
        for p in range(chips)
        for core in range(cores)
    ]


def per_device(
    query,
    new_key,
    new_value,
    cache_keys,
    cache_values,
    lengths,
    out_proj,
    residual,
    norm_gain,
    router,
    routes,
    w_gate,
    w_up,
    w_down,
):
    chips, cores = lax.axis_size("att"), lax.axis_size("exp")
    core = lax.axis_index("exp")
    own_rows = residual.shape[0]
    ring = ("att", "exp")

    def send_right(x):
        return lax.ppermute(x, ring, ring_pairs(chips, cores, 1))

    def send_left(x):
        return lax.ppermute(x, ring, ring_pairs(chips, cores, -1))

    def swap(x):
        return lax.ppermute(x, "exp", [(0, 1), (1, 0)])

    where = jnp.full((1,), core, jnp.int32)
    small = (where, own_rows, lengths, query, new_key, new_value)
    theirs, w_out, own_keys, own_values = attend_theirs(
        *small, cache_keys, cache_values, out_proj.T
    )
    swapped = swap(theirs)
    gate_t, up_t = w_gate.transpose(0, 2, 1), w_up.transpose(0, 2, 1)
    mine, gate_t, up_t = attend_mine(*small, own_keys, own_values, w_out, gate_t, up_t)
    hidden_state, payload = norm_route(mine, swapped, residual, norm_gain, router, routes)

    which = jnp.full((1,), lax.axis_index("att"), jnp.int32)
    experts = router.shape[1]

    def expert(blocks, down):
        return run_expert(which, blocks, gate_t, up_t, down, experts)

    far = chips // 2
    middle = own_rows // 2
    *done, down = expert((payload, swap(payload)), w_down)
    own, own_other = done[0], swap(done[1])
    from_left, from_right = [None], [None]
    right = left = payload
    for k in range(1, far + 1):
        if k == far:
            right, left = right[:middle], left[middle:]
        right, left = send_right(right), send_left(left)
        right, left, *done = lax.optimization_barrier((right, left, *done))
        done = expert((right, swap(right), left, swap(left)), down)
        from_left.append((done[0], swap(done[1])))
        from_right.append((done[2], swap(done[3])))

    def parts(pair, first):
        return [(array, first) for array in pair]

    short_top, short_low = None, None
    long_top, long_low = add_parts(middle, parts(from_left[far], 0), parts(from_right[far], 0))
    long_top, long_low = send_left(long_top), send_right(long_low)
    for k in range(far - 1, 0, -1):
        top, low = parts(from_right[k], 0), parts(from_left[k], middle)
        if short_top is not None:
            top, low = top + [(short_top, 0)], low + [(short_low, 0)]
        short_top, short_low = add_parts(middle, top, low)
        short_top, short_low = send_right(short_top), send_left(short_low)
        top, low = parts(from_left[k], 0), parts(from_right[k], middle)
        long_top, long_low = add_parts(middle, top + [(long_top, 0)], low + [(long_low, 0)])
        long_top, long_low = send_left(long_top), send_right(long_low)
    return finish(hidden_state, own, own_other, (long_top, short_top), (long_low, short_low))


def solution(mesh):
    in_specs = (
        P(("groups", "att"), "exp"),
        P(("groups", "att"), "exp"),
        P(("groups", "att"), "exp"),
        P(("groups", "att"), None, "exp"),
        P(("groups", "att"), None, "exp"),
        P(("groups", "att")),
        P("exp", None),
        P(("groups", "att", "exp"), None),
        P(),
        P(),
        P(("groups", "att", "exp"), None),
        P("att", None, "exp"),
        P("att", None, "exp"),
        P("att", "exp", None),
    )
    out_specs = P(("groups", "att", "exp"), None)
    return jax.shard_map(
        per_device, mesh=mesh, in_specs=in_specs, out_specs=out_specs, check_vma=False
    )
```

```python
import math

import jax
import jax.numpy as jnp
from jax import lax
from jax.experimental import pallas as pl
from jax.experimental.pallas import tpu as pltpu
from jax.sharding import PartitionSpec as P

HEAD = 64
SUB = 8
STEP = 16
GRANT = 12 * 1024 * 1024
ACROSS = (((1,), (1,)), ((), ()))


def place_heads(queries, heads, slots, width):
    group_size = heads // slots
    slot_of_lane = lax.broadcasted_iota(jnp.int32, (SUB, width), 1) // HEAD
    pieces = []
    for head in range(heads):
        block, slot, home = head // slots, head % slots, head // group_size
        piece = queries[:, block * width : (block + 1) * width]
        if slot != home:
            piece = pltpu.roll(piece, ((home - slot) * HEAD) % width, 1)
        pieces.append(jnp.where(slot_of_lane == home, piece, 0.0))
    return jnp.concatenate(pieces, axis=0).astype(jnp.bfloat16)


def score(rows, keys, fresh_k, cache_len):
    request = lax.broadcasted_iota(jnp.int32, (cache_len, rows.shape[0]), 1) % SUB
    spread = lax.dot_general(keys, rows, ACROSS, preferred_element_type=jnp.float32)
    scores = spread[:cache_len]
    for r in range(1, SUB):
        scores = jnp.where(request == r, spread[r * cache_len : (r + 1) * cache_len], scores)
    return scores, lax.dot_general(fresh_k, rows, ACROSS, preferred_element_type=jnp.float32)


def soften(scores, fresh, live, offset, per):
    cache_len, count = scores.shape
    request = lax.broadcasted_iota(jnp.int32, (cache_len, count), 1) % SUB
    place = lax.broadcasted_iota(jnp.int32, (cache_len, count), 0)
    scores = jnp.where(place < live, scores, -1e30)
    fresh_place = lax.broadcasted_iota(jnp.int32, fresh.shape, 0)
    fresh_own = fresh_place == offset + lax.broadcasted_iota(jnp.int32, fresh.shape, 1) % SUB
    fresh_scores = jnp.sum(jnp.where(fresh_own, fresh, 0.0), axis=0, keepdims=True)
    highest = jnp.maximum(jnp.max(scores, axis=0, keepdims=True), fresh_scores)
    cached_exp = jnp.exp(scores - highest)
    fresh_exp = jnp.exp(fresh_scores - highest)
    scale = 1.0 / (jnp.sum(cached_exp, axis=0, keepdims=True) + fresh_exp)
    probs = cached_exp * scale
    fresh_probs = jnp.where(fresh_own, fresh_exp * scale, 0.0)
    return jnp.concatenate(
        [jnp.where(request % per == i, probs, 0.0) for i in range(per)] + [fresh_probs], axis=0
    ).T


def weigh(turned, values, fresh_v, per):
    count, width = turned.shape[0], values.shape[1]
    group = lax.broadcasted_iota(jnp.int32, (count, width), 0) % SUB // per
    wide = jnp.concatenate(
        [jnp.where(group == part, turned[:, :width], 0.0) for part in range(SUB // per)], axis=1
    ).astype(jnp.bfloat16)
    output = jnp.dot(wide, values, preferred_element_type=jnp.float32)
    return output + jnp.dot(
        turned[:, width:].astype(jnp.bfloat16), fresh_v, preferred_element_type=jnp.float32
    )


def gather_heads(output, heads, slots, width):
    group_size = heads // slots
    slot_of_lane = lax.broadcasted_iota(jnp.int32, (SUB, width), 1) // HEAD
    blocks = []
    for block in range(heads // slots):
        merged = None
        for slot in range(slots):
            head = block * slots + slot
            home = head // group_size
            piece = output[head * SUB : (head + 1) * SUB]
            if slot != home:
                piece = pltpu.roll(piece, ((slot - home) * HEAD) % width, 1)
            merged = piece if merged is None else jnp.where(slot_of_lane == slot, piece, merged)
        blocks.append(merged)
    return jnp.concatenate(blocks, axis=-1)


def attend(first, lengths_ref, q_ref, nk_ref, nv_ref, k_ref, v_ref, att_ref, ready):
    width = nk_ref.shape[1]
    slots = width // HEAD
    heads = q_ref.shape[1] // HEAD
    cache_len = k_ref.shape[1]
    per = width // cache_len
    request = lax.broadcasted_iota(jnp.int32, (1, heads * SUB), 1) % SUB
    batches = range(0, att_ref.shape[0], SUB)
    scores = []
    for at in batches:
        step = at // STEP * STEP
        if at == step:
            ready(at)
            queries = q_ref[step : step + STEP].astype(jnp.float32) * (1.0 / math.sqrt(HEAD))
        rows = place_heads(queries[at - step : at - step + SUB], heads, slots, width)
        keys = k_ref[at : at + SUB].reshape(SUB * cache_len, width)
        scores.append(score(rows, keys, nk_ref[step : step + STEP], cache_len))
    turned = []
    for at, (cached, fresh) in zip(batches, scores):
        live = jnp.zeros(request.shape, jnp.int32)
        for i in range(SUB):
            live = jnp.where(request == i, lengths_ref[first + at + i], live)
        turned.append(soften(cached, fresh, live, at % STEP, per))
    outputs = []
    for at, probs in zip(batches, turned):
        step = at // STEP * STEP
        values = v_ref[at : at + SUB].reshape(SUB * cache_len, width)
        outputs.append(weigh(probs, values, nv_ref[step : step + STEP], per))
    for step in range(0, att_ref.shape[0], STEP):
        pair = outputs[step // SUB : (step + STEP) // SUB]
        att_ref[step : step + STEP, :] = jnp.concatenate(
            [gather_heads(output, heads, slots, width) for output in pair], axis=0
        ).astype(jnp.bfloat16)


def project(att_ref, w_ref, out_ref):
    columns = w_ref.shape[0]
    for at in range(0, columns, 768):
        size = min(768, columns - at)
        turned = lax.dot_general(
            w_ref[at : at + size, :], att_ref[...], ACROSS, preferred_element_type=jnp.float32
        )
        out_ref[:, at : at + size] = turned.T


def first_kernel(
    core_ref, lengths_ref, q_hbm, nk_hbm, nv_hbm, k_hbm, v_hbm, w_hbm,
    out_ref, w_ref, own_k, own_v, q_ref, nk_ref, nv_ref, k_ref, v_ref, att_ref, sems,
):
    rows = out_ref.shape[0]
    theirs = pl.multiple_of((1 - core_ref[0]) * rows, rows)
    mine = pl.multiple_of(core_ref[0] * rows, rows)
    copies = []

    def bring(source, target):
        copy = pltpu.make_async_copy(source, target, sems.at[len(copies)])
        copy.start()
        copies.append(copy)
        return copy

    small = [
        bring(source.at[pl.ds(theirs, rows)], target)
        for source, target in ((q_hbm, q_ref), (nk_hbm, nk_ref), (nv_hbm, nv_ref))
    ]
    cache = []
    for at in range(0, rows, STEP):
        span = pl.ds(theirs + at, STEP)
        cache.append(
            (
                bring(k_hbm.at[span], k_ref.at[pl.ds(at, STEP)]),
                bring(v_hbm.at[span], v_ref.at[pl.ds(at, STEP)]),
            )
        )
    pieces = 4
    columns = w_ref.shape[0]
    size = -(-columns // pieces // 16) * 16
    weights = []
    for at in range(0, columns, size):
        span = pl.ds(at, min(size, columns - at))
        weights.append(bring(w_hbm.at[span], w_ref.at[span]))
    later = [
        bring(k_hbm.at[pl.ds(mine, rows)], own_k),
        bring(v_hbm.at[pl.ds(mine, rows)], own_v),
    ]
    for copy in small:
        copy.wait()

    def ready(at):
        for copy in cache[at // STEP]:
            copy.wait()

    attend(theirs, lengths_ref, q_ref, nk_ref, nv_ref, k_ref, v_ref, att_ref, ready)
    for copy in weights:
        copy.wait()
    project(att_ref, w_ref, out_ref)
    for copy in later:
        copy.wait()


def second_kernel(
    core_ref, lengths_ref, q_ref, nk_ref, nv_ref, k_ref, v_ref, w_ref, gate_hbm, up_hbm,
    out_ref, gate_ref, up_ref, att_ref, sems,
):
    copies = [
        pltpu.make_async_copy(gate_hbm.at[0], gate_ref, sems.at[0]),
        pltpu.make_async_copy(up_hbm.at[0], up_ref, sems.at[1]),
    ]
    for copy in copies:
        copy.start()
    rows = out_ref.shape[0]
    mine = pl.multiple_of(core_ref[0] * rows, rows)
    own = [ref.at[pl.ds(mine, rows)] for ref in (q_ref, nk_ref, nv_ref)]
    attend(mine, lengths_ref, *own, k_ref, v_ref, att_ref, lambda at: None)
    project(att_ref, w_ref, out_ref)
    for copy in copies:
        copy.wait()


def attend_theirs(core, rows, lengths, query, new_key, new_value, cache_keys, cache_values, w):
    cache = (rows,) + cache_keys.shape[1:]
    columns = w.shape[0]
    smem = pl.BlockSpec(memory_space=pltpu.SMEM)
    vmem = pl.BlockSpec(memory_space=pltpu.VMEM)
    hbm = pl.BlockSpec(memory_space=pltpu.HBM)
    copies = 3 + 2 * (rows // STEP) + 4 + 2
    return pl.pallas_call(
        first_kernel,
        out_shape=(
            jax.ShapeDtypeStruct((rows, columns), jnp.float32),
            jax.ShapeDtypeStruct(w.shape, jnp.bfloat16),
            jax.ShapeDtypeStruct(cache, jnp.bfloat16),
            jax.ShapeDtypeStruct(cache, jnp.bfloat16),
        ),
        in_specs=[smem, smem] + [hbm] * 6,
        out_specs=[vmem] * 4,
        scratch_shapes=[
            pltpu.VMEM((rows, query.shape[1]), jnp.bfloat16),
            pltpu.VMEM((rows, new_key.shape[1]), jnp.bfloat16),
            pltpu.VMEM((rows, new_key.shape[1]), jnp.bfloat16),
            pltpu.VMEM(cache, jnp.bfloat16),
            pltpu.VMEM(cache, jnp.bfloat16),
            pltpu.VMEM((rows, query.shape[1]), jnp.bfloat16),
            pltpu.SemaphoreType.DMA((copies,)),
        ],
        compiler_params=pltpu.CompilerParams(vmem_limit_bytes=GRANT),
        cost_estimate=pl.CostEstimate(
            flops=2 * rows * w.size, bytes_accessed=2 * w.size, transcendentals=0
        ),
    )(
        core,
        lengths,
        *(
            pltpu.with_memory_space_constraint(x, pltpu.HBM)
            for x in (query, new_key, new_value, cache_keys, cache_values, w)
        ),
    )


def attend_mine(
    core, rows, lengths, query, new_key, new_value, own_keys, own_values, w, gate_t, up_t
):
    smem = pl.BlockSpec(memory_space=pltpu.SMEM)
    vmem = pl.BlockSpec(memory_space=pltpu.VMEM)
    hbm = pl.BlockSpec(memory_space=pltpu.HBM)
    return pl.pallas_call(
        second_kernel,
        out_shape=(
            jax.ShapeDtypeStruct((rows, w.shape[0]), jnp.float32),
            jax.ShapeDtypeStruct(gate_t.shape[1:], jnp.bfloat16),
            jax.ShapeDtypeStruct(up_t.shape[1:], jnp.bfloat16),
        ),
        in_specs=[smem, smem] + [vmem] * 6 + [hbm] * 2,
        out_specs=[vmem] * 3,
        scratch_shapes=[
            pltpu.VMEM((rows, query.shape[1]), jnp.bfloat16),
            pltpu.SemaphoreType.DMA((2,)),
        ],
        compiler_params=pltpu.CompilerParams(vmem_limit_bytes=GRANT),
        cost_estimate=pl.CostEstimate(
            flops=2 * rows * w.size, bytes_accessed=4 * gate_t.size, transcendentals=0
        ),
    )(
        core,
        lengths,
        query,
        new_key,
        new_value,
        own_keys,
        own_values,
        w,
        pltpu.with_memory_space_constraint(gate_t, pltpu.HBM),
        pltpu.with_memory_space_constraint(up_t, pltpu.HBM),
    )


def norm_kernel(
    mine_ref, swapped_ref, residual_ref, gain_ref, router_ref, routes_ref, hidden_ref, payload_ref
):
    hidden = residual_ref[...].astype(jnp.float32) + (mine_ref[...] + swapped_ref[...])
    hidden_ref[...] = hidden
    rows, width = hidden.shape
    mean_square = jnp.sum(hidden * hidden, axis=-1, keepdims=True) * (1.0 / width)
    normed = (hidden * lax.rsqrt(mean_square + 1e-05) * gain_ref[...]).astype(jnp.bfloat16)
    payload_ref[:, :width] = normed
    rest = router_ref[...]
    experts = rest.shape[0]
    terms = []
    for _ in range(3):
        term = rest.astype(jnp.bfloat16).astype(jnp.float32)
        terms.append(term)
        rest = rest - term
    parts = lax.dot_general(
        jnp.concatenate(terms, axis=0).astype(jnp.bfloat16),
        normed,
        (((1,), (1,)), ((), ())),
        preferred_element_type=jnp.float32,
    )
    logits = parts[:experts] + parts[experts : 2 * experts] + parts[2 * experts :]
    number = lax.broadcasted_iota(jnp.int32, (experts, rows), 0)
    chosen = number == routes_ref[0:1, :]
    for k in range(1, routes_ref.shape[0]):
        chosen = chosen | (number == routes_ref[k : k + 1, :])
    squashed = jnp.where(chosen, 1.0 / (1.0 + jnp.exp(-logits)), 0.0)
    gates = squashed / jnp.sum(squashed, axis=0, keepdims=True)
    upper = gates.astype(jnp.bfloat16).astype(jnp.float32)
    both = jnp.concatenate([upper, gates - upper], axis=0).astype(jnp.bfloat16)
    tail = payload_ref.shape[1] - width
    place = lax.broadcasted_iota(jnp.int32, (2 * experts, tail), 0)
    lane = lax.broadcasted_iota(jnp.int32, (2 * experts, tail), 1)
    placed = lax.dot_general(
        both,
        (place == lane).astype(jnp.bfloat16),
        (((0,), (0,)), ((), ())),
        preferred_element_type=jnp.float32,
    )
    payload_ref[:, width:] = placed.astype(jnp.bfloat16)


def norm_route(mine, swapped, residual, norm_gain, router, routes):
    rows, width = residual.shape
    experts = router.shape[1]
    wide = -(-(width + 2 * experts) // 128) * 128
    return pl.pallas_call(
        norm_kernel,
        out_shape=(
            jax.ShapeDtypeStruct((rows, width), jnp.float32),
            jax.ShapeDtypeStruct((rows, wide), jnp.bfloat16),
        ),
        compiler_params=pltpu.CompilerParams(vmem_limit_bytes=GRANT),
    )(mine, swapped, residual, norm_gain[None, :], router.T, routes.T)


def expert_kernel(count, experts, bring, which_ref, *refs):
    blocks, refs = refs[:count], refs[count:]
    gate_ref, up_ref, down_ref = refs[:3]
    outs, refs = refs[3 : 3 + count], refs[3 + count :]
    copy = None
    if bring:
        kept_ref, act_ref, sem = refs
        copy = pltpu.make_async_copy(down_ref.at[0], kept_ref, sem)
        copy.start()
        down_ref = kept_ref
    else:
        (act_ref,) = refs
    hidden, width = gate_ref.shape
    rows = jnp.concatenate([block[...] for block in blocks], axis=0)
    base = width // 128 * 128
    tail = rows[:, base:].astype(jnp.float32)
    lane = lax.broadcasted_iota(jnp.int32, tail.shape, 1) - (width - base)
    named = (lane == which_ref[1]) | (lane == which_ref[1] + experts)
    weight = jnp.sum(jnp.where(named, tail, 0.0), axis=-1, keepdims=True)
    turned = rows[:, :width].T
    for at in range(0, hidden, 256):
        span = slice(at, min(at + 256, hidden))
        gate = jnp.dot(gate_ref[span, :], turned, preferred_element_type=jnp.float32)
        up = jnp.dot(up_ref[span, :], turned, preferred_element_type=jnp.float32)
        act_ref[:, span] = (gate / (1.0 + jnp.exp(-gate)) * up).T.astype(jnp.bfloat16)
    if copy is not None:
        copy.wait()
    for at in range(0, width, 768):
        span = slice(at, min(at + 768, width))
        part = jnp.dot(act_ref[...], down_ref[:, span], preferred_element_type=jnp.float32)
        part = (part * weight).astype(jnp.bfloat16)
        first = 0
        for out in outs:
            out[:, span] = part[first : first + out.shape[0]]
            first += out.shape[0]


def run_expert(which, blocks, gate_t, up_t, down, experts):
    hidden, width = gate_t.shape
    bring = down.ndim == 3
    rows = sum(block.shape[0] for block in blocks)
    count = len(blocks)
    vmem = pl.BlockSpec(memory_space=pltpu.VMEM)
    outs = [jax.ShapeDtypeStruct((b.shape[0], width), jnp.bfloat16) for b in blocks]
    scratch = [pltpu.VMEM((rows, hidden), jnp.bfloat16)]
    source = vmem
    if bring:
        outs.append(jax.ShapeDtypeStruct((hidden, width), jnp.bfloat16))
        scratch.append(pltpu.SemaphoreType.DMA)
        down = pltpu.with_memory_space_constraint(down, pltpu.HBM)
        source = pl.BlockSpec(memory_space=pltpu.HBM)
    return pl.pallas_call(
        lambda *refs: expert_kernel(count, experts, bring, *refs),
        out_shape=outs,
        in_specs=[pl.BlockSpec(memory_space=pltpu.SMEM)] + [vmem] * (count + 2) + [source],
        out_specs=[vmem] * len(outs),
        scratch_shapes=scratch,
        compiler_params=pltpu.CompilerParams(vmem_limit_bytes=GRANT),
        cost_estimate=pl.CostEstimate(
            flops=6 * rows * hidden * width, bytes_accessed=6 * hidden * width, transcendentals=0
        ),
    )(which, *blocks, gate_t, up_t, down)


def add_kernel(plan, *refs):
    count = sum(len(terms) for terms in plan)
    ins, outs = refs[:count], refs[count:]
    at = 0
    for terms, out in zip(plan, outs):
        size = out.shape[0]
        total = None
        for first in terms:
            term = ins[at][first : first + size].astype(jnp.float32)
            total = term if total is None else total + term
            at += 1
        out[...] = total.astype(out.dtype)


def add_parts(rows, *sums):
    plan = [[first for _, first in terms] for terms in sums]
    width = sums[0][0][0].shape[1]
    return pl.pallas_call(
        lambda *refs: add_kernel(plan, *refs),
        out_shape=[jax.ShapeDtypeStruct((rows, width), jnp.bfloat16) for _ in sums],
        compiler_params=pltpu.CompilerParams(vmem_limit_bytes=GRANT),
    )(*[array for terms in sums for array, _ in terms])


def finish_kernel(parts, *refs):
    hidden_ref, own_ref, other_ref = refs[:3]
    out_ref = refs[-1]
    total = hidden_ref[...] + own_ref[...].astype(jnp.float32) + other_ref[...].astype(jnp.float32)
    at = 3
    for first, size, count in parts:
        piece = total[first : first + size]
        for ref in refs[at : at + count]:
            piece = piece + ref[...].astype(jnp.float32)
        at += count
        out_ref[first : first + size, :] = piece.astype(out_ref.dtype)


def finish(hidden_state, own, other, *halves):
    parts, first = [], 0
    for arrays in halves:
        parts.append((first, arrays[0].shape[0], len(arrays)))
        first += arrays[0].shape[0]
    return pl.pallas_call(
        lambda *refs: finish_kernel(parts, *refs),
        out_shape=jax.ShapeDtypeStruct(hidden_state.shape, jnp.bfloat16),
        compiler_params=pltpu.CompilerParams(vmem_limit_bytes=GRANT),
    )(hidden_state, own, other, *[array for arrays in halves for array in arrays])


def ring_pairs(chips, cores, turn):
    order = list(range(0, chips, 2)) + list(range(1, chips, 2))[::-1]
    return [
        (order[p] * cores + core, order[(p + turn) % chips] * cores + core)
        for p in range(chips)
        for core in range(cores)
    ]


def per_device(
    query,
    new_key,
    new_value,
    cache_keys,
    cache_values,
    lengths,
    out_proj,
    residual,
    norm_gain,
    router,
    routes,
    w_gate,
    w_up,
    w_down,
):
    chips, cores = lax.axis_size("att"), lax.axis_size("exp")
    own_rows = residual.shape[0]
    ring = ("att", "exp")

    def send_right(x):
        return lax.ppermute(x, ring, ring_pairs(chips, cores, 1))

    def send_left(x):
        return lax.ppermute(x, ring, ring_pairs(chips, cores, -1))

    def swap(x):
        return lax.ppermute(x, "exp", [(0, 1), (1, 0)])

    where = jnp.stack([lax.axis_index("exp"), lax.axis_index("att")])
    small = (where, own_rows, lengths, query, new_key, new_value)
    theirs, w_out, own_keys, own_values = attend_theirs(
        *small, cache_keys, cache_values, out_proj.T
    )
    swapped = swap(theirs)
    gate_t, up_t = w_gate.transpose(0, 2, 1), w_up.transpose(0, 2, 1)
    mine, gate_t, up_t = attend_mine(*small, own_keys, own_values, w_out, gate_t, up_t)
    hidden_state, payload = norm_route(mine, swapped, residual, norm_gain, router, routes)

    experts = router.shape[1]

    def expert(blocks, down):
        return run_expert(where, blocks, gate_t, up_t, down, experts)

    far = chips // 2
    middle = own_rows // 2
    *done, down = expert((payload, swap(payload)), w_down)
    own, own_other = done[0], swap(done[1])
    from_left, from_right = [None], [None]
    right = left = payload
    for k in range(1, far + 1):
        if k == far:
            right, left = right[:middle], left[middle:]
        right, left = send_right(right), send_left(left)
        right, _ = lax.optimization_barrier((right, done[0]))
        left, _ = lax.optimization_barrier((left, done[1]))
        if k > 2:
            before = (from_left[k - 2], from_right[k - 2])
            right, left, before = lax.optimization_barrier((right, left, before))
            from_left[k - 2], from_right[k - 2] = before
        done = expert((right, swap(right), left, swap(left)), down)
        from_left.append((done[0], swap(done[1])))
        from_right.append((done[2], swap(done[3])))

    def parts(pair, first):
        return [(array, first) for array in pair]

    short_top, short_low = None, None
    long_top, long_low = add_parts(middle, parts(from_left[far], 0), parts(from_right[far], 0))
    long_top, long_low = send_left(long_top), send_right(long_low)
    for k in range(far - 1, 0, -1):
        top, low = parts(from_right[k], 0), parts(from_left[k], middle)
        if short_top is not None:
            top, low = top + [(short_top, 0)], low + [(short_low, 0)]
        short_top, short_low = add_parts(middle, top, low)
        short_top, short_low = send_right(short_top), send_left(short_low)
        top, low = parts(from_left[k], 0), parts(from_right[k], middle)
        long_top, long_low = add_parts(middle, top + [(long_top, 0)], low + [(long_low, 0)])
        long_top, long_low = send_left(long_top), send_right(long_low)
    return finish(hidden_state, own, own_other, (long_top, short_top), (long_low, short_low))


def solution(mesh):
    in_specs = (
        P(("groups", "att"), "exp"),
        P(("groups", "att"), "exp"),
        P(("groups", "att"), "exp"),
        P(("groups", "att"), None, "exp"),
        P(("groups", "att"), None, "exp"),
        P(("groups", "att")),
        P("exp", None),
        P(("groups", "att", "exp"), None),
        P(),
        P(),
        P(("groups", "att", "exp"), None),
        P("att", None, "exp"),
        P("att", None, "exp"),
        P("att", "exp", None),
    )
    out_specs = P(("groups", "att", "exp"), None)
    return jax.shard_map(
        per_device, mesh=mesh, in_specs=in_specs, out_specs=out_specs, check_vma=False
    )
```

```python
import math

import jax
import jax.numpy as jnp
from jax import lax
from jax.experimental import pallas as pl
from jax.experimental.pallas import tpu as pltpu
from jax.sharding import PartitionSpec as P

HEAD = 64
SUB = 8
STEP = 16
GRANT = 12 * 1024 * 1024
ACROSS = (((1,), (1,)), ((), ()))


def place_heads(queries, heads, slots, width):
    group_size = heads // slots
    slot_of_lane = lax.broadcasted_iota(jnp.int32, (SUB, width), 1) // HEAD
    pieces = []
    for head in range(heads):
        block, slot, home = head // slots, head % slots, head // group_size
        piece = queries[:, block * width : (block + 1) * width]
        if slot != home:
            piece = pltpu.roll(piece, ((home - slot) * HEAD) % width, 1)
        pieces.append(jnp.where(slot_of_lane == home, piece, 0.0))
    return jnp.concatenate(pieces, axis=0).astype(jnp.bfloat16)


def score(rows, keys, fresh_k, cache_len):
    request = lax.broadcasted_iota(jnp.int32, (cache_len, rows.shape[0]), 1) % SUB
    spread = lax.dot_general(keys, rows, ACROSS, preferred_element_type=jnp.float32)
    scores = spread[:cache_len]
    for r in range(1, SUB):
        scores = jnp.where(request == r, spread[r * cache_len : (r + 1) * cache_len], scores)
    return scores, lax.dot_general(fresh_k, rows, ACROSS, preferred_element_type=jnp.float32)


def soften(scores, fresh, live, offset, per):
    cache_len, count = scores.shape
    request = lax.broadcasted_iota(jnp.int32, (cache_len, count), 1) % SUB
    place = lax.broadcasted_iota(jnp.int32, (cache_len, count), 0)
    scores = jnp.where(place < live, scores, -1e30)
    fresh_place = lax.broadcasted_iota(jnp.int32, fresh.shape, 0)
    fresh_own = fresh_place == offset + lax.broadcasted_iota(jnp.int32, fresh.shape, 1) % SUB
    fresh_scores = jnp.sum(jnp.where(fresh_own, fresh, 0.0), axis=0, keepdims=True)
    highest = jnp.maximum(jnp.max(scores, axis=0, keepdims=True), fresh_scores)
    cached_exp = jnp.exp(scores - highest)
    fresh_exp = jnp.exp(fresh_scores - highest)
    scale = 1.0 / (jnp.sum(cached_exp, axis=0, keepdims=True) + fresh_exp)
    probs = cached_exp * scale
    fresh_probs = jnp.where(fresh_own, fresh_exp * scale, 0.0)
    return jnp.concatenate(
        [jnp.where(request % per == i, probs, 0.0) for i in range(per)] + [fresh_probs], axis=0
    ).T


def weigh(turned, values, fresh_v, per):
    count, width = turned.shape[0], values.shape[1]
    group = lax.broadcasted_iota(jnp.int32, (count, width), 0) % SUB // per
    wide = jnp.concatenate(
        [jnp.where(group == part, turned[:, :width], 0.0) for part in range(SUB // per)], axis=1
    ).astype(jnp.bfloat16)
    output = jnp.dot(wide, values, preferred_element_type=jnp.float32)
    return output + jnp.dot(
        turned[:, width:].astype(jnp.bfloat16), fresh_v, preferred_element_type=jnp.float32
    )


def gather_heads(output, heads, slots, width):
    group_size = heads // slots
    slot_of_lane = lax.broadcasted_iota(jnp.int32, (SUB, width), 1) // HEAD
    blocks = []
    for block in range(heads // slots):
        merged = None
        for slot in range(slots):
            head = block * slots + slot
            home = head // group_size
            piece = output[head * SUB : (head + 1) * SUB]
            if slot != home:
                piece = pltpu.roll(piece, ((slot - home) * HEAD) % width, 1)
            merged = piece if merged is None else jnp.where(slot_of_lane == slot, piece, merged)
        blocks.append(merged)
    return jnp.concatenate(blocks, axis=-1)


def attend(first, lengths_ref, q_ref, nk_ref, nv_ref, k_ref, v_ref, att_ref, ready):
    width = nk_ref.shape[1]
    slots = width // HEAD
    heads = q_ref.shape[1] // HEAD
    cache_len = k_ref.shape[1]
    per = width // cache_len
    request = lax.broadcasted_iota(jnp.int32, (1, heads * SUB), 1) % SUB
    batches = range(0, att_ref.shape[0], SUB)
    scores = []
    for at in batches:
        step = at // STEP * STEP
        if at == step:
            ready(at)
            queries = q_ref[step : step + STEP].astype(jnp.float32) * (1.0 / math.sqrt(HEAD))
        rows = place_heads(queries[at - step : at - step + SUB], heads, slots, width)
        keys = k_ref[at : at + SUB].reshape(SUB * cache_len, width)
        scores.append(score(rows, keys, nk_ref[step : step + STEP], cache_len))
    turned = []
    for at, (cached, fresh) in zip(batches, scores):
        live = jnp.zeros(request.shape, jnp.int32)
        for i in range(SUB):
            live = jnp.where(request == i, lengths_ref[first + at + i], live)
        turned.append(soften(cached, fresh, live, at % STEP, per))
    outputs = []
    for at, probs in zip(batches, turned):
        step = at // STEP * STEP
        values = v_ref[at : at + SUB].reshape(SUB * cache_len, width)
        outputs.append(weigh(probs, values, nv_ref[step : step + STEP], per))
    for step in range(0, att_ref.shape[0], STEP):
        pair = outputs[step // SUB : (step + STEP) // SUB]
        att_ref[step : step + STEP, :] = jnp.concatenate(
            [gather_heads(output, heads, slots, width) for output in pair], axis=0
        ).astype(jnp.bfloat16)


def project(att_ref, w_ref, out_ref):
    columns = w_ref.shape[0]
    for at in range(0, columns, 768):
        size = min(768, columns - at)
        turned = lax.dot_general(
            w_ref[at : at + size, :], att_ref[...], ACROSS, preferred_element_type=jnp.float32
        )
        out_ref[:, at : at + size] = turned.T


def first_kernel(
    core_ref, lengths_ref, q_hbm, nk_hbm, nv_hbm, k_hbm, v_hbm, w_hbm,
    out_ref, w_ref, own_k, own_v, q_ref, nk_ref, nv_ref, k_ref, v_ref, att_ref, sems,
):
    rows = out_ref.shape[0]
    theirs = pl.multiple_of((1 - core_ref[0]) * rows, rows)
    mine = pl.multiple_of(core_ref[0] * rows, rows)
    copies = []

    def bring(source, target):
        copy = pltpu.make_async_copy(source, target, sems.at[len(copies)])
        copy.start()
        copies.append(copy)
        return copy

    small = [
        bring(source.at[pl.ds(theirs, rows)], target)
        for source, target in ((q_hbm, q_ref), (nk_hbm, nk_ref), (nv_hbm, nv_ref))
    ]
    cache = []
    for at in range(0, rows, STEP):
        span = pl.ds(theirs + at, STEP)
        cache.append(
            (
                bring(k_hbm.at[span], k_ref.at[pl.ds(at, STEP)]),
                bring(v_hbm.at[span], v_ref.at[pl.ds(at, STEP)]),
            )
        )
    pieces = 4
    columns = w_ref.shape[0]
    size = -(-columns // pieces // 16) * 16
    weights = []
    for at in range(0, columns, size):
        span = pl.ds(at, min(size, columns - at))
        weights.append(bring(w_hbm.at[span], w_ref.at[span]))
    later = [
        bring(k_hbm.at[pl.ds(mine, rows)], own_k),
        bring(v_hbm.at[pl.ds(mine, rows)], own_v),
    ]
    for copy in small:
        copy.wait()

    def ready(at):
        for copy in cache[at // STEP]:
            copy.wait()

    attend(theirs, lengths_ref, q_ref, nk_ref, nv_ref, k_ref, v_ref, att_ref, ready)
    for copy in weights:
        copy.wait()
    project(att_ref, w_ref, out_ref)
    for copy in later:
        copy.wait()


def second_kernel(
    core_ref, lengths_ref, q_ref, nk_ref, nv_ref, k_ref, v_ref, w_ref, gate_hbm, up_hbm,
    out_ref, gate_ref, up_ref, att_ref, sems,
):
    copies = [
        pltpu.make_async_copy(gate_hbm.at[0], gate_ref, sems.at[0]),
        pltpu.make_async_copy(up_hbm.at[0], up_ref, sems.at[1]),
    ]
    for copy in copies:
        copy.start()
    rows = out_ref.shape[0]
    mine = pl.multiple_of(core_ref[0] * rows, rows)
    own = [ref.at[pl.ds(mine, rows)] for ref in (q_ref, nk_ref, nv_ref)]
    attend(mine, lengths_ref, *own, k_ref, v_ref, att_ref, lambda at: None)
    project(att_ref, w_ref, out_ref)
    for copy in copies:
        copy.wait()


def attend_theirs(core, rows, lengths, query, new_key, new_value, cache_keys, cache_values, w):
    cache = (rows,) + cache_keys.shape[1:]
    columns = w.shape[0]
    smem = pl.BlockSpec(memory_space=pltpu.SMEM)
    vmem = pl.BlockSpec(memory_space=pltpu.VMEM)
    hbm = pl.BlockSpec(memory_space=pltpu.HBM)
    copies = 3 + 2 * (rows // STEP) + 4 + 2
    return pl.pallas_call(
        first_kernel,
        out_shape=(
            jax.ShapeDtypeStruct((rows, columns), jnp.float32),
            jax.ShapeDtypeStruct(w.shape, jnp.bfloat16),
            jax.ShapeDtypeStruct(cache, jnp.bfloat16),
            jax.ShapeDtypeStruct(cache, jnp.bfloat16),
        ),
        in_specs=[smem, smem] + [hbm] * 6,
        out_specs=[vmem] * 4,
        scratch_shapes=[
            pltpu.VMEM((rows, query.shape[1]), jnp.bfloat16),
            pltpu.VMEM((rows, new_key.shape[1]), jnp.bfloat16),
            pltpu.VMEM((rows, new_key.shape[1]), jnp.bfloat16),
            pltpu.VMEM(cache, jnp.bfloat16),
            pltpu.VMEM(cache, jnp.bfloat16),
            pltpu.VMEM((rows, query.shape[1]), jnp.bfloat16),
            pltpu.SemaphoreType.DMA((copies,)),
        ],
        compiler_params=pltpu.CompilerParams(vmem_limit_bytes=GRANT),
        cost_estimate=pl.CostEstimate(
            flops=2 * rows * w.size, bytes_accessed=2 * w.size, transcendentals=0
        ),
    )(
        core,
        lengths,
        *(
            pltpu.with_memory_space_constraint(x, pltpu.HBM)
            for x in (query, new_key, new_value, cache_keys, cache_values, w)
        ),
    )


def attend_mine(
    core, rows, lengths, query, new_key, new_value, own_keys, own_values, w, gate_t, up_t
):
    smem = pl.BlockSpec(memory_space=pltpu.SMEM)
    vmem = pl.BlockSpec(memory_space=pltpu.VMEM)
    hbm = pl.BlockSpec(memory_space=pltpu.HBM)
    return pl.pallas_call(
        second_kernel,
        out_shape=(
            jax.ShapeDtypeStruct((rows, w.shape[0]), jnp.float32),
            jax.ShapeDtypeStruct(gate_t.shape[1:], jnp.bfloat16),
            jax.ShapeDtypeStruct(up_t.shape[1:], jnp.bfloat16),
        ),
        in_specs=[smem, smem] + [vmem] * 6 + [hbm] * 2,
        out_specs=[vmem] * 3,
        scratch_shapes=[
            pltpu.VMEM((rows, query.shape[1]), jnp.bfloat16),
            pltpu.SemaphoreType.DMA((2,)),
        ],
        compiler_params=pltpu.CompilerParams(vmem_limit_bytes=GRANT),
        cost_estimate=pl.CostEstimate(
            flops=2 * rows * w.size, bytes_accessed=4 * gate_t.size, transcendentals=0
        ),
    )(
        core,
        lengths,
        query,
        new_key,
        new_value,
        own_keys,
        own_values,
        w,
        pltpu.with_memory_space_constraint(gate_t, pltpu.HBM),
        pltpu.with_memory_space_constraint(up_t, pltpu.HBM),
    )


def norm_kernel(
    mine_ref, swapped_ref, residual_ref, gain_ref, router_ref, routes_ref, hidden_ref, payload_ref
):
    hidden = residual_ref[...].astype(jnp.float32) + (mine_ref[...] + swapped_ref[...])
    hidden_ref[...] = hidden
    rows, width = hidden.shape
    mean_square = jnp.sum(hidden * hidden, axis=-1, keepdims=True) * (1.0 / width)
    normed = (hidden * lax.rsqrt(mean_square + 1e-05) * gain_ref[...]).astype(jnp.bfloat16)
    payload_ref[:, :width] = normed
    rest = router_ref[...]
    experts = rest.shape[0]
    terms = []
    for _ in range(3):
        term = rest.astype(jnp.bfloat16).astype(jnp.float32)
        terms.append(term)
        rest = rest - term
    parts = lax.dot_general(
        jnp.concatenate(terms, axis=0).astype(jnp.bfloat16),
        normed,
        (((1,), (1,)), ((), ())),
        preferred_element_type=jnp.float32,
    )
    logits = parts[:experts] + parts[experts : 2 * experts] + parts[2 * experts :]
    number = lax.broadcasted_iota(jnp.int32, (experts, rows), 0)
    chosen = number == routes_ref[0:1, :]
    for k in range(1, routes_ref.shape[0]):
        chosen = chosen | (number == routes_ref[k : k + 1, :])
    squashed = jnp.where(chosen, 1.0 / (1.0 + jnp.exp(-logits)), 0.0)
    gates = squashed / jnp.sum(squashed, axis=0, keepdims=True)
    upper = gates.astype(jnp.bfloat16).astype(jnp.float32)
    both = jnp.concatenate([upper, gates - upper], axis=0).astype(jnp.bfloat16)
    tail = payload_ref.shape[1] - width
    place = lax.broadcasted_iota(jnp.int32, (2 * experts, tail), 0)
    lane = lax.broadcasted_iota(jnp.int32, (2 * experts, tail), 1)
    placed = lax.dot_general(
        both,
        (place == lane).astype(jnp.bfloat16),
        (((0,), (0,)), ((), ())),
        preferred_element_type=jnp.float32,
    )
    payload_ref[:, width:] = placed.astype(jnp.bfloat16)


def norm_route(mine, swapped, residual, norm_gain, router, routes):
    rows, width = residual.shape
    experts = router.shape[1]
    wide = -(-(width + 2 * experts) // 128) * 128
    return pl.pallas_call(
        norm_kernel,
        out_shape=(
            jax.ShapeDtypeStruct((rows, width), jnp.float32),
            jax.ShapeDtypeStruct((rows, wide), jnp.bfloat16),
        ),
        compiler_params=pltpu.CompilerParams(vmem_limit_bytes=GRANT),
    )(mine, swapped, residual, norm_gain[None, :], router.T, routes.T)


def expert_kernel(count, experts, bring, which_ref, *refs):
    blocks, refs = refs[:count], refs[count:]
    gate_ref, up_ref, down_ref = refs[:3]
    outs, refs = refs[3 : 3 + count], refs[3 + count :]
    copy = None
    if bring:
        kept_ref, act_ref, sem = refs
        copy = pltpu.make_async_copy(down_ref.at[0], kept_ref, sem)
        copy.start()
        down_ref = kept_ref
    else:
        (act_ref,) = refs
    hidden, width = gate_ref.shape
    rows = jnp.concatenate([block[...] for block in blocks], axis=0)
    base = width // 128 * 128
    tail = rows[:, base:].astype(jnp.float32)
    lane = lax.broadcasted_iota(jnp.int32, tail.shape, 1) - (width - base)
    named = (lane == which_ref[1]) | (lane == which_ref[1] + experts)
    weight = jnp.sum(jnp.where(named, tail, 0.0), axis=-1, keepdims=True)
    turned = rows[:, :width].T
    for at in range(0, hidden, 256):
        span = slice(at, min(at + 256, hidden))
        gate = jnp.dot(gate_ref[span, :], turned, preferred_element_type=jnp.float32)
        up = jnp.dot(up_ref[span, :], turned, preferred_element_type=jnp.float32)
        act_ref[:, span] = (gate / (1.0 + jnp.exp(-gate)) * up).T.astype(jnp.bfloat16)
    if copy is not None:
        copy.wait()
    for at in range(0, width, 768):
        span = slice(at, min(at + 768, width))
        part = jnp.dot(act_ref[...], down_ref[:, span], preferred_element_type=jnp.float32)
        part = (part * weight).astype(jnp.bfloat16)
        first = 0
        for out in outs:
            out[:, span] = part[first : first + out.shape[0]]
            first += out.shape[0]


def run_expert(which, blocks, gate_t, up_t, down, experts):
    hidden, width = gate_t.shape
    bring = down.ndim == 3
    rows = sum(block.shape[0] for block in blocks)
    count = len(blocks)
    vmem = pl.BlockSpec(memory_space=pltpu.VMEM)
    outs = [jax.ShapeDtypeStruct((b.shape[0], width), jnp.bfloat16) for b in blocks]
    scratch = [pltpu.VMEM((rows, hidden), jnp.bfloat16)]
    source = vmem
    if bring:
        outs.append(jax.ShapeDtypeStruct((hidden, width), jnp.bfloat16))
        scratch.append(pltpu.SemaphoreType.DMA)
        down = pltpu.with_memory_space_constraint(down, pltpu.HBM)
        source = pl.BlockSpec(memory_space=pltpu.HBM)
    return pl.pallas_call(
        lambda *refs: expert_kernel(count, experts, bring, *refs),
        out_shape=outs,
        in_specs=[pl.BlockSpec(memory_space=pltpu.SMEM)] + [vmem] * (count + 2) + [source],
        out_specs=[vmem] * len(outs),
        scratch_shapes=scratch,
        compiler_params=pltpu.CompilerParams(vmem_limit_bytes=GRANT),
        cost_estimate=pl.CostEstimate(
            flops=6 * rows * hidden * width, bytes_accessed=6 * hidden * width, transcendentals=0
        ),
    )(which, *blocks, gate_t, up_t, down)


def add_kernel(*refs):
    total = refs[0][...].astype(jnp.float32)
    for ref in refs[1:-1]:
        total = total + ref[...].astype(jnp.float32)
    refs[-1][...] = total.astype(refs[-1].dtype)


def add_all(*terms):
    return pl.pallas_call(
        add_kernel,
        out_shape=jax.ShapeDtypeStruct(terms[0].shape, jnp.bfloat16),
        compiler_params=pltpu.CompilerParams(vmem_limit_bytes=GRANT),
    )(*terms)


def ring_pairs(chips, cores, cross):
    order = list(range(0, chips, 2)) + list(range(1, chips, 2))[::-1]
    pairs = []
    for p in range(chips):
        for core in range(cores):
            turn = -1 if core % 2 else 1
            to = core ^ 1 if cross else core
            pairs.append((order[p] * cores + core, order[(p + turn) % chips] * cores + to))
    return pairs


def per_device(
    query,
    new_key,
    new_value,
    cache_keys,
    cache_values,
    lengths,
    out_proj,
    residual,
    norm_gain,
    router,
    routes,
    w_gate,
    w_up,
    w_down,
):
    chips, cores = lax.axis_size("att"), lax.axis_size("exp")
    own_rows = residual.shape[0]
    ring = ("att", "exp")

    def send(x, cross=False):
        return lax.ppermute(x, ring, ring_pairs(chips, cores, cross))

    def swap(x):
        return lax.ppermute(x, "exp", [(0, 1), (1, 0)])

    where = jnp.stack([lax.axis_index("exp"), lax.axis_index("att")])
    small = (where, own_rows, lengths, query, new_key, new_value)
    theirs, w_out, own_keys, own_values = attend_theirs(
        *small, cache_keys, cache_values, out_proj.T
    )
    swapped = swap(theirs)
    gate_t, up_t = w_gate.transpose(0, 2, 1), w_up.transpose(0, 2, 1)
    mine, gate_t, up_t = attend_mine(*small, own_keys, own_values, w_out, gate_t, up_t)
    hidden_state, payload = norm_route(mine, swapped, residual, norm_gain, router, routes)

    experts = router.shape[1]

    def expert(blocks, down):
        return run_expert(where, blocks, gate_t, up_t, down, experts)

    far = chips // 2
    x, y = payload, swap(payload)
    *done, down = expert((x, y), w_down)
    own, own_other = done[0], swap(done[1])
    sums_x, sums_y = [None], [None]
    for k in range(1, far + 1):
        x = send(x)
        x, _ = lax.optimization_barrier((x, done[0]))
        blocks = [x, swap(x)]
        if k < far:
            y = send(y)
            y, _ = lax.optimization_barrier((y, done[0]))
            blocks += [y, swap(y)]
        if k > 2:
            before = (sums_x[k - 2], sums_y[k - 2])
            blocks[0], before = lax.optimization_barrier((blocks[0], before))
            sums_x[k - 2], sums_y[k - 2] = before
        done = expert(blocks, down)
        sums_x.append((done[1], swap(done[0])))
        if k < far:
            sums_y.append((done[3], swap(done[2])))

    back_x = back_y = None
    for k in range(far, 0, -1):
        if k < far:
            back_y = send(add_all(*sums_y[k], *([] if back_y is None else [back_y])))
        back_x = send(add_all(*sums_x[k], *([] if back_x is None else [back_x])), k == 1)
    return add_all(hidden_state, own, own_other, back_x, *([] if back_y is None else [back_y]))


def solution(mesh):
    in_specs = (
        P(("groups", "att"), "exp"),
        P(("groups", "att"), "exp"),
        P(("groups", "att"), "exp"),
        P(("groups", "att"), None, "exp"),
        P(("groups", "att"), None, "exp"),
        P(("groups", "att")),
        P("exp", None),
        P(("groups", "att", "exp"), None),
        P(),
        P(),
        P(("groups", "att", "exp"), None),
        P("att", None, "exp"),
        P("att", None, "exp"),
        P("att", "exp", None),
    )
    out_specs = P(("groups", "att", "exp"), None)
    return jax.shard_map(
        per_device, mesh=mesh, in_specs=in_specs, out_specs=out_specs, check_vma=False
    )
```

```python
import math

import jax
import jax.numpy as jnp
from jax import lax
from jax.experimental import pallas as pl
from jax.experimental.pallas import tpu as pltpu
from jax.sharding import PartitionSpec as P

HEAD = 64
SUB = 8
STEP = 16
GRANT = 12 * 1024 * 1024
ACROSS = (((1,), (1,)), ((), ()))


def place_heads(queries, heads, slots, width):
    group_size = heads // slots
    slot_of_lane = lax.broadcasted_iota(jnp.int32, (SUB, width), 1) // HEAD
    pieces = []
    for head in range(heads):
        block, slot, home = head // slots, head % slots, head // group_size
        piece = queries[:, block * width : (block + 1) * width]
        if slot != home:
            piece = pltpu.roll(piece, ((home - slot) * HEAD) % width, 1)
        pieces.append(jnp.where(slot_of_lane == home, piece, 0.0))
    return jnp.concatenate(pieces, axis=0).astype(jnp.bfloat16)


def score(rows, keys, fresh_k, cache_len):
    request = lax.broadcasted_iota(jnp.int32, (cache_len, rows.shape[0]), 1) % SUB
    spread = lax.dot_general(keys, rows, ACROSS, preferred_element_type=jnp.float32)
    scores = spread[:cache_len]
    for r in range(1, SUB):
        scores = jnp.where(request == r, spread[r * cache_len : (r + 1) * cache_len], scores)
    return scores, lax.dot_general(fresh_k, rows, ACROSS, preferred_element_type=jnp.float32)


def soften(scores, fresh, live, offset, per):
    cache_len, count = scores.shape
    request = lax.broadcasted_iota(jnp.int32, (cache_len, count), 1) % SUB
    place = lax.broadcasted_iota(jnp.int32, (cache_len, count), 0)
    scores = jnp.where(place < live, scores, -1e30)
    fresh_place = lax.broadcasted_iota(jnp.int32, fresh.shape, 0)
    fresh_own = fresh_place == offset + lax.broadcasted_iota(jnp.int32, fresh.shape, 1) % SUB
    fresh_scores = jnp.sum(jnp.where(fresh_own, fresh, 0.0), axis=0, keepdims=True)
    highest = jnp.maximum(jnp.max(scores, axis=0, keepdims=True), fresh_scores)
    cached_exp = jnp.exp(scores - highest)
    fresh_exp = jnp.exp(fresh_scores - highest)
    scale = 1.0 / (jnp.sum(cached_exp, axis=0, keepdims=True) + fresh_exp)
    probs = cached_exp * scale
    fresh_probs = jnp.where(fresh_own, fresh_exp * scale, 0.0)
    return jnp.concatenate(
        [jnp.where(request % per == i, probs, 0.0) for i in range(per)] + [fresh_probs], axis=0
    ).T


def weigh(turned, values, fresh_v, per):
    count, width = turned.shape[0], values.shape[1]
    group = lax.broadcasted_iota(jnp.int32, (count, width), 0) % SUB // per
    wide = jnp.concatenate(
        [jnp.where(group == part, turned[:, :width], 0.0) for part in range(SUB // per)], axis=1
    ).astype(jnp.bfloat16)
    output = jnp.dot(wide, values, preferred_element_type=jnp.float32)
    return output + jnp.dot(
        turned[:, width:].astype(jnp.bfloat16), fresh_v, preferred_element_type=jnp.float32
    )


def gather_heads(output, heads, slots, width):
    group_size = heads // slots
    slot_of_lane = lax.broadcasted_iota(jnp.int32, (SUB, width), 1) // HEAD
    blocks = []
    for block in range(heads // slots):
        merged = None
        for slot in range(slots):
            head = block * slots + slot
            home = head // group_size
            piece = output[head * SUB : (head + 1) * SUB]
            if slot != home:
                piece = pltpu.roll(piece, ((slot - home) * HEAD) % width, 1)
            merged = piece if merged is None else jnp.where(slot_of_lane == slot, piece, merged)
        blocks.append(merged)
    return jnp.concatenate(blocks, axis=-1)


def attend(first, lengths_ref, q_ref, nk_ref, nv_ref, k_ref, v_ref, att_ref, ready):
    width = nk_ref.shape[1]
    slots = width // HEAD
    heads = q_ref.shape[1] // HEAD
    cache_len = k_ref.shape[1]
    per = width // cache_len
    request = lax.broadcasted_iota(jnp.int32, (1, heads * SUB), 1) % SUB
    batches = range(0, att_ref.shape[0], SUB)
    scores = []
    for at in batches:
        step = at // STEP * STEP
        if at == step:
            ready(at)
            queries = q_ref[step : step + STEP].astype(jnp.float32) * (1.0 / math.sqrt(HEAD))
        rows = place_heads(queries[at - step : at - step + SUB], heads, slots, width)
        keys = k_ref[at : at + SUB].reshape(SUB * cache_len, width)
        scores.append(score(rows, keys, nk_ref[step : step + STEP], cache_len))
    turned = []
    for at, (cached, fresh) in zip(batches, scores):
        live = jnp.zeros(request.shape, jnp.int32)
        for i in range(SUB):
            live = jnp.where(request == i, lengths_ref[first + at + i], live)
        turned.append(soften(cached, fresh, live, at % STEP, per))
    outputs = []
    for at, probs in zip(batches, turned):
        step = at // STEP * STEP
        values = v_ref[at : at + SUB].reshape(SUB * cache_len, width)
        outputs.append(weigh(probs, values, nv_ref[step : step + STEP], per))
    for step in range(0, att_ref.shape[0], STEP):
        pair = outputs[step // SUB : (step + STEP) // SUB]
        att_ref[step : step + STEP, :] = jnp.concatenate(
            [gather_heads(output, heads, slots, width) for output in pair], axis=0
        ).astype(jnp.bfloat16)


def project(att_ref, w_ref, out_ref):
    columns = w_ref.shape[0]
    for at in range(0, columns, 768):
        size = min(768, columns - at)
        turned = lax.dot_general(
            w_ref[at : at + size, :], att_ref[...], ACROSS, preferred_element_type=jnp.float32
        )
        out_ref[:, at : at + size] = turned.T


def first_kernel(
    core_ref, lengths_ref, q_hbm, nk_hbm, nv_hbm, k_hbm, v_hbm, w_hbm,
    out_ref, w_ref, own_k, own_v, q_ref, nk_ref, nv_ref, k_ref, v_ref, att_ref, sems,
):
    rows = out_ref.shape[0]
    theirs = pl.multiple_of((1 - core_ref[0]) * rows, rows)
    mine = pl.multiple_of(core_ref[0] * rows, rows)
    copies = []

    def bring(source, target):
        copy = pltpu.make_async_copy(source, target, sems.at[len(copies)])
        copy.start()
        copies.append(copy)
        return copy

    small = [
        bring(source.at[pl.ds(theirs, rows)], target)
        for source, target in ((q_hbm, q_ref), (nk_hbm, nk_ref), (nv_hbm, nv_ref))
    ]
    cache = []
    for at in range(0, rows, STEP):
        span = pl.ds(theirs + at, STEP)
        cache.append(
            (
                bring(k_hbm.at[span], k_ref.at[pl.ds(at, STEP)]),
                bring(v_hbm.at[span], v_ref.at[pl.ds(at, STEP)]),
            )
        )
    pieces = 4
    columns = w_ref.shape[0]
    size = -(-columns // pieces // 16) * 16
    weights = []
    for at in range(0, columns, size):
        span = pl.ds(at, min(size, columns - at))
        weights.append(bring(w_hbm.at[span], w_ref.at[span]))
    later = [
        bring(k_hbm.at[pl.ds(mine, rows)], own_k),
        bring(v_hbm.at[pl.ds(mine, rows)], own_v),
    ]
    for copy in small:
        copy.wait()

    def ready(at):
        for copy in cache[at // STEP]:
            copy.wait()

    attend(theirs, lengths_ref, q_ref, nk_ref, nv_ref, k_ref, v_ref, att_ref, ready)
    for copy in weights:
        copy.wait()
    project(att_ref, w_ref, out_ref)
    for copy in later:
        copy.wait()


def second_kernel(
    core_ref, lengths_ref, q_ref, nk_ref, nv_ref, k_ref, v_ref, w_ref, gate_hbm,
    out_ref, gate_ref, att_ref, sem,
):
    copy = pltpu.make_async_copy(gate_hbm.at[0], gate_ref, sem)
    copy.start()
    rows = out_ref.shape[0]
    mine = pl.multiple_of(core_ref[0] * rows, rows)
    own = [ref.at[pl.ds(mine, rows)] for ref in (q_ref, nk_ref, nv_ref)]
    attend(mine, lengths_ref, *own, k_ref, v_ref, att_ref, lambda at: None)
    project(att_ref, w_ref, out_ref)
    copy.wait()


def attend_theirs(core, rows, lengths, query, new_key, new_value, cache_keys, cache_values, w):
    cache = (rows,) + cache_keys.shape[1:]
    columns = w.shape[0]
    smem = pl.BlockSpec(memory_space=pltpu.SMEM)
    vmem = pl.BlockSpec(memory_space=pltpu.VMEM)
    hbm = pl.BlockSpec(memory_space=pltpu.HBM)
    copies = 3 + 2 * (rows // STEP) + 4 + 2
    return pl.pallas_call(
        first_kernel,
        out_shape=(
            jax.ShapeDtypeStruct((rows, columns), jnp.float32),
            jax.ShapeDtypeStruct(w.shape, jnp.bfloat16),
            jax.ShapeDtypeStruct(cache, jnp.bfloat16),
            jax.ShapeDtypeStruct(cache, jnp.bfloat16),
        ),
        in_specs=[smem, smem] + [hbm] * 6,
        out_specs=[vmem] * 4,
        scratch_shapes=[
            pltpu.VMEM((rows, query.shape[1]), jnp.bfloat16),
            pltpu.VMEM((rows, new_key.shape[1]), jnp.bfloat16),
            pltpu.VMEM((rows, new_key.shape[1]), jnp.bfloat16),
            pltpu.VMEM(cache, jnp.bfloat16),
            pltpu.VMEM(cache, jnp.bfloat16),
            pltpu.VMEM((rows, query.shape[1]), jnp.bfloat16),
            pltpu.SemaphoreType.DMA((copies,)),
        ],
        compiler_params=pltpu.CompilerParams(vmem_limit_bytes=GRANT),
        cost_estimate=pl.CostEstimate(
            flops=2 * rows * w.size, bytes_accessed=2 * w.size, transcendentals=0
        ),
    )(
        core,
        lengths,
        *(
            pltpu.with_memory_space_constraint(x, pltpu.HBM)
            for x in (query, new_key, new_value, cache_keys, cache_values, w)
        ),
    )


def attend_mine(core, rows, lengths, query, new_key, new_value, own_keys, own_values, w, gate_t):
    smem = pl.BlockSpec(memory_space=pltpu.SMEM)
    vmem = pl.BlockSpec(memory_space=pltpu.VMEM)
    return pl.pallas_call(
        second_kernel,
        out_shape=(
            jax.ShapeDtypeStruct((rows, w.shape[0]), jnp.float32),
            jax.ShapeDtypeStruct(gate_t.shape[1:], jnp.bfloat16),
        ),
        in_specs=[smem, smem] + [vmem] * 6 + [pl.BlockSpec(memory_space=pltpu.HBM)],
        out_specs=[vmem] * 2,
        scratch_shapes=[
            pltpu.VMEM((rows, query.shape[1]), jnp.bfloat16),
            pltpu.SemaphoreType.DMA,
        ],
        compiler_params=pltpu.CompilerParams(vmem_limit_bytes=GRANT),
        cost_estimate=pl.CostEstimate(
            flops=2 * rows * w.size, bytes_accessed=2 * w.size, transcendentals=0
        ),
    )(
        core,
        lengths,
        query,
        new_key,
        new_value,
        own_keys,
        own_values,
        w,
        pltpu.with_memory_space_constraint(gate_t, pltpu.HBM),
    )


def norm_kernel(
    mine_ref, swapped_ref, residual_ref, gain_ref, router_ref, routes_ref, hidden_ref, payload_ref
):
    hidden = residual_ref[...].astype(jnp.float32) + (mine_ref[...] + swapped_ref[...])
    hidden_ref[...] = hidden
    rows, width = hidden.shape
    mean_square = jnp.sum(hidden * hidden, axis=-1, keepdims=True) * (1.0 / width)
    normed = (hidden * lax.rsqrt(mean_square + 1e-05) * gain_ref[...]).astype(jnp.bfloat16)
    payload_ref[:, :width] = normed
    rest = router_ref[...]
    experts = rest.shape[0]
    terms = []
    for _ in range(3):
        term = rest.astype(jnp.bfloat16).astype(jnp.float32)
        terms.append(term)
        rest = rest - term
    parts = lax.dot_general(
        jnp.concatenate(terms, axis=0).astype(jnp.bfloat16),
        normed,
        (((1,), (1,)), ((), ())),
        preferred_element_type=jnp.float32,
    )
    logits = parts[:experts] + parts[experts : 2 * experts] + parts[2 * experts :]
    number = lax.broadcasted_iota(jnp.int32, (experts, rows), 0)
    chosen = number == routes_ref[0:1, :]
    for k in range(1, routes_ref.shape[0]):
        chosen = chosen | (number == routes_ref[k : k + 1, :])
    squashed = jnp.where(chosen, 1.0 / (1.0 + jnp.exp(-logits)), 0.0)
    gates = squashed / jnp.sum(squashed, axis=0, keepdims=True)
    upper = gates.astype(jnp.bfloat16).astype(jnp.float32)
    both = jnp.concatenate([upper, gates - upper], axis=0).astype(jnp.bfloat16)
    tail = payload_ref.shape[1] - width
    place = lax.broadcasted_iota(jnp.int32, (2 * experts, tail), 0)
    lane = lax.broadcasted_iota(jnp.int32, (2 * experts, tail), 1)
    placed = lax.dot_general(
        both,
        (place == lane).astype(jnp.bfloat16),
        (((0,), (0,)), ((), ())),
        preferred_element_type=jnp.float32,
    )
    payload_ref[:, width:] = placed.astype(jnp.bfloat16)


def norm_route(mine, swapped, residual, norm_gain, router, routes):
    rows, width = residual.shape
    experts = router.shape[1]
    wide = -(-(width + 2 * experts) // 128) * 128
    return pl.pallas_call(
        norm_kernel,
        out_shape=(
            jax.ShapeDtypeStruct((rows, width), jnp.float32),
            jax.ShapeDtypeStruct((rows, wide), jnp.bfloat16),
        ),
        compiler_params=pltpu.CompilerParams(vmem_limit_bytes=GRANT),
    )(mine, swapped, residual, norm_gain[None, :], router.T, routes.T)


def expert_kernel(count, experts, bring, which_ref, *refs):
    blocks, refs = refs[:count], refs[count:]
    gate_ref, up_ref, down_ref = refs[:3]
    outs, refs = refs[3 : 3 + count], refs[3 + count :]
    copies = []
    if bring:
        up_kept, down_kept, act_ref, sems = refs
        copies = [
            pltpu.make_async_copy(up_ref.at[0], up_kept, sems.at[0]),
            pltpu.make_async_copy(down_ref.at[0], down_kept, sems.at[1]),
        ]
        for copy in copies:
            copy.start()
        up_ref, down_ref = up_kept, down_kept
    else:
        (act_ref,) = refs
    hidden, width = gate_ref.shape
    rows = jnp.concatenate([block[...] for block in blocks], axis=0)
    base = width // 128 * 128
    tail = rows[:, base:].astype(jnp.float32)
    lane = lax.broadcasted_iota(jnp.int32, tail.shape, 1) - (width - base)
    named = (lane == which_ref[1]) | (lane == which_ref[1] + experts)
    weight = jnp.sum(jnp.where(named, tail, 0.0), axis=-1, keepdims=True)
    turned = rows[:, :width].T
    spans = [slice(at, min(at + 256, hidden)) for at in range(0, hidden, 256)]

    def into(ref, span):
        return jnp.dot(ref[span, :], turned, preferred_element_type=jnp.float32)

    if bring:
        gates = [into(gate_ref, span) for span in spans]
        copies[0].wait()
    for i, span in enumerate(spans):
        gate = gates[i] if bring else into(gate_ref, span)
        up = into(up_ref, span)
        act_ref[:, span] = (gate / (1.0 + jnp.exp(-gate)) * up).T.astype(jnp.bfloat16)
    if bring:
        copies[1].wait()
    for at in range(0, width, 768):
        span = slice(at, min(at + 768, width))
        part = jnp.dot(act_ref[...], down_ref[:, span], preferred_element_type=jnp.float32)
        part = (part * weight).astype(jnp.bfloat16)
        first = 0
        for out in outs:
            out[:, span] = part[first : first + out.shape[0]]
            first += out.shape[0]


def run_expert(which, blocks, gate_t, up_t, down, experts):
    hidden, width = gate_t.shape
    bring = down.ndim == 3
    rows = sum(block.shape[0] for block in blocks)
    count = len(blocks)
    vmem = pl.BlockSpec(memory_space=pltpu.VMEM)
    outs = [jax.ShapeDtypeStruct((b.shape[0], width), jnp.bfloat16) for b in blocks]
    scratch = [pltpu.VMEM((rows, hidden), jnp.bfloat16)]
    sources = [vmem] * 2
    if bring:
        outs += [jax.ShapeDtypeStruct((hidden, width), jnp.bfloat16)] * 2
        scratch.append(pltpu.SemaphoreType.DMA((2,)))
        up_t, down = (pltpu.with_memory_space_constraint(w, pltpu.HBM) for w in (up_t, down))
        sources = [pl.BlockSpec(memory_space=pltpu.HBM)] * 2
    return pl.pallas_call(
        lambda *refs: expert_kernel(count, experts, bring, *refs),
        out_shape=outs,
        in_specs=[pl.BlockSpec(memory_space=pltpu.SMEM)] + [vmem] * (count + 1) + sources,
        out_specs=[vmem] * len(outs),
        scratch_shapes=scratch,
        compiler_params=pltpu.CompilerParams(vmem_limit_bytes=GRANT),
        cost_estimate=pl.CostEstimate(
            flops=6 * rows * hidden * width, bytes_accessed=6 * hidden * width, transcendentals=0
        ),
    )(which, *blocks, gate_t, up_t, down)


def add_kernel(*refs):
    total = refs[0][...].astype(jnp.float32)
    for ref in refs[1:-1]:
        total = total + ref[...].astype(jnp.float32)
    refs[-1][...] = total.astype(refs[-1].dtype)


def add_all(*terms):
    return pl.pallas_call(
        add_kernel,
        out_shape=jax.ShapeDtypeStruct(terms[0].shape, jnp.bfloat16),
        compiler_params=pltpu.CompilerParams(vmem_limit_bytes=GRANT),
    )(*terms)


def ring_pairs(chips, cores, cross):
    order = list(range(0, chips, 2)) + list(range(1, chips, 2))[::-1]
    pairs = []
    for p in range(chips):
        for core in range(cores):
            turn = -1 if core % 2 else 1
            to = core ^ 1 if cross else core
            pairs.append((order[p] * cores + core, order[(p + turn) % chips] * cores + to))
    return pairs


def per_device(
    query,
    new_key,
    new_value,
    cache_keys,
    cache_values,
    lengths,
    out_proj,
    residual,
    norm_gain,
    router,
    routes,
    w_gate,
    w_up,
    w_down,
):
    chips, cores = lax.axis_size("att"), lax.axis_size("exp")
    own_rows = residual.shape[0]
    ring = ("att", "exp")

    def send(x, cross=False):
        return lax.ppermute(x, ring, ring_pairs(chips, cores, cross))

    def swap(x):
        return lax.ppermute(x, "exp", [(0, 1), (1, 0)])

    where = jnp.stack([lax.axis_index("exp"), lax.axis_index("att")])
    small = (where, own_rows, lengths, query, new_key, new_value)
    theirs, w_out, own_keys, own_values = attend_theirs(
        *small, cache_keys, cache_values, out_proj.T
    )
    swapped = swap(theirs)
    gate_t, up_t = w_gate.transpose(0, 2, 1), w_up.transpose(0, 2, 1)
    mine, gate_t = attend_mine(*small, own_keys, own_values, w_out, gate_t)
    hidden_state, payload = norm_route(mine, swapped, residual, norm_gain, router, routes)

    experts = router.shape[1]

    far = chips // 2
    x, y = payload, swap(payload)
    *done, up_t, down = run_expert(where, (x, y), gate_t, up_t, w_down, experts)
    own, own_other = done[0], swap(done[1])
    sums_x, sums_y = [None], [None]
    for k in range(1, far + 1):
        x = send(x)
        x, _ = lax.optimization_barrier((x, done[0]))
        blocks = [x, swap(x)]
        if k > 1:
            y = send(y)
            y, _ = lax.optimization_barrier((y, done[0]))
            blocks += [y, swap(y)]
        if k > 2:
            blocks[0], sums_x[k - 2] = lax.optimization_barrier((blocks[0], sums_x[k - 2]))
        done = run_expert(where, blocks, gate_t, up_t, down, experts)
        sums_x.append((done[1], swap(done[0])))
        if k > 1:
            sums_y.append((done[3], swap(done[2])))

    back_x = back_y = None
    for k in range(far, 0, -1):
        if k < far:
            back_y = send(add_all(*sums_y[k], *([] if back_y is None else [back_y])))
        back_x = send(add_all(*sums_x[k], *([] if back_x is None else [back_x])), k == 1)
    return add_all(hidden_state, own, own_other, back_x, *([] if back_y is None else [back_y]))


def solution(mesh):
    in_specs = (
        P(("groups", "att"), "exp"),
        P(("groups", "att"), "exp"),
        P(("groups", "att"), "exp"),
        P(("groups", "att"), None, "exp"),
        P(("groups", "att"), None, "exp"),
        P(("groups", "att")),
        P("exp", None),
        P(("groups", "att", "exp"), None),
        P(),
        P(),
        P(("groups", "att", "exp"), None),
        P("att", None, "exp"),
        P("att", None, "exp"),
        P("att", "exp", None),
    )
    out_specs = P(("groups", "att", "exp"), None)
    return jax.shard_map(
        per_device, mesh=mesh, in_specs=in_specs, out_specs=out_specs, check_vma=False
    )
```

```python
import math

import jax
import jax.numpy as jnp
from jax import lax
from jax.experimental import pallas as pl
from jax.experimental.pallas import tpu as pltpu
from jax.sharding import PartitionSpec as P

HEAD = 64
SUB = 8
STEP = 16
GRANT = 12 * 1024 * 1024
ACROSS = (((1,), (1,)), ((), ()))


def place_heads(queries, heads, slots, width):
    group_size = heads // slots
    slot_of_lane = lax.broadcasted_iota(jnp.int32, (SUB, width), 1) // HEAD
    pieces = []
    for head in range(heads):
        block, slot, home = head // slots, head % slots, head // group_size
        piece = queries[:, block * width : (block + 1) * width]
        if slot != home:
            piece = pltpu.roll(piece, ((home - slot) * HEAD) % width, 1)
        pieces.append(jnp.where(slot_of_lane == home, piece, 0.0))
    return jnp.concatenate(pieces, axis=0).astype(jnp.bfloat16)


def score(rows, keys, fresh_k, cache_len):
    request = lax.broadcasted_iota(jnp.int32, (cache_len, rows.shape[0]), 1) % SUB
    spread = lax.dot_general(keys, rows, ACROSS, preferred_element_type=jnp.float32)
    scores = spread[:cache_len]
    for r in range(1, SUB):
        scores = jnp.where(request == r, spread[r * cache_len : (r + 1) * cache_len], scores)
    return scores, lax.dot_general(fresh_k, rows, ACROSS, preferred_element_type=jnp.float32)


def soften(scores, fresh, live, offset, per):
    cache_len, count = scores.shape
    request = lax.broadcasted_iota(jnp.int32, (cache_len, count), 1) % SUB
    place = lax.broadcasted_iota(jnp.int32, (cache_len, count), 0)
    scores = jnp.where(place < live, scores, -1e30)
    fresh_place = lax.broadcasted_iota(jnp.int32, fresh.shape, 0)
    fresh_own = fresh_place == offset + lax.broadcasted_iota(jnp.int32, fresh.shape, 1) % SUB
    fresh_scores = jnp.sum(jnp.where(fresh_own, fresh, 0.0), axis=0, keepdims=True)
    highest = jnp.maximum(jnp.max(scores, axis=0, keepdims=True), fresh_scores)
    cached_exp = jnp.exp(scores - highest)
    fresh_exp = jnp.exp(fresh_scores - highest)
    scale = 1.0 / (jnp.sum(cached_exp, axis=0, keepdims=True) + fresh_exp)
    probs = cached_exp * scale
    fresh_probs = jnp.where(fresh_own, fresh_exp * scale, 0.0)
    return jnp.concatenate(
        [jnp.where(request % per == i, probs, 0.0) for i in range(per)] + [fresh_probs], axis=0
    ).T


def weigh(turned, values, fresh_v, per):
    count, width = turned.shape[0], values.shape[1]
    group = lax.broadcasted_iota(jnp.int32, (count, width), 0) % SUB // per
    wide = jnp.concatenate(
        [jnp.where(group == part, turned[:, :width], 0.0) for part in range(SUB // per)], axis=1
    ).astype(jnp.bfloat16)
    output = jnp.dot(wide, values, preferred_element_type=jnp.float32)
    return output + jnp.dot(
        turned[:, width:].astype(jnp.bfloat16), fresh_v, preferred_element_type=jnp.float32
    )


def gather_heads(output, heads, slots, width):
    group_size = heads // slots
    slot_of_lane = lax.broadcasted_iota(jnp.int32, (SUB, width), 1) // HEAD
    blocks = []
    for block in range(heads // slots):
        merged = None
        for slot in range(slots):
            head = block * slots + slot
            home = head // group_size
            piece = output[head * SUB : (head + 1) * SUB]
            if slot != home:
                piece = pltpu.roll(piece, ((slot - home) * HEAD) % width, 1)
            merged = piece if merged is None else jnp.where(slot_of_lane == slot, piece, merged)
        blocks.append(merged)
    return jnp.concatenate(blocks, axis=-1)


def attend(first, lengths_ref, q_ref, nk_ref, nv_ref, k_ref, v_ref, att_ref, ready):
    width = nk_ref.shape[1]
    slots = width // HEAD
    heads = q_ref.shape[1] // HEAD
    cache_len = k_ref.shape[1]
    per = width // cache_len
    request = lax.broadcasted_iota(jnp.int32, (1, heads * SUB), 1) % SUB
    batches = range(0, att_ref.shape[0], SUB)
    scores = []
    for at in batches:
        step = at // STEP * STEP
        if at == step:
            ready(at)
            queries = q_ref[step : step + STEP].astype(jnp.float32) * (1.0 / math.sqrt(HEAD))
        rows = place_heads(queries[at - step : at - step + SUB], heads, slots, width)
        keys = k_ref[at : at + SUB].reshape(SUB * cache_len, width)
        scores.append(score(rows, keys, nk_ref[step : step + STEP], cache_len))
    turned = []
    for at, (cached, fresh) in zip(batches, scores):
        live = jnp.zeros(request.shape, jnp.int32)
        for i in range(SUB):
            live = jnp.where(request == i, lengths_ref[first + at + i], live)
        turned.append(soften(cached, fresh, live, at % STEP, per))
    outputs = []
    for at, probs in zip(batches, turned):
        step = at // STEP * STEP
        values = v_ref[at : at + SUB].reshape(SUB * cache_len, width)
        outputs.append(weigh(probs, values, nv_ref[step : step + STEP], per))
    for step in range(0, att_ref.shape[0], STEP):
        pair = outputs[step // SUB : (step + STEP) // SUB]
        att_ref[step : step + STEP, :] = jnp.concatenate(
            [gather_heads(output, heads, slots, width) for output in pair], axis=0
        ).astype(jnp.bfloat16)


def project(att_ref, w_ref, out_ref):
    columns = w_ref.shape[0]
    for at in range(0, columns, 768):
        size = min(768, columns - at)
        turned = lax.dot_general(
            w_ref[at : at + size, :], att_ref[...], ACROSS, preferred_element_type=jnp.float32
        )
        out_ref[:, at : at + size] = turned.T


def first_kernel(
    core_ref, lengths_ref, q_hbm, nk_hbm, nv_hbm, k_hbm, v_hbm, w_hbm,
    out_ref, w_ref, own_k, own_v, q_ref, nk_ref, nv_ref, k_ref, v_ref, att_ref, sems,
):
    rows = out_ref.shape[0]
    theirs = pl.multiple_of((1 - core_ref[0]) * rows, rows)
    mine = pl.multiple_of(core_ref[0] * rows, rows)
    copies = []

    def bring(source, target):
        copy = pltpu.make_async_copy(source, target, sems.at[len(copies)])
        copy.start()
        copies.append(copy)
        return copy

    small = [
        bring(source.at[pl.ds(theirs, rows)], target)
        for source, target in ((q_hbm, q_ref), (nk_hbm, nk_ref), (nv_hbm, nv_ref))
    ]
    cache = []
    for at in range(0, rows, STEP):
        span = pl.ds(theirs + at, STEP)
        cache.append(
            (
                bring(k_hbm.at[span], k_ref.at[pl.ds(at, STEP)]),
                bring(v_hbm.at[span], v_ref.at[pl.ds(at, STEP)]),
            )
        )
    pieces = 4
    columns = w_ref.shape[0]
    size = -(-columns // pieces // 16) * 16
    weights = []
    for at in range(0, columns, size):
        span = pl.ds(at, min(size, columns - at))
        weights.append(bring(w_hbm.at[span], w_ref.at[span]))
    later = [
        bring(k_hbm.at[pl.ds(mine, rows)], own_k),
        bring(v_hbm.at[pl.ds(mine, rows)], own_v),
    ]
    for copy in small:
        copy.wait()

    def ready(at):
        for copy in cache[at // STEP]:
            copy.wait()

    attend(theirs, lengths_ref, q_ref, nk_ref, nv_ref, k_ref, v_ref, att_ref, ready)
    for copy in weights:
        copy.wait()
    project(att_ref, w_ref, out_ref)
    for copy in later:
        copy.wait()


def second_kernel(
    core_ref, lengths_ref, q_ref, nk_ref, nv_ref, k_ref, v_ref, w_ref, gate_hbm,
    out_ref, gate_ref, att_ref, sem,
):
    copy = pltpu.make_async_copy(gate_hbm.at[0], gate_ref, sem)
    copy.start()
    rows = out_ref.shape[0]
    mine = pl.multiple_of(core_ref[0] * rows, rows)
    own = [ref.at[pl.ds(mine, rows)] for ref in (q_ref, nk_ref, nv_ref)]
    attend(mine, lengths_ref, *own, k_ref, v_ref, att_ref, lambda at: None)
    project(att_ref, w_ref, out_ref)
    copy.wait()


def attend_theirs(core, rows, lengths, query, new_key, new_value, cache_keys, cache_values, w):
    cache = (rows,) + cache_keys.shape[1:]
    columns = w.shape[0]
    smem = pl.BlockSpec(memory_space=pltpu.SMEM)
    vmem = pl.BlockSpec(memory_space=pltpu.VMEM)
    hbm = pl.BlockSpec(memory_space=pltpu.HBM)
    copies = 3 + 2 * (rows // STEP) + 4 + 2
    return pl.pallas_call(
        first_kernel,
        out_shape=(
            jax.ShapeDtypeStruct((rows, columns), jnp.float32),
            jax.ShapeDtypeStruct(w.shape, jnp.bfloat16),
            jax.ShapeDtypeStruct(cache, jnp.bfloat16),
            jax.ShapeDtypeStruct(cache, jnp.bfloat16),
        ),
        in_specs=[smem, smem] + [hbm] * 6,
        out_specs=[vmem] * 4,
        scratch_shapes=[
            pltpu.VMEM((rows, query.shape[1]), jnp.bfloat16),
            pltpu.VMEM((rows, new_key.shape[1]), jnp.bfloat16),
            pltpu.VMEM((rows, new_key.shape[1]), jnp.bfloat16),
            pltpu.VMEM(cache, jnp.bfloat16),
            pltpu.VMEM(cache, jnp.bfloat16),
            pltpu.VMEM((rows, query.shape[1]), jnp.bfloat16),
            pltpu.SemaphoreType.DMA((copies,)),
        ],
        compiler_params=pltpu.CompilerParams(vmem_limit_bytes=GRANT),
        cost_estimate=pl.CostEstimate(
            flops=2 * rows * w.size, bytes_accessed=2 * w.size, transcendentals=0
        ),
    )(
        core,
        lengths,
        *(
            pltpu.with_memory_space_constraint(x, pltpu.HBM)
            for x in (query, new_key, new_value, cache_keys, cache_values, w)
        ),
    )


def attend_mine(core, rows, lengths, query, new_key, new_value, own_keys, own_values, w, gate_t):
    smem = pl.BlockSpec(memory_space=pltpu.SMEM)
    vmem = pl.BlockSpec(memory_space=pltpu.VMEM)
    return pl.pallas_call(
        second_kernel,
        out_shape=(
            jax.ShapeDtypeStruct((rows, w.shape[0]), jnp.float32),
            jax.ShapeDtypeStruct(gate_t.shape[1:], jnp.bfloat16),
        ),
        in_specs=[smem, smem] + [vmem] * 6 + [pl.BlockSpec(memory_space=pltpu.HBM)],
        out_specs=[vmem] * 2,
        scratch_shapes=[
            pltpu.VMEM((rows, query.shape[1]), jnp.bfloat16),
            pltpu.SemaphoreType.DMA,
        ],
        compiler_params=pltpu.CompilerParams(vmem_limit_bytes=GRANT),
        cost_estimate=pl.CostEstimate(
            flops=2 * rows * w.size, bytes_accessed=2 * w.size, transcendentals=0
        ),
    )(
        core,
        lengths,
        query,
        new_key,
        new_value,
        own_keys,
        own_values,
        w,
        pltpu.with_memory_space_constraint(gate_t, pltpu.HBM),
    )


def norm_kernel(
    mine_ref, swapped_ref, residual_ref, gain_ref, router_ref, routes_ref, hidden_ref, payload_ref
):
    hidden = residual_ref[...].astype(jnp.float32) + (mine_ref[...] + swapped_ref[...])
    hidden_ref[...] = hidden
    rows, width = hidden.shape
    mean_square = jnp.sum(hidden * hidden, axis=-1, keepdims=True) * (1.0 / width)
    normed = (hidden * lax.rsqrt(mean_square + 1e-05) * gain_ref[...]).astype(jnp.bfloat16)
    payload_ref[:, :width] = normed
    rest = router_ref[...]
    experts = rest.shape[0]
    terms = []
    for _ in range(3):
        term = rest.astype(jnp.bfloat16).astype(jnp.float32)
        terms.append(term)
        rest = rest - term
    parts = lax.dot_general(
        jnp.concatenate(terms, axis=0).astype(jnp.bfloat16),
        normed,
        (((1,), (1,)), ((), ())),
        preferred_element_type=jnp.float32,
    )
    logits = parts[:experts] + parts[experts : 2 * experts] + parts[2 * experts :]
    number = lax.broadcasted_iota(jnp.int32, (experts, rows), 0)
    chosen = number == routes_ref[0:1, :]
    for k in range(1, routes_ref.shape[0]):
        chosen = chosen | (number == routes_ref[k : k + 1, :])
    squashed = jnp.where(chosen, 1.0 / (1.0 + jnp.exp(-logits)), 0.0)
    gates = squashed / jnp.sum(squashed, axis=0, keepdims=True)
    upper = gates.astype(jnp.bfloat16).astype(jnp.float32)
    both = jnp.concatenate([upper, gates - upper], axis=0).astype(jnp.bfloat16)
    tail = payload_ref.shape[1] - width
    place = lax.broadcasted_iota(jnp.int32, (2 * experts, tail), 0)
    lane = lax.broadcasted_iota(jnp.int32, (2 * experts, tail), 1)
    placed = lax.dot_general(
        both,
        (place == lane).astype(jnp.bfloat16),
        (((0,), (0,)), ((), ())),
        preferred_element_type=jnp.float32,
    )
    payload_ref[:, width:] = placed.astype(jnp.bfloat16)


def norm_route(mine, swapped, residual, norm_gain, router, routes):
    rows, width = residual.shape
    experts = router.shape[1]
    wide = -(-(width + 2 * experts) // 128) * 128
    return pl.pallas_call(
        norm_kernel,
        out_shape=(
            jax.ShapeDtypeStruct((rows, width), jnp.float32),
            jax.ShapeDtypeStruct((rows, wide), jnp.bfloat16),
        ),
        compiler_params=pltpu.CompilerParams(vmem_limit_bytes=GRANT),
    )(mine, swapped, residual, norm_gain[None, :], router.T, routes.T)


def expert_kernel(count, experts, bring, which_ref, *refs):
    blocks, refs = refs[:count], refs[count:]
    gate_ref, up_ref, down_ref = refs[:3]
    outs, refs = refs[3 : 3 + count], refs[3 + count :]
    copies = []
    if bring:
        up_kept, down_kept, act_ref, sems = refs
        copies = [
            pltpu.make_async_copy(up_ref.at[0], up_kept, sems.at[0]),
            pltpu.make_async_copy(down_ref.at[0], down_kept, sems.at[1]),
        ]
        for copy in copies:
            copy.start()
        up_ref, down_ref = up_kept, down_kept
    else:
        (act_ref,) = refs
    hidden, width = gate_ref.shape
    rows = jnp.concatenate([block[...] for block in blocks], axis=0)
    base = width // 128 * 128
    tail = rows[:, base:].astype(jnp.float32)
    lane = lax.broadcasted_iota(jnp.int32, tail.shape, 1) - (width - base)
    named = (lane == which_ref[1]) | (lane == which_ref[1] + experts)
    weight = jnp.sum(jnp.where(named, tail, 0.0), axis=-1, keepdims=True)
    turned = rows[:, :width].T
    spans = [slice(at, min(at + 256, hidden)) for at in range(0, hidden, 256)]

    def into(ref, span):
        return jnp.dot(ref[span, :], turned, preferred_element_type=jnp.float32)

    if bring:
        gates = [into(gate_ref, span) for span in spans]
        copies[0].wait()
    for i, span in enumerate(spans):
        gate = gates[i] if bring else into(gate_ref, span)
        up = into(up_ref, span)
        act_ref[:, span] = (gate / (1.0 + jnp.exp(-gate)) * up).T.astype(jnp.bfloat16)
    if bring:
        copies[1].wait()
    for at in range(0, width, 768):
        span = slice(at, min(at + 768, width))
        part = jnp.dot(act_ref[...], down_ref[:, span], preferred_element_type=jnp.float32)
        part = (part * weight).astype(jnp.bfloat16)
        first = 0
        for out in outs:
            out[:, span] = part[first : first + out.shape[0]]
            first += out.shape[0]


def run_expert(which, blocks, gate_t, up_t, down, experts):
    hidden, width = gate_t.shape
    bring = down.ndim == 3
    rows = sum(block.shape[0] for block in blocks)
    count = len(blocks)
    vmem = pl.BlockSpec(memory_space=pltpu.VMEM)
    outs = [jax.ShapeDtypeStruct((b.shape[0], width), jnp.bfloat16) for b in blocks]
    scratch = [pltpu.VMEM((rows, hidden), jnp.bfloat16)]
    sources = [vmem] * 2
    if bring:
        outs += [jax.ShapeDtypeStruct((hidden, width), jnp.bfloat16)] * 2
        scratch.append(pltpu.SemaphoreType.DMA((2,)))
        up_t, down = (pltpu.with_memory_space_constraint(w, pltpu.HBM) for w in (up_t, down))
        sources = [pl.BlockSpec(memory_space=pltpu.HBM)] * 2
    return pl.pallas_call(
        lambda *refs: expert_kernel(count, experts, bring, *refs),
        out_shape=outs,
        in_specs=[pl.BlockSpec(memory_space=pltpu.SMEM)] + [vmem] * (count + 1) + sources,
        out_specs=[vmem] * len(outs),
        scratch_shapes=scratch,
        compiler_params=pltpu.CompilerParams(vmem_limit_bytes=GRANT),
        cost_estimate=pl.CostEstimate(
            flops=6 * rows * hidden * width, bytes_accessed=6 * hidden * width, transcendentals=0
        ),
    )(which, *blocks, gate_t, up_t, down)


def add_kernel(*refs):
    total = refs[0][...].astype(jnp.float32)
    for ref in refs[1:-1]:
        total = total + ref[...].astype(jnp.float32)
    refs[-1][...] = total.astype(refs[-1].dtype)


def add_all(*terms):
    return pl.pallas_call(
        add_kernel,
        out_shape=jax.ShapeDtypeStruct(terms[0].shape, jnp.bfloat16),
        compiler_params=pltpu.CompilerParams(vmem_limit_bytes=GRANT),
    )(*terms)


def ring_pairs(chips, cores, cross):
    order = list(range(0, chips, 2)) + list(range(1, chips, 2))[::-1]
    pairs = []
    for p in range(chips):
        for core in range(cores):
            turn = -1 if core % 2 else 1
            to = core ^ 1 if cross else core
            pairs.append((order[p] * cores + core, order[(p + turn) % chips] * cores + to))
    return pairs


def per_device(
    query,
    new_key,
    new_value,
    cache_keys,
    cache_values,
    lengths,
    out_proj,
    residual,
    norm_gain,
    router,
    routes,
    w_gate,
    w_up,
    w_down,
):
    chips, cores = lax.axis_size("att"), lax.axis_size("exp")
    own_rows = residual.shape[0]
    ring = ("att", "exp")

    def send(x, cross=False):
        return lax.ppermute(x, ring, ring_pairs(chips, cores, cross))

    def swap(x):
        return lax.ppermute(x, "exp", [(0, 1), (1, 0)])

    where = jnp.stack([lax.axis_index("exp"), lax.axis_index("att")])
    small = (where, own_rows, lengths, query, new_key, new_value)
    theirs, w_out, own_keys, own_values = attend_theirs(
        *small, cache_keys, cache_values, out_proj.T
    )
    swapped = swap(theirs)
    gate_t, up_t = w_gate.transpose(0, 2, 1), w_up.transpose(0, 2, 1)
    mine, gate_t = attend_mine(*small, own_keys, own_values, w_out, gate_t)
    hidden_state, payload = norm_route(mine, swapped, residual, norm_gain, router, routes)

    experts = router.shape[1]

    far = chips // 2

    def after(value, *earlier):
        return lax.optimization_barrier((value, earlier))[0]

    def expert(blocks, up_t, down):
        return run_expert(where, blocks, gate_t, up_t, down, experts)

    x, y = payload, swap(payload)
    *done, up_t, down = expert((x, y), up_t, w_down)
    own, own_other = done[0], swap(done[1])
    sums_x, sums_y = [None], [None]
    for k in range(1, far + 1):
        x = send(x)
        if k == 1:
            x = after(x, done[0])
        blocks = [x, swap(x)]
        if k < far:
            y = send(y)
            if k > 1:
                y = after(y, done[0])
            blocks += [y, swap(y)]
        else:
            blocks[1] = after(blocks[1], done[0])
        if k > 2:
            blocks[1] = after(blocks[1], sums_x[k - 2][1], sums_y[k - 2][1])
        done = expert(blocks, up_t, down)
        sums_x.append((done[1], swap(done[0])))
        if k < far:
            sums_y.append((done[3], swap(done[2])))

    back_x = back_y = None
    for k in range(far, 0, -1):
        if k < far:
            back_y = send(add_all(*sums_y[k], *([] if back_y is None else [back_y])))
        back_x = send(add_all(*sums_x[k], *([] if back_x is None else [back_x])), k == 1)
    return add_all(hidden_state, own, own_other, back_x, *([] if back_y is None else [back_y]))


def solution(mesh):
    in_specs = (
        P(("groups", "att"), "exp"),
        P(("groups", "att"), "exp"),
        P(("groups", "att"), "exp"),
        P(("groups", "att"), None, "exp"),
        P(("groups", "att"), None, "exp"),
        P(("groups", "att")),
        P("exp", None),
        P(("groups", "att", "exp"), None),
        P(),
        P(),
        P(("groups", "att", "exp"), None),
        P("att", None, "exp"),
        P("att", None, "exp"),
        P("att", "exp", None),
    )
    out_specs = P(("groups", "att", "exp"), None)
    return jax.shard_map(
        per_device, mesh=mesh, in_specs=in_specs, out_specs=out_specs, check_vma=False
    )
```

```python
import math

import jax
import jax.numpy as jnp
from jax import lax
from jax.experimental import pallas as pl
from jax.experimental.pallas import tpu as pltpu
from jax.sharding import PartitionSpec as P

HEAD = 64
SUB = 8
STEP = 16
SPAN = 256
GRANT = 12 * 1024 * 1024
ACROSS = (((1,), (1,)), ((), ()))


def place_heads(queries, heads, slots, width):
    group_size = heads // slots
    slot_of_lane = lax.broadcasted_iota(jnp.int32, (SUB, width), 1) // HEAD
    pieces = []
    for head in range(heads):
        block, slot, home = head // slots, head % slots, head // group_size
        piece = queries[:, block * width : (block + 1) * width]
        if slot != home:
            piece = pltpu.roll(piece, ((home - slot) * HEAD) % width, 1)
        pieces.append(jnp.where(slot_of_lane == home, piece, 0.0))
    return jnp.concatenate(pieces, axis=0).astype(jnp.bfloat16)


def score(rows, keys, fresh_k, cache_len):
    request = lax.broadcasted_iota(jnp.int32, (cache_len, rows.shape[0]), 1) % SUB
    spread = lax.dot_general(keys, rows, ACROSS, preferred_element_type=jnp.float32)
    scores = spread[:cache_len]
    for r in range(1, SUB):
        scores = jnp.where(request == r, spread[r * cache_len : (r + 1) * cache_len], scores)
    return scores, lax.dot_general(fresh_k, rows, ACROSS, preferred_element_type=jnp.float32)


def soften(scores, fresh, live, offset, per):
    cache_len, count = scores.shape
    request = lax.broadcasted_iota(jnp.int32, (cache_len, count), 1) % SUB
    place = lax.broadcasted_iota(jnp.int32, (cache_len, count), 0)
    scores = jnp.where(place < live, scores, -1e30)
    fresh_place = lax.broadcasted_iota(jnp.int32, fresh.shape, 0)
    fresh_own = fresh_place == offset + lax.broadcasted_iota(jnp.int32, fresh.shape, 1) % SUB
    fresh_scores = jnp.sum(jnp.where(fresh_own, fresh, 0.0), axis=0, keepdims=True)
    highest = jnp.maximum(jnp.max(scores, axis=0, keepdims=True), fresh_scores)
    cached_exp = jnp.exp(scores - highest)
    fresh_exp = jnp.exp(fresh_scores - highest)
    scale = 1.0 / (jnp.sum(cached_exp, axis=0, keepdims=True) + fresh_exp)
    probs = cached_exp * scale
    fresh_probs = jnp.where(fresh_own, fresh_exp * scale, 0.0)
    return jnp.concatenate(
        [jnp.where(request % per == i, probs, 0.0) for i in range(per)] + [fresh_probs], axis=0
    ).T


def weigh(turned, values, fresh_v, per):
    count, width = turned.shape[0], values.shape[1]
    group = lax.broadcasted_iota(jnp.int32, (count, width), 0) % SUB // per
    wide = jnp.concatenate(
        [jnp.where(group == part, turned[:, :width], 0.0) for part in range(SUB // per)], axis=1
    ).astype(jnp.bfloat16)
    output = jnp.dot(wide, values, preferred_element_type=jnp.float32)
    return output + jnp.dot(
        turned[:, width:].astype(jnp.bfloat16), fresh_v, preferred_element_type=jnp.float32
    )


def gather_heads(output, heads, slots, width):
    group_size = heads // slots
    slot_of_lane = lax.broadcasted_iota(jnp.int32, (SUB, width), 1) // HEAD
    blocks = []
    for block in range(heads // slots):
        merged = None
        for slot in range(slots):
            head = block * slots + slot
            home = head // group_size
            piece = output[head * SUB : (head + 1) * SUB]
            if slot != home:
                piece = pltpu.roll(piece, ((slot - home) * HEAD) % width, 1)
            merged = piece if merged is None else jnp.where(slot_of_lane == slot, piece, merged)
        blocks.append(merged)
    return jnp.concatenate(blocks, axis=-1)


def attend(first, lengths_ref, q_ref, nk_ref, nv_ref, k_ref, v_ref, att_ref, ready):
    width = nk_ref.shape[1]
    slots = width // HEAD
    heads = q_ref.shape[1] // HEAD
    cache_len = k_ref.shape[1]
    per = width // cache_len
    request = lax.broadcasted_iota(jnp.int32, (1, heads * SUB), 1) % SUB
    batches = range(0, att_ref.shape[0], SUB)
    scores = []
    for at in batches:
        step = at // STEP * STEP
        if at == step:
            ready(at)
            queries = q_ref[step : step + STEP].astype(jnp.float32) * (1.0 / math.sqrt(HEAD))
        rows = place_heads(queries[at - step : at - step + SUB], heads, slots, width)
        keys = k_ref[at : at + SUB].reshape(SUB * cache_len, width)
        scores.append(score(rows, keys, nk_ref[step : step + STEP], cache_len))
    turned = []
    for at, (cached, fresh) in zip(batches, scores):
        live = jnp.zeros(request.shape, jnp.int32)
        for i in range(SUB):
            live = jnp.where(request == i, lengths_ref[first + at + i], live)
        turned.append(soften(cached, fresh, live, at % STEP, per))
    outputs = []
    for at, probs in zip(batches, turned):
        step = at // STEP * STEP
        values = v_ref[at : at + SUB].reshape(SUB * cache_len, width)
        outputs.append(weigh(probs, values, nv_ref[step : step + STEP], per))
    for step in range(0, att_ref.shape[0], STEP):
        pair = outputs[step // SUB : (step + STEP) // SUB]
        att_ref[step : step + STEP, :] = jnp.concatenate(
            [gather_heads(output, heads, slots, width) for output in pair], axis=0
        ).astype(jnp.bfloat16)


def project(att_ref, w_ref, out_ref):
    columns = w_ref.shape[0]
    for at in range(0, columns, 768):
        size = min(768, columns - at)
        turned = lax.dot_general(
            w_ref[at : at + size, :], att_ref[...], ACROSS, preferred_element_type=jnp.float32
        )
        out_ref[:, at : at + size] = turned.T


def first_kernel(
    core_ref, lengths_ref, q_hbm, nk_hbm, nv_hbm, k_hbm, v_hbm, w_hbm,
    out_ref, w_ref, own_k, own_v, q_ref, nk_ref, nv_ref, k_ref, v_ref, att_ref, sems,
):
    rows = out_ref.shape[0]
    theirs = pl.multiple_of((1 - core_ref[0]) * rows, rows)
    mine = pl.multiple_of(core_ref[0] * rows, rows)
    copies = []

    def bring(source, target):
        copy = pltpu.make_async_copy(source, target, sems.at[len(copies)])
        copy.start()
        copies.append(copy)
        return copy

    small = [
        bring(source.at[pl.ds(theirs, rows)], target)
        for source, target in ((q_hbm, q_ref), (nk_hbm, nk_ref), (nv_hbm, nv_ref))
    ]
    cache = []
    for at in range(0, rows, STEP):
        span = pl.ds(theirs + at, STEP)
        cache.append(
            (
                bring(k_hbm.at[span], k_ref.at[pl.ds(at, STEP)]),
                bring(v_hbm.at[span], v_ref.at[pl.ds(at, STEP)]),
            )
        )
    pieces = 4
    columns = w_ref.shape[0]
    size = -(-columns // pieces // 16) * 16
    weights = []
    for at in range(0, columns, size):
        span = pl.ds(at, min(size, columns - at))
        weights.append(bring(w_hbm.at[span], w_ref.at[span]))
    later = [
        bring(k_hbm.at[pl.ds(mine, rows)], own_k),
        bring(v_hbm.at[pl.ds(mine, rows)], own_v),
    ]
    for copy in small:
        copy.wait()

    def ready(at):
        for copy in cache[at // STEP]:
            copy.wait()

    attend(theirs, lengths_ref, q_ref, nk_ref, nv_ref, k_ref, v_ref, att_ref, ready)
    for copy in weights:
        copy.wait()
    project(att_ref, w_ref, out_ref)
    for copy in later:
        copy.wait()


def second_kernel(
    core_ref, lengths_ref, q_ref, nk_ref, nv_ref, k_ref, v_ref, w_ref, gate_hbm, up_hbm,
    out_ref, gate_ref, up_ref, att_ref, sems,
):
    copies = [
        pltpu.make_async_copy(gate_hbm.at[0], gate_ref, sems.at[0]),
        pltpu.make_async_copy(up_hbm.at[0, pl.ds(0, up_ref.shape[0])], up_ref, sems.at[1]),
    ]
    for copy in copies:
        copy.start()
    rows = out_ref.shape[0]
    mine = pl.multiple_of(core_ref[0] * rows, rows)
    own = [ref.at[pl.ds(mine, rows)] for ref in (q_ref, nk_ref, nv_ref)]
    attend(mine, lengths_ref, *own, k_ref, v_ref, att_ref, lambda at: None)
    project(att_ref, w_ref, out_ref)
    for copy in copies:
        copy.wait()


def attend_theirs(core, rows, lengths, query, new_key, new_value, cache_keys, cache_values, w):
    cache = (rows,) + cache_keys.shape[1:]
    columns = w.shape[0]
    smem = pl.BlockSpec(memory_space=pltpu.SMEM)
    vmem = pl.BlockSpec(memory_space=pltpu.VMEM)
    hbm = pl.BlockSpec(memory_space=pltpu.HBM)
    copies = 3 + 2 * (rows // STEP) + 4 + 2
    return pl.pallas_call(
        first_kernel,
        out_shape=(
            jax.ShapeDtypeStruct((rows, columns), jnp.float32),
            jax.ShapeDtypeStruct(w.shape, jnp.bfloat16),
            jax.ShapeDtypeStruct(cache, jnp.bfloat16),
            jax.ShapeDtypeStruct(cache, jnp.bfloat16),
        ),
        in_specs=[smem, smem] + [hbm] * 6,
        out_specs=[vmem] * 4,
        scratch_shapes=[
            pltpu.VMEM((rows, query.shape[1]), jnp.bfloat16),
            pltpu.VMEM((rows, new_key.shape[1]), jnp.bfloat16),
            pltpu.VMEM((rows, new_key.shape[1]), jnp.bfloat16),
            pltpu.VMEM(cache, jnp.bfloat16),
            pltpu.VMEM(cache, jnp.bfloat16),
            pltpu.VMEM((rows, query.shape[1]), jnp.bfloat16),
            pltpu.SemaphoreType.DMA((copies,)),
        ],
        compiler_params=pltpu.CompilerParams(vmem_limit_bytes=GRANT),
        cost_estimate=pl.CostEstimate(
            flops=2 * rows * w.size, bytes_accessed=2 * w.size, transcendentals=0
        ),
    )(
        core,
        lengths,
        *(
            pltpu.with_memory_space_constraint(x, pltpu.HBM)
            for x in (query, new_key, new_value, cache_keys, cache_values, w)
        ),
    )


def attend_mine(
    core, rows, lengths, query, new_key, new_value, own_keys, own_values, w, gate_t, up_t
):
    smem = pl.BlockSpec(memory_space=pltpu.SMEM)
    vmem = pl.BlockSpec(memory_space=pltpu.VMEM)
    return pl.pallas_call(
        second_kernel,
        out_shape=(
            jax.ShapeDtypeStruct((rows, w.shape[0]), jnp.float32),
            jax.ShapeDtypeStruct(gate_t.shape[1:], jnp.bfloat16),
            jax.ShapeDtypeStruct((SPAN, up_t.shape[2]), jnp.bfloat16),
        ),
        in_specs=[smem, smem] + [vmem] * 6 + [pl.BlockSpec(memory_space=pltpu.HBM)] * 2,
        out_specs=[vmem] * 3,
        scratch_shapes=[
            pltpu.VMEM((rows, query.shape[1]), jnp.bfloat16),
            pltpu.SemaphoreType.DMA((2,)),
        ],
        compiler_params=pltpu.CompilerParams(vmem_limit_bytes=GRANT),
        cost_estimate=pl.CostEstimate(
            flops=2 * rows * w.size, bytes_accessed=2 * w.size, transcendentals=0
        ),
    )(
        core,
        lengths,
        query,
        new_key,
        new_value,
        own_keys,
        own_values,
        w,
        pltpu.with_memory_space_constraint(gate_t, pltpu.HBM),
        pltpu.with_memory_space_constraint(up_t, pltpu.HBM),
    )


def norm_kernel(
    mine_ref, swapped_ref, residual_ref, gain_ref, router_ref, routes_ref, hidden_ref, payload_ref
):
    hidden = residual_ref[...].astype(jnp.float32) + (mine_ref[...] + swapped_ref[...])
    hidden_ref[...] = hidden
    rows, width = hidden.shape
    mean_square = jnp.sum(hidden * hidden, axis=-1, keepdims=True) * (1.0 / width)
    normed = (hidden * lax.rsqrt(mean_square + 1e-05) * gain_ref[...]).astype(jnp.bfloat16)
    payload_ref[:, :width] = normed
    rest = router_ref[...]
    experts = rest.shape[0]
    terms = []
    for _ in range(3):
        term = rest.astype(jnp.bfloat16).astype(jnp.float32)
        terms.append(term)
        rest = rest - term
    parts = lax.dot_general(
        jnp.concatenate(terms, axis=0).astype(jnp.bfloat16),
        normed,
        (((1,), (1,)), ((), ())),
        preferred_element_type=jnp.float32,
    )
    logits = parts[:experts] + parts[experts : 2 * experts] + parts[2 * experts :]
    number = lax.broadcasted_iota(jnp.int32, (experts, rows), 0)
    chosen = number == routes_ref[0:1, :]
    for k in range(1, routes_ref.shape[0]):
        chosen = chosen | (number == routes_ref[k : k + 1, :])
    squashed = jnp.where(chosen, 1.0 / (1.0 + jnp.exp(-logits)), 0.0)
    gates = squashed / jnp.sum(squashed, axis=0, keepdims=True)
    upper = gates.astype(jnp.bfloat16).astype(jnp.float32)
    both = jnp.concatenate([upper, gates - upper], axis=0).astype(jnp.bfloat16)
    tail = payload_ref.shape[1] - width
    place = lax.broadcasted_iota(jnp.int32, (2 * experts, tail), 0)
    lane = lax.broadcasted_iota(jnp.int32, (2 * experts, tail), 1)
    placed = lax.dot_general(
        both,
        (place == lane).astype(jnp.bfloat16),
        (((0,), (0,)), ((), ())),
        preferred_element_type=jnp.float32,
    )
    payload_ref[:, width:] = placed.astype(jnp.bfloat16)


def norm_route(mine, swapped, residual, norm_gain, router, routes):
    rows, width = residual.shape
    experts = router.shape[1]
    wide = -(-(width + 2 * experts) // 128) * 128
    return pl.pallas_call(
        norm_kernel,
        out_shape=(
            jax.ShapeDtypeStruct((rows, width), jnp.float32),
            jax.ShapeDtypeStruct((rows, wide), jnp.bfloat16),
        ),
        compiler_params=pltpu.CompilerParams(vmem_limit_bytes=GRANT),
    )(mine, swapped, residual, norm_gain[None, :], router.T, routes.T)


def expert_kernel(count, experts, bring, which_ref, *refs):
    blocks, refs = refs[:count], refs[count:]
    gate_ref, up_ref, rest_ref, down_ref = refs[:4]
    outs, refs = refs[4 : 4 + count], refs[4 + count :]
    hidden, width = gate_ref.shape
    copies = []
    if bring:
        rest_kept, down_kept, act_ref, sems = refs
        copies = [
            pltpu.make_async_copy(
                rest_ref.at[0, pl.ds(SPAN, hidden - SPAN)], rest_kept, sems.at[0]
            ),
            pltpu.make_async_copy(down_ref.at[0], down_kept, sems.at[1]),
        ]
        for copy in copies:
            copy.start()
        rest_ref, down_ref = rest_kept, down_kept
    else:
        (act_ref,) = refs
    rows = jnp.concatenate([block[...] for block in blocks], axis=0)
    base = width // 128 * 128
    tail = rows[:, base:].astype(jnp.float32)
    lane = lax.broadcasted_iota(jnp.int32, tail.shape, 1) - (width - base)
    named = (lane == which_ref[1]) | (lane == which_ref[1] + experts)
    weight = jnp.sum(jnp.where(named, tail, 0.0), axis=-1, keepdims=True)
    turned = rows[:, :width].T
    spans = [slice(at, min(at + SPAN, hidden)) for at in range(0, hidden, SPAN)]

    def into(ref, span):
        return jnp.dot(ref[span, :], turned, preferred_element_type=jnp.float32)

    if bring:
        gates = [into(gate_ref, span) for span in spans]
    for i, span in enumerate(spans):
        gate = gates[i] if bring else into(gate_ref, span)
        if i == 1 and bring:
            copies[0].wait()
        if i == 0:
            up = into(up_ref, span)
        else:
            up = into(rest_ref, slice(span.start - SPAN, span.stop - SPAN))
        act_ref[:, span] = (gate / (1.0 + jnp.exp(-gate)) * up).T.astype(jnp.bfloat16)
    if bring:
        copies[1].wait()
    for at in range(0, width, 768):
        span = slice(at, min(at + 768, width))
        part = jnp.dot(act_ref[...], down_ref[:, span], preferred_element_type=jnp.float32)
        part = (part * weight).astype(jnp.bfloat16)
        first = 0
        for out in outs:
            out[:, span] = part[first : first + out.shape[0]]
            first += out.shape[0]


def run_expert(which, blocks, gate_t, up_t, rest, down, experts):
    hidden, width = gate_t.shape
    bring = down.ndim == 3
    rows = sum(block.shape[0] for block in blocks)
    count = len(blocks)
    vmem = pl.BlockSpec(memory_space=pltpu.VMEM)
    outs = [jax.ShapeDtypeStruct((b.shape[0], width), jnp.bfloat16) for b in blocks]
    scratch = [pltpu.VMEM((rows, hidden), jnp.bfloat16)]
    sources = [vmem] * 2
    if bring:
        outs.append(jax.ShapeDtypeStruct((hidden - SPAN, width), jnp.bfloat16))
        outs.append(jax.ShapeDtypeStruct((hidden, width), jnp.bfloat16))
        scratch.append(pltpu.SemaphoreType.DMA((2,)))
        rest, down = (pltpu.with_memory_space_constraint(w, pltpu.HBM) for w in (rest, down))
        sources = [pl.BlockSpec(memory_space=pltpu.HBM)] * 2
    return pl.pallas_call(
        lambda *refs: expert_kernel(count, experts, bring, *refs),
        out_shape=outs,
        in_specs=[pl.BlockSpec(memory_space=pltpu.SMEM)] + [vmem] * (count + 2) + sources,
        out_specs=[vmem] * len(outs),
        scratch_shapes=scratch,
        compiler_params=pltpu.CompilerParams(vmem_limit_bytes=GRANT),
        cost_estimate=pl.CostEstimate(
            flops=6 * rows * hidden * width, bytes_accessed=6 * hidden * width, transcendentals=0
        ),
    )(which, *blocks, gate_t, up_t, rest, down)


def add_kernel(firsts, *refs):
    size = refs[-1].shape[0]
    total = None
    for first, ref in zip(firsts, refs):
        term = ref[first : first + size].astype(jnp.float32)
        total = term if total is None else total + term
    refs[-1][...] = total.astype(refs[-1].dtype)


def add_rows(size, *parts):
    firsts = [first for _, first in parts]
    width = parts[0][0].shape[1]
    return pl.pallas_call(
        lambda *refs: add_kernel(firsts, *refs),
        out_shape=jax.ShapeDtypeStruct((size, width), jnp.bfloat16),
        compiler_params=pltpu.CompilerParams(vmem_limit_bytes=GRANT),
    )(*[array for array, _ in parts])


def add_all(*terms):
    return add_rows(terms[0].shape[0], *[(term, 0) for term in terms])


def finish_kernel(*refs):
    *whole, top, low, out = refs
    first = 0
    for half in (top, low):
        size = half.shape[0]
        total = half[...].astype(jnp.float32)
        for ref in whole:
            total = total + ref[first : first + size].astype(jnp.float32)
        out[first : first + size, :] = total.astype(out.dtype)
        first += size


def finish(hidden_state, own, own_other, back_y, back_x):
    return pl.pallas_call(
        finish_kernel,
        out_shape=jax.ShapeDtypeStruct(hidden_state.shape, jnp.bfloat16),
        compiler_params=pltpu.CompilerParams(vmem_limit_bytes=GRANT),
    )(hidden_state, own, own_other, back_y, *back_x)


def ring_pairs(chips, cores, cross):
    order = list(range(0, chips, 2)) + list(range(1, chips, 2))[::-1]
    pairs = []
    for p in range(chips):
        for core in range(cores):
            turn = -1 if core % 2 else 1
            to = core ^ 1 if cross else core
            pairs.append((order[p] * cores + core, order[(p + turn) % chips] * cores + to))
    return pairs


def per_device(
    query,
    new_key,
    new_value,
    cache_keys,
    cache_values,
    lengths,
    out_proj,
    residual,
    norm_gain,
    router,
    routes,
    w_gate,
    w_up,
    w_down,
):
    chips, cores = lax.axis_size("att"), lax.axis_size("exp")
    own_rows = residual.shape[0]
    ring = ("att", "exp")

    def send(x, cross=False):
        return lax.ppermute(x, ring, ring_pairs(chips, cores, cross))

    def swap(x):
        return lax.ppermute(x, "exp", [(0, 1), (1, 0)])

    where = jnp.stack([lax.axis_index("exp"), lax.axis_index("att")])
    small = (where, own_rows, lengths, query, new_key, new_value)
    theirs, w_out, own_keys, own_values = attend_theirs(
        *small, cache_keys, cache_values, out_proj.T
    )
    swapped = swap(theirs)
    gate_t, up_t = w_gate.transpose(0, 2, 1), w_up.transpose(0, 2, 1)
    mine, gate, up = attend_mine(*small, own_keys, own_values, w_out, gate_t, up_t)
    hidden_state, payload = norm_route(mine, swapped, residual, norm_gain, router, routes)

    experts = router.shape[1]

    far = chips // 2

    def after(value, *earlier):
        return lax.optimization_barrier((value, earlier))[0]

    def expert(blocks, rest, down):
        return run_expert(where, blocks, gate, up, rest, down, experts)

    x, y = payload, swap(payload)
    *done, rest, down = expert((x, y), up_t, w_down)
    own, own_other = done[0], swap(done[1])
    sums_x, sums_y = [None], [None]
    back_x, back_y = [None, None], None
    for k in range(1, far + 1):
        x = send(x)
        if k in (1, far):
            x = after(x, done[0])
        blocks = [x, swap(x)]
        if k < far:
            y = send(y)
            if k > 1:
                y = after(y, done[0])
            blocks += [y, swap(y)]
        else:
            first_back = add_all(*sums_y[k - 1])
            blocks[1] = after(blocks[1], first_back)
            back_y = send(first_back)
        if k > 2:
            blocks[1] = after(blocks[1], sums_x[k - 2][1], sums_y[k - 2][1])
        done = expert(blocks, rest, down)
        sums_x.append((done[1], swap(done[0])))
        if k < far:
            sums_y.append((done[3], swap(done[2])))

    middle = own_rows // 2
    for k in range(far, 0, -1):
        if k < far - 1:
            back_y = send(add_all(*sums_y[k], back_y))
        for half in (0, 1):
            parts = [(term, half * middle) for term in sums_x[k]]
            if back_x[half] is not None:
                parts.append((back_x[half], 0))
            back_x[half] = send(add_rows(middle, *parts), k == 1)
    return finish(hidden_state, own, own_other, back_y, back_x)


def solution(mesh):
    in_specs = (
        P(("groups", "att"), "exp"),
        P(("groups", "att"), "exp"),
        P(("groups", "att"), "exp"),
        P(("groups", "att"), None, "exp"),
        P(("groups", "att"), None, "exp"),
        P(("groups", "att")),
        P("exp", None),
        P(("groups", "att", "exp"), None),
        P(),
        P(),
        P(("groups", "att", "exp"), None),
        P("att", None, "exp"),
        P("att", None, "exp"),
        P("att", "exp", None),
    )
    out_specs = P(("groups", "att", "exp"), None)
    return jax.shard_map(
        per_device, mesh=mesh, in_specs=in_specs, out_specs=out_specs, check_vma=False
    )
```

```python
import math

import jax
import jax.numpy as jnp
from jax import lax
from jax.experimental import pallas as pl
from jax.experimental.pallas import tpu as pltpu
from jax.sharding import PartitionSpec as P

HEAD = 64
SUB = 8
STEP = 16
GRANT = 12 * 1024 * 1024
ACROSS = (((1,), (1,)), ((), ()))


def place_heads(queries, heads, slots, width):
    group_size = heads // slots
    slot_of_lane = lax.broadcasted_iota(jnp.int32, (SUB, width), 1) // HEAD
    pieces = []
    for head in range(heads):
        block, slot, home = head // slots, head % slots, head // group_size
        piece = queries[:, block * width : (block + 1) * width]
        if slot != home:
            piece = pltpu.roll(piece, ((home - slot) * HEAD) % width, 1)
        pieces.append(jnp.where(slot_of_lane == home, piece, 0.0))
    return jnp.concatenate(pieces, axis=0).astype(jnp.bfloat16)


def score(rows, keys, fresh_k, cache_len):
    request = lax.broadcasted_iota(jnp.int32, (cache_len, rows.shape[0]), 1) % SUB
    spread = lax.dot_general(keys, rows, ACROSS, preferred_element_type=jnp.float32)
    scores = spread[:cache_len]
    for r in range(1, SUB):
        scores = jnp.where(request == r, spread[r * cache_len : (r + 1) * cache_len], scores)
    return scores, lax.dot_general(fresh_k, rows, ACROSS, preferred_element_type=jnp.float32)


def soften(scores, fresh, live, offset, per):
    cache_len, count = scores.shape
    request = lax.broadcasted_iota(jnp.int32, (cache_len, count), 1) % SUB
    place = lax.broadcasted_iota(jnp.int32, (cache_len, count), 0)
    scores = jnp.where(place < live, scores, -1e30)
    fresh_place = lax.broadcasted_iota(jnp.int32, fresh.shape, 0)
    fresh_own = fresh_place == offset + lax.broadcasted_iota(jnp.int32, fresh.shape, 1) % SUB
    fresh_scores = jnp.sum(jnp.where(fresh_own, fresh, 0.0), axis=0, keepdims=True)
    highest = jnp.maximum(jnp.max(scores, axis=0, keepdims=True), fresh_scores)
    cached_exp = jnp.exp(scores - highest)
    fresh_exp = jnp.exp(fresh_scores - highest)
    scale = 1.0 / (jnp.sum(cached_exp, axis=0, keepdims=True) + fresh_exp)
    probs = cached_exp * scale
    fresh_probs = jnp.where(fresh_own, fresh_exp * scale, 0.0)
    return jnp.concatenate(
        [jnp.where(request % per == i, probs, 0.0) for i in range(per)] + [fresh_probs], axis=0
    ).T


def weigh(turned, values, fresh_v, per):
    count, width = turned.shape[0], values.shape[1]
    group = lax.broadcasted_iota(jnp.int32, (count, width), 0) % SUB // per
    wide = jnp.concatenate(
        [jnp.where(group == part, turned[:, :width], 0.0) for part in range(SUB // per)], axis=1
    ).astype(jnp.bfloat16)
    output = jnp.dot(wide, values, preferred_element_type=jnp.float32)
    return output + jnp.dot(
        turned[:, width:].astype(jnp.bfloat16), fresh_v, preferred_element_type=jnp.float32
    )


def gather_heads(output, heads, slots, width):
    group_size = heads // slots
    slot_of_lane = lax.broadcasted_iota(jnp.int32, (SUB, width), 1) // HEAD
    blocks = []
    for block in range(heads // slots):
        merged = None
        for slot in range(slots):
            head = block * slots + slot
            home = head // group_size
            piece = output[head * SUB : (head + 1) * SUB]
            if slot != home:
                piece = pltpu.roll(piece, ((slot - home) * HEAD) % width, 1)
            merged = piece if merged is None else jnp.where(slot_of_lane == slot, piece, merged)
        blocks.append(merged)
    return jnp.concatenate(blocks, axis=-1)


def attend(first, lengths_ref, q_ref, nk_ref, nv_ref, k_ref, v_ref, att_ref, ready):
    width = nk_ref.shape[1]
    slots = width // HEAD
    heads = q_ref.shape[1] // HEAD
    cache_len = k_ref.shape[1]
    per = width // cache_len
    request = lax.broadcasted_iota(jnp.int32, (1, heads * SUB), 1) % SUB
    batches = range(0, att_ref.shape[0], SUB)
    scores = []
    for at in batches:
        step = at // STEP * STEP
        if at == step:
            ready(at)
            queries = q_ref[step : step + STEP].astype(jnp.float32) * (1.0 / math.sqrt(HEAD))
        rows = place_heads(queries[at - step : at - step + SUB], heads, slots, width)
        keys = k_ref[at : at + SUB].reshape(SUB * cache_len, width)
        scores.append(score(rows, keys, nk_ref[step : step + STEP], cache_len))
    turned = []
    for at, (cached, fresh) in zip(batches, scores):
        live = jnp.zeros(request.shape, jnp.int32)
        for i in range(SUB):
            live = jnp.where(request == i, lengths_ref[first + at + i], live)
        turned.append(soften(cached, fresh, live, at % STEP, per))
    outputs = []
    for at, probs in zip(batches, turned):
        step = at // STEP * STEP
        values = v_ref[at : at + SUB].reshape(SUB * cache_len, width)
        outputs.append(weigh(probs, values, nv_ref[step : step + STEP], per))
    for step in range(0, att_ref.shape[0], STEP):
        pair = outputs[step // SUB : (step + STEP) // SUB]
        att_ref[step : step + STEP, :] = jnp.concatenate(
            [gather_heads(output, heads, slots, width) for output in pair], axis=0
        ).astype(jnp.bfloat16)


def project(att_ref, w_ref, out_ref):
    columns = w_ref.shape[0]
    for at in range(0, columns, 768):
        size = min(768, columns - at)
        turned = lax.dot_general(
            w_ref[at : at + size, :], att_ref[...], ACROSS, preferred_element_type=jnp.float32
        )
        out_ref[:, at : at + size] = turned.T


def first_kernel(
    core_ref, chip_ref, lengths_ref, q_hbm, nk_hbm, nv_hbm, k_hbm, v_hbm, w_hbm,
    out_ref, w_ref, own_k, own_v, q_ref, nk_ref, nv_ref, k_ref, v_ref, att_ref, sems,
):
    rows = out_ref.shape[0]
    theirs = pl.multiple_of((1 - core_ref[0]) * rows, rows)
    mine = pl.multiple_of(core_ref[0] * rows, rows)
    copies = []

    def bring(source, target):
        copy = pltpu.make_async_copy(source, target, sems.at[len(copies)])
        copy.start()
        copies.append(copy)
        return copy

    small = [
        bring(source.at[pl.ds(theirs, rows)], target)
        for source, target in ((q_hbm, q_ref), (nk_hbm, nk_ref), (nv_hbm, nv_ref))
    ]
    cache = []
    for at in range(0, rows, STEP):
        span = pl.ds(theirs + at, STEP)
        cache.append(
            (
                bring(k_hbm.at[span], k_ref.at[pl.ds(at, STEP)]),
                bring(v_hbm.at[span], v_ref.at[pl.ds(at, STEP)]),
            )
        )
    pieces = 4
    columns = w_ref.shape[0]
    size = -(-columns // pieces // 16) * 16
    weights = []
    for at in range(0, columns, size):
        span = pl.ds(at, min(size, columns - at))
        weights.append(bring(w_hbm.at[span], w_ref.at[span]))
    later = [
        bring(k_hbm.at[pl.ds(mine, rows)], own_k),
        bring(v_hbm.at[pl.ds(mine, rows)], own_v),
    ]
    for copy in small:
        copy.wait()

    def ready(at):
        for copy in cache[at // STEP]:
            copy.wait()

    attend(theirs, lengths_ref, q_ref, nk_ref, nv_ref, k_ref, v_ref, att_ref, ready)
    for copy in weights:
        copy.wait()
    project(att_ref, w_ref, out_ref)
    for copy in later:
        copy.wait()


def second_kernel(
    core_ref, lengths_ref, q_ref, nk_ref, nv_ref, k_ref, v_ref, w_ref, out_ref, att_ref
):
    rows = out_ref.shape[0]
    mine = pl.multiple_of(core_ref[0] * rows, rows)
    own = [ref.at[pl.ds(mine, rows)] for ref in (q_ref, nk_ref, nv_ref)]
    attend(mine, lengths_ref, *own, k_ref, v_ref, att_ref, lambda at: None)
    project(att_ref, w_ref, out_ref)


def attend_theirs(
    core, rows, lengths, query, new_key, new_value, cache_keys, cache_values, w, chip
):
    cache = (rows,) + cache_keys.shape[1:]
    columns = w.shape[0]
    smem = pl.BlockSpec(memory_space=pltpu.SMEM)
    vmem = pl.BlockSpec(memory_space=pltpu.VMEM)
    hbm = pl.BlockSpec(memory_space=pltpu.HBM)
    copies = 3 + 2 * (rows // STEP) + 4 + 2
    return pl.pallas_call(
        first_kernel,
        out_shape=(
            jax.ShapeDtypeStruct((rows, columns), jnp.float32),
            jax.ShapeDtypeStruct(w.shape, jnp.bfloat16),
            jax.ShapeDtypeStruct(cache, jnp.bfloat16),
            jax.ShapeDtypeStruct(cache, jnp.bfloat16),
        ),
        in_specs=[smem] * 3 + [hbm] * 6,
        out_specs=[vmem] * 4,
        scratch_shapes=[
            pltpu.VMEM((rows, query.shape[1]), jnp.bfloat16),
            pltpu.VMEM((rows, new_key.shape[1]), jnp.bfloat16),
            pltpu.VMEM((rows, new_key.shape[1]), jnp.bfloat16),
            pltpu.VMEM(cache, jnp.bfloat16),
            pltpu.VMEM(cache, jnp.bfloat16),
            pltpu.VMEM((rows, query.shape[1]), jnp.bfloat16),
            pltpu.SemaphoreType.DMA((copies,)),
        ],
        compiler_params=pltpu.CompilerParams(vmem_limit_bytes=GRANT),
        cost_estimate=pl.CostEstimate(
            flops=2 * rows * w.size, bytes_accessed=2 * w.size, transcendentals=0
        ),
    )(
        core,
        chip,
        lengths,
        *(
            pltpu.with_memory_space_constraint(x, pltpu.HBM)
            for x in (query, new_key, new_value, cache_keys, cache_values, w)
        ),
    )


def attend_mine(core, rows, lengths, query, new_key, new_value, own_keys, own_values, w):
    smem = pl.BlockSpec(memory_space=pltpu.SMEM)
    vmem = pl.BlockSpec(memory_space=pltpu.VMEM)
    return pl.pallas_call(
        second_kernel,
        out_shape=jax.ShapeDtypeStruct((rows, w.shape[0]), jnp.float32),
        in_specs=[smem, smem] + [vmem] * 6,
        out_specs=vmem,
        scratch_shapes=[pltpu.VMEM((rows, query.shape[1]), jnp.bfloat16)],
        compiler_params=pltpu.CompilerParams(vmem_limit_bytes=GRANT),
        cost_estimate=pl.CostEstimate(
            flops=2 * rows * w.size, bytes_accessed=2 * w.size, transcendentals=0
        ),
    )(core, lengths, query, new_key, new_value, own_keys, own_values, w)


def norm_kernel(
    mine_ref, swapped_ref, residual_ref, gain_ref, router_ref, routes_ref, hidden_ref, payload_ref
):
    hidden = residual_ref[...].astype(jnp.float32) + (mine_ref[...] + swapped_ref[...])
    hidden_ref[...] = hidden
    rows, width = hidden.shape
    mean_square = jnp.sum(hidden * hidden, axis=-1, keepdims=True) * (1.0 / width)
    normed = (hidden * lax.rsqrt(mean_square + 1e-05) * gain_ref[...]).astype(jnp.bfloat16)
    payload_ref[:, :width] = normed
    rest = router_ref[...]
    experts = rest.shape[0]
    terms = []
    for _ in range(3):
        term = rest.astype(jnp.bfloat16).astype(jnp.float32)
        terms.append(term)
        rest = rest - term
    parts = lax.dot_general(
        jnp.concatenate(terms, axis=0).astype(jnp.bfloat16),
        normed,
        (((1,), (1,)), ((), ())),
        preferred_element_type=jnp.float32,
    )
    logits = parts[:experts] + parts[experts : 2 * experts] + parts[2 * experts :]
    number = lax.broadcasted_iota(jnp.int32, (experts, rows), 0)
    chosen = number == routes_ref[0:1, :]
    for k in range(1, routes_ref.shape[0]):
        chosen = chosen | (number == routes_ref[k : k + 1, :])
    squashed = jnp.where(chosen, 1.0 / (1.0 + jnp.exp(-logits)), 0.0)
    gates = squashed / jnp.sum(squashed, axis=0, keepdims=True)
    upper = gates.astype(jnp.bfloat16).astype(jnp.float32)
    both = jnp.concatenate([upper, gates - upper], axis=0).astype(jnp.bfloat16)
    tail = payload_ref.shape[1] - width
    place = lax.broadcasted_iota(jnp.int32, (2 * experts, tail), 0)
    lane = lax.broadcasted_iota(jnp.int32, (2 * experts, tail), 1)
    placed = lax.dot_general(
        both,
        (place == lane).astype(jnp.bfloat16),
        (((0,), (0,)), ((), ())),
        preferred_element_type=jnp.float32,
    )
    payload_ref[:, width:] = placed.astype(jnp.bfloat16)


def norm_route(mine, swapped, residual, norm_gain, router, routes):
    rows, width = residual.shape
    experts = router.shape[1]
    wide = -(-(width + 2 * experts) // 128) * 128
    return pl.pallas_call(
        norm_kernel,
        out_shape=(
            jax.ShapeDtypeStruct((rows, width), jnp.float32),
            jax.ShapeDtypeStruct((rows, wide), jnp.bfloat16),
        ),
        compiler_params=pltpu.CompilerParams(vmem_limit_bytes=GRANT),
    )(mine, swapped, residual, norm_gain[None, :], router.T, routes.T)


def expert_kernel(count, experts, chip_ref, *refs):
    blocks, refs = refs[:count], refs[count:]
    gate_ref, up_ref, down_ref = refs[:3]
    outs, act_ref = refs[3:-1], refs[-1]
    _, hidden, width = gate_ref.shape
    rows = jnp.concatenate([block[...] for block in blocks], axis=0)
    base = width // 128 * 128
    tail = rows[:, base:].astype(jnp.float32)
    lane = lax.broadcasted_iota(jnp.int32, tail.shape, 1) - (width - base)
    named = (lane == chip_ref[0]) | (lane == chip_ref[0] + experts)
    weight = jnp.sum(jnp.where(named, tail, 0.0), axis=-1, keepdims=True)
    turned = rows[:, :width].T
    for at in range(0, hidden, 256):
        span = slice(at, min(at + 256, hidden))
        gate = jnp.dot(gate_ref[0, span, :], turned, preferred_element_type=jnp.float32)
        up = jnp.dot(up_ref[0, span, :], turned, preferred_element_type=jnp.float32)
        act_ref[:, span] = (gate / (1.0 + jnp.exp(-gate)) * up).T.astype(jnp.bfloat16)
    for at in range(0, width, 768):
        span = slice(at, min(at + 768, width))
        part = jnp.dot(act_ref[...], down_ref[0, :, span], preferred_element_type=jnp.float32)
        part = (part * weight).astype(jnp.bfloat16)
        first = 0
        for out in outs:
            out[:, span] = part[first : first + out.shape[0]]
            first += out.shape[0]


def run_expert(chip, blocks, gate_t, up_t, down, experts):
    _, hidden, width = down.shape
    rows = sum(block.shape[0] for block in blocks)
    count = len(blocks)
    vmem = pl.BlockSpec(memory_space=pltpu.VMEM)
    return pl.pallas_call(
        lambda *refs: expert_kernel(count, experts, *refs),
        out_shape=[jax.ShapeDtypeStruct((b.shape[0], width), jnp.bfloat16) for b in blocks],
        in_specs=[pl.BlockSpec(memory_space=pltpu.SMEM)] + [vmem] * (count + 3),
        out_specs=[vmem] * count,
        scratch_shapes=[pltpu.VMEM((rows, hidden), jnp.bfloat16)],
        compiler_params=pltpu.CompilerParams(vmem_limit_bytes=GRANT),
        cost_estimate=pl.CostEstimate(
            flops=6 * rows * hidden * width, bytes_accessed=6 * hidden * width, transcendentals=0
        ),
    )(chip, *blocks, gate_t, up_t, down)


def add_kernel(*refs):
    total = refs[0][...].astype(jnp.float32)
    for ref in refs[1:-1]:
        total = total + ref[...].astype(jnp.float32)
    refs[-1][...] = total.astype(refs[-1].dtype)


def add_all(*terms):
    return pl.pallas_call(
        add_kernel,
        out_shape=jax.ShapeDtypeStruct(terms[0].shape, jnp.bfloat16),
        compiler_params=pltpu.CompilerParams(vmem_limit_bytes=GRANT),
    )(*terms)


def ring_pairs(chips, cores, cross):
    order = list(range(0, chips, 2)) + list(range(1, chips, 2))[::-1]
    pairs = []
    for p in range(chips):
        for core in range(cores):
            turn = -1 if core % 2 else 1
            to = core ^ 1 if cross else core
            pairs.append((order[p] * cores + core, order[(p + turn) % chips] * cores + to))
    return pairs


def per_device(
    query,
    new_key,
    new_value,
    cache_keys,
    cache_values,
    lengths,
    out_proj,
    residual,
    norm_gain,
    router,
    routes,
    w_gate,
    w_up,
    w_down,
):
    chips, cores = lax.axis_size("att"), lax.axis_size("exp")
    own_rows = residual.shape[0]
    ring = ("att", "exp")

    def send(x, cross=False):
        return lax.ppermute(x, ring, ring_pairs(chips, cores, cross))

    def swap(x):
        return lax.ppermute(x, "exp", [(0, 1), (1, 0)])

    core = jnp.full((1,), lax.axis_index("exp"), jnp.int32)
    chip = jnp.full((1,), lax.axis_index("att"), jnp.int32)
    small = (core, own_rows, lengths, query, new_key, new_value)
    theirs, w_out, own_keys, own_values = attend_theirs(
        *small, cache_keys, cache_values, out_proj.T, chip
    )
    swapped = swap(theirs)
    mine = attend_mine(*small, own_keys, own_values, w_out)
    hidden_state, payload = norm_route(mine, swapped, residual, norm_gain, router, routes)

    experts = router.shape[1]

    far = chips // 2

    def after(value, *earlier):
        return lax.optimization_barrier((value, earlier))[0]

    gate_t, up_t = w_gate.transpose(0, 2, 1), w_up.transpose(0, 2, 1)

    def expert(blocks):
        return run_expert(chip, blocks, gate_t, up_t, w_down, experts)

    x, y = payload, swap(payload)
    done = expert((x, y))
    own, own_other = done[0], swap(done[1])
    sums_x, sums_y = [None], [None]
    for k in range(1, far + 1):
        x = send(x)
        if k in (1, far):
            x = after(x, done[0])
        blocks = [x, swap(x)]
        if k < far:
            y = send(y)
            if k > 1:
                y = after(y, done[0])
            blocks += [y, swap(y)]
        if k > 2:
            blocks[1] = after(blocks[1], sums_x[k - 2][1], sums_y[k - 2][1])
        done = expert(blocks)
        sums_x.append((done[1], swap(done[0])))
        if k < far:
            sums_y.append((done[3], swap(done[2])))

    back_x, back_y = [], []
    for k in range(far, 0, -1):
        if k < far:
            back_y = [send(add_all(*sums_y[k], *back_y))]
        back_x = [send(add_all(*sums_x[k], *back_x), k == 1)]
    return add_all(hidden_state, own, own_other, *back_x, *back_y)


def solution(mesh):
    in_specs = (
        P(("groups", "att"), "exp"),
        P(("groups", "att"), "exp"),
        P(("groups", "att"), "exp"),
        P(("groups", "att"), None, "exp"),
        P(("groups", "att"), None, "exp"),
        P(("groups", "att")),
        P("exp", None),
        P(("groups", "att", "exp"), None),
        P(),
        P(),
        P(("groups", "att", "exp"), None),
        P("att", None, "exp"),
        P("att", None, "exp"),
        P("att", "exp", None),
    )
    out_specs = P(("groups", "att", "exp"), None)
    return jax.shard_map(
        per_device, mesh=mesh, in_specs=in_specs, out_specs=out_specs, check_vma=False
    )
```

```python
import math

import jax
import jax.numpy as jnp
from jax import lax
from jax.experimental import pallas as pl
from jax.experimental.pallas import tpu as pltpu
from jax.sharding import PartitionSpec as P

HEAD = 64
SUB = 8
STEP = 16
GRANT = 12 * 1024 * 1024
ACROSS = (((1,), (1,)), ((), ()))


def place_heads(queries, heads, slots, width):
    group_size = heads // slots
    slot_of_lane = lax.broadcasted_iota(jnp.int32, (SUB, width), 1) // HEAD
    pieces = []
    for head in range(heads):
        block, slot, home = head // slots, head % slots, head // group_size
        piece = queries[:, block * width : (block + 1) * width]
        if slot != home:
            piece = pltpu.roll(piece, ((home - slot) * HEAD) % width, 1)
        pieces.append(jnp.where(slot_of_lane == home, piece, 0.0))
    return jnp.concatenate(pieces, axis=0).astype(jnp.bfloat16)


def score(rows, keys, fresh_k, cache_len):
    request = lax.broadcasted_iota(jnp.int32, (cache_len, rows.shape[0]), 1) % SUB
    spread = lax.dot_general(keys, rows, ACROSS, preferred_element_type=jnp.float32)
    scores = spread[:cache_len]
    for r in range(1, SUB):
        scores = jnp.where(request == r, spread[r * cache_len : (r + 1) * cache_len], scores)
    return scores, lax.dot_general(fresh_k, rows, ACROSS, preferred_element_type=jnp.float32)


def soften(scores, fresh, live, offset, per):
    cache_len, count = scores.shape
    request = lax.broadcasted_iota(jnp.int32, (cache_len, count), 1) % SUB
    place = lax.broadcasted_iota(jnp.int32, (cache_len, count), 0)
    scores = jnp.where(place < live, scores, -1e30)
    fresh_place = lax.broadcasted_iota(jnp.int32, fresh.shape, 0)
    fresh_own = fresh_place == offset + lax.broadcasted_iota(jnp.int32, fresh.shape, 1) % SUB
    fresh_scores = jnp.sum(jnp.where(fresh_own, fresh, 0.0), axis=0, keepdims=True)
    highest = jnp.maximum(jnp.max(scores, axis=0, keepdims=True), fresh_scores)
    cached_exp = jnp.exp(scores - highest)
    fresh_exp = jnp.exp(fresh_scores - highest)
    scale = 1.0 / (jnp.sum(cached_exp, axis=0, keepdims=True) + fresh_exp)
    probs = cached_exp * scale
    fresh_probs = jnp.where(fresh_own, fresh_exp * scale, 0.0)
    return jnp.concatenate(
        [jnp.where(request % per == i, probs, 0.0) for i in range(per)] + [fresh_probs], axis=0
    ).T


def weigh(turned, values, fresh_v, per):
    count, width = turned.shape[0], values.shape[1]
    group = lax.broadcasted_iota(jnp.int32, (count, width), 0) % SUB // per
    wide = jnp.concatenate(
        [jnp.where(group == part, turned[:, :width], 0.0) for part in range(SUB // per)], axis=1
    ).astype(jnp.bfloat16)
    output = jnp.dot(wide, values, preferred_element_type=jnp.float32)
    return output + jnp.dot(
        turned[:, width:].astype(jnp.bfloat16), fresh_v, preferred_element_type=jnp.float32
    )


def gather_heads(output, heads, slots, width):
    group_size = heads // slots
    slot_of_lane = lax.broadcasted_iota(jnp.int32, (SUB, width), 1) // HEAD
    blocks = []
    for block in range(heads // slots):
        merged = None
        for slot in range(slots):
            head = block * slots + slot
            home = head // group_size
            piece = output[head * SUB : (head + 1) * SUB]
            if slot != home:
                piece = pltpu.roll(piece, ((slot - home) * HEAD) % width, 1)
            merged = piece if merged is None else jnp.where(slot_of_lane == slot, piece, merged)
        blocks.append(merged)
    return jnp.concatenate(blocks, axis=-1)


def attend(first, lengths_ref, q_ref, nk_ref, nv_ref, k_ref, v_ref, att_ref, ready):
    width = nk_ref.shape[1]
    slots = width // HEAD
    heads = q_ref.shape[1] // HEAD
    cache_len = k_ref.shape[1]
    per = width // cache_len
    request = lax.broadcasted_iota(jnp.int32, (1, heads * SUB), 1) % SUB
    batches = range(0, att_ref.shape[0], SUB)
    scores = []
    for at in batches:
        step = at // STEP * STEP
        if at == step:
            ready(at)
            queries = q_ref[step : step + STEP].astype(jnp.float32) * (1.0 / math.sqrt(HEAD))
        rows = place_heads(queries[at - step : at - step + SUB], heads, slots, width)
        keys = k_ref[at : at + SUB].reshape(SUB * cache_len, width)
        scores.append(score(rows, keys, nk_ref[step : step + STEP], cache_len))
    turned = []
    for at, (cached, fresh) in zip(batches, scores):
        live = jnp.zeros(request.shape, jnp.int32)
        for i in range(SUB):
            live = jnp.where(request == i, lengths_ref[first + at + i], live)
        turned.append(soften(cached, fresh, live, at % STEP, per))
    outputs = []
    for at, probs in zip(batches, turned):
        step = at // STEP * STEP
        values = v_ref[at : at + SUB].reshape(SUB * cache_len, width)
        outputs.append(weigh(probs, values, nv_ref[step : step + STEP], per))
    for step in range(0, att_ref.shape[0], STEP):
        pair = outputs[step // SUB : (step + STEP) // SUB]
        att_ref[step : step + STEP, :] = jnp.concatenate(
            [gather_heads(output, heads, slots, width) for output in pair], axis=0
        ).astype(jnp.bfloat16)


def project(att_ref, w_ref, out_ref):
    columns = w_ref.shape[0]
    for at in range(0, columns, 768):
        size = min(768, columns - at)
        turned = lax.dot_general(
            w_ref[at : at + size, :], att_ref[...], ACROSS, preferred_element_type=jnp.float32
        )
        out_ref[:, at : at + size] = turned.T


def first_kernel(
    core_ref, chip_ref, lengths_ref, q_hbm, nk_hbm, nv_hbm, k_hbm, v_hbm, w_hbm,
    out_ref, w_ref, own_k, own_v, q_ref, nk_ref, nv_ref, k_ref, v_ref, att_ref, sems,
):
    rows = out_ref.shape[0]
    theirs = pl.multiple_of((1 - core_ref[0]) * rows, rows)
    mine = pl.multiple_of(core_ref[0] * rows, rows)
    copies = []

    def bring(source, target):
        copy = pltpu.make_async_copy(source, target, sems.at[len(copies)])
        copy.start()
        copies.append(copy)
        return copy

    small = [
        bring(source.at[pl.ds(theirs, rows)], target)
        for source, target in ((q_hbm, q_ref), (nk_hbm, nk_ref), (nv_hbm, nv_ref))
    ]
    cache = []
    for at in range(0, rows, STEP):
        span = pl.ds(theirs + at, STEP)
        cache.append(
            (
                bring(k_hbm.at[span], k_ref.at[pl.ds(at, STEP)]),
                bring(v_hbm.at[span], v_ref.at[pl.ds(at, STEP)]),
            )
        )
    pieces = 4
    columns = w_ref.shape[0]
    size = -(-columns // pieces // 16) * 16
    weights = []
    for at in range(0, columns, size):
        span = pl.ds(at, min(size, columns - at))
        weights.append(bring(w_hbm.at[span], w_ref.at[span]))
    later = [
        bring(k_hbm.at[pl.ds(mine, rows)], own_k),
        bring(v_hbm.at[pl.ds(mine, rows)], own_v),
    ]
    for copy in small:
        copy.wait()

    def ready(at):
        for copy in cache[at // STEP]:
            copy.wait()

    attend(theirs, lengths_ref, q_ref, nk_ref, nv_ref, k_ref, v_ref, att_ref, ready)
    for copy in weights:
        copy.wait()
    project(att_ref, w_ref, out_ref)
    for copy in later:
        copy.wait()


def second_kernel(
    core_ref, lengths_ref, q_ref, nk_ref, nv_ref, k_ref, v_ref, w_ref, out_ref, att_ref
):
    rows = out_ref.shape[0]
    mine = pl.multiple_of(core_ref[0] * rows, rows)
    own = [ref.at[pl.ds(mine, rows)] for ref in (q_ref, nk_ref, nv_ref)]
    attend(mine, lengths_ref, *own, k_ref, v_ref, att_ref, lambda at: None)
    project(att_ref, w_ref, out_ref)


def attend_theirs(
    core, rows, lengths, query, new_key, new_value, cache_keys, cache_values, w, chip
):
    cache = (rows,) + cache_keys.shape[1:]
    columns = w.shape[0]
    smem = pl.BlockSpec(memory_space=pltpu.SMEM)
    vmem = pl.BlockSpec(memory_space=pltpu.VMEM)
    hbm = pl.BlockSpec(memory_space=pltpu.HBM)
    copies = 3 + 2 * (rows // STEP) + 4 + 2
    return pl.pallas_call(
        first_kernel,
        out_shape=(
            jax.ShapeDtypeStruct((rows, columns), jnp.float32),
            jax.ShapeDtypeStruct(w.shape, jnp.bfloat16),
            jax.ShapeDtypeStruct(cache, jnp.bfloat16),
            jax.ShapeDtypeStruct(cache, jnp.bfloat16),
        ),
        in_specs=[smem] * 3 + [hbm] * 6,
        out_specs=[vmem] * 4,
        scratch_shapes=[
            pltpu.VMEM((rows, query.shape[1]), jnp.bfloat16),
            pltpu.VMEM((rows, new_key.shape[1]), jnp.bfloat16),
            pltpu.VMEM((rows, new_key.shape[1]), jnp.bfloat16),
            pltpu.VMEM(cache, jnp.bfloat16),
            pltpu.VMEM(cache, jnp.bfloat16),
            pltpu.VMEM((rows, query.shape[1]), jnp.bfloat16),
            pltpu.SemaphoreType.DMA((copies,)),
        ],
        compiler_params=pltpu.CompilerParams(vmem_limit_bytes=GRANT),
        cost_estimate=pl.CostEstimate(
            flops=2 * rows * w.size, bytes_accessed=2 * w.size, transcendentals=0
        ),
    )(
        core,
        chip,
        lengths,
        *(
            pltpu.with_memory_space_constraint(x, pltpu.HBM)
            for x in (query, new_key, new_value, cache_keys, cache_values, w)
        ),
    )


def attend_mine(core, rows, lengths, query, new_key, new_value, own_keys, own_values, w):
    smem = pl.BlockSpec(memory_space=pltpu.SMEM)
    vmem = pl.BlockSpec(memory_space=pltpu.VMEM)
    return pl.pallas_call(
        second_kernel,
        out_shape=jax.ShapeDtypeStruct((rows, w.shape[0]), jnp.float32),
        in_specs=[smem, smem] + [vmem] * 6,
        out_specs=vmem,
        scratch_shapes=[pltpu.VMEM((rows, query.shape[1]), jnp.bfloat16)],
        compiler_params=pltpu.CompilerParams(vmem_limit_bytes=GRANT),
        cost_estimate=pl.CostEstimate(
            flops=2 * rows * w.size, bytes_accessed=2 * w.size, transcendentals=0
        ),
    )(core, lengths, query, new_key, new_value, own_keys, own_values, w)


def norm_kernel(
    mine_ref, swapped_ref, residual_ref, gain_ref, router_ref, routes_ref, hidden_ref, payload_ref
):
    hidden = residual_ref[...].astype(jnp.float32) + (mine_ref[...] + swapped_ref[...])
    hidden_ref[...] = hidden
    rows, width = hidden.shape
    mean_square = jnp.sum(hidden * hidden, axis=-1, keepdims=True) * (1.0 / width)
    normed = (hidden * lax.rsqrt(mean_square + 1e-05) * gain_ref[...]).astype(jnp.bfloat16)
    payload_ref[:, :width] = normed
    rest = router_ref[...]
    experts = rest.shape[0]
    terms = []
    for _ in range(3):
        term = rest.astype(jnp.bfloat16).astype(jnp.float32)
        terms.append(term)
        rest = rest - term
    parts = lax.dot_general(
        jnp.concatenate(terms, axis=0).astype(jnp.bfloat16),
        normed,
        (((1,), (1,)), ((), ())),
        preferred_element_type=jnp.float32,
    )
    logits = parts[:experts] + parts[experts : 2 * experts] + parts[2 * experts :]
    number = lax.broadcasted_iota(jnp.int32, (experts, rows), 0)
    chosen = number == routes_ref[0:1, :]
    for k in range(1, routes_ref.shape[0]):
        chosen = chosen | (number == routes_ref[k : k + 1, :])
    squashed = jnp.where(chosen, 1.0 / (1.0 + jnp.exp(-logits)), 0.0)
    gates = squashed / jnp.sum(squashed, axis=0, keepdims=True)
    upper = gates.astype(jnp.bfloat16).astype(jnp.float32)
    both = jnp.concatenate([upper, gates - upper], axis=0).astype(jnp.bfloat16)
    tail = payload_ref.shape[1] - width
    place = lax.broadcasted_iota(jnp.int32, (2 * experts, tail), 0)
    lane = lax.broadcasted_iota(jnp.int32, (2 * experts, tail), 1)
    placed = lax.dot_general(
        both,
        (place == lane).astype(jnp.bfloat16),
        (((0,), (0,)), ((), ())),
        preferred_element_type=jnp.float32,
    )
    payload_ref[:, width:] = placed.astype(jnp.bfloat16)


def norm_route(mine, swapped, residual, norm_gain, router, routes):
    rows, width = residual.shape
    experts = router.shape[1]
    wide = -(-(width + 2 * experts) // 128) * 128
    return pl.pallas_call(
        norm_kernel,
        out_shape=(
            jax.ShapeDtypeStruct((rows, width), jnp.float32),
            jax.ShapeDtypeStruct((rows, wide), jnp.bfloat16),
        ),
        compiler_params=pltpu.CompilerParams(vmem_limit_bytes=GRANT),
    )(mine, swapped, residual, norm_gain[None, :], router.T, routes.T)


def expert_kernel(count, experts, chip_ref, *refs):
    blocks, refs = refs[:count], refs[count:]
    gate_ref, up_ref, down_ref = refs[:3]
    outs, act_ref = refs[3:-1], refs[-1]
    _, hidden, width = gate_ref.shape
    rows = jnp.concatenate([block[...] for block in blocks], axis=0)
    base = width // 128 * 128
    tail = rows[:, base:].astype(jnp.float32)
    lane = lax.broadcasted_iota(jnp.int32, tail.shape, 1) - (width - base)
    named = (lane == chip_ref[0]) | (lane == chip_ref[0] + experts)
    weight = jnp.sum(jnp.where(named, tail, 0.0), axis=-1, keepdims=True)
    turned = rows[:, :width].T
    for at in range(0, hidden, 256):
        span = slice(at, min(at + 256, hidden))
        gate = jnp.dot(gate_ref[0, span, :], turned, preferred_element_type=jnp.float32)
        up = jnp.dot(up_ref[0, span, :], turned, preferred_element_type=jnp.float32)
        act_ref[:, span] = (gate / (1.0 + jnp.exp(-gate)) * up).T.astype(jnp.bfloat16)
    for at in range(0, width, 768):
        span = slice(at, min(at + 768, width))
        part = jnp.dot(act_ref[...], down_ref[0, :, span], preferred_element_type=jnp.float32)
        part = (part * weight).astype(jnp.bfloat16)
        first = 0
        for out in outs:
            out[:, span] = part[first : first + out.shape[0]]
            first += out.shape[0]


def run_expert(chip, blocks, gate_t, up_t, down, experts, cost):
    _, hidden, width = down.shape
    rows = sum(block.shape[0] for block in blocks)
    count = len(blocks)
    vmem = pl.BlockSpec(memory_space=pltpu.VMEM)
    return pl.pallas_call(
        lambda *refs: expert_kernel(count, experts, *refs),
        out_shape=[jax.ShapeDtypeStruct((b.shape[0], width), jnp.bfloat16) for b in blocks],
        in_specs=[pl.BlockSpec(memory_space=pltpu.SMEM)] + [vmem] * (count + 3),
        out_specs=[vmem] * count,
        scratch_shapes=[pltpu.VMEM((rows, hidden), jnp.bfloat16)],
        compiler_params=pltpu.CompilerParams(vmem_limit_bytes=GRANT),
        cost_estimate=pl.CostEstimate(
            flops=6 * cost * rows * hidden * width,
            bytes_accessed=6 * cost * hidden * width,
            transcendentals=0,
        ),
    )(chip, *blocks, gate_t, up_t, down)


def add_kernel(*refs):
    total = refs[0][...].astype(jnp.float32)
    for ref in refs[1:-1]:
        total = total + ref[...].astype(jnp.float32)
    refs[-1][...] = total.astype(refs[-1].dtype)


def add_all(*terms):
    return pl.pallas_call(
        add_kernel,
        out_shape=jax.ShapeDtypeStruct(terms[0].shape, jnp.bfloat16),
        compiler_params=pltpu.CompilerParams(vmem_limit_bytes=GRANT),
    )(*terms)


def ring_pairs(chips, cores, cross):
    order = list(range(0, chips, 2)) + list(range(1, chips, 2))[::-1]
    pairs = []
    for p in range(chips):
        for core in range(cores):
            turn = -1 if core % 2 else 1
            to = core ^ 1 if cross else core
            pairs.append((order[p] * cores + core, order[(p + turn) % chips] * cores + to))
    return pairs


def per_device(
    query,
    new_key,
    new_value,
    cache_keys,
    cache_values,
    lengths,
    out_proj,
    residual,
    norm_gain,
    router,
    routes,
    w_gate,
    w_up,
    w_down,
):
    chips, cores = lax.axis_size("att"), lax.axis_size("exp")
    own_rows = residual.shape[0]
    ring = ("att", "exp")

    def send(x, cross=False):
        return lax.ppermute(x, ring, ring_pairs(chips, cores, cross))

    def swap(x):
        return lax.ppermute(x, "exp", [(0, 1), (1, 0)])

    core = jnp.full((1,), lax.axis_index("exp"), jnp.int32)
    chip = jnp.full((1,), lax.axis_index("att"), jnp.int32)
    small = (core, own_rows, lengths, query, new_key, new_value)
    theirs, w_out, own_keys, own_values = attend_theirs(
        *small, cache_keys, cache_values, out_proj.T, chip
    )
    swapped = swap(theirs)
    mine = attend_mine(*small, own_keys, own_values, w_out)
    hidden_state, payload = norm_route(mine, swapped, residual, norm_gain, router, routes)

    experts = router.shape[1]

    far = chips // 2

    def after(value, *earlier):
        return lax.optimization_barrier((value, earlier))[0]

    gate_t, up_t = w_gate.transpose(0, 2, 1), w_up.transpose(0, 2, 1)

    def expert(blocks, cost=5):
        return run_expert(chip, blocks, gate_t, up_t, w_down, experts, cost)

    x, y = payload, swap(payload)
    done = expert((x, y), cost=1)
    own, own_other = done[0], swap(done[1])
    sums_x, sums_y = [None], [None]
    swapped_y = None
    for k in range(1, far + 1):
        x = send(x)
        if k in (1, far):
            x = after(x, done[0])
        blocks = [x, swap(x)]
        if k > 1:
            blocks += swapped_y
        if k < far:
            y = send(y)
            if k > 1:
                y = after(y, done[0])
            swapped_y = [y, swap(y)]
        if 2 < k < far:
            blocks[1] = after(blocks[1], sums_x[k - 2][1], *([sums_y[k - 2][1]] if k > 3 else []))
        done = expert(blocks)
        sums_x.append((done[1], swap(done[0])))
        if k > 1:
            sums_y.append((done[3], swap(done[2])))

    back_x, back_y = [], []
    for k in range(far, 0, -1):
        if k < far:
            back_y = [send(add_all(*sums_y[k], *back_y))]
        back_x = [send(add_all(*sums_x[k], *back_x), k == 1)]
    return add_all(hidden_state, own, own_other, *back_x, *back_y)


def solution(mesh):
    in_specs = (
        P(("groups", "att"), "exp"),
        P(("groups", "att"), "exp"),
        P(("groups", "att"), "exp"),
        P(("groups", "att"), None, "exp"),
        P(("groups", "att"), None, "exp"),
        P(("groups", "att")),
        P("exp", None),
        P(("groups", "att", "exp"), None),
        P(),
        P(),
        P(("groups", "att", "exp"), None),
        P("att", None, "exp"),
        P("att", None, "exp"),
        P("att", "exp", None),
    )
    out_specs = P(("groups", "att", "exp"), None)
    return jax.shard_map(
        per_device, mesh=mesh, in_specs=in_specs, out_specs=out_specs, check_vma=False
    )
```

```python
import math

import jax
import jax.numpy as jnp
from jax import lax
from jax.experimental import pallas as pl
from jax.experimental.pallas import tpu as pltpu
from jax.sharding import PartitionSpec as P

HEAD = 64
SUB = 8
STEP = 16
GRANT = 12 * 1024 * 1024
ACROSS = (((1,), (1,)), ((), ()))


def place_heads(queries, heads, slots, width):
    group_size = heads // slots
    slot_of_lane = lax.broadcasted_iota(jnp.int32, (SUB, width), 1) // HEAD
    pieces = []
    for head in range(heads):
        block, slot, home = head // slots, head % slots, head // group_size
        piece = queries[:, block * width : (block + 1) * width]
        if slot != home:
            piece = pltpu.roll(piece, ((home - slot) * HEAD) % width, 1)
        pieces.append(jnp.where(slot_of_lane == home, piece, 0.0))
    return jnp.concatenate(pieces, axis=0).astype(jnp.bfloat16)


def score(rows, keys, fresh_k, cache_len):
    request = lax.broadcasted_iota(jnp.int32, (cache_len, rows.shape[0]), 1) % SUB
    spread = lax.dot_general(keys, rows, ACROSS, preferred_element_type=jnp.float32)
    scores = spread[:cache_len]
    for r in range(1, SUB):
        scores = jnp.where(request == r, spread[r * cache_len : (r + 1) * cache_len], scores)
    return scores, lax.dot_general(fresh_k, rows, ACROSS, preferred_element_type=jnp.float32)


def soften(scores, fresh, live, offset, per):
    cache_len, count = scores.shape
    request = lax.broadcasted_iota(jnp.int32, (cache_len, count), 1) % SUB
    place = lax.broadcasted_iota(jnp.int32, (cache_len, count), 0)
    scores = jnp.where(place < live, scores, -1e30)
    fresh_place = lax.broadcasted_iota(jnp.int32, fresh.shape, 0)
    fresh_own = fresh_place == offset + lax.broadcasted_iota(jnp.int32, fresh.shape, 1) % SUB
    fresh_scores = jnp.sum(jnp.where(fresh_own, fresh, 0.0), axis=0, keepdims=True)
    highest = jnp.maximum(jnp.max(scores, axis=0, keepdims=True), fresh_scores)
    cached_exp = jnp.exp(scores - highest)
    fresh_exp = jnp.exp(fresh_scores - highest)
    scale = 1.0 / (jnp.sum(cached_exp, axis=0, keepdims=True) + fresh_exp)
    probs = cached_exp * scale
    fresh_probs = jnp.where(fresh_own, fresh_exp * scale, 0.0)
    return jnp.concatenate(
        [jnp.where(request % per == i, probs, 0.0) for i in range(per)] + [fresh_probs], axis=0
    ).T


def weigh(turned, values, fresh_v, per):
    count, width = turned.shape[0], values.shape[1]
    group = lax.broadcasted_iota(jnp.int32, (count, width), 0) % SUB // per
    wide = jnp.concatenate(
        [jnp.where(group == part, turned[:, :width], 0.0) for part in range(SUB // per)], axis=1
    ).astype(jnp.bfloat16)
    output = jnp.dot(wide, values, preferred_element_type=jnp.float32)
    return output + jnp.dot(
        turned[:, width:].astype(jnp.bfloat16), fresh_v, preferred_element_type=jnp.float32
    )


def gather_heads(output, heads, slots, width):
    group_size = heads // slots
    slot_of_lane = lax.broadcasted_iota(jnp.int32, (SUB, width), 1) // HEAD
    blocks = []
    for block in range(heads // slots):
        merged = None
        for slot in range(slots):
            head = block * slots + slot
            home = head // group_size
            piece = output[head * SUB : (head + 1) * SUB]
            if slot != home:
                piece = pltpu.roll(piece, ((slot - home) * HEAD) % width, 1)
            merged = piece if merged is None else jnp.where(slot_of_lane == slot, piece, merged)
        blocks.append(merged)
    return jnp.concatenate(blocks, axis=-1)


def attend(first, lengths_ref, q_ref, nk_ref, nv_ref, k_ref, v_ref, att_ref, ready):
    width = nk_ref.shape[1]
    slots = width // HEAD
    heads = q_ref.shape[1] // HEAD
    cache_len = k_ref.shape[1]
    per = width // cache_len
    request = lax.broadcasted_iota(jnp.int32, (1, heads * SUB), 1) % SUB
    batches = range(0, att_ref.shape[0], SUB)
    scores = []
    for at in batches:
        step = at // STEP * STEP
        if at == step:
            ready(at)
            queries = q_ref[step : step + STEP].astype(jnp.float32) * (1.0 / math.sqrt(HEAD))
        rows = place_heads(queries[at - step : at - step + SUB], heads, slots, width)
        keys = k_ref[at : at + SUB].reshape(SUB * cache_len, width)
        scores.append(score(rows, keys, nk_ref[step : step + STEP], cache_len))
    turned = []
    for at, (cached, fresh) in zip(batches, scores):
        live = jnp.zeros(request.shape, jnp.int32)
        for i in range(SUB):
            live = jnp.where(request == i, lengths_ref[first + at + i], live)
        turned.append(soften(cached, fresh, live, at % STEP, per))
    outputs = []
    for at, probs in zip(batches, turned):
        step = at // STEP * STEP
        values = v_ref[at : at + SUB].reshape(SUB * cache_len, width)
        outputs.append(weigh(probs, values, nv_ref[step : step + STEP], per))
    for step in range(0, att_ref.shape[0], STEP):
        pair = outputs[step // SUB : (step + STEP) // SUB]
        att_ref[step : step + STEP, :] = jnp.concatenate(
            [gather_heads(output, heads, slots, width) for output in pair], axis=0
        ).astype(jnp.bfloat16)


def project(att_ref, w_ref, out_ref):
    turned = lax.dot_general(
        w_ref[...], att_ref[...], ACROSS, preferred_element_type=jnp.float32
    )
    out_ref[...] = turned.T


def first_kernel(
    core_ref, chip_ref, lengths_hbm, q_hbm, nk_hbm, nv_hbm, k_hbm, v_hbm, w_hbm,
    out_ref, w_ref, own_k, own_v, lengths_ref, q_ref, nk_ref, nv_ref, k_ref, v_ref, att_ref, sems,
):
    rows = out_ref.shape[0]
    theirs = pl.multiple_of((1 - core_ref[0]) * rows, rows)
    mine = pl.multiple_of(core_ref[0] * rows, rows)
    copies = []

    def bring(source, target):
        copy = pltpu.make_async_copy(source, target, sems.at[len(copies)])
        copy.start()
        copies.append(copy)
        return copy

    small = [bring(lengths_hbm, lengths_ref)] + [
        bring(source.at[pl.ds(theirs, rows)], target)
        for source, target in ((q_hbm, q_ref), (nk_hbm, nk_ref), (nv_hbm, nv_ref))
    ]
    cache = []
    for at in range(0, rows, STEP):
        span = pl.ds(theirs + at, STEP)
        cache.append(
            (
                bring(k_hbm.at[span], k_ref.at[pl.ds(at, STEP)]),
                bring(v_hbm.at[span], v_ref.at[pl.ds(at, STEP)]),
            )
        )
    pieces = 4
    columns = w_ref.shape[0]
    size = -(-columns // pieces // 16) * 16
    weights = []
    for at in range(0, columns, size):
        span = pl.ds(at, min(size, columns - at))
        weights.append(bring(w_hbm.at[span], w_ref.at[span]))
    later = [
        bring(k_hbm.at[pl.ds(mine, rows)], own_k),
        bring(v_hbm.at[pl.ds(mine, rows)], own_v),
    ]
    for copy in small:
        copy.wait()

    def ready(at):
        for copy in cache[at // STEP]:
            copy.wait()

    attend(theirs, lengths_ref, q_ref, nk_ref, nv_ref, k_ref, v_ref, att_ref, ready)
    for copy in weights:
        copy.wait()
    project(att_ref, w_ref, out_ref)
    for copy in later:
        copy.wait()


def second_kernel(
    core_ref, lengths_ref, q_ref, nk_ref, nv_ref, k_ref, v_ref, w_ref, out_ref, att_ref
):
    rows = out_ref.shape[0]
    mine = pl.multiple_of(core_ref[0] * rows, rows)
    own = [ref.at[pl.ds(mine, rows)] for ref in (q_ref, nk_ref, nv_ref)]
    attend(mine, lengths_ref, *own, k_ref, v_ref, att_ref, lambda at: None)
    project(att_ref, w_ref, out_ref)


def attend_theirs(
    core, rows, lengths, query, new_key, new_value, cache_keys, cache_values, w, chip
):
    cache = (rows,) + cache_keys.shape[1:]
    columns = w.shape[0]
    smem = pl.BlockSpec(memory_space=pltpu.SMEM)
    vmem = pl.BlockSpec(memory_space=pltpu.VMEM)
    hbm = pl.BlockSpec(memory_space=pltpu.HBM)
    copies = 4 + 2 * (rows // STEP) + 4 + 2
    return pl.pallas_call(
        first_kernel,
        out_shape=(
            jax.ShapeDtypeStruct((rows, columns), jnp.float32),
            jax.ShapeDtypeStruct(w.shape, jnp.bfloat16),
            jax.ShapeDtypeStruct(cache, jnp.bfloat16),
            jax.ShapeDtypeStruct(cache, jnp.bfloat16),
        ),
        in_specs=[smem] * 2 + [hbm] * 7,
        out_specs=[vmem] * 4,
        scratch_shapes=[
            pltpu.SMEM(lengths.shape, jnp.int32),
            pltpu.VMEM((rows, query.shape[1]), jnp.bfloat16),
            pltpu.VMEM((rows, new_key.shape[1]), jnp.bfloat16),
            pltpu.VMEM((rows, new_key.shape[1]), jnp.bfloat16),
            pltpu.VMEM(cache, jnp.bfloat16),
            pltpu.VMEM(cache, jnp.bfloat16),
            pltpu.VMEM((rows, query.shape[1]), jnp.bfloat16),
            pltpu.SemaphoreType.DMA((copies,)),
        ],
        compiler_params=pltpu.CompilerParams(vmem_limit_bytes=GRANT),
        cost_estimate=pl.CostEstimate(
            flops=2 * rows * w.size, bytes_accessed=2 * w.size, transcendentals=0
        ),
    )(
        core,
        chip,
        *(
            pltpu.with_memory_space_constraint(x, pltpu.HBM)
            for x in (lengths, query, new_key, new_value, cache_keys, cache_values, w)
        ),
    )


def attend_mine(core, rows, lengths, query, new_key, new_value, own_keys, own_values, w):
    smem = pl.BlockSpec(memory_space=pltpu.SMEM)
    vmem = pl.BlockSpec(memory_space=pltpu.VMEM)
    return pl.pallas_call(
        second_kernel,
        out_shape=jax.ShapeDtypeStruct((rows, w.shape[0]), jnp.float32),
        in_specs=[smem, smem] + [vmem] * 6,
        out_specs=vmem,
        scratch_shapes=[pltpu.VMEM((rows, query.shape[1]), jnp.bfloat16)],
        compiler_params=pltpu.CompilerParams(vmem_limit_bytes=GRANT),
        cost_estimate=pl.CostEstimate(
            flops=2 * rows * w.size, bytes_accessed=2 * w.size, transcendentals=0
        ),
    )(core, lengths, query, new_key, new_value, own_keys, own_values, w)


def norm_kernel(
    mine_ref, swapped_ref, residual_ref, gain_ref, router_ref, routes_ref, hidden_ref, payload_ref
):
    hidden = residual_ref[...].astype(jnp.float32) + (mine_ref[...] + swapped_ref[...])
    hidden_ref[...] = hidden
    rows, width = hidden.shape
    mean_square = jnp.sum(hidden * hidden, axis=-1, keepdims=True) * (1.0 / width)
    normed = (hidden * lax.rsqrt(mean_square + 1e-05) * gain_ref[...]).astype(jnp.bfloat16)
    payload_ref[:, :width] = normed
    rest = router_ref[...]
    experts = rest.shape[0]
    terms = []
    for _ in range(3):
        term = rest.astype(jnp.bfloat16).astype(jnp.float32)
        terms.append(term)
        rest = rest - term
    parts = lax.dot_general(
        jnp.concatenate(terms, axis=0).astype(jnp.bfloat16),
        normed,
        (((1,), (1,)), ((), ())),
        preferred_element_type=jnp.float32,
    )
    logits = parts[:experts] + parts[experts : 2 * experts] + parts[2 * experts :]
    number = lax.broadcasted_iota(jnp.int32, (experts, rows), 0)
    chosen = number == routes_ref[0:1, :]
    for k in range(1, routes_ref.shape[0]):
        chosen = chosen | (number == routes_ref[k : k + 1, :])
    squashed = jnp.where(chosen, 1.0 / (1.0 + jnp.exp(-logits)), 0.0)
    gates = squashed / jnp.sum(squashed, axis=0, keepdims=True)
    upper = gates.astype(jnp.bfloat16).astype(jnp.float32)
    both = jnp.concatenate([upper, gates - upper], axis=0).astype(jnp.bfloat16)
    tail = payload_ref.shape[1] - width
    place = lax.broadcasted_iota(jnp.int32, (2 * experts, tail), 0)
    lane = lax.broadcasted_iota(jnp.int32, (2 * experts, tail), 1)
    placed = lax.dot_general(
        both,
        (place == lane).astype(jnp.bfloat16),
        (((0,), (0,)), ((), ())),
        preferred_element_type=jnp.float32,
    )
    payload_ref[:, width:] = placed.astype(jnp.bfloat16)


def norm_route(mine, swapped, residual, norm_gain, router, routes):
    rows, width = residual.shape
    experts = router.shape[1]
    wide = -(-(width + 2 * experts) // 128) * 128
    return pl.pallas_call(
        norm_kernel,
        out_shape=(
            jax.ShapeDtypeStruct((rows, width), jnp.float32),
            jax.ShapeDtypeStruct((rows, wide), jnp.bfloat16),
        ),
        compiler_params=pltpu.CompilerParams(vmem_limit_bytes=GRANT),
    )(mine, swapped, residual, norm_gain[None, :], router.T, routes.T)


def expert_kernel(count, experts, chip_ref, *refs):
    blocks, refs = refs[:count], refs[count:]
    gate_ref, up_ref, down_ref = refs[:3]
    outs, act_ref = refs[3:-1], refs[-1]
    _, hidden, width = gate_ref.shape
    rows = jnp.concatenate([block[...] for block in blocks], axis=0)
    base = width // 128 * 128
    tail = rows[:, base:].astype(jnp.float32)
    lane = lax.broadcasted_iota(jnp.int32, tail.shape, 1) - (width - base)
    named = (lane == chip_ref[0]) | (lane == chip_ref[0] + experts)
    weight = jnp.sum(jnp.where(named, tail, 0.0), axis=-1, keepdims=True)
    turned = rows[:, :width].T
    gate = jnp.dot(gate_ref[0], turned, preferred_element_type=jnp.float32)
    up = jnp.dot(up_ref[0], turned, preferred_element_type=jnp.float32)
    act_ref[...] = (gate / (1.0 + jnp.exp(-gate)) * up).T.astype(jnp.bfloat16)
    for at in range(0, width, 768):
        span = slice(at, min(at + 768, width))
        part = jnp.dot(act_ref[...], down_ref[0, :, span], preferred_element_type=jnp.float32)
        part = (part * weight).astype(jnp.bfloat16)
        first = 0
        for out in outs:
            out[:, span] = part[first : first + out.shape[0]]
            first += out.shape[0]


def run_expert(chip, blocks, gate_t, up_t, down, experts, cost):
    _, hidden, width = down.shape
    rows = sum(block.shape[0] for block in blocks)
    count = len(blocks)
    vmem = pl.BlockSpec(memory_space=pltpu.VMEM)
    return pl.pallas_call(
        lambda *refs: expert_kernel(count, experts, *refs),
        out_shape=[jax.ShapeDtypeStruct((b.shape[0], width), jnp.bfloat16) for b in blocks],
        in_specs=[pl.BlockSpec(memory_space=pltpu.SMEM)] + [vmem] * (count + 3),
        out_specs=[vmem] * count,
        scratch_shapes=[pltpu.VMEM((rows, hidden), jnp.bfloat16)],
        compiler_params=pltpu.CompilerParams(vmem_limit_bytes=GRANT),
        cost_estimate=pl.CostEstimate(
            flops=6 * cost * rows * hidden * width,
            bytes_accessed=6 * cost * hidden * width,
            transcendentals=0,
        ),
    )(chip, *blocks, gate_t, up_t, down)


def add_kernel(*refs):
    total = refs[0][...].astype(jnp.float32)
    for ref in refs[1:-1]:
        total = total + ref[...].astype(jnp.float32)
    refs[-1][...] = total.astype(refs[-1].dtype)


def add_all(*terms, dtype=jnp.bfloat16):
    return pl.pallas_call(
        add_kernel,
        out_shape=jax.ShapeDtypeStruct(terms[0].shape, dtype),
        compiler_params=pltpu.CompilerParams(vmem_limit_bytes=GRANT),
    )(*terms)


def ring_pairs(chips, cores, cross):
    order = list(range(0, chips, 2)) + list(range(1, chips, 2))[::-1]
    pairs = []
    for p in range(chips):
        for core in range(cores):
            turn = -1 if core % 2 else 1
            to = core ^ 1 if cross else core
            pairs.append((order[p] * cores + core, order[(p + turn) % chips] * cores + to))
    return pairs


def per_device(
    query,
    new_key,
    new_value,
    cache_keys,
    cache_values,
    lengths,
    out_proj,
    residual,
    norm_gain,
    router,
    routes,
    w_gate,
    w_up,
    w_down,
):
    chips, cores = lax.axis_size("att"), lax.axis_size("exp")
    own_rows = residual.shape[0]
    ring = ("att", "exp")

    def send(x, cross=False):
        return lax.ppermute(x, ring, ring_pairs(chips, cores, cross))

    def swap(x):
        return lax.ppermute(x, "exp", [(0, 1), (1, 0)])

    core = jnp.full((1,), lax.axis_index("exp"), jnp.int32)
    chip = jnp.full((1,), lax.axis_index("att"), jnp.int32)
    small = (core, own_rows, lengths, query, new_key, new_value)
    theirs, w_out, own_keys, own_values = attend_theirs(
        *small, cache_keys, cache_values, out_proj.T, chip
    )
    swapped = swap(theirs)
    mine = attend_mine(*small, own_keys, own_values, w_out)
    hidden_state, payload = norm_route(mine, swapped, residual, norm_gain, router, routes)

    experts = router.shape[1]

    far = chips // 2

    def after(value, *earlier):
        return lax.optimization_barrier((value, earlier))[0]

    gate_t, up_t = w_gate.transpose(0, 2, 1), w_up.transpose(0, 2, 1)

    def expert(blocks, cost=5):
        return run_expert(chip, blocks, gate_t, up_t, w_down, experts, cost)

    x, y = payload, swap(payload)
    done = expert((x, y), cost=1)
    own, own_other = done[0], swap(done[1])
    sums_x, sums_y = [None], [None]
    swapped_y = None
    for k in range(1, far + 1):
        x = send(x)
        if k in (1, far):
            x = after(x, done[0])
        blocks = [x, swap(x)]
        if k > 1:
            blocks += swapped_y
        if k < far:
            y = send(y)
            if k > 1:
                y = after(y, done[0])
            swapped_y = [y, swap(y)]
        if 2 < k < far:
            blocks[1] = after(blocks[1], sums_x[k - 2][1], *([sums_y[k - 2][1]] if k > 3 else []))
        done = expert(blocks)
        sums_x.append((done[1], swap(done[0])))
        if k > 1:
            sums_y.append((done[3], swap(done[2])))

    held = add_all(hidden_state, own, own_other, dtype=jnp.float32)
    back_x, back_y = [], []
    for k in range(far, 0, -1):
        if k < far:
            back_y = [send(add_all(*sums_y[k], *back_y))]
        back_x = [send(add_all(*sums_x[k], *back_x), k == 1)]
    return add_all(held, *back_x, *back_y)


def solution(mesh):
    in_specs = (
        P(("groups", "att"), "exp"),
        P(("groups", "att"), "exp"),
        P(("groups", "att"), "exp"),
        P(("groups", "att"), None, "exp"),
        P(("groups", "att"), None, "exp"),
        P(("groups", "att")),
        P("exp", None),
        P(("groups", "att", "exp"), None),
        P(),
        P(),
        P(("groups", "att", "exp"), None),
        P("att", None, "exp"),
        P("att", None, "exp"),
        P("att", "exp", None),
    )
    out_specs = P(("groups", "att", "exp"), None)
    return jax.shard_map(
        per_device, mesh=mesh, in_specs=in_specs, out_specs=out_specs, check_vma=False
    )
```

```python
import math

import jax
import jax.numpy as jnp
from jax import lax
from jax.experimental import pallas as pl
from jax.experimental.pallas import tpu as pltpu
from jax.sharding import PartitionSpec as P

HEAD = 64
SUB = 8
STEP = 16
GRANT = 12 * 1024 * 1024
ACROSS = (((1,), (1,)), ((), ()))


def place_heads(queries, heads, slots, width):
    group_size = heads // slots
    slot_of_lane = lax.broadcasted_iota(jnp.int32, (SUB, width), 1) // HEAD
    pieces = []
    for head in range(heads):
        block, slot, home = head // slots, head % slots, head // group_size
        piece = queries[:, block * width : (block + 1) * width]
        if slot != home:
            piece = pltpu.roll(piece, ((home - slot) * HEAD) % width, 1)
        pieces.append(jnp.where(slot_of_lane == home, piece, 0.0))
    return jnp.concatenate(pieces, axis=0).astype(jnp.bfloat16)


def score(rows, keys, fresh_k, cache_len):
    request = lax.broadcasted_iota(jnp.int32, (cache_len, rows.shape[0]), 1) % SUB
    spread = lax.dot_general(keys, rows, ACROSS, preferred_element_type=jnp.float32)
    scores = spread[:cache_len]
    for r in range(1, SUB):
        scores = jnp.where(request == r, spread[r * cache_len : (r + 1) * cache_len], scores)
    return scores, lax.dot_general(fresh_k, rows, ACROSS, preferred_element_type=jnp.float32)


def soften(scores, fresh, live, offset, per):
    cache_len, count = scores.shape
    request = lax.broadcasted_iota(jnp.int32, (cache_len, count), 1) % SUB
    place = lax.broadcasted_iota(jnp.int32, (cache_len, count), 0)
    scores = jnp.where(place < live, scores, -1e30)
    fresh_place = lax.broadcasted_iota(jnp.int32, fresh.shape, 0)
    fresh_own = fresh_place == offset + lax.broadcasted_iota(jnp.int32, fresh.shape, 1) % SUB
    fresh_scores = jnp.sum(jnp.where(fresh_own, fresh, 0.0), axis=0, keepdims=True)
    highest = jnp.maximum(jnp.max(scores, axis=0, keepdims=True), fresh_scores)
    cached_exp = jnp.exp(scores - highest)
    fresh_exp = jnp.exp(fresh_scores - highest)
    scale = 1.0 / (jnp.sum(cached_exp, axis=0, keepdims=True) + fresh_exp)
    probs = cached_exp * scale
    fresh_probs = jnp.where(fresh_own, fresh_exp * scale, 0.0)
    return jnp.concatenate(
        [jnp.where(request % per == i, probs, 0.0) for i in range(per)] + [fresh_probs], axis=0
    ).T


def weigh(turned, values, fresh_v, per):
    count, width = turned.shape[0], values.shape[1]
    group = lax.broadcasted_iota(jnp.int32, (count, width), 0) % SUB // per
    wide = jnp.concatenate(
        [jnp.where(group == part, turned[:, :width], 0.0) for part in range(SUB // per)], axis=1
    ).astype(jnp.bfloat16)
    output = jnp.dot(wide, values, preferred_element_type=jnp.float32)
    return output + jnp.dot(
        turned[:, width:].astype(jnp.bfloat16), fresh_v, preferred_element_type=jnp.float32
    )


def gather_heads(output, heads, slots, width):
    group_size = heads // slots
    slot_of_lane = lax.broadcasted_iota(jnp.int32, (SUB, width), 1) // HEAD
    blocks = []
    for block in range(heads // slots):
        merged = None
        for slot in range(slots):
            head = block * slots + slot
            home = head // group_size
            piece = output[head * SUB : (head + 1) * SUB]
            if slot != home:
                piece = pltpu.roll(piece, ((slot - home) * HEAD) % width, 1)
            merged = piece if merged is None else jnp.where(slot_of_lane == slot, piece, merged)
        blocks.append(merged)
    return jnp.concatenate(blocks, axis=-1)


def attend(
    first, lengths_ref, q_ref, nk_ref, nv_ref, k_ref, v_ref, att_ref, keys_ready, values_ready
):
    width = nk_ref.shape[1]
    slots = width // HEAD
    heads = q_ref.shape[1] // HEAD
    cache_len = k_ref.shape[1]
    per = width // cache_len
    request = lax.broadcasted_iota(jnp.int32, (1, heads * SUB), 1) % SUB
    batches = range(0, att_ref.shape[0], SUB)
    scores = []
    for at in batches:
        step = at // STEP * STEP
        if at == step:
            keys_ready(at)
            queries = q_ref[step : step + STEP].astype(jnp.float32) * (1.0 / math.sqrt(HEAD))
        rows = place_heads(queries[at - step : at - step + SUB], heads, slots, width)
        keys = k_ref[at : at + SUB].reshape(SUB * cache_len, width)
        scores.append(score(rows, keys, nk_ref[step : step + STEP], cache_len))
    turned = []
    for at, (cached, fresh) in zip(batches, scores):
        live = jnp.zeros(request.shape, jnp.int32)
        for i in range(SUB):
            live = jnp.where(request == i, lengths_ref[first + at + i], live)
        turned.append(soften(cached, fresh, live, at % STEP, per))
    outputs = []
    for at, probs in zip(batches, turned):
        step = at // STEP * STEP
        if at == step:
            values_ready(at)
        values = v_ref[at : at + SUB].reshape(SUB * cache_len, width)
        outputs.append(weigh(probs, values, nv_ref[step : step + STEP], per))
    for step in range(0, att_ref.shape[0], STEP):
        pair = outputs[step // SUB : (step + STEP) // SUB]
        att_ref[step : step + STEP, :] = jnp.concatenate(
            [gather_heads(output, heads, slots, width) for output in pair], axis=0
        ).astype(jnp.bfloat16)


def project(att_ref, w_ref, out_ref):
    turned = lax.dot_general(
        w_ref[...], att_ref[...], ACROSS, preferred_element_type=jnp.float32
    )
    out_ref[...] = turned.T


def first_kernel(
    core_ref, chip_ref, lengths_hbm, q_hbm, nk_hbm, nv_hbm, k_hbm, v_hbm, w_hbm,
    out_ref, w_ref, own_k, own_v, lengths_ref, q_ref, nk_ref, nv_ref, k_ref, v_ref, att_ref, sems,
):
    rows = out_ref.shape[0]
    theirs = pl.multiple_of((1 - core_ref[0]) * rows, rows)
    mine = pl.multiple_of(core_ref[0] * rows, rows)
    copies = []

    def bring(source, target):
        copy = pltpu.make_async_copy(source, target, sems.at[len(copies)])
        copy.start()
        copies.append(copy)
        return copy

    small = [bring(lengths_hbm, lengths_ref)] + [
        bring(source.at[pl.ds(theirs, rows)], target)
        for source, target in ((q_hbm, q_ref), (nk_hbm, nk_ref), (nv_hbm, nv_ref))
    ]
    steps = range(0, rows, STEP)
    keys = [
        bring(k_hbm.at[pl.ds(theirs + at, STEP)], k_ref.at[pl.ds(at, STEP)]) for at in steps
    ]
    values = [
        bring(v_hbm.at[pl.ds(theirs + at, STEP)], v_ref.at[pl.ds(at, STEP)]) for at in steps
    ]
    pieces = 4
    columns = w_ref.shape[0]
    size = -(-columns // pieces // 16) * 16
    weights = []
    for at in range(0, columns, size):
        span = pl.ds(at, min(size, columns - at))
        weights.append(bring(w_hbm.at[span], w_ref.at[span]))
    later = [
        bring(k_hbm.at[pl.ds(mine, rows)], own_k),
        bring(v_hbm.at[pl.ds(mine, rows)], own_v),
    ]
    for copy in small:
        copy.wait()

    attend(
        theirs, lengths_ref, q_ref, nk_ref, nv_ref, k_ref, v_ref, att_ref,
        lambda at: keys[at // STEP].wait(),
        lambda at: values[at // STEP].wait(),
    )
    for copy in weights:
        copy.wait()
    project(att_ref, w_ref, out_ref)
    for copy in later:
        copy.wait()


def second_kernel(
    core_ref, lengths_ref, q_ref, nk_ref, nv_ref, k_ref, v_ref, w_ref, out_ref, att_ref
):
    rows = out_ref.shape[0]
    mine = pl.multiple_of(core_ref[0] * rows, rows)
    own = [ref.at[pl.ds(mine, rows)] for ref in (q_ref, nk_ref, nv_ref)]
    attend(mine, lengths_ref, *own, k_ref, v_ref, att_ref, lambda at: None, lambda at: None)
    project(att_ref, w_ref, out_ref)


def attend_theirs(
    core, rows, lengths, query, new_key, new_value, cache_keys, cache_values, w, chip
):
    cache = (rows,) + cache_keys.shape[1:]
    columns = w.shape[0]
    smem = pl.BlockSpec(memory_space=pltpu.SMEM)
    vmem = pl.BlockSpec(memory_space=pltpu.VMEM)
    hbm = pl.BlockSpec(memory_space=pltpu.HBM)
    copies = 4 + 2 * (rows // STEP) + 4 + 2
    return pl.pallas_call(
        first_kernel,
        out_shape=(
            jax.ShapeDtypeStruct((rows, columns), jnp.float32),
            jax.ShapeDtypeStruct(w.shape, jnp.bfloat16),
            jax.ShapeDtypeStruct(cache, jnp.bfloat16),
            jax.ShapeDtypeStruct(cache, jnp.bfloat16),
        ),
        in_specs=[smem] * 2 + [hbm] * 7,
        out_specs=[vmem] * 4,
        scratch_shapes=[
            pltpu.SMEM(lengths.shape, jnp.int32),
            pltpu.VMEM((rows, query.shape[1]), jnp.bfloat16),
            pltpu.VMEM((rows, new_key.shape[1]), jnp.bfloat16),
            pltpu.VMEM((rows, new_key.shape[1]), jnp.bfloat16),
            pltpu.VMEM(cache, jnp.bfloat16),
            pltpu.VMEM(cache, jnp.bfloat16),
            pltpu.VMEM((rows, query.shape[1]), jnp.bfloat16),
            pltpu.SemaphoreType.DMA((copies,)),
        ],
        compiler_params=pltpu.CompilerParams(vmem_limit_bytes=GRANT),
        cost_estimate=pl.CostEstimate(
            flops=2 * rows * w.size, bytes_accessed=2 * w.size, transcendentals=0
        ),
    )(
        core,
        chip,
        *(
            pltpu.with_memory_space_constraint(x, pltpu.HBM)
            for x in (lengths, query, new_key, new_value, cache_keys, cache_values, w)
        ),
    )


def attend_mine(core, rows, lengths, query, new_key, new_value, own_keys, own_values, w):
    smem = pl.BlockSpec(memory_space=pltpu.SMEM)
    vmem = pl.BlockSpec(memory_space=pltpu.VMEM)
    return pl.pallas_call(
        second_kernel,
        out_shape=jax.ShapeDtypeStruct((rows, w.shape[0]), jnp.float32),
        in_specs=[smem, smem] + [vmem] * 6,
        out_specs=vmem,
        scratch_shapes=[pltpu.VMEM((rows, query.shape[1]), jnp.bfloat16)],
        compiler_params=pltpu.CompilerParams(vmem_limit_bytes=GRANT),
        cost_estimate=pl.CostEstimate(
            flops=2 * rows * w.size, bytes_accessed=2 * w.size, transcendentals=0
        ),
    )(core, lengths, query, new_key, new_value, own_keys, own_values, w)


def norm_kernel(
    mine_ref, swapped_ref, residual_ref, gain_ref, router_ref, routes_ref, hidden_ref, payload_ref
):
    hidden = residual_ref[...].astype(jnp.float32) + (mine_ref[...] + swapped_ref[...])
    hidden_ref[...] = hidden
    rows, width = hidden.shape
    mean_square = jnp.sum(hidden * hidden, axis=-1, keepdims=True) * (1.0 / width)
    normed = (hidden * lax.rsqrt(mean_square + 1e-05) * gain_ref[...]).astype(jnp.bfloat16)
    payload_ref[:, :width] = normed
    rest = router_ref[...]
    experts = rest.shape[0]
    terms = []
    for _ in range(3):
        term = rest.astype(jnp.bfloat16).astype(jnp.float32)
        terms.append(term)
        rest = rest - term
    parts = lax.dot_general(
        jnp.concatenate(terms, axis=0).astype(jnp.bfloat16),
        normed,
        (((1,), (1,)), ((), ())),
        preferred_element_type=jnp.float32,
    )
    logits = parts[:experts] + parts[experts : 2 * experts] + parts[2 * experts :]
    number = lax.broadcasted_iota(jnp.int32, (experts, rows), 0)
    chosen = number == routes_ref[0:1, :]
    for k in range(1, routes_ref.shape[0]):
        chosen = chosen | (number == routes_ref[k : k + 1, :])
    squashed = jnp.where(chosen, 1.0 / (1.0 + jnp.exp(-logits)), 0.0)
    gates = squashed / jnp.sum(squashed, axis=0, keepdims=True)
    upper = gates.astype(jnp.bfloat16).astype(jnp.float32)
    both = jnp.concatenate([upper, gates - upper], axis=0).astype(jnp.bfloat16)
    tail = payload_ref.shape[1] - width
    place = lax.broadcasted_iota(jnp.int32, (2 * experts, tail), 0)
    lane = lax.broadcasted_iota(jnp.int32, (2 * experts, tail), 1)
    placed = lax.dot_general(
        both,
        (place == lane).astype(jnp.bfloat16),
        (((0,), (0,)), ((), ())),
        preferred_element_type=jnp.float32,
    )
    payload_ref[:, width:] = placed.astype(jnp.bfloat16)


def norm_route(mine, swapped, residual, norm_gain, router, routes):
    rows, width = residual.shape
    experts = router.shape[1]
    wide = -(-(width + 2 * experts) // 128) * 128
    return pl.pallas_call(
        norm_kernel,
        out_shape=(
            jax.ShapeDtypeStruct((rows, width), jnp.float32),
            jax.ShapeDtypeStruct((rows, wide), jnp.bfloat16),
        ),
        compiler_params=pltpu.CompilerParams(vmem_limit_bytes=GRANT),
    )(mine, swapped, residual, norm_gain[None, :], router.T, routes.T)


def expert_kernel(count, experts, chip_ref, *refs):
    blocks, refs = refs[:count], refs[count:]
    gate_ref, up_ref, down_ref = refs[:3]
    outs, act_ref = refs[3:-1], refs[-1]
    _, hidden, width = gate_ref.shape
    rows = jnp.concatenate([block[...] for block in blocks], axis=0)
    base = width // 128 * 128
    tail = rows[:, base:].astype(jnp.float32)
    lane = lax.broadcasted_iota(jnp.int32, tail.shape, 1) - (width - base)
    named = (lane == chip_ref[0]) | (lane == chip_ref[0] + experts)
    weight = jnp.sum(jnp.where(named, tail, 0.0), axis=-1, keepdims=True)
    turned = rows[:, :width].T
    gate = jnp.dot(gate_ref[0], turned, preferred_element_type=jnp.float32)
    up = jnp.dot(up_ref[0], turned, preferred_element_type=jnp.float32)
    act_ref[...] = (gate / (1.0 + jnp.exp(-gate)) * up).T.astype(jnp.bfloat16)
    for at in range(0, width, 768):
        span = slice(at, min(at + 768, width))
        part = jnp.dot(act_ref[...], down_ref[0, :, span], preferred_element_type=jnp.float32)
        part = (part * weight).astype(jnp.bfloat16)
        first = 0
        for out in outs:
            out[:, span] = part[first : first + out.shape[0]]
            first += out.shape[0]


def run_expert(chip, blocks, gate_t, up_t, down, experts, cost):
    _, hidden, width = down.shape
    rows = sum(block.shape[0] for block in blocks)
    count = len(blocks)
    vmem = pl.BlockSpec(memory_space=pltpu.VMEM)
    return pl.pallas_call(
        lambda *refs: expert_kernel(count, experts, *refs),
        out_shape=[jax.ShapeDtypeStruct((b.shape[0], width), jnp.bfloat16) for b in blocks],
        in_specs=[pl.BlockSpec(memory_space=pltpu.SMEM)] + [vmem] * (count + 3),
        out_specs=[vmem] * count,
        scratch_shapes=[pltpu.VMEM((rows, hidden), jnp.bfloat16)],
        compiler_params=pltpu.CompilerParams(vmem_limit_bytes=GRANT),
        cost_estimate=pl.CostEstimate(
            flops=6 * cost * rows * hidden * width,
            bytes_accessed=6 * cost * hidden * width,
            transcendentals=0,
        ),
    )(chip, *blocks, gate_t, up_t, down)


def add_kernel(*refs):
    total = refs[0][...].astype(jnp.float32)
    for ref in refs[1:-1]:
        total = total + ref[...].astype(jnp.float32)
    refs[-1][...] = total.astype(refs[-1].dtype)


def add_all(*terms, dtype=jnp.bfloat16):
    return pl.pallas_call(
        add_kernel,
        out_shape=jax.ShapeDtypeStruct(terms[0].shape, dtype),
        compiler_params=pltpu.CompilerParams(vmem_limit_bytes=GRANT),
    )(*terms)


def ring_pairs(chips, cores, cross):
    order = list(range(0, chips, 2)) + list(range(1, chips, 2))[::-1]
    pairs = []
    for p in range(chips):
        for core in range(cores):
            turn = -1 if core % 2 else 1
            to = core ^ 1 if cross else core
            pairs.append((order[p] * cores + core, order[(p + turn) % chips] * cores + to))
    return pairs


def per_device(
    query,
    new_key,
    new_value,
    cache_keys,
    cache_values,
    lengths,
    out_proj,
    residual,
    norm_gain,
    router,
    routes,
    w_gate,
    w_up,
    w_down,
):
    chips, cores = lax.axis_size("att"), lax.axis_size("exp")
    own_rows = residual.shape[0]
    ring = ("att", "exp")

    def send(x, cross=False):
        return lax.ppermute(x, ring, ring_pairs(chips, cores, cross))

    def swap(x):
        return lax.ppermute(x, "exp", [(0, 1), (1, 0)])

    core = jnp.full((1,), lax.axis_index("exp"), jnp.int32)
    chip = jnp.full((1,), lax.axis_index("att"), jnp.int32)
    small = (core, own_rows, lengths, query, new_key, new_value)
    theirs, w_out, own_keys, own_values = attend_theirs(
        *small, cache_keys, cache_values, out_proj.T, chip
    )
    swapped = swap(theirs)
    mine = attend_mine(*small, own_keys, own_values, w_out)
    hidden_state, payload = norm_route(mine, swapped, residual, norm_gain, router, routes)

    experts = router.shape[1]

    far = chips // 2

    def after(value, *earlier):
        return lax.optimization_barrier((value, earlier))[0]

    gate_t, up_t = w_gate.transpose(0, 2, 1), w_up.transpose(0, 2, 1)

    def expert(blocks, cost=5):
        return run_expert(chip, blocks, gate_t, up_t, w_down, experts, cost)

    x, y = payload, swap(payload)
    done = expert((x, y), cost=1)
    own, own_other = done[0], swap(done[1])
    sums_x, sums_y = [None], [None]
    swapped_y = None
    for k in range(1, far + 1):
        x = send(x)
        if k in (1, far):
            x = after(x, done[0])
        blocks = [x, swap(x)]
        if k > 1:
            blocks += swapped_y
        if k < far:
            y = send(y)
            if k > 1:
                y = after(y, done[0])
            swapped_y = [y, swap(y)]
        if 2 < k < far:
            blocks[1] = after(blocks[1], sums_x[k - 2][1], *([sums_y[k - 2][1]] if k > 3 else []))
        done = expert(blocks)
        sums_x.append((done[1], swap(done[0])))
        if k > 1:
            sums_y.append((done[3], swap(done[2])))

    held = add_all(hidden_state, own, own_other, dtype=jnp.float32)
    back_x, back_y = [], []
    for k in range(far, 0, -1):
        if k < far:
            back_y = [send(add_all(*sums_y[k], *back_y))]
        back_x = [send(add_all(*sums_x[k], *back_x), k == 1)]
    return add_all(held, *back_x, *back_y)


def solution(mesh):
    in_specs = (
        P(("groups", "att"), "exp"),
        P(("groups", "att"), "exp"),
        P(("groups", "att"), "exp"),
        P(("groups", "att"), None, "exp"),
        P(("groups", "att"), None, "exp"),
        P(("groups", "att")),
        P("exp", None),
        P(("groups", "att", "exp"), None),
        P(),
        P(),
        P(("groups", "att", "exp"), None),
        P("att", None, "exp"),
        P("att", None, "exp"),
        P("att", "exp", None),
    )
    out_specs = P(("groups", "att", "exp"), None)
    return jax.shard_map(
        per_device, mesh=mesh, in_specs=in_specs, out_specs=out_specs, check_vma=False
    )
```

```python
import math

import jax
import jax.numpy as jnp
from jax import lax
from jax.experimental import pallas as pl
from jax.experimental.pallas import tpu as pltpu
from jax.sharding import PartitionSpec as P

HEAD = 64
SUB = 8
STEP = 16
GRANT = 12 * 1024 * 1024
ACROSS = (((1,), (1,)), ((), ()))


def place_heads(queries, heads, slots, width):
    group_size = heads // slots
    slot_of_lane = lax.broadcasted_iota(jnp.int32, (SUB, width), 1) // HEAD
    pieces = []
    for head in range(heads):
        block, slot, home = head // slots, head % slots, head // group_size
        piece = queries[:, block * width : (block + 1) * width]
        if slot != home:
            piece = pltpu.roll(piece, ((home - slot) * HEAD) % width, 1)
        pieces.append(jnp.where(slot_of_lane == home, piece, 0.0))
    return jnp.concatenate(pieces, axis=0).astype(jnp.bfloat16)


def score(rows, keys, fresh_k, cache_len):
    request = lax.broadcasted_iota(jnp.int32, (cache_len, rows.shape[0]), 1) % SUB
    spread = lax.dot_general(keys, rows, ACROSS, preferred_element_type=jnp.float32)
    scores = spread[:cache_len]
    for r in range(1, SUB):
        scores = jnp.where(request == r, spread[r * cache_len : (r + 1) * cache_len], scores)
    return scores, lax.dot_general(fresh_k, rows, ACROSS, preferred_element_type=jnp.float32)


def soften(scores, fresh, live, offset, per):
    cache_len, count = scores.shape
    request = lax.broadcasted_iota(jnp.int32, (cache_len, count), 1) % SUB
    place = lax.broadcasted_iota(jnp.int32, (cache_len, count), 0)
    scores = jnp.where(place < live, scores, -1e30)
    fresh_place = lax.broadcasted_iota(jnp.int32, fresh.shape, 0)
    fresh_own = fresh_place == offset + lax.broadcasted_iota(jnp.int32, fresh.shape, 1) % SUB
    fresh_scores = jnp.sum(jnp.where(fresh_own, fresh, 0.0), axis=0, keepdims=True)
    highest = jnp.maximum(jnp.max(scores, axis=0, keepdims=True), fresh_scores)
    cached_exp = jnp.exp(scores - highest)
    fresh_exp = jnp.exp(fresh_scores - highest)
    scale = 1.0 / (jnp.sum(cached_exp, axis=0, keepdims=True) + fresh_exp)
    probs = cached_exp * scale
    fresh_probs = jnp.where(fresh_own, fresh_exp * scale, 0.0)
    return jnp.concatenate(
        [jnp.where(request % per == i, probs, 0.0) for i in range(per)] + [fresh_probs], axis=0
    ).T


def weigh(turned, values, fresh_v, per):
    count, width = turned.shape[0], values.shape[1]
    group = lax.broadcasted_iota(jnp.int32, (count, width), 0) % SUB // per
    wide = jnp.concatenate(
        [jnp.where(group == part, turned[:, :width], 0.0) for part in range(SUB // per)], axis=1
    ).astype(jnp.bfloat16)
    output = jnp.dot(wide, values, preferred_element_type=jnp.float32)
    return output + jnp.dot(
        turned[:, width:].astype(jnp.bfloat16), fresh_v, preferred_element_type=jnp.float32
    )


def gather_heads(output, heads, slots, width):
    group_size = heads // slots
    slot_of_lane = lax.broadcasted_iota(jnp.int32, (SUB, width), 1) // HEAD
    blocks = []
    for block in range(heads // slots):
        merged = None
        for slot in range(slots):
            head = block * slots + slot
            home = head // group_size
            piece = output[head * SUB : (head + 1) * SUB]
            if slot != home:
                piece = pltpu.roll(piece, ((slot - home) * HEAD) % width, 1)
            merged = piece if merged is None else jnp.where(slot_of_lane == slot, piece, merged)
        blocks.append(merged)
    return jnp.concatenate(blocks, axis=-1)


def attend(first, lengths_ref, q_ref, nk_ref, nv_ref, k_ref, v_ref, att_ref, ready):
    width = nk_ref.shape[1]
    slots = width // HEAD
    heads = q_ref.shape[1] // HEAD
    cache_len = k_ref.shape[1]
    per = width // cache_len
    request = lax.broadcasted_iota(jnp.int32, (1, heads * SUB), 1) % SUB
    batches = range(0, att_ref.shape[0], SUB)
    scores = []
    for at in batches:
        step = at // STEP * STEP
        if at == step:
            ready(at)
            queries = q_ref[step : step + STEP].astype(jnp.float32) * (1.0 / math.sqrt(HEAD))
        rows = place_heads(queries[at - step : at - step + SUB], heads, slots, width)
        keys = k_ref[at : at + SUB].reshape(SUB * cache_len, width)
        scores.append(score(rows, keys, nk_ref[step : step + STEP], cache_len))
    turned = []
    for at, (cached, fresh) in zip(batches, scores):
        live = jnp.zeros(request.shape, jnp.int32)
        for i in range(SUB):
            live = jnp.where(request == i, lengths_ref[first + at + i], live)
        turned.append(soften(cached, fresh, live, at % STEP, per))
    outputs = []
    for at, probs in zip(batches, turned):
        step = at // STEP * STEP
        values = v_ref[at : at + SUB].reshape(SUB * cache_len, width)
        outputs.append(weigh(probs, values, nv_ref[step : step + STEP], per))
    for step in range(0, att_ref.shape[0], STEP):
        pair = outputs[step // SUB : (step + STEP) // SUB]
        att_ref[step : step + STEP, :] = jnp.concatenate(
            [gather_heads(output, heads, slots, width) for output in pair], axis=0
        ).astype(jnp.bfloat16)


def project(att_ref, w_ref, out_ref):
    turned = lax.dot_general(
        w_ref[...], att_ref[...], ACROSS, preferred_element_type=jnp.float32
    )
    out_ref[...] = turned.T


def first_kernel(
    core_ref, chip_ref, lengths_hbm, q_hbm, nk_hbm, nv_hbm, k_hbm, v_hbm, w_hbm,
    out_ref, w_ref, own_k, own_v, lengths_ref, q_ref, nk_ref, nv_ref, k_ref, v_ref, att_ref, sems,
):
    rows = out_ref.shape[0]
    theirs = pl.multiple_of((1 - core_ref[0]) * rows, rows)
    mine = pl.multiple_of(core_ref[0] * rows, rows)
    copies = []

    def bring(source, target):
        copy = pltpu.make_async_copy(source, target, sems.at[len(copies)])
        copy.start()
        copies.append(copy)
        return copy

    small = [bring(lengths_hbm, lengths_ref)] + [
        bring(source.at[pl.ds(theirs, rows)], target)
        for source, target in ((q_hbm, q_ref), (nk_hbm, nk_ref), (nv_hbm, nv_ref))
    ]
    cache = []
    for at in range(0, rows, STEP):
        span = pl.ds(theirs + at, STEP)
        cache.append(
            (
                bring(k_hbm.at[span], k_ref.at[pl.ds(at, STEP)]),
                bring(v_hbm.at[span], v_ref.at[pl.ds(at, STEP)]),
            )
        )
    pieces = 4
    columns = w_ref.shape[0]
    size = -(-columns // pieces // 16) * 16
    weights = []
    for at in range(0, columns, size):
        span = pl.ds(at, min(size, columns - at))
        weights.append(bring(w_hbm.at[span], w_ref.at[span]))
    later = [
        bring(k_hbm.at[pl.ds(mine, rows)], own_k),
        bring(v_hbm.at[pl.ds(mine, rows)], own_v),
    ]
    for copy in small:
        copy.wait()

    def ready(at):
        for copy in cache[at // STEP]:
            copy.wait()

    attend(theirs, lengths_ref, q_ref, nk_ref, nv_ref, k_ref, v_ref, att_ref, ready)
    for copy in weights:
        copy.wait()
    project(att_ref, w_ref, out_ref)
    for copy in later:
        copy.wait()


def second_kernel(
    core_ref, lengths_ref, q_ref, nk_ref, nv_ref, k_ref, v_ref, w_ref, out_ref, att_ref
):
    rows = out_ref.shape[0]
    mine = pl.multiple_of(core_ref[0] * rows, rows)
    own = [ref.at[pl.ds(mine, rows)] for ref in (q_ref, nk_ref, nv_ref)]
    attend(mine, lengths_ref, *own, k_ref, v_ref, att_ref, lambda at: None)
    project(att_ref, w_ref, out_ref)


def attend_theirs(
    core, rows, lengths, query, new_key, new_value, cache_keys, cache_values, w, chip
):
    cache = (rows,) + cache_keys.shape[1:]
    columns = w.shape[0]
    smem = pl.BlockSpec(memory_space=pltpu.SMEM)
    vmem = pl.BlockSpec(memory_space=pltpu.VMEM)
    hbm = pl.BlockSpec(memory_space=pltpu.HBM)
    copies = 4 + 2 * (rows // STEP) + 4 + 2
    return pl.pallas_call(
        first_kernel,
        out_shape=(
            jax.ShapeDtypeStruct((rows, columns), jnp.float32),
            jax.ShapeDtypeStruct(w.shape, jnp.bfloat16),
            jax.ShapeDtypeStruct(cache, jnp.bfloat16),
            jax.ShapeDtypeStruct(cache, jnp.bfloat16),
        ),
        in_specs=[smem] * 2 + [hbm] * 7,
        out_specs=[vmem] * 4,
        scratch_shapes=[
            pltpu.SMEM(lengths.shape, jnp.int32),
            pltpu.VMEM((rows, query.shape[1]), jnp.bfloat16),
            pltpu.VMEM((rows, new_key.shape[1]), jnp.bfloat16),
            pltpu.VMEM((rows, new_key.shape[1]), jnp.bfloat16),
            pltpu.VMEM(cache, jnp.bfloat16),
            pltpu.VMEM(cache, jnp.bfloat16),
            pltpu.VMEM((rows, query.shape[1]), jnp.bfloat16),
            pltpu.SemaphoreType.DMA((copies,)),
        ],
        compiler_params=pltpu.CompilerParams(vmem_limit_bytes=GRANT),
        cost_estimate=pl.CostEstimate(
            flops=2 * rows * w.size, bytes_accessed=2 * w.size, transcendentals=0
        ),
    )(
        core,
        chip,
        *(
            pltpu.with_memory_space_constraint(x, pltpu.HBM)
            for x in (lengths, query, new_key, new_value, cache_keys, cache_values, w)
        ),
    )


def attend_mine(core, rows, lengths, query, new_key, new_value, own_keys, own_values, w):
    smem = pl.BlockSpec(memory_space=pltpu.SMEM)
    vmem = pl.BlockSpec(memory_space=pltpu.VMEM)
    return pl.pallas_call(
        second_kernel,
        out_shape=jax.ShapeDtypeStruct((rows, w.shape[0]), jnp.float32),
        in_specs=[smem, smem] + [vmem] * 6,
        out_specs=vmem,
        scratch_shapes=[pltpu.VMEM((rows, query.shape[1]), jnp.bfloat16)],
        compiler_params=pltpu.CompilerParams(vmem_limit_bytes=GRANT),
        cost_estimate=pl.CostEstimate(
            flops=2 * rows * w.size, bytes_accessed=2 * w.size, transcendentals=0
        ),
    )(core, lengths, query, new_key, new_value, own_keys, own_values, w)


def norm_kernel(
    mine_ref, swapped_ref, residual_ref, gain_ref, router_ref, routes_ref, hidden_ref, payload_ref
):
    hidden = residual_ref[...].astype(jnp.float32) + (mine_ref[...] + swapped_ref[...])
    hidden_ref[...] = hidden
    rows, width = hidden.shape
    mean_square = jnp.sum(hidden * hidden, axis=-1, keepdims=True) * (1.0 / width)
    normed = (hidden * lax.rsqrt(mean_square + 1e-05) * gain_ref[...]).astype(jnp.bfloat16)
    payload_ref[:, :width] = normed
    rest = router_ref[...]
    experts = rest.shape[0]
    terms = []
    for _ in range(3):
        term = rest.astype(jnp.bfloat16).astype(jnp.float32)
        terms.append(term)
        rest = rest - term
    parts = lax.dot_general(
        jnp.concatenate(terms, axis=0).astype(jnp.bfloat16),
        normed,
        (((1,), (1,)), ((), ())),
        preferred_element_type=jnp.float32,
    )
    logits = parts[:experts] + parts[experts : 2 * experts] + parts[2 * experts :]
    number = lax.broadcasted_iota(jnp.int32, (experts, rows), 0)
    chosen = number == routes_ref[0:1, :]
    for k in range(1, routes_ref.shape[0]):
        chosen = chosen | (number == routes_ref[k : k + 1, :])
    squashed = jnp.where(chosen, 1.0 / (1.0 + jnp.exp(-logits)), 0.0)
    gates = squashed / jnp.sum(squashed, axis=0, keepdims=True)
    upper = gates.astype(jnp.bfloat16).astype(jnp.float32)
    both = jnp.concatenate([upper, gates - upper], axis=0).astype(jnp.bfloat16)
    tail = payload_ref.shape[1] - width
    place = lax.broadcasted_iota(jnp.int32, (2 * experts, tail), 0)
    lane = lax.broadcasted_iota(jnp.int32, (2 * experts, tail), 1)
    placed = lax.dot_general(
        both,
        (place == lane).astype(jnp.bfloat16),
        (((0,), (0,)), ((), ())),
        preferred_element_type=jnp.float32,
    )
    payload_ref[:, width:] = placed.astype(jnp.bfloat16)


def norm_route(mine, swapped, residual, norm_gain, router, routes):
    rows, width = residual.shape
    experts = router.shape[1]
    wide = -(-(width + 2 * experts) // 128) * 128
    return pl.pallas_call(
        norm_kernel,
        out_shape=(
            jax.ShapeDtypeStruct((rows, width), jnp.float32),
            jax.ShapeDtypeStruct((rows, wide), jnp.bfloat16),
        ),
        compiler_params=pltpu.CompilerParams(vmem_limit_bytes=GRANT),
    )(mine, swapped, residual, norm_gain[None, :], router.T, routes.T)


def expert_kernel(count, experts, chip_ref, *refs):
    blocks, refs = refs[:count], refs[count:]
    gate_ref, up_ref, down_ref = refs[:3]
    outs, act_ref = refs[3:-1], refs[-1]
    _, hidden, width = gate_ref.shape
    rows = jnp.concatenate([block[...] for block in blocks], axis=0)
    base = width // 128 * 128
    tail = rows[:, base:].astype(jnp.float32)
    lane = lax.broadcasted_iota(jnp.int32, tail.shape, 1) - (width - base)
    named = (lane == chip_ref[0]) | (lane == chip_ref[0] + experts)
    weight = jnp.sum(jnp.where(named, tail, 0.0), axis=-1, keepdims=True)
    inputs = rows[:, :width]
    gate = lax.dot_general(gate_ref[0], inputs, ACROSS, preferred_element_type=jnp.float32)
    up = lax.dot_general(up_ref[0], inputs, ACROSS, preferred_element_type=jnp.float32)
    act_ref[...] = (gate / (1.0 + jnp.exp(-gate)) * up).T.astype(jnp.bfloat16)
    for at in range(0, width, 768):
        span = slice(at, min(at + 768, width))
        part = jnp.dot(act_ref[...], down_ref[0, :, span], preferred_element_type=jnp.float32)
        part = (part * weight).astype(jnp.bfloat16)
        first = 0
        for out in outs:
            out[:, span] = part[first : first + out.shape[0]]
            first += out.shape[0]


def run_expert(chip, blocks, gate_t, up_t, down, experts, cost):
    _, hidden, width = down.shape
    rows = sum(block.shape[0] for block in blocks)
    count = len(blocks)
    vmem = pl.BlockSpec(memory_space=pltpu.VMEM)
    return pl.pallas_call(
        lambda *refs: expert_kernel(count, experts, *refs),
        out_shape=[jax.ShapeDtypeStruct((b.shape[0], width), jnp.bfloat16) for b in blocks],
        in_specs=[pl.BlockSpec(memory_space=pltpu.SMEM)] + [vmem] * (count + 3),
        out_specs=[vmem] * count,
        scratch_shapes=[pltpu.VMEM((rows, hidden), jnp.bfloat16)],
        compiler_params=pltpu.CompilerParams(vmem_limit_bytes=GRANT),
        cost_estimate=pl.CostEstimate(
            flops=6 * cost * rows * hidden * width,
            bytes_accessed=6 * cost * hidden * width,
            transcendentals=0,
        ),
    )(chip, *blocks, gate_t, up_t, down)


def add_kernel(*refs):
    total = refs[0][...].astype(jnp.float32)
    for ref in refs[1:-1]:
        total = total + ref[...].astype(jnp.float32)
    refs[-1][...] = total.astype(refs[-1].dtype)


def add_all(*terms, dtype=jnp.bfloat16):
    return pl.pallas_call(
        add_kernel,
        out_shape=jax.ShapeDtypeStruct(terms[0].shape, dtype),
        compiler_params=pltpu.CompilerParams(vmem_limit_bytes=GRANT),
    )(*terms)


def ring_pairs(chips, cores, cross):
    order = list(range(0, chips, 2)) + list(range(1, chips, 2))[::-1]
    pairs = []
    for p in range(chips):
        for core in range(cores):
            turn = -1 if core % 2 else 1
            to = core ^ 1 if cross else core
            pairs.append((order[p] * cores + core, order[(p + turn) % chips] * cores + to))
    return pairs


def per_device(
    query,
    new_key,
    new_value,
    cache_keys,
    cache_values,
    lengths,
    out_proj,
    residual,
    norm_gain,
    router,
    routes,
    w_gate,
    w_up,
    w_down,
):
    chips, cores = lax.axis_size("att"), lax.axis_size("exp")
    own_rows = residual.shape[0]
    ring = ("att", "exp")

    def send(x, cross=False):
        return lax.ppermute(x, ring, ring_pairs(chips, cores, cross))

    def swap(x):
        return lax.ppermute(x, "exp", [(0, 1), (1, 0)])

    core = jnp.full((1,), lax.axis_index("exp"), jnp.int32)
    chip = jnp.full((1,), lax.axis_index("att"), jnp.int32)
    small = (core, own_rows, lengths, query, new_key, new_value)
    theirs, w_out, own_keys, own_values = attend_theirs(
        *small, cache_keys, cache_values, out_proj.T, chip
    )
    swapped = swap(theirs)
    mine = attend_mine(*small, own_keys, own_values, w_out)
    hidden_state, payload = norm_route(mine, swapped, residual, norm_gain, router, routes)

    experts = router.shape[1]

    far = chips // 2

    def after(value, *earlier):
        return lax.optimization_barrier((value, earlier))[0]

    gate_t, up_t = w_gate.transpose(0, 2, 1), w_up.transpose(0, 2, 1)

    def expert(blocks, cost=5):
        return run_expert(chip, blocks, gate_t, up_t, w_down, experts, cost)

    x, y = payload, swap(payload)
    done = expert((x, y), cost=1)
    own, own_other = done[0], swap(done[1])
    sums_x, sums_y = [None], [None]
    swapped_y = None
    for k in range(1, far + 1):
        x = send(x)
        if k in (1, far):
            x = after(x, done[0])
        blocks = [x, swap(x)]
        if k > 1:
            blocks += swapped_y
        if k < far:
            y = send(y)
            if k > 1:
                y = after(y, done[0])
            swapped_y = [y, swap(y)]
        if 2 < k < far:
            blocks[1] = after(blocks[1], sums_x[k - 2][1], *([sums_y[k - 2][1]] if k > 3 else []))
        done = expert(blocks)
        sums_x.append((done[1], swap(done[0])))
        if k > 1:
            sums_y.append((done[3], swap(done[2])))

    held = add_all(hidden_state, own, own_other, dtype=jnp.float32)
    back_x, back_y = [], []
    for k in range(far, 0, -1):
        if k < far:
            back_y = [send(add_all(*sums_y[k], *back_y))]
        back_x = [send(add_all(*sums_x[k], *back_x), k == 1)]
    return add_all(held, *back_x, *back_y)


def solution(mesh):
    in_specs = (
        P(("groups", "att"), "exp"),
        P(("groups", "att"), "exp"),
        P(("groups", "att"), "exp"),
        P(("groups", "att"), None, "exp"),
        P(("groups", "att"), None, "exp"),
        P(("groups", "att")),
        P("exp", None),
        P(("groups", "att", "exp"), None),
        P(),
        P(),
        P(("groups", "att", "exp"), None),
        P("att", None, "exp"),
        P("att", None, "exp"),
        P("att", "exp", None),
    )
    out_specs = P(("groups", "att", "exp"), None)
    return jax.shard_map(
        per_device, mesh=mesh, in_specs=in_specs, out_specs=out_specs, check_vma=False
    )
```

```python
import math

import jax
import jax.numpy as jnp
from jax import lax
from jax.experimental import pallas as pl
from jax.experimental.pallas import tpu as pltpu
from jax.sharding import PartitionSpec as P

HEAD = 64
SUB = 8
STEP = 16
GRANT = 12 * 1024 * 1024
ACROSS = (((1,), (1,)), ((), ()))


def place_heads(queries, heads, slots, width):
    group_size = heads // slots
    slot_of_lane = lax.broadcasted_iota(jnp.int32, (SUB, width), 1) // HEAD
    pieces = []
    for head in range(heads):
        block, slot, home = head // slots, head % slots, head // group_size
        piece = queries[:, block * width : (block + 1) * width]
        if slot != home:
            piece = pltpu.roll(piece, ((home - slot) * HEAD) % width, 1)
        pieces.append(jnp.where(slot_of_lane == home, piece, 0.0))
    return jnp.concatenate(pieces, axis=0).astype(jnp.bfloat16)


def score(rows, keys, fresh_k, cache_len):
    request = lax.broadcasted_iota(jnp.int32, (cache_len, rows.shape[0]), 1) % SUB
    spread = lax.dot_general(keys, rows, ACROSS, preferred_element_type=jnp.float32)
    scores = spread[:cache_len]
    for r in range(1, SUB):
        scores = jnp.where(request == r, spread[r * cache_len : (r + 1) * cache_len], scores)
    return scores, lax.dot_general(fresh_k, rows, ACROSS, preferred_element_type=jnp.float32)


def soften(scores, fresh, live, offset, per):
    cache_len, count = scores.shape
    request = lax.broadcasted_iota(jnp.int32, (cache_len, count), 1) % SUB
    place = lax.broadcasted_iota(jnp.int32, (cache_len, count), 0)
    scores = jnp.where(place < live, scores, -1e30)
    fresh_place = lax.broadcasted_iota(jnp.int32, fresh.shape, 0)
    fresh_own = fresh_place == offset + lax.broadcasted_iota(jnp.int32, fresh.shape, 1) % SUB
    fresh_scores = jnp.sum(jnp.where(fresh_own, fresh, 0.0), axis=0, keepdims=True)
    highest = jnp.maximum(jnp.max(scores, axis=0, keepdims=True), fresh_scores)
    cached_exp = jnp.exp(scores - highest)
    fresh_exp = jnp.exp(fresh_scores - highest)
    scale = 1.0 / (jnp.sum(cached_exp, axis=0, keepdims=True) + fresh_exp)
    probs = cached_exp * scale
    fresh_probs = jnp.where(fresh_own, fresh_exp * scale, 0.0)
    return jnp.concatenate(
        [jnp.where(request % per == i, probs, 0.0) for i in range(per)] + [fresh_probs], axis=0
    ).T


def weigh(turned, values, fresh_v, per):
    count, width = turned.shape[0], values.shape[1]
    group = lax.broadcasted_iota(jnp.int32, (count, width), 0) % SUB // per
    wide = jnp.concatenate(
        [jnp.where(group == part, turned[:, :width], 0.0) for part in range(SUB // per)], axis=1
    ).astype(jnp.bfloat16)
    output = jnp.dot(wide, values, preferred_element_type=jnp.float32)
    return output + jnp.dot(
        turned[:, width:].astype(jnp.bfloat16), fresh_v, preferred_element_type=jnp.float32
    )


def gather_heads(output, heads, slots, width):
    group_size = heads // slots
    slot_of_lane = lax.broadcasted_iota(jnp.int32, (SUB, width), 1) // HEAD
    blocks = []
    for block in range(heads // slots):
        merged = None
        for slot in range(slots):
            head = block * slots + slot
            home = head // group_size
            piece = output[head * SUB : (head + 1) * SUB]
            if slot != home:
                piece = pltpu.roll(piece, ((slot - home) * HEAD) % width, 1)
            merged = piece if merged is None else jnp.where(slot_of_lane == slot, piece, merged)
        blocks.append(merged)
    return jnp.concatenate(blocks, axis=-1)


def attend(first, lengths_ref, q_ref, nk_ref, nv_ref, k_ref, v_ref, att_ref, ready):
    width = nk_ref.shape[1]
    slots = width // HEAD
    heads = q_ref.shape[1] // HEAD
    cache_len = k_ref.shape[1]
    per = width // cache_len
    request = lax.broadcasted_iota(jnp.int32, (1, heads * SUB), 1) % SUB
    batches = range(0, att_ref.shape[0], SUB)
    scores = []
    for at in batches:
        step = at // STEP * STEP
        if at == step:
            ready(at)
            queries = q_ref[step : step + STEP].astype(jnp.float32) * (1.0 / math.sqrt(HEAD))
        rows = place_heads(queries[at - step : at - step + SUB], heads, slots, width)
        keys = k_ref[at : at + SUB].reshape(SUB * cache_len, width)
        scores.append(score(rows, keys, nk_ref[step : step + STEP], cache_len))
    turned = []
    for at, (cached, fresh) in zip(batches, scores):
        live = jnp.zeros(request.shape, jnp.int32)
        for i in range(SUB):
            live = jnp.where(request == i, lengths_ref[first + at + i], live)
        turned.append(soften(cached, fresh, live, at % STEP, per))
    outputs = []
    for at, probs in zip(batches, turned):
        step = at // STEP * STEP
        values = v_ref[at : at + SUB].reshape(SUB * cache_len, width)
        outputs.append(weigh(probs, values, nv_ref[step : step + STEP], per))
    for step in range(0, att_ref.shape[0], STEP):
        pair = outputs[step // SUB : (step + STEP) // SUB]
        att_ref[step : step + STEP, :] = jnp.concatenate(
            [gather_heads(output, heads, slots, width) for output in pair], axis=0
        ).astype(jnp.bfloat16)


def project(att_ref, w_ref, out_ref):
    turned = lax.dot_general(
        w_ref[...], att_ref[...], ACROSS, preferred_element_type=jnp.float32
    )
    out_ref[...] = turned.T


def first_kernel(
    core_ref, chip_ref, lengths_hbm, q_hbm, nk_hbm, nv_hbm, k_hbm, v_hbm, w_hbm,
    out_ref, w_ref, own_k, own_v, lengths_ref, q_ref, nk_ref, nv_ref, k_ref, v_ref, att_ref, sems,
):
    rows = out_ref.shape[0]
    theirs = pl.multiple_of((1 - core_ref[0]) * rows, rows)
    mine = pl.multiple_of(core_ref[0] * rows, rows)
    copies = []

    def bring(source, target):
        copy = pltpu.make_async_copy(source, target, sems.at[len(copies)])
        copy.start()
        copies.append(copy)
        return copy

    small = [bring(lengths_hbm, lengths_ref)] + [
        bring(source.at[pl.ds(theirs, rows)], target)
        for source, target in ((q_hbm, q_ref), (nk_hbm, nk_ref), (nv_hbm, nv_ref))
    ]
    cache = []
    for at in range(0, rows, STEP):
        span = pl.ds(theirs + at, STEP)
        cache.append(
            (
                bring(k_hbm.at[span], k_ref.at[pl.ds(at, STEP)]),
                bring(v_hbm.at[span], v_ref.at[pl.ds(at, STEP)]),
            )
        )
    pieces = 4
    columns = w_ref.shape[0]
    size = -(-columns // pieces // 16) * 16
    weights = []
    for at in range(0, columns, size):
        span = pl.ds(at, min(size, columns - at))
        weights.append(bring(w_hbm.at[span], w_ref.at[span]))
    later = [
        bring(k_hbm.at[pl.ds(mine, rows)], own_k),
        bring(v_hbm.at[pl.ds(mine, rows)], own_v),
    ]
    for copy in small:
        copy.wait()

    def ready(at):
        for copy in cache[at // STEP]:
            copy.wait()

    attend(theirs, lengths_ref, q_ref, nk_ref, nv_ref, k_ref, v_ref, att_ref, ready)
    for copy in weights:
        copy.wait()
    project(att_ref, w_ref, out_ref)
    for copy in later:
        copy.wait()


def second_kernel(
    core_ref, lengths_ref, q_ref, nk_ref, nv_ref, k_ref, v_ref, w_ref, out_ref, att_ref
):
    rows = out_ref.shape[0]
    mine = pl.multiple_of(core_ref[0] * rows, rows)
    own = [ref.at[pl.ds(mine, rows)] for ref in (q_ref, nk_ref, nv_ref)]
    attend(mine, lengths_ref, *own, k_ref, v_ref, att_ref, lambda at: None)
    project(att_ref, w_ref, out_ref)


def attend_theirs(
    core, rows, lengths, query, new_key, new_value, cache_keys, cache_values, w, chip
):
    cache = (rows,) + cache_keys.shape[1:]
    columns = w.shape[0]
    smem = pl.BlockSpec(memory_space=pltpu.SMEM)
    vmem = pl.BlockSpec(memory_space=pltpu.VMEM)
    hbm = pl.BlockSpec(memory_space=pltpu.HBM)
    copies = 4 + 2 * (rows // STEP) + 4 + 2
    return pl.pallas_call(
        first_kernel,
        out_shape=(
            jax.ShapeDtypeStruct((rows, columns), jnp.float32),
            jax.ShapeDtypeStruct(w.shape, jnp.bfloat16),
            jax.ShapeDtypeStruct(cache, jnp.bfloat16),
            jax.ShapeDtypeStruct(cache, jnp.bfloat16),
        ),
        in_specs=[smem] * 2 + [hbm] * 7,
        out_specs=[vmem] * 4,
        scratch_shapes=[
            pltpu.SMEM(lengths.shape, jnp.int32),
            pltpu.VMEM((rows, query.shape[1]), jnp.bfloat16),
            pltpu.VMEM((rows, new_key.shape[1]), jnp.bfloat16),
            pltpu.VMEM((rows, new_key.shape[1]), jnp.bfloat16),
            pltpu.VMEM(cache, jnp.bfloat16),
            pltpu.VMEM(cache, jnp.bfloat16),
            pltpu.VMEM((rows, query.shape[1]), jnp.bfloat16),
            pltpu.SemaphoreType.DMA((copies,)),
        ],
        compiler_params=pltpu.CompilerParams(vmem_limit_bytes=GRANT),
        cost_estimate=pl.CostEstimate(
            flops=2 * rows * w.size, bytes_accessed=2 * w.size, transcendentals=0
        ),
    )(
        core,
        chip,
        *(
            pltpu.with_memory_space_constraint(x, pltpu.HBM)
            for x in (lengths, query, new_key, new_value, cache_keys, cache_values, w)
        ),
    )


def attend_mine(core, rows, lengths, query, new_key, new_value, own_keys, own_values, w):
    smem = pl.BlockSpec(memory_space=pltpu.SMEM)
    vmem = pl.BlockSpec(memory_space=pltpu.VMEM)
    return pl.pallas_call(
        second_kernel,
        out_shape=jax.ShapeDtypeStruct((rows, w.shape[0]), jnp.float32),
        in_specs=[smem, smem] + [vmem] * 6,
        out_specs=vmem,
        scratch_shapes=[pltpu.VMEM((rows, query.shape[1]), jnp.bfloat16)],
        compiler_params=pltpu.CompilerParams(vmem_limit_bytes=GRANT),
        cost_estimate=pl.CostEstimate(
            flops=2 * rows * w.size, bytes_accessed=2 * w.size, transcendentals=0
        ),
    )(core, lengths, query, new_key, new_value, own_keys, own_values, w)


def norm_kernel(
    mine_ref, swapped_ref, residual_ref, gain_ref, router_ref, routes_ref, hidden_ref, payload_ref
):
    hidden = residual_ref[...].astype(jnp.float32) + (mine_ref[...] + swapped_ref[...])
    hidden_ref[...] = hidden
    rows, width = hidden.shape
    mean_square = jnp.sum(hidden * hidden, axis=-1, keepdims=True) * (1.0 / width)
    normed = (hidden * lax.rsqrt(mean_square + 1e-05) * gain_ref[...]).astype(jnp.bfloat16)
    payload_ref[:, :width] = normed
    rest = router_ref[...]
    experts = rest.shape[0]
    terms = []
    for _ in range(3):
        term = rest.astype(jnp.bfloat16).astype(jnp.float32)
        terms.append(term)
        rest = rest - term
    parts = lax.dot_general(
        jnp.concatenate(terms, axis=0).astype(jnp.bfloat16),
        normed,
        (((1,), (1,)), ((), ())),
        preferred_element_type=jnp.float32,
    )
    logits = parts[:experts] + parts[experts : 2 * experts] + parts[2 * experts :]
    number = lax.broadcasted_iota(jnp.int32, (experts, rows), 0)
    chosen = number == routes_ref[0:1, :]
    for k in range(1, routes_ref.shape[0]):
        chosen = chosen | (number == routes_ref[k : k + 1, :])
    squashed = jnp.where(chosen, 1.0 / (1.0 + jnp.exp(-logits)), 0.0)
    gates = squashed / jnp.sum(squashed, axis=0, keepdims=True)
    upper = gates.astype(jnp.bfloat16).astype(jnp.float32)
    both = jnp.concatenate([upper, gates - upper], axis=0).astype(jnp.bfloat16)
    tail = payload_ref.shape[1] - width
    place = lax.broadcasted_iota(jnp.int32, (2 * experts, tail), 0)
    lane = lax.broadcasted_iota(jnp.int32, (2 * experts, tail), 1)
    placed = lax.dot_general(
        both,
        (place == lane).astype(jnp.bfloat16),
        (((0,), (0,)), ((), ())),
        preferred_element_type=jnp.float32,
    )
    payload_ref[:, width:] = placed.astype(jnp.bfloat16)


def norm_route(mine, swapped, residual, norm_gain, router, routes):
    rows, width = residual.shape
    experts = router.shape[1]
    wide = -(-(width + 2 * experts) // 128) * 128
    return pl.pallas_call(
        norm_kernel,
        out_shape=(
            jax.ShapeDtypeStruct((rows, width), jnp.float32),
            jax.ShapeDtypeStruct((rows, wide), jnp.bfloat16),
        ),
        compiler_params=pltpu.CompilerParams(vmem_limit_bytes=GRANT),
    )(mine, swapped, residual, norm_gain[None, :], router.T, routes.T)


def expert_kernel(count, experts, chip_ref, *refs):
    blocks, refs = refs[:count], refs[count:]
    gate_ref, up_ref, down_ref = refs[:3]
    outs, act_ref = refs[3:-1], refs[-1]
    _, hidden, width = gate_ref.shape
    rows = jnp.concatenate([block[...] for block in blocks], axis=0)
    base = width // 128 * 128
    tail = rows[:, base:].astype(jnp.float32)
    lane = lax.broadcasted_iota(jnp.int32, tail.shape, 1) - (width - base)
    named = (lane == chip_ref[0]) | (lane == chip_ref[0] + experts)
    weight = jnp.sum(jnp.where(named, tail, 0.0), axis=-1, keepdims=True)
    turned = rows[:, :width].T
    gate = jnp.dot(gate_ref[0], turned, preferred_element_type=jnp.float32)
    up = jnp.dot(up_ref[0], turned, preferred_element_type=jnp.float32)
    act_ref[...] = (gate / (1.0 + jnp.exp(-gate)) * up).T.astype(jnp.bfloat16)
    for at in range(0, width, 768):
        span = slice(at, min(at + 768, width))
        part = jnp.dot(act_ref[...], down_ref[0, :, span], preferred_element_type=jnp.float32)
        part = (part * weight).astype(jnp.bfloat16)
        first = 0
        for out in outs:
            out[:, span] = part[first : first + out.shape[0]]
            first += out.shape[0]


def run_expert(chip, blocks, gate_t, up_t, down, experts, cost):
    _, hidden, width = down.shape
    rows = sum(block.shape[0] for block in blocks)
    count = len(blocks)
    vmem = pl.BlockSpec(memory_space=pltpu.VMEM)
    return pl.pallas_call(
        lambda *refs: expert_kernel(count, experts, *refs),
        out_shape=[jax.ShapeDtypeStruct((b.shape[0], width), jnp.bfloat16) for b in blocks],
        in_specs=[pl.BlockSpec(memory_space=pltpu.SMEM)] + [vmem] * (count + 3),
        out_specs=[vmem] * count,
        scratch_shapes=[pltpu.VMEM((rows, hidden), jnp.bfloat16)],
        compiler_params=pltpu.CompilerParams(vmem_limit_bytes=GRANT),
        cost_estimate=pl.CostEstimate(
            flops=6 * cost * rows * hidden * width,
            bytes_accessed=6 * cost * hidden * width,
            transcendentals=0,
        ),
    )(chip, *blocks, gate_t, up_t, down)


def add_kernel(firsts, *refs):
    size = refs[-1].shape[0]
    total = None
    for first, ref in zip(firsts, refs):
        term = ref[first : first + size].astype(jnp.float32)
        total = term if total is None else total + term
    refs[-1][...] = total.astype(refs[-1].dtype)


def add_rows(size, *parts, dtype=jnp.bfloat16):
    firsts = [first for _, first in parts]
    width = parts[0][0].shape[1]
    return pl.pallas_call(
        lambda *refs: add_kernel(firsts, *refs),
        out_shape=jax.ShapeDtypeStruct((size, width), dtype),
        compiler_params=pltpu.CompilerParams(vmem_limit_bytes=GRANT),
    )(*[array for array, _ in parts])


def add_all(*terms, dtype=jnp.bfloat16):
    return add_rows(terms[0].shape[0], *[(term, 0) for term in terms], dtype=dtype)


def finish_kernel(*refs):
    *whole, top, low, top_y, low_y, out = refs
    first = 0
    for half, half_y in ((top, top_y), (low, low_y)):
        size = half.shape[0]
        total = half[...].astype(jnp.float32) + half_y[...].astype(jnp.float32)
        for ref in whole:
            total = total + ref[first : first + size].astype(jnp.float32)
        out[first : first + size, :] = total.astype(out.dtype)
        first += size


def finish(*arrays):
    return pl.pallas_call(
        finish_kernel,
        out_shape=jax.ShapeDtypeStruct(arrays[0].shape, jnp.bfloat16),
        compiler_params=pltpu.CompilerParams(vmem_limit_bytes=GRANT),
    )(*arrays)


def ring_pairs(chips, cores, cross):
    order = list(range(0, chips, 2)) + list(range(1, chips, 2))[::-1]
    pairs = []
    for p in range(chips):
        for core in range(cores):
            turn = -1 if core % 2 else 1
            to = core ^ 1 if cross else core
            pairs.append((order[p] * cores + core, order[(p + turn) % chips] * cores + to))
    return pairs


def per_device(
    query,
    new_key,
    new_value,
    cache_keys,
    cache_values,
    lengths,
    out_proj,
    residual,
    norm_gain,
    router,
    routes,
    w_gate,
    w_up,
    w_down,
):
    chips, cores = lax.axis_size("att"), lax.axis_size("exp")
    own_rows = residual.shape[0]
    ring = ("att", "exp")

    def send(x, cross=False):
        return lax.ppermute(x, ring, ring_pairs(chips, cores, cross))

    def swap(x):
        return lax.ppermute(x, "exp", [(0, 1), (1, 0)])

    core = jnp.full((1,), lax.axis_index("exp"), jnp.int32)
    chip = jnp.full((1,), lax.axis_index("att"), jnp.int32)
    small = (core, own_rows, lengths, query, new_key, new_value)
    theirs, w_out, own_keys, own_values = attend_theirs(
        *small, cache_keys, cache_values, out_proj.T, chip
    )
    swapped = swap(theirs)
    mine = attend_mine(*small, own_keys, own_values, w_out)
    hidden_state, payload = norm_route(mine, swapped, residual, norm_gain, router, routes)

    experts = router.shape[1]

    far = chips // 2

    def after(value, *earlier):
        return lax.optimization_barrier((value, earlier))[0]

    gate_t, up_t = w_gate.transpose(0, 2, 1), w_up.transpose(0, 2, 1)

    def expert(blocks, cost=5):
        return run_expert(chip, blocks, gate_t, up_t, w_down, experts, cost)

    x, y = payload, swap(payload)
    done = expert((x, y), cost=1)
    own, own_other = done[0], swap(done[1])
    sums_x, sums_y = [None], [None]
    swapped_y = None
    for k in range(1, far + 1):
        x = send(x)
        if k in (1, far):
            x = after(x, done[0])
        blocks = [x, swap(x)]
        if k > 1:
            blocks += swapped_y
        if k < far:
            y = send(y)
            if k > 1:
                y = after(y, done[0])
            swapped_y = [y, swap(y)]
        if 2 < k < far:
            blocks[1] = after(blocks[1], sums_x[k - 2][1], *([sums_y[k - 2][1]] if k > 3 else []))
        done = expert(blocks)
        sums_x.append((done[1], swap(done[0])))
        if k > 1:
            sums_y.append((done[3], swap(done[2])))

    held = add_all(hidden_state, own, own_other, dtype=jnp.float32)
    middle = own_rows // 2
    back_x, back_y = [[], []], [[], []]
    for k in range(far, 0, -1):
        for half in (0, 1):
            mine_x = [(term, half * middle) for term in sums_x[k]] + back_x[half]
            back_x[half] = [(send(add_rows(middle, *mine_x), k == 1), 0)]
            if k < far:
                mine_y = [(term, half * middle) for term in sums_y[k]] + back_y[half]
                back_y[half] = [(send(add_rows(middle, *mine_y)), 0)]
    return finish(held, *[half[0][0] for half in back_x + back_y])


def solution(mesh):
    in_specs = (
        P(("groups", "att"), "exp"),
        P(("groups", "att"), "exp"),
        P(("groups", "att"), "exp"),
        P(("groups", "att"), None, "exp"),
        P(("groups", "att"), None, "exp"),
        P(("groups", "att")),
        P("exp", None),
        P(("groups", "att", "exp"), None),
        P(),
        P(),
        P(("groups", "att", "exp"), None),
        P("att", None, "exp"),
        P("att", None, "exp"),
        P("att", "exp", None),
    )
    out_specs = P(("groups", "att", "exp"), None)
    return jax.shard_map(
        per_device, mesh=mesh, in_specs=in_specs, out_specs=out_specs, check_vma=False
    )
```

```python
import math

import jax
import jax.numpy as jnp
from jax import lax
from jax.experimental import pallas as pl
from jax.experimental.pallas import tpu as pltpu
from jax.sharding import PartitionSpec as P

HEAD = 64
SUB = 8
STEP = 16
GRANT = 12 * 1024 * 1024
ACROSS = (((1,), (1,)), ((), ()))


def place_heads(queries, heads, slots, width):
    group_size = heads // slots
    slot_of_lane = lax.broadcasted_iota(jnp.int32, (SUB, width), 1) // HEAD
    pieces = []
    for head in range(heads):
        block, slot, home = head // slots, head % slots, head // group_size
        piece = queries[:, block * width : (block + 1) * width]
        if slot != home:
            piece = pltpu.roll(piece, ((home - slot) * HEAD) % width, 1)
        pieces.append(jnp.where(slot_of_lane == home, piece, 0.0))
    return jnp.concatenate(pieces, axis=0).astype(jnp.bfloat16)


def score(rows, keys, fresh_k, cache_len):
    request = lax.broadcasted_iota(jnp.int32, (cache_len, rows.shape[0]), 1) % SUB
    spread = lax.dot_general(keys, rows, ACROSS, preferred_element_type=jnp.float32)
    scores = spread[:cache_len]
    for r in range(1, SUB):
        scores = jnp.where(request == r, spread[r * cache_len : (r + 1) * cache_len], scores)
    return scores, lax.dot_general(fresh_k, rows, ACROSS, preferred_element_type=jnp.float32)


def soften(scores, fresh, live, offset, per):
    cache_len, count = scores.shape
    request = lax.broadcasted_iota(jnp.int32, (cache_len, count), 1) % SUB
    place = lax.broadcasted_iota(jnp.int32, (cache_len, count), 0)
    scores = jnp.where(place < live, scores, -1e30)
    fresh_place = lax.broadcasted_iota(jnp.int32, fresh.shape, 0)
    fresh_own = fresh_place == offset + lax.broadcasted_iota(jnp.int32, fresh.shape, 1) % SUB
    fresh_scores = jnp.sum(jnp.where(fresh_own, fresh, 0.0), axis=0, keepdims=True)
    highest = jnp.maximum(jnp.max(scores, axis=0, keepdims=True), fresh_scores)
    cached_exp = jnp.exp(scores - highest)
    fresh_exp = jnp.exp(fresh_scores - highest)
    scale = 1.0 / (jnp.sum(cached_exp, axis=0, keepdims=True) + fresh_exp)
    probs = cached_exp * scale
    fresh_probs = jnp.where(fresh_own, fresh_exp * scale, 0.0)
    return jnp.concatenate(
        [jnp.where(request % per == i, probs, 0.0) for i in range(per)] + [fresh_probs], axis=0
    ).T


def weigh(turned, values, fresh_v, per):
    count, width = turned.shape[0], values.shape[1]
    group = lax.broadcasted_iota(jnp.int32, (count, width), 0) % SUB // per
    wide = jnp.concatenate(
        [jnp.where(group == part, turned[:, :width], 0.0) for part in range(SUB // per)], axis=1
    ).astype(jnp.bfloat16)
    output = jnp.dot(wide, values, preferred_element_type=jnp.float32)
    return output + jnp.dot(
        turned[:, width:].astype(jnp.bfloat16), fresh_v, preferred_element_type=jnp.float32
    )


def gather_heads(output, heads, slots, width):
    group_size = heads // slots
    slot_of_lane = lax.broadcasted_iota(jnp.int32, (SUB, width), 1) // HEAD
    blocks = []
    for block in range(heads // slots):
        merged = None
        for slot in range(slots):
            head = block * slots + slot
            home = head // group_size
            piece = output[head * SUB : (head + 1) * SUB]
            if slot != home:
                piece = pltpu.roll(piece, ((slot - home) * HEAD) % width, 1)
            merged = piece if merged is None else jnp.where(slot_of_lane == slot, piece, merged)
        blocks.append(merged)
    return jnp.concatenate(blocks, axis=-1)


def attend(first, lengths_ref, q_ref, nk_ref, nv_ref, k_ref, v_ref, att_ref, ready):
    width = nk_ref.shape[1]
    slots = width // HEAD
    heads = q_ref.shape[1] // HEAD
    cache_len = k_ref.shape[1]
    per = width // cache_len
    request = lax.broadcasted_iota(jnp.int32, (1, heads * SUB), 1) % SUB
    batches = range(0, att_ref.shape[0], SUB)
    scores = []
    for at in batches:
        step = at // STEP * STEP
        if at == step:
            ready(at)
            queries = q_ref[step : step + STEP].astype(jnp.float32) * (1.0 / math.sqrt(HEAD))
        rows = place_heads(queries[at - step : at - step + SUB], heads, slots, width)
        keys = k_ref[at : at + SUB].reshape(SUB * cache_len, width)
        scores.append(score(rows, keys, nk_ref[step : step + STEP], cache_len))
    turned = []
    for at, (cached, fresh) in zip(batches, scores):
        live = jnp.zeros(request.shape, jnp.int32)
        for i in range(SUB):
            live = jnp.where(request == i, lengths_ref[first + at + i], live)
        turned.append(soften(cached, fresh, live, at % STEP, per))
    outputs = []
    for at, probs in zip(batches, turned):
        step = at // STEP * STEP
        values = v_ref[at : at + SUB].reshape(SUB * cache_len, width)
        outputs.append(weigh(probs, values, nv_ref[step : step + STEP], per))
    for step in range(0, att_ref.shape[0], STEP):
        pair = outputs[step // SUB : (step + STEP) // SUB]
        att_ref[step : step + STEP, :] = jnp.concatenate(
            [gather_heads(output, heads, slots, width) for output in pair], axis=0
        ).astype(jnp.bfloat16)


def project(att_ref, w_ref, out_ref):
    turned = lax.dot_general(
        w_ref[...], att_ref[...], ACROSS, preferred_element_type=jnp.float32
    )
    out_ref[...] = turned.T


def first_kernel(
    core_ref, chip_ref, lengths_hbm, q_hbm, nk_hbm, nv_hbm, k_hbm, v_hbm, w_hbm,
    out_ref, w_ref, own_k, own_v, lengths_ref, q_ref, nk_ref, nv_ref, k_ref, v_ref, att_ref, sems,
):
    rows = out_ref.shape[0]
    theirs = pl.multiple_of((1 - core_ref[0]) * rows, rows)
    mine = pl.multiple_of(core_ref[0] * rows, rows)
    copies = []

    def bring(source, target):
        copy = pltpu.make_async_copy(source, target, sems.at[len(copies)])
        copy.start()
        copies.append(copy)
        return copy

    small = [bring(lengths_hbm, lengths_ref)] + [
        bring(source.at[pl.ds(theirs, rows)], target)
        for source, target in ((q_hbm, q_ref), (nk_hbm, nk_ref), (nv_hbm, nv_ref))
    ]
    cache = []
    for at in range(0, rows, STEP):
        span = pl.ds(theirs + at, STEP)
        cache.append(
            (
                bring(k_hbm.at[span], k_ref.at[pl.ds(at, STEP)]),
                bring(v_hbm.at[span], v_ref.at[pl.ds(at, STEP)]),
            )
        )
    pieces = 4
    columns = w_ref.shape[0]
    size = -(-columns // pieces // 16) * 16
    weights = []
    for at in range(0, columns, size):
        span = pl.ds(at, min(size, columns - at))
        weights.append(bring(w_hbm.at[span], w_ref.at[span]))
    later = [
        bring(k_hbm.at[pl.ds(mine, rows)], own_k),
        bring(v_hbm.at[pl.ds(mine, rows)], own_v),
    ]
    for copy in small:
        copy.wait()

    def ready(at):
        for copy in cache[at // STEP]:
            copy.wait()

    attend(theirs, lengths_ref, q_ref, nk_ref, nv_ref, k_ref, v_ref, att_ref, ready)
    for copy in weights:
        copy.wait()
    project(att_ref, w_ref, out_ref)
    for copy in later:
        copy.wait()


def second_kernel(
    core_ref, lengths_ref, q_ref, nk_ref, nv_ref, k_ref, v_ref, w_ref, down_hbm,
    out_ref, down_ref, att_ref, sem,
):
    copy = pltpu.make_async_copy(down_hbm.at[0], down_ref, sem)
    copy.start()
    rows = out_ref.shape[0]
    mine = pl.multiple_of(core_ref[0] * rows, rows)
    own = [ref.at[pl.ds(mine, rows)] for ref in (q_ref, nk_ref, nv_ref)]
    attend(mine, lengths_ref, *own, k_ref, v_ref, att_ref, lambda at: None)
    project(att_ref, w_ref, out_ref)
    copy.wait()


def attend_theirs(
    core, rows, lengths, query, new_key, new_value, cache_keys, cache_values, w, chip
):
    cache = (rows,) + cache_keys.shape[1:]
    columns = w.shape[0]
    smem = pl.BlockSpec(memory_space=pltpu.SMEM)
    vmem = pl.BlockSpec(memory_space=pltpu.VMEM)
    hbm = pl.BlockSpec(memory_space=pltpu.HBM)
    copies = 4 + 2 * (rows // STEP) + 4 + 2
    return pl.pallas_call(
        first_kernel,
        out_shape=(
            jax.ShapeDtypeStruct((rows, columns), jnp.float32),
            jax.ShapeDtypeStruct(w.shape, jnp.bfloat16),
            jax.ShapeDtypeStruct(cache, jnp.bfloat16),
            jax.ShapeDtypeStruct(cache, jnp.bfloat16),
        ),
        in_specs=[smem] * 2 + [hbm] * 7,
        out_specs=[vmem] * 4,
        scratch_shapes=[
            pltpu.SMEM(lengths.shape, jnp.int32),
            pltpu.VMEM((rows, query.shape[1]), jnp.bfloat16),
            pltpu.VMEM((rows, new_key.shape[1]), jnp.bfloat16),
            pltpu.VMEM((rows, new_key.shape[1]), jnp.bfloat16),
            pltpu.VMEM(cache, jnp.bfloat16),
            pltpu.VMEM(cache, jnp.bfloat16),
            pltpu.VMEM((rows, query.shape[1]), jnp.bfloat16),
            pltpu.SemaphoreType.DMA((copies,)),
        ],
        compiler_params=pltpu.CompilerParams(vmem_limit_bytes=GRANT),
        cost_estimate=pl.CostEstimate(
            flops=2 * rows * w.size, bytes_accessed=2 * w.size, transcendentals=0
        ),
    )(
        core,
        chip,
        *(
            pltpu.with_memory_space_constraint(x, pltpu.HBM)
            for x in (lengths, query, new_key, new_value, cache_keys, cache_values, w)
        ),
    )


def attend_mine(core, rows, lengths, query, new_key, new_value, own_keys, own_values, w, down):
    smem = pl.BlockSpec(memory_space=pltpu.SMEM)
    vmem = pl.BlockSpec(memory_space=pltpu.VMEM)
    return pl.pallas_call(
        second_kernel,
        out_shape=(
            jax.ShapeDtypeStruct((rows, w.shape[0]), jnp.float32),
            jax.ShapeDtypeStruct(down.shape[1:], jnp.bfloat16),
        ),
        in_specs=[smem, smem] + [vmem] * 6 + [pl.BlockSpec(memory_space=pltpu.HBM)],
        out_specs=[vmem] * 2,
        scratch_shapes=[
            pltpu.VMEM((rows, query.shape[1]), jnp.bfloat16),
            pltpu.SemaphoreType.DMA,
        ],
        compiler_params=pltpu.CompilerParams(vmem_limit_bytes=GRANT),
        cost_estimate=pl.CostEstimate(
            flops=2 * rows * w.size, bytes_accessed=2 * w.size, transcendentals=0
        ),
    )(
        core,
        lengths,
        query,
        new_key,
        new_value,
        own_keys,
        own_values,
        w,
        pltpu.with_memory_space_constraint(down, pltpu.HBM),
    )


def norm_kernel(
    mine_ref, swapped_ref, residual_ref, gain_ref, router_ref, routes_ref, hidden_ref, payload_ref
):
    hidden = residual_ref[...].astype(jnp.float32) + (mine_ref[...] + swapped_ref[...])
    hidden_ref[...] = hidden
    rows, width = hidden.shape
    mean_square = jnp.sum(hidden * hidden, axis=-1, keepdims=True) * (1.0 / width)
    normed = (hidden * lax.rsqrt(mean_square + 1e-05) * gain_ref[...]).astype(jnp.bfloat16)
    payload_ref[:, :width] = normed
    rest = router_ref[...]
    experts = rest.shape[0]
    terms = []
    for _ in range(3):
        term = rest.astype(jnp.bfloat16).astype(jnp.float32)
        terms.append(term)
        rest = rest - term
    parts = lax.dot_general(
        jnp.concatenate(terms, axis=0).astype(jnp.bfloat16),
        normed,
        (((1,), (1,)), ((), ())),
        preferred_element_type=jnp.float32,
    )
    logits = parts[:experts] + parts[experts : 2 * experts] + parts[2 * experts :]
    number = lax.broadcasted_iota(jnp.int32, (experts, rows), 0)
    chosen = number == routes_ref[0:1, :]
    for k in range(1, routes_ref.shape[0]):
        chosen = chosen | (number == routes_ref[k : k + 1, :])
    squashed = jnp.where(chosen, 1.0 / (1.0 + jnp.exp(-logits)), 0.0)
    gates = squashed / jnp.sum(squashed, axis=0, keepdims=True)
    upper = gates.astype(jnp.bfloat16).astype(jnp.float32)
    both = jnp.concatenate([upper, gates - upper], axis=0).astype(jnp.bfloat16)
    tail = payload_ref.shape[1] - width
    place = lax.broadcasted_iota(jnp.int32, (2 * experts, tail), 0)
    lane = lax.broadcasted_iota(jnp.int32, (2 * experts, tail), 1)
    placed = lax.dot_general(
        both,
        (place == lane).astype(jnp.bfloat16),
        (((0,), (0,)), ((), ())),
        preferred_element_type=jnp.float32,
    )
    payload_ref[:, width:] = placed.astype(jnp.bfloat16)


def norm_route(mine, swapped, residual, norm_gain, router, routes):
    rows, width = residual.shape
    experts = router.shape[1]
    wide = -(-(width + 2 * experts) // 128) * 128
    return pl.pallas_call(
        norm_kernel,
        out_shape=(
            jax.ShapeDtypeStruct((rows, width), jnp.float32),
            jax.ShapeDtypeStruct((rows, wide), jnp.bfloat16),
        ),
        compiler_params=pltpu.CompilerParams(vmem_limit_bytes=GRANT),
    )(mine, swapped, residual, norm_gain[None, :], router.T, routes.T)


def expert_kernel(count, experts, chip_ref, *refs):
    blocks, refs = refs[:count], refs[count:]
    gate_ref, up_ref, down_ref = refs[:3]
    outs, act_ref = refs[3:-1], refs[-1]
    _, hidden, width = gate_ref.shape
    rows = jnp.concatenate([block[...] for block in blocks], axis=0)
    base = width // 128 * 128
    tail = rows[:, base:].astype(jnp.float32)
    lane = lax.broadcasted_iota(jnp.int32, tail.shape, 1) - (width - base)
    named = (lane == chip_ref[0]) | (lane == chip_ref[0] + experts)
    weight = jnp.sum(jnp.where(named, tail, 0.0), axis=-1, keepdims=True)
    turned = rows[:, :width].T
    gate = jnp.dot(gate_ref[0], turned, preferred_element_type=jnp.float32)
    up = jnp.dot(up_ref[0], turned, preferred_element_type=jnp.float32)
    active = (gate / (1.0 + jnp.exp(-gate)) * up).T
    act_ref[...] = (active * weight).astype(jnp.bfloat16)
    for at in range(0, width, 768):
        span = slice(at, min(at + 768, width))
        part = jnp.dot(act_ref[...], down_ref[:, span], preferred_element_type=jnp.float32)
        part = part.astype(jnp.bfloat16)
        first = 0
        for out in outs:
            out[:, span] = part[first : first + out.shape[0]]
            first += out.shape[0]


def run_expert(chip, blocks, gate_t, up_t, down, experts, cost):
    hidden, width = down.shape
    rows = sum(block.shape[0] for block in blocks)
    count = len(blocks)
    vmem = pl.BlockSpec(memory_space=pltpu.VMEM)
    return pl.pallas_call(
        lambda *refs: expert_kernel(count, experts, *refs),
        out_shape=[jax.ShapeDtypeStruct((b.shape[0], width), jnp.bfloat16) for b in blocks],
        in_specs=[pl.BlockSpec(memory_space=pltpu.SMEM)] + [vmem] * (count + 3),
        out_specs=[vmem] * count,
        scratch_shapes=[pltpu.VMEM((rows, hidden), jnp.bfloat16)],
        compiler_params=pltpu.CompilerParams(vmem_limit_bytes=GRANT),
        cost_estimate=pl.CostEstimate(
            flops=6 * cost * rows * hidden * width,
            bytes_accessed=6 * cost * hidden * width,
            transcendentals=0,
        ),
    )(chip, *blocks, gate_t, up_t, down)


def add_kernel(*refs):
    total = refs[0][...].astype(jnp.float32)
    for ref in refs[1:-1]:
        total = total + ref[...].astype(jnp.float32)
    refs[-1][...] = total.astype(refs[-1].dtype)


def add_all(*terms, dtype=jnp.bfloat16):
    return pl.pallas_call(
        add_kernel,
        out_shape=jax.ShapeDtypeStruct(terms[0].shape, dtype),
        compiler_params=pltpu.CompilerParams(vmem_limit_bytes=GRANT),
    )(*terms)


def ring_pairs(chips, cores, cross):
    order = list(range(0, chips, 2)) + list(range(1, chips, 2))[::-1]
    pairs = []
    for p in range(chips):
        for core in range(cores):
            turn = -1 if core % 2 else 1
            to = core ^ 1 if cross else core
            pairs.append((order[p] * cores + core, order[(p + turn) % chips] * cores + to))
    return pairs


def per_device(
    query,
    new_key,
    new_value,
    cache_keys,
    cache_values,
    lengths,
    out_proj,
    residual,
    norm_gain,
    router,
    routes,
    w_gate,
    w_up,
    w_down,
):
    chips, cores = lax.axis_size("att"), lax.axis_size("exp")
    own_rows = residual.shape[0]
    ring = ("att", "exp")

    def send(x, cross=False):
        return lax.ppermute(x, ring, ring_pairs(chips, cores, cross))

    def swap(x):
        return lax.ppermute(x, "exp", [(0, 1), (1, 0)])

    core = jnp.full((1,), lax.axis_index("exp"), jnp.int32)
    chip = jnp.full((1,), lax.axis_index("att"), jnp.int32)
    small = (core, own_rows, lengths, query, new_key, new_value)
    theirs, w_out, own_keys, own_values = attend_theirs(
        *small, cache_keys, cache_values, out_proj.T, chip
    )
    swapped = swap(theirs)
    mine, down = attend_mine(*small, own_keys, own_values, w_out, w_down)
    hidden_state, payload = norm_route(mine, swapped, residual, norm_gain, router, routes)

    experts = router.shape[1]

    far = chips // 2

    def after(value, *earlier):
        return lax.optimization_barrier((value, earlier))[0]

    gate_t, up_t = w_gate.transpose(0, 2, 1), w_up.transpose(0, 2, 1)

    def expert(blocks, cost=5):
        return run_expert(chip, blocks, gate_t, up_t, down, experts, cost)

    x, y = payload, swap(payload)
    done = expert((x, y), cost=1)
    own, own_other = done[0], swap(done[1])
    sums_x, sums_y = [None], [None]
    swapped_y = None
    for k in range(1, far + 1):
        x = send(x)
        if k in (1, far):
            x = after(x, done[0])
        blocks = [x, swap(x)]
        if k > 1:
            blocks += swapped_y
        if k < far:
            y = send(y)
            if k > 1:
                y = after(y, done[0])
            swapped_y = [y, swap(y)]
        if 2 < k < far:
            blocks[1] = after(blocks[1], sums_x[k - 2][1], *([sums_y[k - 2][1]] if k > 3 else []))
        done = expert(blocks)
        sums_x.append((done[1], swap(done[0])))
        if k > 1:
            sums_y.append((done[3], swap(done[2])))

    held = add_all(hidden_state, own, own_other, dtype=jnp.float32)
    back_x, back_y = [], []
    for k in range(far, 0, -1):
        if k < far:
            back_y = [send(add_all(*sums_y[k], *back_y))]
        back_x = [send(add_all(*sums_x[k], *back_x), k == 1)]
    return add_all(held, *back_x, *back_y)


def solution(mesh):
    in_specs = (
        P(("groups", "att"), "exp"),
        P(("groups", "att"), "exp"),
        P(("groups", "att"), "exp"),
        P(("groups", "att"), None, "exp"),
        P(("groups", "att"), None, "exp"),
        P(("groups", "att")),
        P("exp", None),
        P(("groups", "att", "exp"), None),
        P(),
        P(),
        P(("groups", "att", "exp"), None),
        P("att", None, "exp"),
        P("att", None, "exp"),
        P("att", "exp", None),
    )
    out_specs = P(("groups", "att", "exp"), None)
    return jax.shard_map(
        per_device, mesh=mesh, in_specs=in_specs, out_specs=out_specs, check_vma=False
    )
```

```python
import math

import jax
import jax.numpy as jnp
from jax import lax
from jax.experimental import pallas as pl
from jax.experimental.pallas import tpu as pltpu
from jax.sharding import PartitionSpec as P

HEAD = 64
SUB = 8
STEP = 16
GRANT = 12 * 1024 * 1024
ACROSS = (((1,), (1,)), ((), ()))


def place_heads(queries, heads, slots, width):
    group_size = heads // slots
    slot_of_lane = lax.broadcasted_iota(jnp.int32, (SUB, width), 1) // HEAD
    pieces = []
    for head in range(heads):
        block, slot, home = head // slots, head % slots, head // group_size
        piece = queries[:, block * width : (block + 1) * width]
        if slot != home:
            piece = pltpu.roll(piece, ((home - slot) * HEAD) % width, 1)
        pieces.append(jnp.where(slot_of_lane == home, piece, 0.0))
    return jnp.concatenate(pieces, axis=0).astype(jnp.bfloat16)


def score(rows, keys, fresh_k, cache_len):
    request = lax.broadcasted_iota(jnp.int32, (cache_len, rows.shape[0]), 1) % SUB
    spread = lax.dot_general(keys, rows, ACROSS, preferred_element_type=jnp.float32)
    scores = spread[:cache_len]
    for r in range(1, SUB):
        scores = jnp.where(request == r, spread[r * cache_len : (r + 1) * cache_len], scores)
    return scores, lax.dot_general(fresh_k, rows, ACROSS, preferred_element_type=jnp.float32)


def soften(scores, fresh, live, offset, per):
    cache_len, count = scores.shape
    request = lax.broadcasted_iota(jnp.int32, (cache_len, count), 1) % SUB
    place = lax.broadcasted_iota(jnp.int32, (cache_len, count), 0)
    scores = jnp.where(place < live, scores, -1e30)
    fresh_place = lax.broadcasted_iota(jnp.int32, fresh.shape, 0)
    fresh_own = fresh_place == offset + lax.broadcasted_iota(jnp.int32, fresh.shape, 1) % SUB
    fresh_scores = jnp.sum(jnp.where(fresh_own, fresh, 0.0), axis=0, keepdims=True)
    highest = jnp.maximum(jnp.max(scores, axis=0, keepdims=True), fresh_scores)
    cached_exp = jnp.exp(scores - highest)
    fresh_exp = jnp.exp(fresh_scores - highest)
    scale = 1.0 / (jnp.sum(cached_exp, axis=0, keepdims=True) + fresh_exp)
    probs = cached_exp * scale
    fresh_probs = jnp.where(fresh_own, fresh_exp * scale, 0.0)
    return jnp.concatenate(
        [jnp.where(request % per == i, probs, 0.0) for i in range(per)] + [fresh_probs], axis=0
    ).T


def weigh(turned, values, fresh_v, per):
    count, width = turned.shape[0], values.shape[1]
    group = lax.broadcasted_iota(jnp.int32, (count, width), 0) % SUB // per
    wide = jnp.concatenate(
        [jnp.where(group == part, turned[:, :width], 0.0) for part in range(SUB // per)], axis=1
    ).astype(jnp.bfloat16)
    output = jnp.dot(wide, values, preferred_element_type=jnp.float32)
    return output + jnp.dot(
        turned[:, width:].astype(jnp.bfloat16), fresh_v, preferred_element_type=jnp.float32
    )


def gather_heads(output, heads, slots, width):
    group_size = heads // slots
    slot_of_lane = lax.broadcasted_iota(jnp.int32, (SUB, width), 1) // HEAD
    blocks = []
    for block in range(heads // slots):
        merged = None
        for slot in range(slots):
            head = block * slots + slot
            home = head // group_size
            piece = output[head * SUB : (head + 1) * SUB]
            if slot != home:
                piece = pltpu.roll(piece, ((slot - home) * HEAD) % width, 1)
            merged = piece if merged is None else jnp.where(slot_of_lane == slot, piece, merged)
        blocks.append(merged)
    return jnp.concatenate(blocks, axis=-1)


def attend(first, lengths_ref, q_ref, nk_ref, nv_ref, k_ref, v_ref, att_ref, ready):
    width = nk_ref.shape[1]
    slots = width // HEAD
    heads = q_ref.shape[1] // HEAD
    cache_len = k_ref.shape[1]
    per = width // cache_len
    request = lax.broadcasted_iota(jnp.int32, (1, heads * SUB), 1) % SUB
    batches = range(0, att_ref.shape[0], SUB)
    scores = []
    for at in batches:
        step = at // STEP * STEP
        if at == step:
            ready(at)
            queries = q_ref[step : step + STEP].astype(jnp.float32) * (1.0 / math.sqrt(HEAD))
        rows = place_heads(queries[at - step : at - step + SUB], heads, slots, width)
        keys = k_ref[at : at + SUB].reshape(SUB * cache_len, width)
        scores.append(score(rows, keys, nk_ref[step : step + STEP], cache_len))
    turned = []
    for at, (cached, fresh) in zip(batches, scores):
        live = jnp.zeros(request.shape, jnp.int32)
        for i in range(SUB):
            live = jnp.where(request == i, lengths_ref[first + at + i], live)
        turned.append(soften(cached, fresh, live, at % STEP, per))
    outputs = []
    for at, probs in zip(batches, turned):
        step = at // STEP * STEP
        values = v_ref[at : at + SUB].reshape(SUB * cache_len, width)
        outputs.append(weigh(probs, values, nv_ref[step : step + STEP], per))
    for step in range(0, att_ref.shape[0], STEP):
        pair = outputs[step // SUB : (step + STEP) // SUB]
        att_ref[step : step + STEP, :] = jnp.concatenate(
            [gather_heads(output, heads, slots, width) for output in pair], axis=0
        ).astype(jnp.bfloat16)


def project(att_ref, w_ref, out_ref):
    turned = lax.dot_general(
        w_ref[...], att_ref[...], ACROSS, preferred_element_type=jnp.float32
    )
    out_ref[...] = turned.T


def first_kernel(
    core_ref, chip_ref, lengths_hbm, q_hbm, nk_hbm, nv_hbm, k_hbm, v_hbm, w_hbm,
    out_ref, w_ref, own_k, own_v, lengths_ref, q_ref, nk_ref, nv_ref, k_ref, v_ref, att_ref, sems,
):
    rows = out_ref.shape[0]
    theirs = pl.multiple_of((1 - core_ref[0]) * rows, rows)
    mine = pl.multiple_of(core_ref[0] * rows, rows)
    copies = []

    def bring(source, target):
        copy = pltpu.make_async_copy(source, target, sems.at[len(copies)])
        copy.start()
        copies.append(copy)
        return copy

    small = [bring(lengths_hbm, lengths_ref)] + [
        bring(source.at[pl.ds(theirs, rows)], target)
        for source, target in ((q_hbm, q_ref), (nk_hbm, nk_ref), (nv_hbm, nv_ref))
    ]
    cache = []
    for at in range(0, rows, STEP):
        span = pl.ds(theirs + at, STEP)
        cache.append(
            (
                bring(k_hbm.at[span], k_ref.at[pl.ds(at, STEP)]),
                bring(v_hbm.at[span], v_ref.at[pl.ds(at, STEP)]),
            )
        )
    pieces = 4
    columns = w_ref.shape[0]
    size = -(-columns // pieces // 16) * 16
    weights = []
    for at in range(0, columns, size):
        span = pl.ds(at, min(size, columns - at))
        weights.append(bring(w_hbm.at[span], w_ref.at[span]))
    later = [
        bring(k_hbm.at[pl.ds(mine, rows)], own_k),
        bring(v_hbm.at[pl.ds(mine, rows)], own_v),
    ]
    for copy in small:
        copy.wait()

    def ready(at):
        for copy in cache[at // STEP]:
            copy.wait()

    attend(theirs, lengths_ref, q_ref, nk_ref, nv_ref, k_ref, v_ref, att_ref, ready)
    for copy in weights:
        copy.wait()
    project(att_ref, w_ref, out_ref)
    for copy in later:
        copy.wait()


def second_kernel(
    core_ref, lengths_ref, q_ref, nk_ref, nv_ref, k_ref, v_ref, w_ref, out_ref, att_ref
):
    rows = out_ref.shape[0]
    mine = pl.multiple_of(core_ref[0] * rows, rows)
    own = [ref.at[pl.ds(mine, rows)] for ref in (q_ref, nk_ref, nv_ref)]
    attend(mine, lengths_ref, *own, k_ref, v_ref, att_ref, lambda at: None)
    project(att_ref, w_ref, out_ref)


def attend_theirs(
    core, rows, lengths, query, new_key, new_value, cache_keys, cache_values, w, chip
):
    cache = (rows,) + cache_keys.shape[1:]
    columns = w.shape[0]
    smem = pl.BlockSpec(memory_space=pltpu.SMEM)
    vmem = pl.BlockSpec(memory_space=pltpu.VMEM)
    hbm = pl.BlockSpec(memory_space=pltpu.HBM)
    copies = 4 + 2 * (rows // STEP) + 4 + 2
    return pl.pallas_call(
        first_kernel,
        out_shape=(
            jax.ShapeDtypeStruct((rows, columns), jnp.float32),
            jax.ShapeDtypeStruct(w.shape, jnp.bfloat16),
            jax.ShapeDtypeStruct(cache, jnp.bfloat16),
            jax.ShapeDtypeStruct(cache, jnp.bfloat16),
        ),
        in_specs=[smem] * 2 + [hbm] * 7,
        out_specs=[vmem] * 4,
        scratch_shapes=[
            pltpu.SMEM(lengths.shape, jnp.int32),
            pltpu.VMEM((rows, query.shape[1]), jnp.bfloat16),
            pltpu.VMEM((rows, new_key.shape[1]), jnp.bfloat16),
            pltpu.VMEM((rows, new_key.shape[1]), jnp.bfloat16),
            pltpu.VMEM(cache, jnp.bfloat16),
            pltpu.VMEM(cache, jnp.bfloat16),
            pltpu.VMEM((rows, query.shape[1]), jnp.bfloat16),
            pltpu.SemaphoreType.DMA((copies,)),
        ],
        compiler_params=pltpu.CompilerParams(vmem_limit_bytes=GRANT),
        cost_estimate=pl.CostEstimate(
            flops=2 * rows * w.size, bytes_accessed=2 * w.size, transcendentals=0
        ),
    )(
        core,
        chip,
        *(
            pltpu.with_memory_space_constraint(x, pltpu.HBM)
            for x in (lengths, query, new_key, new_value, cache_keys, cache_values, w)
        ),
    )


def attend_mine(core, rows, lengths, query, new_key, new_value, own_keys, own_values, w):
    smem = pl.BlockSpec(memory_space=pltpu.SMEM)
    vmem = pl.BlockSpec(memory_space=pltpu.VMEM)
    return pl.pallas_call(
        second_kernel,
        out_shape=jax.ShapeDtypeStruct((rows, w.shape[0]), jnp.float32),
        in_specs=[smem, smem] + [vmem] * 6,
        out_specs=vmem,
        scratch_shapes=[pltpu.VMEM((rows, query.shape[1]), jnp.bfloat16)],
        compiler_params=pltpu.CompilerParams(vmem_limit_bytes=GRANT),
        cost_estimate=pl.CostEstimate(
            flops=2 * rows * w.size, bytes_accessed=2 * w.size, transcendentals=0
        ),
    )(core, lengths, query, new_key, new_value, own_keys, own_values, w)


def norm_kernel(
    mine_ref, swapped_ref, residual_ref, gain_ref, router_ref, routes_ref, hidden_ref, payload_ref
):
    hidden = residual_ref[...].astype(jnp.float32) + (mine_ref[...] + swapped_ref[...])
    hidden_ref[...] = hidden
    rows, width = hidden.shape
    mean_square = jnp.sum(hidden * hidden, axis=-1, keepdims=True) * (1.0 / width)
    normed = (hidden * lax.rsqrt(mean_square + 1e-05) * gain_ref[...]).astype(jnp.bfloat16)
    payload_ref[:, :width] = normed
    rest = router_ref[...]
    experts = rest.shape[0]
    terms = []
    for _ in range(3):
        term = rest.astype(jnp.bfloat16).astype(jnp.float32)
        terms.append(term)
        rest = rest - term
    parts = lax.dot_general(
        jnp.concatenate(terms, axis=0).astype(jnp.bfloat16),
        normed,
        (((1,), (1,)), ((), ())),
        preferred_element_type=jnp.float32,
    )
    logits = parts[:experts] + parts[experts : 2 * experts] + parts[2 * experts :]
    number = lax.broadcasted_iota(jnp.int32, (experts, rows), 0)
    chosen = number == routes_ref[0:1, :]
    for k in range(1, routes_ref.shape[0]):
        chosen = chosen | (number == routes_ref[k : k + 1, :])
    squashed = jnp.where(chosen, 1.0 / (1.0 + jnp.exp(-logits)), 0.0)
    gates = squashed / jnp.sum(squashed, axis=0, keepdims=True)
    upper = gates.astype(jnp.bfloat16).astype(jnp.float32)
    both = jnp.concatenate([upper, gates - upper], axis=0).astype(jnp.bfloat16)
    tail = payload_ref.shape[1] - width
    place = lax.broadcasted_iota(jnp.int32, (2 * experts, tail), 0)
    lane = lax.broadcasted_iota(jnp.int32, (2 * experts, tail), 1)
    placed = lax.dot_general(
        both,
        (place == lane).astype(jnp.bfloat16),
        (((0,), (0,)), ((), ())),
        preferred_element_type=jnp.float32,
    )
    payload_ref[:, width:] = placed.astype(jnp.bfloat16)


def norm_route(mine, swapped, residual, norm_gain, router, routes):
    rows, width = residual.shape
    experts = router.shape[1]
    wide = -(-(width + 2 * experts) // 128) * 128
    return pl.pallas_call(
        norm_kernel,
        out_shape=(
            jax.ShapeDtypeStruct((rows, width), jnp.float32),
            jax.ShapeDtypeStruct((rows, wide), jnp.bfloat16),
        ),
        compiler_params=pltpu.CompilerParams(vmem_limit_bytes=GRANT),
    )(mine, swapped, residual, norm_gain[None, :], router.T, routes.T)


def expert_kernel(count, experts, chip_ref, *refs):
    blocks, refs = refs[:count], refs[count:]
    gate_ref, up_ref, down_ref = refs[:3]
    outs, act_ref = refs[3:-1], refs[-1]
    _, hidden, width = gate_ref.shape
    rows = jnp.concatenate([block[...] for block in blocks], axis=0)
    base = width // 128 * 128
    tail = rows[:, base:].astype(jnp.float32)
    lane = lax.broadcasted_iota(jnp.int32, tail.shape, 1) - (width - base)
    named = (lane == chip_ref[0]) | (lane == chip_ref[0] + experts)
    weight = jnp.sum(jnp.where(named, tail, 0.0), axis=-1, keepdims=True)
    turned = rows[:, :width].T
    gate = jnp.dot(gate_ref[0], turned, preferred_element_type=jnp.float32)
    up = jnp.dot(up_ref[0], turned, preferred_element_type=jnp.float32)
    act_ref[...] = (gate / (1.0 + jnp.exp(-gate)) * up).T.astype(jnp.bfloat16)
    for at in range(0, width, 768):
        span = slice(at, min(at + 768, width))
        part = jnp.dot(act_ref[...], down_ref[0, :, span], preferred_element_type=jnp.float32)
        part = (part * weight).astype(jnp.bfloat16)
        first = 0
        for out in outs:
            out[:, span] = part[first : first + out.shape[0]]
            first += out.shape[0]


def run_expert(chip, blocks, gate_t, up_t, down, experts, cost):
    _, hidden, width = down.shape
    rows = sum(block.shape[0] for block in blocks)
    count = len(blocks)
    vmem = pl.BlockSpec(memory_space=pltpu.VMEM)
    return pl.pallas_call(
        lambda *refs: expert_kernel(count, experts, *refs),
        out_shape=[jax.ShapeDtypeStruct((b.shape[0], width), jnp.bfloat16) for b in blocks],
        in_specs=[pl.BlockSpec(memory_space=pltpu.SMEM)] + [vmem] * (count + 3),
        out_specs=[vmem] * count,
        scratch_shapes=[pltpu.VMEM((rows, hidden), jnp.bfloat16)],
        compiler_params=pltpu.CompilerParams(vmem_limit_bytes=GRANT),
        cost_estimate=pl.CostEstimate(
            flops=6 * cost * rows * hidden * width,
            bytes_accessed=6 * cost * hidden * width,
            transcendentals=0,
        ),
    )(chip, *blocks, gate_t, up_t, down)


def add_kernel(*refs):
    total = refs[0][...].astype(jnp.float32)
    for ref in refs[1:-1]:
        total = total + ref[...].astype(jnp.float32)
    refs[-1][...] = total.astype(refs[-1].dtype)


def add_all(*terms, dtype=jnp.bfloat16):
    return pl.pallas_call(
        add_kernel,
        out_shape=jax.ShapeDtypeStruct(terms[0].shape, dtype),
        compiler_params=pltpu.CompilerParams(vmem_limit_bytes=GRANT),
    )(*terms)


def ring_pairs(chips, cores, cross):
    order = list(range(0, chips, 2)) + list(range(1, chips, 2))[::-1]
    pairs = []
    for p in range(chips):
        for core in range(cores):
            turn = -1 if core % 2 else 1
            to = core ^ 1 if cross else core
            pairs.append((order[p] * cores + core, order[(p + turn) % chips] * cores + to))
    return pairs


def per_device(
    query,
    new_key,
    new_value,
    cache_keys,
    cache_values,
    lengths,
    out_proj,
    residual,
    norm_gain,
    router,
    routes,
    w_gate,
    w_up,
    w_down,
):
    chips, cores = lax.axis_size("att"), lax.axis_size("exp")
    own_rows = residual.shape[0]
    ring = ("att", "exp")

    def send(x, cross=False):
        return lax.ppermute(x, ring, ring_pairs(chips, cores, cross))

    def swap(x):
        return lax.ppermute(x, "exp", [(0, 1), (1, 0)])

    core = jnp.full((1,), lax.axis_index("exp"), jnp.int32)
    chip = jnp.full((1,), lax.axis_index("att"), jnp.int32)
    small = (core, own_rows, lengths, query, new_key, new_value)
    theirs, w_out, own_keys, own_values = attend_theirs(
        *small, cache_keys, cache_values, out_proj.T, chip
    )
    swapped = swap(theirs)
    mine = attend_mine(*small, own_keys, own_values, w_out)
    hidden_state, payload = norm_route(mine, swapped, residual, norm_gain, router, routes)

    experts = router.shape[1]

    far = chips // 2

    def after(value, *earlier):
        return lax.optimization_barrier((value, earlier))[0]

    gate_t, up_t = w_gate.transpose(0, 2, 1), w_up.transpose(0, 2, 1)

    def expert(blocks, cost=5):
        return run_expert(chip, blocks, gate_t, up_t, w_down, experts, cost)

    x, y = payload, swap(payload)
    done = expert((x, y), cost=1)
    own, own_other = done[0], swap(done[1])
    sums_x, sums_y = [None], [None]
    for k in range(1, far + 1):
        x = send(x)
        if k in (1, far):
            x = after(x, done[0])
        blocks = [x, swap(x)]
        if k < far:
            y = send(y)
            if k > 1:
                y = after(y, done[0])
            swapped_y = [y, swap(y)]
        if k != far - 1:
            blocks += swapped_y
        done = expert(blocks)
        sums_x.append((done[1], swap(done[0])))
        if k != far - 1:
            sums_y.append((done[3], swap(done[2])))

    held = add_all(hidden_state, own, own_other, dtype=jnp.float32)
    back_x, back_y = [], []
    for k in range(far, 0, -1):
        if k < far:
            back_y = [send(add_all(*sums_y[k], *back_y))]
        back_x = [send(add_all(*sums_x[k], *back_x), k == 1)]
    return add_all(held, *back_x, *back_y)


def solution(mesh):
    in_specs = (
        P(("groups", "att"), "exp"),
        P(("groups", "att"), "exp"),
        P(("groups", "att"), "exp"),
        P(("groups", "att"), None, "exp"),
        P(("groups", "att"), None, "exp"),
        P(("groups", "att")),
        P("exp", None),
        P(("groups", "att", "exp"), None),
        P(),
        P(),
        P(("groups", "att", "exp"), None),
        P("att", None, "exp"),
        P("att", None, "exp"),
        P("att", "exp", None),
    )
    out_specs = P(("groups", "att", "exp"), None)
    return jax.shard_map(
        per_device, mesh=mesh, in_specs=in_specs, out_specs=out_specs, check_vma=False
    )
```

```python
import math

import jax
import jax.numpy as jnp
from jax import lax
from jax.experimental import pallas as pl
from jax.experimental.pallas import tpu as pltpu
from jax.sharding import PartitionSpec as P

HEAD = 64
SUB = 8
STEP = 16
GRANT = 12 * 1024 * 1024
ACROSS = (((1,), (1,)), ((), ()))


def place_heads(queries, heads, slots, width):
    group_size = heads // slots
    slot_of_lane = lax.broadcasted_iota(jnp.int32, (SUB, width), 1) // HEAD
    pieces = []
    for head in range(heads):
        block, slot, home = head // slots, head % slots, head // group_size
        piece = queries[:, block * width : (block + 1) * width]
        if slot != home:
            piece = pltpu.roll(piece, ((home - slot) * HEAD) % width, 1)
        pieces.append(jnp.where(slot_of_lane == home, piece, 0.0))
    return jnp.concatenate(pieces, axis=0).astype(jnp.bfloat16)


def score(rows, keys, fresh_k, cache_len):
    request = lax.broadcasted_iota(jnp.int32, (cache_len, rows.shape[0]), 1) % SUB
    spread = lax.dot_general(keys, rows, ACROSS, preferred_element_type=jnp.float32)
    scores = spread[:cache_len]
    for r in range(1, SUB):
        scores = jnp.where(request == r, spread[r * cache_len : (r + 1) * cache_len], scores)
    return scores, lax.dot_general(fresh_k, rows, ACROSS, preferred_element_type=jnp.float32)


def soften(scores, fresh, live, offset, per):
    cache_len, count = scores.shape
    request = lax.broadcasted_iota(jnp.int32, (cache_len, count), 1) % SUB
    place = lax.broadcasted_iota(jnp.int32, (cache_len, count), 0)
    scores = jnp.where(place < live, scores, -1e30)
    fresh_place = lax.broadcasted_iota(jnp.int32, fresh.shape, 0)
    fresh_own = fresh_place == offset + lax.broadcasted_iota(jnp.int32, fresh.shape, 1) % SUB
    fresh_scores = jnp.sum(jnp.where(fresh_own, fresh, 0.0), axis=0, keepdims=True)
    highest = jnp.maximum(jnp.max(scores, axis=0, keepdims=True), fresh_scores)
    cached_exp = jnp.exp(scores - highest)
    fresh_exp = jnp.exp(fresh_scores - highest)
    scale = 1.0 / (jnp.sum(cached_exp, axis=0, keepdims=True) + fresh_exp)
    probs = cached_exp * scale
    fresh_probs = jnp.where(fresh_own, fresh_exp * scale, 0.0)
    return jnp.concatenate(
        [jnp.where(request % per == i, probs, 0.0) for i in range(per)] + [fresh_probs], axis=0
    ).T


def weigh(turned, values, fresh_v, per):
    count, width = turned.shape[0], values.shape[1]
    group = lax.broadcasted_iota(jnp.int32, (count, width), 0) % SUB // per
    wide = jnp.concatenate(
        [jnp.where(group == part, turned[:, :width], 0.0) for part in range(SUB // per)], axis=1
    ).astype(jnp.bfloat16)
    output = jnp.dot(wide, values, preferred_element_type=jnp.float32)
    return output + jnp.dot(
        turned[:, width:].astype(jnp.bfloat16), fresh_v, preferred_element_type=jnp.float32
    )


def gather_heads(output, heads, slots, width):
    group_size = heads // slots
    slot_of_lane = lax.broadcasted_iota(jnp.int32, (SUB, width), 1) // HEAD
    blocks = []
    for block in range(heads // slots):
        merged = None
        for slot in range(slots):
            head = block * slots + slot
            home = head // group_size
            piece = output[head * SUB : (head + 1) * SUB]
            if slot != home:
                piece = pltpu.roll(piece, ((slot - home) * HEAD) % width, 1)
            merged = piece if merged is None else jnp.where(slot_of_lane == slot, piece, merged)
        blocks.append(merged)
    return jnp.concatenate(blocks, axis=-1)


def attend(
    first, lengths_ref, q_ref, nk_ref, nv_ref, k_ref, v_ref, att_ref, keys_ready, values_ready
):
    width = nk_ref.shape[1]
    slots = width // HEAD
    heads = q_ref.shape[1] // HEAD
    cache_len = k_ref.shape[1]
    per = width // cache_len
    request = lax.broadcasted_iota(jnp.int32, (1, heads * SUB), 1) % SUB
    batches = range(0, att_ref.shape[0], SUB)
    scores = []
    for at in batches:
        step = at // STEP * STEP
        if at == step:
            keys_ready(at)
            queries = q_ref[step : step + STEP].astype(jnp.float32) * (1.0 / math.sqrt(HEAD))
        rows = place_heads(queries[at - step : at - step + SUB], heads, slots, width)
        keys = k_ref[at : at + SUB].reshape(SUB * cache_len, width)
        scores.append(score(rows, keys, nk_ref[step : step + STEP], cache_len))
    turned = []
    for at, (cached, fresh) in zip(batches, scores):
        live = jnp.zeros(request.shape, jnp.int32)
        for i in range(SUB):
            live = jnp.where(request == i, lengths_ref[first + at + i], live)
        turned.append(soften(cached, fresh, live, at % STEP, per))
    outputs = []
    for at, probs in zip(batches, turned):
        step = at // STEP * STEP
        if at == step:
            values_ready(at)
        values = v_ref[at : at + SUB].reshape(SUB * cache_len, width)
        outputs.append(weigh(probs, values, nv_ref[step : step + STEP], per))
    for step in range(0, att_ref.shape[0], STEP):
        pair = outputs[step // SUB : (step + STEP) // SUB]
        att_ref[step : step + STEP, :] = jnp.concatenate(
            [gather_heads(output, heads, slots, width) for output in pair], axis=0
        ).astype(jnp.bfloat16)


def project(att_ref, w_ref, out_ref):
    turned = lax.dot_general(
        w_ref[...], att_ref[...], ACROSS, preferred_element_type=jnp.float32
    )
    out_ref[...] = turned.T


def first_kernel(
    core_ref, chip_ref, lengths_hbm, q_hbm, nk_hbm, nv_hbm, k_hbm, v_hbm, w_hbm,
    out_ref, w_ref, own_k, own_v, lengths_ref, q_ref, nk_ref, nv_ref, k_ref, v_ref, att_ref, sems,
):
    rows = out_ref.shape[0]
    theirs = pl.multiple_of((1 - core_ref[0]) * rows, rows)
    mine = pl.multiple_of(core_ref[0] * rows, rows)
    copies = []

    def bring(source, target):
        copy = pltpu.make_async_copy(source, target, sems.at[len(copies)])
        copy.start()
        copies.append(copy)
        return copy

    small = [bring(lengths_hbm, lengths_ref)] + [
        bring(source.at[pl.ds(theirs, rows)], target)
        for source, target in ((q_hbm, q_ref), (nk_hbm, nk_ref), (nv_hbm, nv_ref))
    ]
    steps = range(0, rows, STEP)
    keys = [
        bring(k_hbm.at[pl.ds(theirs + at, STEP)], k_ref.at[pl.ds(at, STEP)]) for at in steps
    ]
    values = [
        bring(v_hbm.at[pl.ds(theirs + at, STEP)], v_ref.at[pl.ds(at, STEP)]) for at in steps
    ]
    pieces = 4
    columns = w_ref.shape[0]
    size = -(-columns // pieces // 16) * 16
    weights = []
    for at in range(0, columns, size):
        span = pl.ds(at, min(size, columns - at))
        weights.append(bring(w_hbm.at[span], w_ref.at[span]))
    later = [
        bring(k_hbm.at[pl.ds(mine, rows)], own_k),
        bring(v_hbm.at[pl.ds(mine, rows)], own_v),
    ]
    for copy in small:
        copy.wait()

    attend(
        theirs, lengths_ref, q_ref, nk_ref, nv_ref, k_ref, v_ref, att_ref,
        lambda at: keys[at // STEP].wait(),
        lambda at: values[at // STEP].wait(),
    )
    for copy in weights:
        copy.wait()
    project(att_ref, w_ref, out_ref)
    for copy in later:
        copy.wait()


def second_kernel(
    core_ref, lengths_ref, q_ref, nk_ref, nv_ref, k_ref, v_ref, w_ref, out_ref, att_ref
):
    rows = out_ref.shape[0]
    mine = pl.multiple_of(core_ref[0] * rows, rows)
    own = [ref.at[pl.ds(mine, rows)] for ref in (q_ref, nk_ref, nv_ref)]
    attend(mine, lengths_ref, *own, k_ref, v_ref, att_ref, lambda at: None, lambda at: None)
    project(att_ref, w_ref, out_ref)


def attend_theirs(
    core, rows, lengths, query, new_key, new_value, cache_keys, cache_values, w, chip
):
    cache = (rows,) + cache_keys.shape[1:]
    columns = w.shape[0]
    smem = pl.BlockSpec(memory_space=pltpu.SMEM)
    vmem = pl.BlockSpec(memory_space=pltpu.VMEM)
    hbm = pl.BlockSpec(memory_space=pltpu.HBM)
    copies = 4 + 2 * (rows // STEP) + 4 + 2
    return pl.pallas_call(
        first_kernel,
        out_shape=(
            jax.ShapeDtypeStruct((rows, columns), jnp.float32),
            jax.ShapeDtypeStruct(w.shape, jnp.bfloat16),
            jax.ShapeDtypeStruct(cache, jnp.bfloat16),
            jax.ShapeDtypeStruct(cache, jnp.bfloat16),
        ),
        in_specs=[smem] * 2 + [hbm] * 7,
        out_specs=[vmem] * 4,
        scratch_shapes=[
            pltpu.SMEM(lengths.shape, jnp.int32),
            pltpu.VMEM((rows, query.shape[1]), jnp.bfloat16),
            pltpu.VMEM((rows, new_key.shape[1]), jnp.bfloat16),
            pltpu.VMEM((rows, new_key.shape[1]), jnp.bfloat16),
            pltpu.VMEM(cache, jnp.bfloat16),
            pltpu.VMEM(cache, jnp.bfloat16),
            pltpu.VMEM((rows, query.shape[1]), jnp.bfloat16),
            pltpu.SemaphoreType.DMA((copies,)),
        ],
        compiler_params=pltpu.CompilerParams(vmem_limit_bytes=GRANT),
        cost_estimate=pl.CostEstimate(
            flops=2 * rows * w.size, bytes_accessed=2 * w.size, transcendentals=0
        ),
    )(
        core,
        chip,
        *(
            pltpu.with_memory_space_constraint(x, pltpu.HBM)
            for x in (lengths, query, new_key, new_value, cache_keys, cache_values, w)
        ),
    )


def attend_mine(core, rows, lengths, query, new_key, new_value, own_keys, own_values, w):
    smem = pl.BlockSpec(memory_space=pltpu.SMEM)
    vmem = pl.BlockSpec(memory_space=pltpu.VMEM)
    return pl.pallas_call(
        second_kernel,
        out_shape=jax.ShapeDtypeStruct((rows, w.shape[0]), jnp.float32),
        in_specs=[smem, smem] + [vmem] * 6,
        out_specs=vmem,
        scratch_shapes=[pltpu.VMEM((rows, query.shape[1]), jnp.bfloat16)],
        compiler_params=pltpu.CompilerParams(vmem_limit_bytes=GRANT),
        cost_estimate=pl.CostEstimate(
            flops=2 * rows * w.size, bytes_accessed=2 * w.size, transcendentals=0
        ),
    )(core, lengths, query, new_key, new_value, own_keys, own_values, w)


def norm_kernel(
    mine_ref, swapped_ref, residual_ref, gain_ref, router_ref, routes_ref, hidden_ref, payload_ref
):
    hidden = residual_ref[...].astype(jnp.float32) + (mine_ref[...] + swapped_ref[...])
    hidden_ref[...] = hidden
    rows, width = hidden.shape
    mean_square = jnp.sum(hidden * hidden, axis=-1, keepdims=True) * (1.0 / width)
    normed = (hidden * lax.rsqrt(mean_square + 1e-05) * gain_ref[...]).astype(jnp.bfloat16)
    payload_ref[:, :width] = normed
    rest = router_ref[...]
    experts = rest.shape[0]
    terms = []
    for _ in range(3):
        term = rest.astype(jnp.bfloat16).astype(jnp.float32)
        terms.append(term)
        rest = rest - term
    parts = lax.dot_general(
        jnp.concatenate(terms, axis=0).astype(jnp.bfloat16),
        normed,
        (((1,), (1,)), ((), ())),
        preferred_element_type=jnp.float32,
    )
    logits = parts[:experts] + parts[experts : 2 * experts] + parts[2 * experts :]
    number = lax.broadcasted_iota(jnp.int32, (experts, rows), 0)
    chosen = number == routes_ref[0:1, :]
    for k in range(1, routes_ref.shape[0]):
        chosen = chosen | (number == routes_ref[k : k + 1, :])
    squashed = jnp.where(chosen, 1.0 / (1.0 + jnp.exp(-logits)), 0.0)
    gates = squashed / jnp.sum(squashed, axis=0, keepdims=True)
    upper = gates.astype(jnp.bfloat16).astype(jnp.float32)
    both = jnp.concatenate([upper, gates - upper], axis=0).astype(jnp.bfloat16)
    tail = payload_ref.shape[1] - width
    place = lax.broadcasted_iota(jnp.int32, (2 * experts, tail), 0)
    lane = lax.broadcasted_iota(jnp.int32, (2 * experts, tail), 1)
    placed = lax.dot_general(
        both,
        (place == lane).astype(jnp.bfloat16),
        (((0,), (0,)), ((), ())),
        preferred_element_type=jnp.float32,
    )
    payload_ref[:, width:] = placed.astype(jnp.bfloat16)


def norm_route(mine, swapped, residual, norm_gain, router, routes):
    rows, width = residual.shape
    experts = router.shape[1]
    wide = -(-(width + 2 * experts) // 128) * 128
    return pl.pallas_call(
        norm_kernel,
        out_shape=(
            jax.ShapeDtypeStruct((rows, width), jnp.float32),
            jax.ShapeDtypeStruct((rows, wide), jnp.bfloat16),
        ),
        compiler_params=pltpu.CompilerParams(vmem_limit_bytes=GRANT),
    )(mine, swapped, residual, norm_gain[None, :], router.T, routes.T)


def expert_kernel(count, experts, chip_ref, *refs):
    blocks, refs = refs[:count], refs[count:]
    gate_ref, up_ref, down_ref = refs[:3]
    outs, act_ref = refs[3:-1], refs[-1]
    _, hidden, width = gate_ref.shape
    rows = jnp.concatenate([block[...] for block in blocks], axis=0)
    base = width // 128 * 128
    tail = rows[:, base:].astype(jnp.float32)
    lane = lax.broadcasted_iota(jnp.int32, tail.shape, 1) - (width - base)
    named = (lane == chip_ref[0]) | (lane == chip_ref[0] + experts)
    weight = jnp.sum(jnp.where(named, tail, 0.0), axis=-1, keepdims=True)
    turned = rows[:, :width].T
    gate = jnp.dot(gate_ref[0], turned, preferred_element_type=jnp.float32)
    up = jnp.dot(up_ref[0], turned, preferred_element_type=jnp.float32)
    act_ref[...] = (gate / (1.0 + jnp.exp(-gate)) * up).T.astype(jnp.bfloat16)
    for at in range(0, width, 768):
        span = slice(at, min(at + 768, width))
        part = jnp.dot(act_ref[...], down_ref[0, :, span], preferred_element_type=jnp.float32)
        part = (part * weight).astype(jnp.bfloat16)
        first = 0
        for out in outs:
            out[:, span] = part[first : first + out.shape[0]]
            first += out.shape[0]


def run_expert(chip, blocks, gate_t, up_t, down, experts, cost):
    _, hidden, width = down.shape
    rows = sum(block.shape[0] for block in blocks)
    count = len(blocks)
    vmem = pl.BlockSpec(memory_space=pltpu.VMEM)
    return pl.pallas_call(
        lambda *refs: expert_kernel(count, experts, *refs),
        out_shape=[jax.ShapeDtypeStruct((b.shape[0], width), jnp.bfloat16) for b in blocks],
        in_specs=[pl.BlockSpec(memory_space=pltpu.SMEM)] + [vmem] * (count + 3),
        out_specs=[vmem] * count,
        scratch_shapes=[pltpu.VMEM((rows, hidden), jnp.bfloat16)],
        compiler_params=pltpu.CompilerParams(vmem_limit_bytes=GRANT),
        cost_estimate=pl.CostEstimate(
            flops=6 * cost * rows * hidden * width,
            bytes_accessed=6 * cost * hidden * width,
            transcendentals=0,
        ),
    )(chip, *blocks, gate_t, up_t, down)


def add_kernel(firsts, *refs):
    size = refs[-1].shape[0]
    total = None
    for first, ref in zip(firsts, refs):
        term = ref[first : first + size].astype(jnp.float32)
        total = term if total is None else total + term
    refs[-1][...] = total.astype(refs[-1].dtype)


def add_rows(size, *parts, dtype=jnp.bfloat16):
    firsts = [first for _, first in parts]
    width = parts[0][0].shape[1]
    return pl.pallas_call(
        lambda *refs: add_kernel(firsts, *refs),
        out_shape=jax.ShapeDtypeStruct((size, width), dtype),
        compiler_params=pltpu.CompilerParams(vmem_limit_bytes=GRANT),
    )(*[array for array, _ in parts])


def add_all(*terms, dtype=jnp.bfloat16):
    return add_rows(terms[0].shape[0], *[(term, 0) for term in terms], dtype=dtype)


def finish_kernel(*refs):
    *whole, top, low, top_y, low_y, out = refs
    first = 0
    for half, half_y in ((top, top_y), (low, low_y)):
        size = half.shape[0]
        total = half[...].astype(jnp.float32) + half_y[...].astype(jnp.float32)
        for ref in whole:
            total = total + ref[first : first + size].astype(jnp.float32)
        out[first : first + size, :] = total.astype(out.dtype)
        first += size


def finish(*arrays):
    return pl.pallas_call(
        finish_kernel,
        out_shape=jax.ShapeDtypeStruct(arrays[0].shape, jnp.bfloat16),
        compiler_params=pltpu.CompilerParams(vmem_limit_bytes=GRANT),
    )(*arrays)


def ring_pairs(chips, cores, cross):
    order = list(range(0, chips, 2)) + list(range(1, chips, 2))[::-1]
    pairs = []
    for p in range(chips):
        for core in range(cores):
            turn = -1 if core % 2 else 1
            to = core ^ 1 if cross else core
            pairs.append((order[p] * cores + core, order[(p + turn) % chips] * cores + to))
    return pairs


def per_device(
    query,
    new_key,
    new_value,
    cache_keys,
    cache_values,
    lengths,
    out_proj,
    residual,
    norm_gain,
    router,
    routes,
    w_gate,
    w_up,
    w_down,
):
    chips, cores = lax.axis_size("att"), lax.axis_size("exp")
    own_rows = residual.shape[0]
    ring = ("att", "exp")

    def send(x, cross=False):
        return lax.ppermute(x, ring, ring_pairs(chips, cores, cross))

    def swap(x):
        return lax.ppermute(x, "exp", [(0, 1), (1, 0)])

    core = jnp.full((1,), lax.axis_index("exp"), jnp.int32)
    chip = jnp.full((1,), lax.axis_index("att"), jnp.int32)
    small = (core, own_rows, lengths, query, new_key, new_value)
    theirs, w_out, own_keys, own_values = attend_theirs(
        *small, cache_keys, cache_values, out_proj.T, chip
    )
    swapped = swap(theirs)
    mine = attend_mine(*small, own_keys, own_values, w_out)
    hidden_state, payload = norm_route(mine, swapped, residual, norm_gain, router, routes)

    experts = router.shape[1]

    far = chips // 2

    def after(value, *earlier):
        return lax.optimization_barrier((value, earlier))[0]

    gate_t, up_t = w_gate.transpose(0, 2, 1), w_up.transpose(0, 2, 1)

    def expert(blocks, cost=5):
        return run_expert(chip, blocks, gate_t, up_t, w_down, experts, cost)

    x, y = payload, swap(payload)
    done = expert((x, y), cost=1)
    own, own_other = done[0], swap(done[1])
    sums_x, sums_y = [None], [None]
    for k in range(1, far + 1):
        x = send(x)
        if k in (1, far):
            x = after(x, done[0])
        blocks = [x, swap(x)]
        if k < far:
            y = send(y)
            if k > 1:
                y = after(y, done[0])
            swapped_y = [y, swap(y)]
        if k != far - 1:
            blocks += swapped_y
        done = expert(blocks)
        sums_x.append((done[1], swap(done[0])))
        if k != far - 1:
            sums_y.append((done[3], swap(done[2])))

    held = add_all(hidden_state, own, own_other, dtype=jnp.float32)
    middle = own_rows // 2
    back_x, back_y = [[], []], [[], []]
    for k in range(far, 0, -1):
        for half in (0, 1):
            mine_x = [(term, half * middle) for term in sums_x[k]] + back_x[half]
            back_x[half] = [(send(add_rows(middle, *mine_x), k == 1), 0)]
            if k < far:
                mine_y = [(term, half * middle) for term in sums_y[k]] + back_y[half]
                back_y[half] = [(send(add_rows(middle, *mine_y)), 0)]
    return finish(held, *[half[0][0] for half in back_x + back_y])


def solution(mesh):
    in_specs = (
        P(("groups", "att"), "exp"),
        P(("groups", "att"), "exp"),
        P(("groups", "att"), "exp"),
        P(("groups", "att"), None, "exp"),
        P(("groups", "att"), None, "exp"),
        P(("groups", "att")),
        P("exp", None),
        P(("groups", "att", "exp"), None),
        P(),
        P(),
        P(("groups", "att", "exp"), None),
        P("att", None, "exp"),
        P("att", None, "exp"),
        P("att", "exp", None),
    )
    out_specs = P(("groups", "att", "exp"), None)
    return jax.shard_map(
        per_device, mesh=mesh, in_specs=in_specs, out_specs=out_specs, check_vma=False
    )
```
